128 devices in a mesh: section: 2 (over y_hi), dp: 16 (over y_lo, z, core), tensor: 4 (over x).
Axes of the slice: x: 4, y: 4 (y_hi: 2, y_lo: 2; y = y_hi * 2 + y_lo), z: 4, core: 2. Of those that a mesh axis runs over, the one named last changes fastest.
Arguments:
- words: bfloat16 [2, 128, 20, 768], P('section', 'dp'), may hold values from -6 to 6
- regions: bfloat16 [2, 128, 36, 768], P('section', 'dp'), may hold values from -6 to 6
- word_lengths: int32 [128], P('dp'), may hold values from 3 to 20, as said below
- task_flags: int32 [128], P('dp'), may hold values from 0 to 2
- attn_qkv: bfloat16 [2, 2, 768, 3, 768], P('section', None, None, None, 'tensor'), may hold values from -0.21875 to 0.21875
- attn_qv_bias: float32 [2, 2, 2, 12, 64], P('section', None, None, 'tensor'), may hold values from -3 to 3
- attn_out: bfloat16 [2, 2, 768, 768], P('section', None, 'tensor'), may hold values from -0.875 to 0.875
- ffn_in: bfloat16 [2, 2, 768, 3072], P('section', None, None, 'tensor'), may hold values from -0.21875 to 0.21875
- ffn_in_bias: float32 [2, 2, 24, 128], P('section', None, 'tensor'), may hold values from -3 to 3
- ffn_out: bfloat16 [2, 2, 3072, 768], P('section', None, 'tensor'), may hold values from -0.109375 to 0.109375
- out_bias: float32 [2, 2, 2, 768], P('section'), may hold values from -2 to 2
- norm_gain: float32 [2, 2, 2, 768], P('section'), may hold values from 0.5 to 1.5
- norm_bias: float32 [2, 2, 2, 768], P('section'), may hold values from -2 to 2
- cross_qkv: bfloat16 [768, 3, 768], P(None, None, 'tensor'), may hold values from -0.21875 to 0.21875
- cross_qv_bias: float32 [2, 12, 64], P(None, 'tensor'), may hold values from -3 to 3
- cross_out: bfloat16 [768, 768], P('tensor'), may hold values from -0.875 to 0.875
- cross_out_bias: float32 [768], replicated, may hold values from -2 to 2
- cross_norm_gain: float32 [768], replicated, may hold values from 0.5 to 1.5
- cross_norm_bias: float32 [768], replicated, may hold values from -2 to 2
Outputs:
- words_out: float32 [2, 128, 20, 768], P('section', 'dp')
- regions_out: float32 [2, 128, 36, 768], P('section', 'dp')
- attn_qkv_grad: float32 [2, 2, 768, 3, 768], P('section', None, 'dp', None, 'tensor')
- attn_qv_bias_grad: float32 [2, 2, 2, 12, 64], P('section', None, None, 'tensor', 'dp')
- attn_out_grad: float32 [2, 2, 768, 768], P('section', None, 'tensor', 'dp')
- ffn_in_grad: float32 [2, 2, 768, 3072], P('section', None, 'dp', 'tensor')
- ffn_in_bias_grad: float32 [2, 2, 24, 128], P('section', None, 'tensor', 'dp')
- ffn_out_grad: float32 [2, 2, 3072, 768], P('section', None, 'tensor', 'dp')
- out_bias_grad: float32 [2, 2, 2, 768], P('section', None, None, 'dp')
- norm_gain_grad: float32 [2, 2, 2, 768], P('section', None, None, 'dp')
- norm_bias_grad: float32 [2, 2, 2, 768], P('section', None, None, 'dp')
- cross_qkv_grad: float32 [768, 3, 768], P(('section', 'dp'), None, 'tensor')
- cross_qv_bias_grad: float32 [2, 12, 64], P(None, 'tensor', ('section', 'dp'))
- cross_out_grad: float32 [768, 768], P('tensor', ('section', 'dp'))
- cross_out_bias_grad: float32 [768], P(('section', 'dp'))
- cross_norm_gain_grad: float32 [768], P(('section', 'dp'))
- cross_norm_bias_grad: float32 [768], P(('section', 'dp'))
The draws below stay inside these ranges and needn't reach their ends.
Inputs may be any that keep to these rules, and one draw needn't show every extreme that they name: `word_lengths`: valid words of an item, counted from its first word; some item has 20. `task_flags`: 0 masked words, 1 masked regions, 2 matching or answering.
All inputs are finite; a program needn't handle non-finite values.
Results may differ from the reference program's by a relative error of at most 0.035.
Values may be sent and summed in bfloat16 or wider, within the bound.
A program may use at most 384 MiB of HBM per device.

```python
import jax
import jax.numpy as jnp
from jax import lax

D = 768
HEADS = 12
HEAD_DIM = 64
FF = 3072
BIAS_COLS = 128
WORDS = 20
REGIONS = 36
ITEMS = 128
N_DP = 16


def draw_word_lengths(key, part):
    lengths = jax.random.randint(jax.random.fold_in(key, 1), (ITEMS,), 3, WORDS + 1)
    chosen = jax.random.randint(jax.random.fold_in(key, 2), (), 0, ITEMS)
    return jnp.where(jnp.arange(ITEMS) == chosen, WORDS, lengths).astype(jnp.int32)


def plant(drawn, rng, smallest, high):
    index_at = [jax.random.randint(jax.random.fold_in(rng, axis), (), 0, length) for axis, length in enumerate(drawn.shape)]
    longest = drawn.shape.index(max(drawn.shape))
    beside = index_at[:longest] + [(index_at[longest] + 1) % drawn.shape[longest]] + index_at[longest + 1:]
    return drawn.at[tuple(index_at)].set(smallest).at[tuple(beside)].set(high)


def shard_levels(rng, dims, cuts, least, top_value):
    def one(axis_at, parts):
        heights = jax.random.uniform(jax.random.fold_in(jax.random.fold_in(rng, 6), axis_at), (parts,), jnp.float32, least / len(cuts), top_value / len(cuts))
        return jnp.repeat(jnp.exp(heights), dims[axis_at] // parts).reshape((-1,) + (1,) * (len(dims) - axis_at - 1))

    loudness = one(*cuts[0])
    for cut in cuts[1:]:
        loudness = loudness * one(*cut)
    return loudness


def bell_draw(rng, dims, scale, most, split=(), held_as=jnp.bfloat16):
    drawn = scale * jax.random.normal(rng, dims, jnp.float32)
    if split:
        drawn = drawn * shard_levels(rng, dims, split, -0.22, 0.18)
    return jnp.clip(drawn, -most, most).astype(held_as)


def setup_inputs(seed: int = 0) -> dict:
    key_of = jax.random.split(jax.random.key(seed), 20)
    words = bell_draw(key_of[0], (2, ITEMS, WORDS, D), 1.0, 6.0, ((0, 2), (1, 16)))
    regions = bell_draw(key_of[1], (2, ITEMS, REGIONS, D), 1.0, 6.0, ((0, 2), (1, 16)))
    word_lengths = draw_word_lengths(jax.random.fold_in(key_of[19], 71), 0)
    task_flags = plant(jax.random.randint(key_of[3], (ITEMS,), 0, 3), jax.random.fold_in(key_of[3], 1), 0, 2).astype(jnp.int32)
    attn_qkv = bell_draw(key_of[4], (2, 2, D, 3, D), D ** -0.5, 0.21875, ((0, 2), (4, 4)))
    attn_qv_bias = bell_draw(key_of[5], (2, 2, 2, HEADS, HEAD_DIM), 0.5, 3.0, ((0, 2), (3, 4)), jnp.float32)
    attn_out = bell_draw(key_of[6], (2, 2, D, D), (D // 16) ** -0.5, 0.875, ((0, 2), (2, 4)))
    ffn_in = bell_draw(key_of[7], (2, 2, D, FF), D ** -0.5, 0.21875, ((0, 2), (3, 4)))
    ffn_in_bias = bell_draw(key_of[8], (2, 2, FF // BIAS_COLS, BIAS_COLS), 0.5, 3.0, ((0, 2), (2, 4)), jnp.float32)
    ffn_out = bell_draw(key_of[9], (2, 2, FF, D), FF ** -0.5, 0.109375, ((0, 2), (2, 4)))
    out_bias = bell_draw(key_of[10], (2, 2, 2, D), 0.3, 2.0, ((0, 2),), jnp.float32)
    norm_gain = jnp.clip(1.0 + 0.1 * jax.random.normal(key_of[11], (2, 2, 2, D), jnp.float32), 0.5, 1.5)
    norm_bias = bell_draw(key_of[12], (2, 2, 2, D), 0.3, 2.0, ((0, 2),), jnp.float32)
    cross_qkv = bell_draw(key_of[13], (D, 3, D), D ** -0.5, 0.21875, ((2, 4),))
    cross_qv_bias = bell_draw(key_of[14], (2, HEADS, HEAD_DIM), 0.5, 3.0, ((1, 4),), jnp.float32)
    cross_out = bell_draw(key_of[15], (D, D), (D // 16) ** -0.5, 0.875, ((0, 4),))
    cross_out_bias = bell_draw(key_of[16], (D,), 0.3, 2.0, (), jnp.float32)
    cross_norm_gain = jnp.clip(1.0 + 0.1 * jax.random.normal(key_of[17], (D,), jnp.float32), 0.5, 1.5)
    cross_norm_bias = bell_draw(key_of[18], (D,), 0.3, 2.0, (), jnp.float32)
    return dict(words=words, regions=regions, word_lengths=word_lengths, task_flags=task_flags, attn_qkv=attn_qkv, attn_qv_bias=attn_qv_bias, attn_out=attn_out, ffn_in=ffn_in, ffn_in_bias=ffn_in_bias, ffn_out=ffn_out, out_bias=out_bias, norm_gain=norm_gain, norm_bias=norm_bias, cross_qkv=cross_qkv, cross_qv_bias=cross_qv_bias, cross_out=cross_out, cross_out_bias=cross_out_bias, cross_norm_gain=cross_norm_gain, cross_norm_bias=cross_norm_bias)


EPSILON = 1e-06
MASKED_SCORE = -1000000000.0
HIGHEST = lax.Precision.HIGHEST

@jax.custom_vjp
def low(v):
    return lax.optimization_barrier(v.astype(jnp.bfloat16)).astype(jnp.float32)

@jax.custom_vjp
def low_back(v):
    return v

def low_keep(v):
    return (low(v), None)

def low_pass(kept, grad):
    return (grad,)

def back_keep(v):
    return (v, None)

def back_low(kept, grad):
    return (low(grad),)
low.defvjp(low_keep, low_pass)
low_back.defvjp(back_keep, back_low)

def matmul_high(left_op, right_op):
    return jnp.einsum('...i,ij->...j', left_op, right_op, precision=HIGHEST)

def norm_apply(residual, gain_vec, shift_vec):
    center = residual - lax.optimization_barrier(jnp.mean(residual, axis=-1, keepdims=True))
    spread = lax.optimization_barrier(jnp.mean(center * center, axis=-1, keepdims=True))
    return center * lax.rsqrt(spread + EPSILON) * gain_vec + shift_vec

def split_heads(values):
    return values.reshape(values.shape[0], values.shape[1], values.shape[2] // HEAD_DIM, HEAD_DIM)

def attention(query_in, key_in, valid_keys, w_qkv, bias_qv, w_out, bias_out):
    model_width = w_qkv.shape[2]
    scaling = HEAD_DIM ** (-0.5)
    queries = low(low_back(matmul_high(query_in, w_qkv[:, 0]) + bias_qv[0].reshape(model_width)))
    key_rows = low(low_back(matmul_high(key_in, w_qkv[:, 1])))
    values = low(low_back(matmul_high(key_in, w_qkv[:, 2]) + bias_qv[1].reshape(model_width)))
    scores = jnp.einsum('bqhd,bkhd->bhqk', split_heads(queries), split_heads(key_rows), precision=HIGHEST)
    scores = low_back(scores * scaling)
    attn_probs = low(jax.nn.softmax(jnp.where(valid_keys[:, None, None, :], scores, MASKED_SCORE), axis=-1))
    mixed_heads = jnp.einsum('bhqk,bkhd->bqhd', attn_probs, split_heads(values), precision=HIGHEST)
    mixed_heads = low(low_back(mixed_heads.reshape(queries.shape)))
    return low_back(matmul_high(mixed_heads, w_out) + bias_out)

def feed_forward(hidden, w_in, b_in, w_out, b_out):
    inner_act = low_back(matmul_high(low(hidden), w_in) + b_in.reshape(-1))
    active = low(jax.nn.gelu(inner_act, approximate=False))
    return low_back(matmul_high(active, w_out) + b_out)

def layer_block(params, section_index, modality, hidden, valid_keys):
    attn_qkv, attn_qv_bias, attn_out, ffn_in, ffn_in_bias, ffn_out, out_bias, norm_gain, norm_bias = params[:9]
    lowered = low(hidden)
    branch = attention(lowered, lowered, valid_keys, attn_qkv[section_index, modality], attn_qv_bias[section_index, modality], attn_out[section_index, modality], out_bias[section_index, modality, 0])
    middle = norm_apply(hidden + branch, norm_gain[section_index, modality, 0], norm_bias[section_index, modality, 0])
    branch = feed_forward(middle, ffn_in[section_index, modality], ffn_in_bias[section_index, modality], ffn_out[section_index, modality], out_bias[section_index, modality, 1])
    return norm_apply(middle + branch, norm_gain[section_index, modality, 1], norm_bias[section_index, modality, 1])

def two_layers(params, word_in, region_in, lengths):
    word_valid = jnp.arange(WORDS)[None, :] < lengths[:, None]
    region_valid = jnp.ones(region_in.shape[:2], dtype=bool)
    word_mid = layer_block(params, 0, 0, word_in, word_valid)
    region_mid = layer_block(params, 0, 1, region_in, region_valid)
    word_mid = low(low_back(word_mid))
    region_mid = low(low_back(region_mid))
    cross_qkv, cross_qv_bias, cross_out, cross_out_bias, cross_norm_gain, cross_norm_bias = params[9:]
    word_low = low(word_mid)
    region_low = low(region_mid)
    word_cross = norm_apply(word_mid + attention(word_low, region_low, region_valid, cross_qkv, cross_qv_bias, cross_out, cross_out_bias), cross_norm_gain, cross_norm_bias)
    region_cross = norm_apply(region_mid + attention(region_low, word_low, word_valid, cross_qkv, cross_qv_bias, cross_out, cross_out_bias), cross_norm_gain, cross_norm_bias)
    return (layer_block(params, 1, 0, word_cross, word_valid), layer_block(params, 1, 1, region_cross, region_valid))

def reference(words, regions, word_lengths, task_flags, attn_qkv, attn_qv_bias, attn_out, ffn_in, ffn_in_bias, ffn_out, out_bias, norm_gain, norm_bias, cross_qkv, cross_qv_bias, cross_out, cross_out_bias, cross_norm_gain, cross_norm_bias):
    params = tuple((weight.astype(jnp.float32) for weight in (attn_qkv, attn_qv_bias, attn_out, ffn_in, ffn_in_bias, ffn_out, out_bias, norm_gain, norm_bias, cross_qkv, cross_qv_bias, cross_out, cross_out_bias, cross_norm_gain, cross_norm_bias)))
    word_in = words[0].astype(jnp.float32)
    region_in = regions[0].astype(jnp.float32)
    word_scale = jnp.where(task_flags == 1, 0.25, 1.0).astype(jnp.float32)
    region_scale = jnp.where(task_flags == 0, 0.25, 1.0).astype(jnp.float32)
    word_cot = words[1].astype(jnp.float32) * word_scale[:, None, None]
    region_cot = regions[1].astype(jnp.float32) * region_scale[:, None, None]
    groups = word_lengths.reshape(N_DP, -1)

    def forward(weights, word_arg, region_arg):

        def one_group(packed):
            return two_layers(weights, packed[0], packed[1], packed[2])
        outputs = lax.map(jax.checkpoint(one_group), (word_arg.reshape(N_DP, -1, WORDS, D), region_arg.reshape(N_DP, -1, REGIONS, D), groups))
        return (outputs[0].reshape(word_arg.shape), outputs[1].reshape(region_arg.shape))
    (word_out, region_out), pullback = jax.vjp(forward, params, word_in, region_in)
    grad_params, grad_words, grad_regions = pullback((word_cot, region_cot))
    return (jnp.stack([grad_words, word_out]), jnp.stack([grad_regions, region_out]), grad_params[0], grad_params[1], grad_params[2], grad_params[3], grad_params[4], grad_params[5], grad_params[6], grad_params[7], grad_params[8], grad_params[9], grad_params[10], grad_params[11], grad_params[12], grad_params[13], grad_params[14])
```

```python
import functools

import jax
import jax.numpy as jnp
from jax import lax
from jax.experimental import pallas as pl
from jax.experimental.pallas import tpu as pltpu
from jax.sharding import PartitionSpec as P

MESH = pl.DeviceIdType.MESH
BF = jnp.bfloat16
F32 = jnp.float32
HEAD_DIM = 64
LOCAL_HEADS = 3
HW = HEAD_DIM * LOCAL_HEADS
WORDS = 20
REGIONS = 36
D = 768
ITEMS_LOCAL = 8
TENSOR = 4

ITEMS_MB = 2
MB = ITEMS_LOCAL // ITEMS_MB
RW = 48
RR = 80
R = RW + RR
C = R // TENSOR
SPANS = ((0, RW), (RW, R))

EPSILON = 1e-06
MASKED = -1000000000.0
SCALING = HEAD_DIM ** (-0.5)


def dot(a, b):
    return lax.dot_general(a, b, (((1,), (0,)), ((), ())), preferred_element_type=F32)


def dot_nt(a, b):
    return lax.dot_general(a, b, (((1,), (1,)), ((), ())), preferred_element_type=F32)


def dot_tn(a, b):
    return lax.dot_general(a, b, (((0,), (0,)), ((), ())), preferred_element_type=F32)


def head_masks():
    lane = lax.broadcasted_iota(jnp.int32, (1, HW), 1)
    return [
        ((lane >= h * HEAD_DIM) & (lane < (h + 1) * HEAD_DIM)).astype(F32) for h in range(LOCAL_HEADS)
    ]


def by_head(a):
    masks = [m.astype(BF) for m in head_masks()]
    return jnp.concatenate([a * m for m in masks], axis=0)


def join_heads(stacked):
    rows = stacked.shape[0] // LOCAL_HEADS
    masks = head_masks()
    total = stacked[:rows] * masks[0]
    for h in range(1, LOCAL_HEADS):
        total = total + stacked[h * rows : (h + 1) * rows] * masks[h]
    return total


def item_of(shape, axis, length):
    index = lax.broadcasted_iota(jnp.int32, shape, axis)
    item = jnp.zeros(shape, jnp.int32)
    for k in range(1, ITEMS_MB + 1):
        item = item + (index >= k * length).astype(jnp.int32)
    return item


def key_mask(q_rows, q_len, k_rows, k_len, key_valid):
    shape = (q_rows, k_rows)
    same = item_of(shape, 0, q_len) == item_of(shape, 1, k_len)
    inside = lax.broadcasted_iota(jnp.int32, shape, 1) < ITEMS_MB * k_len
    mask = same & inside
    if key_valid is not None:
        mask = mask & (jnp.broadcast_to(key_valid, shape) > 0.5)
    return mask


def attend(q, k, v, mask):
    scores = dot_nt(by_head(q), k) * SCALING
    mask = jnp.concatenate([mask] * LOCAL_HEADS, axis=0)
    scores = jnp.where(mask, scores, MASKED)
    e = jnp.exp(scores - jnp.max(scores, axis=-1, keepdims=True))
    probs = e / jnp.sum(e, axis=-1, keepdims=True)
    mixed = join_heads(dot(probs.astype(BF), v)).astype(BF)
    return probs, mixed


def attend_back(dmix, probs, q, k, v):
    d3 = by_head(dmix)
    dp = dot_nt(d3, v)
    ds = (probs * (dp - jnp.sum(probs * dp, axis=-1, keepdims=True))).astype(BF)
    dv = dot_tn(probs.astype(BF), d3).astype(BF)
    dq = (join_heads(dot(ds, k)) * SCALING).astype(BF)
    dk = (dot_tn(ds, by_head(q)) * SCALING).astype(BF)
    return dq, dk, dv


def norm_forward(r, gain, shift):
    center = r - jnp.mean(r, axis=-1, keepdims=True)
    spread = jnp.mean(center * center, axis=-1, keepdims=True)
    rstd = lax.rsqrt(spread + EPSILON)
    n = center * rstd
    return n, rstd, n * gain + shift


def norm_back(dh, n, rstd, gain):
    dn = dh * gain
    return rstd * (
        dn - jnp.mean(dn, axis=-1, keepdims=True) - n * jnp.mean(dn * n, axis=-1, keepdims=True)
    )


def kernel(
    x_ref, scale_ref, valid_ref, wqkv_ref, bqkv_ref, wo_ref, w1_ref, b1_ref, w2_ref, vec_ref,
    cwqkv_ref, cbqkv_ref, cwo_ref, cvec_ref,
    y_ref, g_ref, s_ref,
    send, recv, xlow, midf, alow, dyf, dya, dyc, ybuf, back,
    qkv, mixed, dqkv, cqkv, cmixed, cdqkv, act, dup, dgelu,
    p_w, p_r, cp_w, cp_r, cur, res, nrm, rstd, acc, rowp, bsum, bqsum,
    rs_send, rs_recv, ag_send, ag_recv, y_send, y_recv, sec_send, sec_recv,
):
    sec = lax.axis_index("section")
    me = lax.axis_index("tensor")
    head = sec == 0
    cross = sec == 1
    own = pl.ds(pl.multiple_of(me * C, C), C)

    def peer(o):
        return {"tensor": lax.rem(me + o, TENSOR)}

    def rows_of(t):
        return pl.ds(pl.multiple_of(t * C, C), C)

    partner = {"section": 1 - sec}

    barrier = pltpu.get_barrier_semaphore()
    for o in range(1, TENSOR):
        pl.semaphore_signal(barrier, inc=1, device_id=peer(o), device_id_type=MESH)
    pl.semaphore_signal(barrier, inc=1, device_id=partner, device_id_type=MESH)

    row = lax.broadcasted_iota(jnp.int32, (C, 1), 0) + me * C
    is_word = row < RW
    for k in range(6):
        rowp[k] = jnp.where(is_word, vec_ref[2 * k : 2 * k + 1, :], vec_ref[2 * k + 1 : 2 * k + 2, :])
    acc[...] = jnp.zeros_like(acc)
    bsum[...] = jnp.zeros_like(bsum)
    bqsum[...] = jnp.zeros_like(bqsum)

    pl.semaphore_wait(barrier, TENSOR)

    def rs_copies(m):
        return [
            pltpu.make_async_remote_copy(
                src_ref=send.at[m, rows_of(lax.rem(me + o, TENSOR))],
                dst_ref=recv.at[m, o - 1],
                send_sem=rs_send.at[m, o - 1],
                recv_sem=rs_recv.at[m, o - 1],
                device_id=peer(o),
                device_id_type=MESH,
            )
            for o in range(1, TENSOR)
        ]

    def rs_start(m):
        for copy in rs_copies(m):
            copy.start()

    def rs_finish(m):
        for copy in rs_copies(m):
            copy.wait()
        total = send[m, own].astype(F32)
        for o in range(TENSOR - 1):
            total = total + recv[m, o].astype(F32)
        return total

    def ag_copies(buf, m, ss, rs):
        return [
            pltpu.make_async_remote_copy(
                src_ref=buf.at[m, own],
                dst_ref=buf.at[m, own],
                send_sem=ss.at[m, o - 1],
                recv_sem=rs.at[m, o - 1],
                device_id=peer(o),
                device_id_type=MESH,
            )
            for o in range(1, TENSOR)
        ]

    def ag_start(buf, m, ss=ag_send, rs=ag_recv):
        for copy in ag_copies(buf, m, ss, rs):
            copy.start()

    def ag_finish(buf, m, ss=ag_send, rs=ag_recv):
        for copy in ag_copies(buf, m, ss, rs):
            copy.wait()

    def sec_copy(buf, m):
        return pltpu.make_async_remote_copy(
            src_ref=buf.at[m, own],
            dst_ref=buf.at[m, own],
            send_sem=sec_send.at[m],
            recv_sem=sec_recv.at[m],
            device_id=partner,
            device_id_type=MESH,
        )

    def save_norm(l, m, n, r):
        nrm[l, m] = n
        rstd[l, m] = jnp.broadcast_to(r, (C, 128))

    def norm_step_back(l, m, dh, gain):
        n = nrm[l, m]
        dr = norm_back(dh, n, rstd[l, m][:, :1], gain)
        low = dr.astype(BF)
        acc[3 * l] += dh * n
        acc[3 * l + 1] += dh
        acc[3 * l + 2] += low.astype(F32)
        res[m] = dr
        return low

    def word_keys(m, q_rows, q_len):
        return key_mask(q_rows, q_len, RW, WORDS, valid_ref[m])

    def region_keys(q_rows, q_len):
        return key_mask(q_rows, q_len, RR, REGIONS, None)

    def cross_a(m):
        sec_copy(midf, m).wait_recv()
        ag_start(midf, m)

    def cross_b(m):
        ag_finish(midf, m)
        out = dot(midf[m], cwqkv_ref[...]) + cbqkv_ref[...]
        out = out.astype(BF)
        q, k, v = out[:, :HW], out[:, HW : 2 * HW], out[:, 2 * HW :]
        cqkv[0, m], cqkv[1, m], cqkv[2, m] = q, k, v
        probs, mix = attend(q[:RW], k[RW:], v[RW:], region_keys(RW, WORDS))
        cp_w[m] = probs
        cmixed[m, :RW] = mix
        probs, mix = attend(q[RW:], k[:RW], v[:RW], word_keys(m, RR, REGIONS))
        cp_r[m] = probs
        cmixed[m, RW:] = mix
        send[m] = dot(cmixed[m], cwo_ref[...]).astype(BF)
        rs_start(m)

    def cross_c(m):
        r = midf[m, own].astype(F32) + rs_finish(m) + cvec_ref[0:1, :]
        n, rs, h = norm_forward(r, cvec_ref[1:2, :], cvec_ref[2:3, :])
        save_norm(2, m, n, rs)
        cur[m] = h
        xlow[m, own] = h.astype(BF)
        ag_start(xlow, m)

    def layer_a(m):
        @pl.when(head)
        def _():
            xlow[m] = x_ref[m]
            cur[m] = x_ref[m, own].astype(F32)

        @pl.when(cross)
        def _():
            ag_finish(xlow, m)

        for mod, (lo, hi) in enumerate(SPANS):
            out = (dot(xlow[m, lo:hi], wqkv_ref[mod]) + bqkv_ref[mod]).astype(BF)
            q, k, v = out[:, :HW], out[:, HW : 2 * HW], out[:, 2 * HW :]
            qkv[0, m, lo:hi], qkv[1, m, lo:hi], qkv[2, m, lo:hi] = q, k, v
            if mod == 0:
                probs, mix = attend(q, k, v, word_keys(m, RW, WORDS))
                p_w[m] = probs
            else:
                probs, mix = attend(q, k, v, region_keys(RR, REGIONS))
                p_r[m] = probs
            mixed[m, lo:hi] = mix
            send[m, lo:hi] = dot(mix, wo_ref[mod]).astype(BF)
        rs_start(m)

    def layer_b(m):
        r = cur[m] + rs_finish(m) + rowp[0]
        n, rs, h = norm_forward(r, rowp[2], rowp[4])
        save_norm(0, m, n, rs)
        cur[m] = h
        alow[m, own] = h.astype(BF)
        ag_start(alow, m)

    def layer_c(m):
        ag_finish(alow, m)
        for mod, (lo, hi) in enumerate(SPANS):
            up = dot(alow[m, lo:hi], w1_ref[mod]) + b1_ref[mod]
            cdf = 0.5 * (1.0 + lax.erf(up * (0.5**0.5)))
            dgelu[m, lo:hi] = cdf + up * jnp.exp(-0.5 * up * up) * 0.3989422804014327
            active = (up * cdf).astype(BF)
            act[m, lo:hi] = active
            send[m, lo:hi] = dot(active, w2_ref[mod]).astype(BF)
        rs_start(m)

    def layer_d(m):
        r = cur[m] + rs_finish(m) + rowp[1]
        n, rs, h = norm_forward(r, rowp[3], rowp[5])
        save_norm(1, m, n, rs)
        return h

    def back_e(m, dh):
        low = norm_step_back(1, m, dh, rowp[3])
        dyf[m, own] = low
        ag_start(dyf, m)

    def back_f(m):
        ag_finish(dyf, m)
        for mod, (lo, hi) in enumerate(SPANS):
            d = (dot_nt(dyf[m, lo:hi], w2_ref[mod]) * dgelu[m, lo:hi]).astype(BF)
            dup[m, lo:hi] = d
            bsum[mod] += jnp.sum(d.astype(F32), axis=0, keepdims=True)
            send[m, lo:hi] = dot_nt(d, w1_ref[mod]).astype(BF)
        rs_start(m)

    def back_g(m):
        dh = res[m] + rs_finish(m)
        low = norm_step_back(0, m, dh, rowp[2])
        dya[m, own] = low
        ag_start(dya, m)

    def back_h(m):
        ag_finish(dya, m)
        for mod, (lo, hi) in enumerate(SPANS):
            dmix = dot_nt(dya[m, lo:hi], wo_ref[mod]).astype(BF)
            probs = p_w[m] if mod == 0 else p_r[m]
            parts = attend_back(
                dmix, probs, qkv[0, m, lo:hi], qkv[1, m, lo:hi], qkv[2, m, lo:hi]
            )
            d = jnp.concatenate(parts, axis=1)
            dqkv[m, lo:hi] = d
            bqsum[mod] += jnp.sum(d.astype(F32), axis=0, keepdims=True)
            send[m, lo:hi] = dot_nt(d, wqkv_ref[mod]).astype(BF)
        rs_start(m)

    def cross_back_a(m):
        dh = res[m] + rs_finish(m)
        low = norm_step_back(2, m, dh, cvec_ref[1:2, :])
        dyc[m, own] = low
        ag_start(dyc, m)

    def cross_back_b(m):
        ag_finish(dyc, m)
        dmix = dot_nt(dyc[m], cwo_ref[...]).astype(BF)
        q, k, v = cqkv[0, m], cqkv[1, m], cqkv[2, m]
        dq_w, dk_r, dv_r = attend_back(dmix[:RW], cp_w[m], q[:RW], k[RW:], v[RW:])
        dq_r, dk_w, dv_w = attend_back(dmix[RW:], cp_r[m], q[RW:], k[:RW], v[:RW])
        cdqkv[m, :RW] = jnp.concatenate([dq_w, dk_w, dv_w], axis=1)
        cdqkv[m, RW:] = jnp.concatenate([dq_r, dk_r, dv_r], axis=1)
        d = cdqkv[m]
        bqsum[2] += jnp.sum(d.astype(F32), axis=0, keepdims=True)
        send[m] = dot_nt(d, cwqkv_ref[...]).astype(BF)
        rs_start(m)

    def cross_back_c(m):
        back[m, own] = (res[m] + rs_finish(m)).astype(BF)
        sec_copy(back, m).start()

    def outer(left, right, lo, hi, store):
        def tile(j):
            columns = pl.ds(pl.multiple_of(j * (D // 2), D // 2), D // 2)
            a = left[:, lo:hi, columns].reshape(MB * (hi - lo), D // 2)
            b = right[:, lo:hi, :].reshape(MB * (hi - lo), right.shape[-1])
            store(j, dot_tn(a, b).astype(BF))

        pl.loop(0, 2)(tile)

    def store_at(block, lo, hi):
        def store(j, value):
            g_ref[block, j, :, :, :, lo:hi] = value.reshape(4, 2, 48, hi - lo)

        return store

    def ffn_outer():
        for mod, (lo, hi) in enumerate(SPANS):
            outer(alow, dup, lo, hi, store_at(2 + 2 * mod, 0, D))
            outer(dyf, act, lo, hi, store_at(3 + 2 * mod, 0, D))

    def attn_outer():
        for mod, (lo, hi) in enumerate(SPANS):
            outer(xlow, dqkv, lo, hi, store_at(mod, 0, 3 * HW))
            outer(dya, mixed, lo, hi, store_at(mod, 3 * HW, D))

    def cross_outer():
        outer(midf, cdqkv, 0, R, store_at(6, 0, 3 * HW))
        outer(dyc, cmixed, 0, R, store_at(6, 3 * HW, D))

    def each(*steps):
        def body(m):
            for step in steps:
                step(m)

        pl.loop(0, MB)(body)

    @pl.when(cross)
    def _():
        each(cross_a)
        each(cross_b)
        each(cross_c)

    each(layer_a)
    each(layer_b)
    each(layer_c)

    @pl.when(head)
    def _():
        def to_partner(m):
            midf[m, own] = layer_d(m).astype(BF)
            sec_copy(midf, m).start()

        def from_partner(m):
            sec_copy(midf, m).wait_send()
            sec_copy(back, m).wait_recv()
            back_e(m, back[m, own].astype(F32))

        each(to_partner)
        each(from_partner)

    @pl.when(cross)
    def _():
        def turn(m):
            h = layer_d(m)
            back_e(m, x_ref[m, own].astype(F32) * scale_ref[m, own])
            ybuf[m, own] = h.astype(BF)
            ag_start(ybuf, m, y_send, y_recv)

        each(turn)

    each(back_f)
    each(back_g)
    each(back_h)

    @pl.when(head)
    def _():
        def last(m):
            ybuf[m, own] = (res[m] + rs_finish(m)).astype(BF)
            ag_start(ybuf, m, y_send, y_recv)

        each(last)
        g_ref[6] = jnp.zeros(g_ref.shape[1:], BF)

    @pl.when(cross)
    def _():
        each(cross_back_a)
        each(cross_back_b)
        each(cross_back_c)
        cross_outer()

    ffn_outer()
    attn_outer()

    def write(m):
        ag_finish(ybuf, m, y_send, y_recv)
        y_ref[m] = ybuf[m]

    each(write)

    @pl.when(cross)
    def _():
        each(lambda m: sec_copy(back, m).wait_send())

    s_ref[...] = jnp.zeros_like(s_ref)
    for l in range(2):
        for k in range(3):
            a = acc[3 * l + k]
            at = 2 * (3 * l + k)
            s_ref[at : at + 1, :] = jnp.sum(jnp.where(is_word, a, 0.0), axis=0, keepdims=True)
            s_ref[at + 1 : at + 2, :] = jnp.sum(jnp.where(is_word, 0.0, a), axis=0, keepdims=True)
    for k in range(3):
        s_ref[12 + k : 13 + k, :] = jnp.sum(acc[6 + k], axis=0, keepdims=True)
    for mod in range(2):
        s_ref[16 + mod : 17 + mod, :] = bsum[mod]
    for k in range(3):
        s_ref[18 + k : 19 + k, : 3 * HW] = bqsum[k]


def local(
    words, regions, word_lengths, task_flags, attn_qkv, attn_qv_bias, attn_out, ffn_in, ffn_in_bias,
    ffn_out, out_bias, norm_gain, norm_bias, cross_qkv, cross_qv_bias, cross_out, cross_out_bias,
    cross_norm_gain, cross_norm_bias,
):
    def rows(w, r):
        w = w.reshape(MB, ITEMS_MB * WORDS, -1)
        r = r.reshape(MB, ITEMS_MB * REGIONS, -1)
        w = jnp.pad(w, ((0, 0), (0, RW - w.shape[1]), (0, 0)))
        r = jnp.pad(r, ((0, 0), (0, RR - r.shape[1]), (0, 0)))
        return jnp.concatenate([w, r], axis=1)

    x = rows(words[0], regions[0])
    word_scale = jnp.where(task_flags == 1, 0.25, 1.0).astype(F32)
    region_scale = jnp.where(task_flags == 0, 0.25, 1.0).astype(F32)
    scale = rows(
        jnp.broadcast_to(word_scale[:, None], (ITEMS_LOCAL, WORDS)),
        jnp.broadcast_to(region_scale[:, None], (ITEMS_LOCAL, REGIONS)),
    )
    valid = (jnp.arange(WORDS)[None, :] < word_lengths[:, None]).astype(F32)
    valid = valid.reshape(MB, 1, ITEMS_MB * WORDS)
    valid = jnp.pad(valid, ((0, 0), (0, 0), (0, RW - ITEMS_MB * WORDS)))

    def qkv_bias(b):
        b = b.reshape(*b.shape[:-3], 2, HW)
        return jnp.concatenate(
            [b[..., 0:1, :], jnp.zeros_like(b[..., 0:1, :]), b[..., 1:2, :]], axis=-1
        )

    vec = jnp.concatenate(
        [a[0][:, k] for a in (out_bias, norm_gain, norm_bias) for k in range(2)], axis=0
    )
    cvec = jnp.stack([cross_out_bias, cross_norm_gain, cross_norm_bias])
    inputs = (
        x, scale, valid, attn_qkv[0].reshape(2, D, 3 * HW), qkv_bias(attn_qv_bias[0]), attn_out[0],
        ffn_in[0], ffn_in_bias[0].reshape(2, 1, D), ffn_out[0], vec,
        cross_qkv.reshape(D, 3 * HW), qkv_bias(cross_qv_bias), cross_out, cvec,
    )

    vmem = pl.BlockSpec(memory_space=pltpu.VMEM)
    mb_rows = lambda width, dtype: pltpu.VMEM((MB, R, width), dtype)
    own_rows = lambda count: pltpu.VMEM((count, MB, C, D), F32)
    y, g, s = pl.pallas_call(
        kernel,
        out_shape=(
            jax.ShapeDtypeStruct((MB, R, D), BF),
            jax.ShapeDtypeStruct((7, 2, 4, 2, 48, D), BF),
            jax.ShapeDtypeStruct((24, D), F32),
        ),
        in_specs=[vmem] * len(inputs),
        out_specs=[vmem] * 3,
        scratch_shapes=[
            mb_rows(D, BF),
            pltpu.VMEM((MB, TENSOR - 1, C, D), BF),
            *[mb_rows(D, BF) for _ in range(8)],
            pltpu.VMEM((3, MB, R, HW), BF),
            mb_rows(HW, BF),
            mb_rows(3 * HW, BF),
            pltpu.VMEM((3, MB, R, HW), BF),
            mb_rows(HW, BF),
            mb_rows(3 * HW, BF),
            mb_rows(D, BF),
            mb_rows(D, BF),
            mb_rows(D, F32),
            pltpu.VMEM((MB, 3 * RW, RW), F32),
            pltpu.VMEM((MB, 3 * RR, RR), F32),
            pltpu.VMEM((MB, 3 * RW, RR), F32),
            pltpu.VMEM((MB, 3 * RR, RW), F32),
            pltpu.VMEM((MB, C, D), F32),
            pltpu.VMEM((MB, C, D), F32),
            own_rows(3),
            pltpu.VMEM((3, MB, C, 128), F32),
            pltpu.VMEM((9, C, D), F32),
            pltpu.VMEM((6, C, D), F32),
            pltpu.VMEM((2, 1, D), F32),
            pltpu.VMEM((3, 1, 3 * HW), F32),
            *[pltpu.SemaphoreType.DMA((MB, TENSOR - 1)) for _ in range(6)],
            pltpu.SemaphoreType.DMA((MB,)),
            pltpu.SemaphoreType.DMA((MB,)),
        ],
        compiler_params=pltpu.CompilerParams(
            collective_id=0, has_side_effects=True, vmem_limit_bytes=60 * 2**20
        ),
    )(*inputs)

    g = g.reshape(7, D, D)
    layer = lax.psum_scatter(g[:6], "dp", scatter_dimension=1, tiled=True).astype(F32)
    s_dp = lax.psum(s, "dp")
    s_all = lax.psum(s_dp[:16], "tensor")
    dp = lax.axis_index("dp")
    both = lax.axis_index("section") * 16 + dp

    def part(a, index, width):
        return lax.dynamic_slice_in_dim(a, index * width, width, axis=a.ndim - 1)

    qkv_g = layer[:2, :, : 3 * HW].reshape(1, 2, 48, 3, HW)
    out_g = jnp.swapaxes(layer[:2, :, 3 * HW :], 1, 2)[None]
    in_g = layer[2:6:2][None]
    ffo_g = jnp.swapaxes(layer[3:6:2], 1, 2)[None]
    qb = s_dp[18:21, : 3 * HW].reshape(3, 3, LOCAL_HEADS, HEAD_DIM)[:, 0::2]
    qv_bias_g = part(qb[:2], dp, 4)[None]
    b1_g = part(s_dp[16:18].reshape(2, 6, 128), dp, 8)[None]
    small = part(s_all[:12].reshape(2, 3, 2, D), dp, 48)
    gain_g, shift_g, obias_g = (jnp.swapaxes(small[:, k], 0, 1)[None] for k in range(3))

    c = lax.psum(g[6].astype(F32), ("section", "dp"))
    c = lax.dynamic_slice_in_dim(c, both * 24, 24, axis=0)
    cs = lax.psum(s_all[12:15], "section")
    cqb = lax.psum(qb[2], "section")
    c_small = part(cs, both, 24)
    word_rows = y[:, : ITEMS_MB * WORDS].reshape(1, ITEMS_LOCAL, WORDS, D).astype(F32)
    region_rows = y[:, RW : RW + ITEMS_MB * REGIONS].reshape(1, ITEMS_LOCAL, REGIONS, D).astype(F32)
    return (
        word_rows, region_rows, qkv_g, qv_bias_g, out_g, in_g, b1_g, ffo_g, obias_g, gain_g, shift_g,
        c[:, : 3 * HW].reshape(24, 3, HW), part(cqb, both, 2), c[:, 3 * HW :].T,
        c_small[2], c_small[0], c_small[1],
    )


def solution(mesh):
    in_specs = (
        P("section", "dp", None, None),
        P("section", "dp", None, None),
        P("dp"),
        P("dp"),
        P("section", None, None, None, "tensor"),
        P("section", None, None, "tensor", None),
        P("section", None, "tensor", None),
        P("section", None, None, "tensor"),
        P("section", None, "tensor", None),
        P("section", None, "tensor", None),
        P("section", None, None, None),
        P("section", None, None, None),
        P("section", None, None, None),
        P(None, None, "tensor"),
        P(None, "tensor", None),
        P("tensor", None),
        P(),
        P(),
        P(),
    )
    out_specs = (
        P("section", "dp", None, None),
        P("section", "dp", None, None),
        P("section", None, "dp", None, "tensor"),
        P("section", None, None, "tensor", "dp"),
        P("section", None, "tensor", "dp"),
        P("section", None, "dp", "tensor"),
        P("section", None, "tensor", "dp"),
        P("section", None, "tensor", "dp"),
        P("section", None, None, "dp"),
        P("section", None, None, "dp"),
        P("section", None, None, "dp"),
        P(("section", "dp"), None, "tensor"),
        P(None, "tensor", ("section", "dp")),
        P("tensor", ("section", "dp")),
        P(("section", "dp")),
        P(("section", "dp")),
        P(("section", "dp")),
    )
    return jax.shard_map(local, mesh=mesh, in_specs=in_specs, out_specs=out_specs, check_vma=False)
```

```python
import functools

import jax
import jax.numpy as jnp
from jax import lax
from jax.experimental import pallas as pl
from jax.experimental.pallas import tpu as pltpu
from jax.sharding import PartitionSpec as P

MESH = pl.DeviceIdType.MESH
BF = jnp.bfloat16
F32 = jnp.float32
HEAD_DIM = 64
LOCAL_HEADS = 3
HW = HEAD_DIM * LOCAL_HEADS
WORDS = 20
REGIONS = 36
D = 768
ITEMS_LOCAL = 8
TENSOR = 4

ITEMS_MB = 2
MB = ITEMS_LOCAL // ITEMS_MB
RW = 48
RR = 80
R = RW + RR
C = R // TENSOR
SPANS = ((0, RW), (RW, R))

EPSILON = 1e-06
MASKED = -1000000000.0
SCALING = HEAD_DIM ** (-0.5)


def dot(a, b):
    return lax.dot_general(a, b, (((1,), (0,)), ((), ())), preferred_element_type=F32)


def dot_nt(a, b):
    return lax.dot_general(a, b, (((1,), (1,)), ((), ())), preferred_element_type=F32)


def dot_tn(a, b):
    return lax.dot_general(a, b, (((0,), (0,)), ((), ())), preferred_element_type=F32)


def head_masks():
    lane = lax.broadcasted_iota(jnp.int32, (1, HW), 1)
    return [
        ((lane >= h * HEAD_DIM) & (lane < (h + 1) * HEAD_DIM)).astype(F32) for h in range(LOCAL_HEADS)
    ]


def by_head(a):
    masks = [m.astype(BF) for m in head_masks()]
    return jnp.concatenate([a * m for m in masks], axis=0)


def join_heads(stacked):
    rows = stacked.shape[0] // LOCAL_HEADS
    masks = head_masks()
    total = stacked[:rows] * masks[0]
    for h in range(1, LOCAL_HEADS):
        total = total + stacked[h * rows : (h + 1) * rows] * masks[h]
    return total


def item_of(shape, axis, length):
    index = lax.broadcasted_iota(jnp.int32, shape, axis)
    item = jnp.zeros(shape, jnp.int32)
    for k in range(1, ITEMS_MB + 1):
        item = item + (index >= k * length).astype(jnp.int32)
    return item


def key_mask(q_rows, q_len, k_rows, k_len, key_valid):
    shape = (q_rows, k_rows)
    same = item_of(shape, 0, q_len) == item_of(shape, 1, k_len)
    inside = lax.broadcasted_iota(jnp.int32, shape, 1) < ITEMS_MB * k_len
    mask = same & inside
    if key_valid is not None:
        mask = mask & (jnp.broadcast_to(key_valid, shape) > 0.5)
    return mask


def attend(q, k, v, mask):
    scores = dot_nt(by_head(q), k) * SCALING
    mask = jnp.concatenate([mask] * LOCAL_HEADS, axis=0)
    scores = jnp.where(mask, scores, MASKED)
    e = jnp.exp(scores - jnp.max(scores, axis=-1, keepdims=True))
    probs = e / jnp.sum(e, axis=-1, keepdims=True)
    mixed = join_heads(dot(probs.astype(BF), v)).astype(BF)
    return probs, mixed


def attend_back(dmix, probs, q, k, v):
    d3 = by_head(dmix)
    dp = dot_nt(d3, v)
    ds = (probs * (dp - jnp.sum(probs * dp, axis=-1, keepdims=True))).astype(BF)
    dv = dot_tn(probs.astype(BF), d3).astype(BF)
    dq = (join_heads(dot(ds, k)) * SCALING).astype(BF)
    dk = (dot_tn(ds, by_head(q)) * SCALING).astype(BF)
    return dq, dk, dv


def norm_forward(r, gain, shift):
    center = r - jnp.mean(r, axis=-1, keepdims=True)
    spread = jnp.mean(center * center, axis=-1, keepdims=True)
    rstd = lax.rsqrt(spread + EPSILON)
    n = center * rstd
    return n, rstd, n * gain + shift


def norm_back(dh, n, rstd, gain):
    dn = dh * gain
    return rstd * (
        dn - jnp.mean(dn, axis=-1, keepdims=True) - n * jnp.mean(dn * n, axis=-1, keepdims=True)
    )


def kernel(
    x_ref, scale_ref, valid_ref, wqkv_ref, bqkv_ref, wo_ref, w1_ref, b1_ref, w2_ref, vec_ref,
    cwqkv_ref, cbqkv_ref, cwo_ref, cvec_ref,
    y_ref, dw_ref, s_ref, dc_ref, sc_ref,
    send, recv, xlow, midf, alow, dyf, dya, dyc, ybuf, back,
    qkv, mixed, dqkv, cqkv, cmixed, cdqkv, act, dup, dgelu,
    p_w, p_r, cp_w, cp_r, cur, res, nrm, rstd, acc, rowp, bsum, bqsum,
    g_ref, from_core, from_y, from_zs, from_z, from_ys, wide, sums, sums_t, sums_c, sums_y, sums_z, pack,
    rs_send, rs_recv, ag_send, ag_recv, y_send, y_recv, sec_send, sec_recv,
    dw_send, dw_recv, sm_send, sm_recv, pk_send, pk_recv,
):
    sec = lax.axis_index("section")
    me = lax.axis_index("tensor")
    head = sec == 0
    cross = sec == 1
    own = pl.ds(pl.multiple_of(me * C, C), C)

    def peer(o):
        return {"tensor": lax.rem(me + o, TENSOR)}

    def rows_of(t):
        return pl.ds(pl.multiple_of(t * C, C), C)

    partner = {"section": 1 - sec}
    place = lax.axis_index("dp")
    y_at, z_at, core = place // 8, lax.rem(place // 2, 4), lax.rem(place, 2)

    def dp_device(y, z, c):
        return {"dp": (y * 4 + z) * 2 + c}

    other_core = dp_device(y_at, z_at, 1 - core)
    other_y = dp_device(1 - y_at, z_at, core)

    def z_next(o):
        return lax.rem(z_at + o, 4)

    barrier = pltpu.get_barrier_semaphore()
    for o in range(1, TENSOR):
        pl.semaphore_signal(barrier, inc=1, device_id=peer(o), device_id_type=MESH)
    for device in (partner, other_core, other_y, *(dp_device(y_at, z_next(o), core) for o in (1, 2, 3))):
        pl.semaphore_signal(barrier, inc=1, device_id=device, device_id_type=MESH)

    row = lax.broadcasted_iota(jnp.int32, (C, 1), 0) + me * C
    is_word = row < RW
    for k in range(6):
        rowp[k] = jnp.where(is_word, vec_ref[2 * k : 2 * k + 1, :], vec_ref[2 * k + 1 : 2 * k + 2, :])
    acc[...] = jnp.zeros_like(acc)
    bsum[...] = jnp.zeros_like(bsum)
    bqsum[...] = jnp.zeros_like(bqsum)

    pl.semaphore_wait(barrier, 9)

    def rs_copies(m):
        return [
            pltpu.make_async_remote_copy(
                src_ref=send.at[m, rows_of(lax.rem(me + o, TENSOR))],
                dst_ref=recv.at[m, o - 1],
                send_sem=rs_send.at[m, o - 1],
                recv_sem=rs_recv.at[m, o - 1],
                device_id=peer(o),
                device_id_type=MESH,
            )
            for o in range(1, TENSOR)
        ]

    def rs_start(m):
        for copy in rs_copies(m):
            copy.start()

    def rs_finish(m):
        for copy in rs_copies(m):
            copy.wait()
        total = send[m, own].astype(F32)
        for o in range(TENSOR - 1):
            total = total + recv[m, o].astype(F32)
        return total

    def ag_copies(buf, m, ss, rs):
        return [
            pltpu.make_async_remote_copy(
                src_ref=buf.at[m, own],
                dst_ref=buf.at[m, own],
                send_sem=ss.at[m, o - 1],
                recv_sem=rs.at[m, o - 1],
                device_id=peer(o),
                device_id_type=MESH,
            )
            for o in range(1, TENSOR)
        ]

    def ag_start(buf, m, ss=ag_send, rs=ag_recv):
        for copy in ag_copies(buf, m, ss, rs):
            copy.start()

    def ag_finish(buf, m, ss=ag_send, rs=ag_recv):
        for copy in ag_copies(buf, m, ss, rs):
            copy.wait()

    def sec_copy(buf, m):
        return pltpu.make_async_remote_copy(
            src_ref=buf.at[m, own],
            dst_ref=buf.at[m, own],
            send_sem=sec_send.at[m],
            recv_sem=sec_recv.at[m],
            device_id=partner,
            device_id_type=MESH,
        )

    def save_norm(l, m, n, r):
        nrm[l, m] = n
        rstd[l, m] = jnp.broadcast_to(r, (C, 128))

    def norm_step_back(l, m, dh, gain):
        n = nrm[l, m]
        dr = norm_back(dh, n, rstd[l, m][:, :1], gain)
        low = dr.astype(BF)
        acc[3 * l] += dh * n
        acc[3 * l + 1] += dh
        acc[3 * l + 2] += low.astype(F32)
        res[m] = dr
        return low

    def word_keys(m, q_rows, q_len):
        return key_mask(q_rows, q_len, RW, WORDS, valid_ref[m])

    def region_keys(q_rows, q_len):
        return key_mask(q_rows, q_len, RR, REGIONS, None)

    def cross_a(m):
        sec_copy(midf, m).wait_recv()
        ag_start(midf, m)

    def cross_b(m):
        ag_finish(midf, m)
        out = dot(midf[m], cwqkv_ref[...]) + cbqkv_ref[...]
        out = out.astype(BF)
        q, k, v = out[:, :HW], out[:, HW : 2 * HW], out[:, 2 * HW :]
        cqkv[0, m], cqkv[1, m], cqkv[2, m] = q, k, v
        probs, mix = attend(q[:RW], k[RW:], v[RW:], region_keys(RW, WORDS))
        cp_w[m] = probs
        cmixed[m, :RW] = mix
        probs, mix = attend(q[RW:], k[:RW], v[:RW], word_keys(m, RR, REGIONS))
        cp_r[m] = probs
        cmixed[m, RW:] = mix
        send[m] = dot(cmixed[m], cwo_ref[...]).astype(BF)
        rs_start(m)

    def cross_c(m):
        r = midf[m, own].astype(F32) + rs_finish(m) + cvec_ref[0:1, :]
        n, rs, h = norm_forward(r, cvec_ref[1:2, :], cvec_ref[2:3, :])
        save_norm(2, m, n, rs)
        cur[m] = h
        xlow[m, own] = h.astype(BF)
        ag_start(xlow, m)

    def layer_a(m):
        @pl.when(head)
        def _():
            xlow[m] = x_ref[m]
            cur[m] = x_ref[m, own].astype(F32)

        @pl.when(cross)
        def _():
            ag_finish(xlow, m)

        for mod, (lo, hi) in enumerate(SPANS):
            out = (dot(xlow[m, lo:hi], wqkv_ref[mod]) + bqkv_ref[mod]).astype(BF)
            q, k, v = out[:, :HW], out[:, HW : 2 * HW], out[:, 2 * HW :]
            qkv[0, m, lo:hi], qkv[1, m, lo:hi], qkv[2, m, lo:hi] = q, k, v
            if mod == 0:
                probs, mix = attend(q, k, v, word_keys(m, RW, WORDS))
                p_w[m] = probs
            else:
                probs, mix = attend(q, k, v, region_keys(RR, REGIONS))
                p_r[m] = probs
            mixed[m, lo:hi] = mix
            send[m, lo:hi] = dot(mix, wo_ref[mod]).astype(BF)
        rs_start(m)

    def layer_b(m):
        r = cur[m] + rs_finish(m) + rowp[0]
        n, rs, h = norm_forward(r, rowp[2], rowp[4])
        save_norm(0, m, n, rs)
        cur[m] = h
        alow[m, own] = h.astype(BF)
        ag_start(alow, m)

    def layer_c(m):
        ag_finish(alow, m)
        for mod, (lo, hi) in enumerate(SPANS):
            up = dot(alow[m, lo:hi], w1_ref[mod]) + b1_ref[mod]
            cdf = 0.5 * (1.0 + lax.erf(up * (0.5**0.5)))
            dgelu[m, lo:hi] = cdf + up * jnp.exp(-0.5 * up * up) * 0.3989422804014327
            active = (up * cdf).astype(BF)
            act[m, lo:hi] = active
            send[m, lo:hi] = dot(active, w2_ref[mod]).astype(BF)
        rs_start(m)

    def layer_d(m):
        r = cur[m] + rs_finish(m) + rowp[1]
        n, rs, h = norm_forward(r, rowp[3], rowp[5])
        save_norm(1, m, n, rs)
        return h

    def back_e(m, dh):
        low = norm_step_back(1, m, dh, rowp[3])
        dyf[m, own] = low
        ag_start(dyf, m)

    def back_f(m):
        ag_finish(dyf, m)
        for mod, (lo, hi) in enumerate(SPANS):
            d = (dot_nt(dyf[m, lo:hi], w2_ref[mod]) * dgelu[m, lo:hi]).astype(BF)
            dup[m, lo:hi] = d
            bsum[mod] += jnp.sum(d.astype(F32), axis=0, keepdims=True)
            send[m, lo:hi] = dot_nt(d, w1_ref[mod]).astype(BF)
        rs_start(m)

    def back_g(m):
        dh = res[m] + rs_finish(m)
        low = norm_step_back(0, m, dh, rowp[2])
        dya[m, own] = low
        ag_start(dya, m)

    def back_h(m):
        ag_finish(dya, m)
        for mod, (lo, hi) in enumerate(SPANS):
            dmix = dot_nt(dya[m, lo:hi], wo_ref[mod]).astype(BF)
            probs = p_w[m] if mod == 0 else p_r[m]
            parts = attend_back(
                dmix, probs, qkv[0, m, lo:hi], qkv[1, m, lo:hi], qkv[2, m, lo:hi]
            )
            d = jnp.concatenate(parts, axis=1)
            dqkv[m, lo:hi] = d
            bqsum[mod] += jnp.sum(d.astype(F32), axis=0, keepdims=True)
            send[m, lo:hi] = dot_nt(d, wqkv_ref[mod]).astype(BF)
        rs_start(m)

    def cross_back_a(m):
        dh = res[m] + rs_finish(m)
        low = norm_step_back(2, m, dh, cvec_ref[1:2, :])
        dyc[m, own] = low
        ag_start(dyc, m)

    def cross_back_b(m):
        ag_finish(dyc, m)
        dmix = dot_nt(dyc[m], cwo_ref[...]).astype(BF)
        q, k, v = cqkv[0, m], cqkv[1, m], cqkv[2, m]
        dq_w, dk_r, dv_r = attend_back(dmix[:RW], cp_w[m], q[:RW], k[RW:], v[RW:])
        dq_r, dk_w, dv_w = attend_back(dmix[RW:], cp_r[m], q[RW:], k[:RW], v[:RW])
        cdqkv[m, :RW] = jnp.concatenate([dq_w, dk_w, dv_w], axis=1)
        cdqkv[m, RW:] = jnp.concatenate([dq_r, dk_r, dv_r], axis=1)
        d = cdqkv[m]
        bqsum[2] += jnp.sum(d.astype(F32), axis=0, keepdims=True)
        send[m] = dot_nt(d, cwqkv_ref[...]).astype(BF)
        rs_start(m)

    def cross_back_c(m):
        back[m, own] = (res[m] + rs_finish(m)).astype(BF)
        sec_copy(back, m).start()

    def outer(left, right, lo, hi, store):
        def tile(j):
            columns = pl.ds(pl.multiple_of(j * (D // 2), D // 2), D // 2)
            a = left[:, lo:hi, columns].reshape(MB * (hi - lo), D // 2)
            b = right[:, lo:hi, :].reshape(MB * (hi - lo), right.shape[-1])
            store(j, dot_tn(a, b))

        pl.loop(0, 2)(tile)

    def store_at(block, lo, hi):
        def store(j, value):
            g_ref[block, j, :, :, :, lo:hi] = value.astype(BF).reshape(4, 2, 48, hi - lo)

        return store

    def ffn_outer():
        for mod, (lo, hi) in enumerate(SPANS):
            outer(alow, dup, lo, hi, store_at(1 + 4 * mod, 0, D))
            outer(dyf, act, lo, hi, store_at(2 + 4 * mod, 0, D))

    def attn_outer():
        for mod, (lo, hi) in enumerate(SPANS):
            outer(xlow, dqkv, lo, hi, store_at(4 * mod, 0, 3 * HW))
            outer(dya, mixed, lo, hi, store_at(4 * mod, 3 * HW, D))

    def cross_outer():
        def store(lo, hi):
            def put(j, value):
                wide[j, :, :, lo:hi] = value.reshape(16, 24, hi - lo)

            return put

        outer(midf, cdqkv, 0, R, store(0, 3 * HW))
        outer(dyc, cmixed, 0, R, store(3 * HW, D))
        for y in range(2):
            for z in range(4):
                for c in range(2):
                    at = (y * 4 + z) * 2 + c
                    both = jnp.concatenate([wide[0, at], wide[1, at]], axis=0)
                    g_ref[3, y, z, c] = both.astype(BF)

    def moved(src, dst, send_sem, recv_sem, device):
        return pltpu.make_async_remote_copy(
            src_ref=src, dst_ref=dst, send_sem=send_sem, recv_sem=recv_sem, device_id=device,
            device_id_type=MESH,
        )

    def dw_copies(group, phase):
        (a0, a1), (b0, b1) = group[1:]
        sems = lambda k: (dw_send.at[group[0], k], dw_recv.at[group[0], k])
        na, nb = slice(a0, a1), slice(b0, b1)
        nbr = slice(b0 - 4, b1 - 4)
        copies = []
        if phase == 0:
            copies.append(
                moved(g_ref.at[na, :, :, 1 - core], from_core.at[na], *sems(0), other_core)
            )
            if b1 > b0:
                copies.append(
                    moved(g_ref.at[nb, :, :, 1 - core], from_core.at[nb], *sems(1), other_core)
                )
        if phase == 1:
            copies.append(moved(g_ref.at[na, 1 - y_at, :, core], from_y.at[na], *sems(2), other_y))
            if b1 > b0:
                for o in (1, 2, 3):
                    copies.append(
                        moved(
                            g_ref.at[nb, :, z_next(o), core], from_zs.at[nbr, o - 1], *sems(2 + o),
                            dp_device(y_at, z_next(o), core),
                        )
                    )
        if phase == 2:
            for o in (1, 2, 3):
                copies.append(
                    moved(
                        g_ref.at[na, y_at, z_next(o), core], from_z.at[na, o - 1], *sems(5 + o),
                        dp_device(y_at, z_next(o), core),
                    )
                )
            if b1 > b0:
                copies.append(
                    moved(g_ref.at[nb, 1 - y_at, z_at, core], from_ys.at[nbr], *sems(9), other_y)
                )
        return copies

    def dw_start(group, phase):
        for copy in dw_copies(group, phase):
            copy.start()

    def dw_finish(group, phase):
        for copy in dw_copies(group, phase):
            copy.wait()
        (a0, a1), (b0, b1) = group[1:]
        if phase == 0:
            for lo, hi in ((a0, a1), (b0, b1)):

                def add(k, lo=lo):
                    b, y = lo + k // 2, lax.rem(k, 2)
                    mine = g_ref[b, y, :, core].astype(F32)
                    g_ref[b, y, :, core] = (mine + from_core[b, y].astype(F32)).astype(BF)

                pl.loop(0, 2 * (hi - lo))(add)
        if phase == 1:

            def add_a(b):
                mine = g_ref[b, y_at, :, core].astype(F32)
                g_ref[b, y_at, :, core] = (mine + from_y[b].astype(F32)).astype(BF)

            def add_b(b):
                total = g_ref[b, :, z_at, core].astype(F32)
                for o in range(3):
                    total = total + from_zs[b - 4, o].astype(F32)
                g_ref[b, :, z_at, core] = total.astype(BF)

            pl.loop(a0, a1)(add_a)
            pl.loop(b0, b1)(add_b)
        if phase == 2:

            def last_a(b):
                total = g_ref[b, y_at, z_at, core].astype(F32)
                for o in range(3):
                    total = total + from_z[b, o].astype(F32)
                dw_ref[b] = total

            def last_b(b):
                dw_ref[b] = g_ref[b, y_at, z_at, core].astype(F32) + from_ys[b - 4].astype(F32)

            pl.loop(a0, a1)(last_a)
            pl.loop(b0, b1)(last_b)

    FFN = (0, (1, 3), (5, 7))
    ATTN = (1, (0, 1), (4, 5))
    CROSS = (2, (3, 4), (4, 4))

    def sm_copies(step):
        sems = lambda k: (sm_send.at[k], sm_recv.at[k])
        if step == 0:
            return [
                moved(sums_t.at[me], sums_t.at[me], *sems(o - 1), peer(o)) for o in range(1, TENSOR)
            ]
        if step == 1:
            return [moved(sums.at[0], sums_c, *sems(3), other_core)]
        if step == 2:
            return [moved(sums.at[1], sums_y, *sems(4), other_y)]
        return [
            moved(
                sums.at[2], sums_z.at[o - 1], *sems(4 + o), dp_device(y_at, z_next(o), core)
            )
            for o in (1, 2, 3)
        ]

    def sm_start(step):
        for copy in sm_copies(step):
            copy.start()

    def sm_wait(step):
        for copy in sm_copies(step):
            copy.wait()

    def small_norms():
        sums_t[me] = jnp.zeros((16, D), F32)
        for l in range(2):
            for k in range(3):
                a = acc[3 * l + k]
                at = 2 * (3 * l + k)
                sums_t[me, at : at + 1, :] = jnp.sum(jnp.where(is_word, a, 0.0), axis=0, keepdims=True)
                sums_t[me, at + 1 : at + 2, :] = jnp.sum(
                    jnp.where(is_word, 0.0, a), axis=0, keepdims=True
                )
        for k in range(3):
            sums_t[me, 12 + k : 13 + k, :] = jnp.sum(acc[6 + k], axis=0, keepdims=True)
        sm_start(0)

    def small_biases():
        sm_wait(0)
        sums[0] = jnp.zeros((24, D), F32)
        sums[0, :16] = sums_t[0] + sums_t[1] + sums_t[2] + sums_t[3]
        for mod in range(2):
            sums[0, 16 + mod : 17 + mod, :] = bsum[mod]
        for k in range(3):
            sums[0, 18 + k : 19 + k, : 3 * HW] = bqsum[k]
        sm_start(1)

    def small_y():
        sm_wait(1)
        sums[1] = sums[0] + sums_c[...]
        sm_start(2)

    def small_z():
        sm_wait(2)
        sums[2] = sums[1] + sums_y[...]
        sm_start(3)

    def small_last():
        sm_wait(3)
        s_ref[...] = sums[2] + sums_z[0] + sums_z[1] + sums_z[2]

    def packet():
        return moved(pack.at[0], pack.at[1], pk_send, pk_recv, partner)

    def each(*steps):
        def body(m):
            for step in steps:
                step(m)

        pl.loop(0, MB)(body)

    @pl.when(cross)
    def _():
        each(cross_a)
        each(cross_b)
        each(cross_c)

    each(layer_a)
    each(layer_b)
    each(layer_c)

    @pl.when(head)
    def _():
        def to_partner(m):
            midf[m, own] = layer_d(m).astype(BF)
            sec_copy(midf, m).start()

        def from_partner(m):
            sec_copy(midf, m).wait_send()
            sec_copy(back, m).wait_recv()
            back_e(m, back[m, own].astype(F32))

        each(to_partner)
        each(from_partner)

    @pl.when(cross)
    def _():
        def turn(m):
            h = layer_d(m)
            back_e(m, x_ref[m, own].astype(F32) * scale_ref[m, own])
            ybuf[m, own] = h.astype(BF)
            ag_start(ybuf, m, y_send, y_recv)

        each(turn)

    each(back_f)

    @pl.when(head)
    def _():
        ffn_outer()
        dw_start(FFN, 0)

    each(back_g)

    @pl.when(head)
    def _():
        dw_finish(FFN, 0)
        dw_start(FFN, 1)

    each(back_h)

    @pl.when(head)
    def _():
        def last(m):
            ybuf[m, own] = (res[m] + rs_finish(m)).astype(BF)
            ag_start(ybuf, m, y_send, y_recv)

        attn_outer()
        dw_start(ATTN, 0)
        small_norms()
        each(last)
        dw_finish(FFN, 1)
        dw_start(FFN, 2)
        small_biases()
        dw_finish(ATTN, 0)
        dw_start(ATTN, 1)
        small_y()
        small_z()

    @pl.when(cross)
    def _():
        each(cross_back_a)
        each(cross_back_b)
        each(cross_back_c)
        ffn_outer()
        dw_start(FFN, 0)
        small_norms()
        attn_outer()
        dw_start(ATTN, 0)
        dw_finish(FFN, 0)
        dw_start(FFN, 1)
        small_biases()
        cross_outer()
        dw_start(CROSS, 0)
        dw_finish(ATTN, 0)
        dw_start(ATTN, 1)
        small_y()
        dw_finish(CROSS, 0)
        dw_start(CROSS, 1)
        small_z()
        dw_finish(FFN, 1)
        dw_start(FFN, 2)

    def write(m):
        ag_finish(ybuf, m, y_send, y_recv)
        y_ref[m] = ybuf[m]

    each(write)
    small_last()
    dw_finish(FFN, 2)
    dw_finish(ATTN, 1)
    dw_start(ATTN, 2)

    @pl.when(cross)
    def _():
        each(lambda m: sec_copy(back, m).wait_send())
        dw_finish(CROSS, 1)
        dw_start(CROSS, 2)
        dw_finish(CROSS, 2)
        pack[0, :24] = dw_ref[3, :24]
        pack[0, 24:] = s_ref[...]
        packet().start()
        dc_ref[...] = dw_ref[3, 24:]
        sc_ref[...] = s_ref[...]
        packet().wait_send()

    dw_finish(ATTN, 2)

    @pl.when(head)
    def _():
        packet().wait_recv()
        dc_ref[...] = pack[1, :24]
        sc_ref[...] = pack[1, 24:]


def local(
    words, regions, word_lengths, task_flags, attn_qkv, attn_qv_bias, attn_out, ffn_in, ffn_in_bias,
    ffn_out, out_bias, norm_gain, norm_bias, cross_qkv, cross_qv_bias, cross_out, cross_out_bias,
    cross_norm_gain, cross_norm_bias,
):
    def rows(w, r):
        w = w.reshape(MB, ITEMS_MB * WORDS, -1)
        r = r.reshape(MB, ITEMS_MB * REGIONS, -1)
        w = jnp.pad(w, ((0, 0), (0, RW - w.shape[1]), (0, 0)))
        r = jnp.pad(r, ((0, 0), (0, RR - r.shape[1]), (0, 0)))
        return jnp.concatenate([w, r], axis=1)

    x = rows(words[0], regions[0])
    word_scale = jnp.where(task_flags == 1, 0.25, 1.0).astype(F32)
    region_scale = jnp.where(task_flags == 0, 0.25, 1.0).astype(F32)
    scale = rows(
        jnp.broadcast_to(word_scale[:, None], (ITEMS_LOCAL, WORDS)),
        jnp.broadcast_to(region_scale[:, None], (ITEMS_LOCAL, REGIONS)),
    )
    valid = (jnp.arange(WORDS)[None, :] < word_lengths[:, None]).astype(F32)
    valid = valid.reshape(MB, 1, ITEMS_MB * WORDS)
    valid = jnp.pad(valid, ((0, 0), (0, 0), (0, RW - ITEMS_MB * WORDS)))

    def qkv_bias(b):
        b = b.reshape(*b.shape[:-3], 2, HW)
        return jnp.concatenate(
            [b[..., 0:1, :], jnp.zeros_like(b[..., 0:1, :]), b[..., 1:2, :]], axis=-1
        )

    vec = jnp.concatenate(
        [a[0][:, k] for a in (out_bias, norm_gain, norm_bias) for k in range(2)], axis=0
    )
    cvec = jnp.stack([cross_out_bias, cross_norm_gain, cross_norm_bias])
    inputs = (
        x, scale, valid, attn_qkv[0].reshape(2, D, 3 * HW), qkv_bias(attn_qv_bias[0]), attn_out[0],
        ffn_in[0], ffn_in_bias[0].reshape(2, 1, D), ffn_out[0], vec,
        cross_qkv.reshape(D, 3 * HW), qkv_bias(cross_qv_bias), cross_out, cvec,
    )

    vmem = pl.BlockSpec(memory_space=pltpu.VMEM)
    mb_rows = lambda width, dtype: pltpu.VMEM((MB, R, width), dtype)
    own_rows = lambda count: pltpu.VMEM((count, MB, C, D), F32)
    y, g, s, dc, sc = pl.pallas_call(
        kernel,
        out_shape=(
            jax.ShapeDtypeStruct((MB, R, D), BF),
            jax.ShapeDtypeStruct((7, 48, D), F32),
            jax.ShapeDtypeStruct((24, D), F32),
            jax.ShapeDtypeStruct((24, D), F32),
            jax.ShapeDtypeStruct((24, D), F32),
        ),
        in_specs=[vmem] * len(inputs),
        out_specs=[vmem] * 5,
        scratch_shapes=[
            mb_rows(D, BF),
            pltpu.VMEM((MB, TENSOR - 1, C, D), BF),
            *[mb_rows(D, BF) for _ in range(8)],
            pltpu.VMEM((3, MB, R, HW), BF),
            mb_rows(HW, BF),
            mb_rows(3 * HW, BF),
            pltpu.VMEM((3, MB, R, HW), BF),
            mb_rows(HW, BF),
            mb_rows(3 * HW, BF),
            mb_rows(D, BF),
            mb_rows(D, BF),
            mb_rows(D, F32),
            pltpu.VMEM((MB, 3 * RW, RW), F32),
            pltpu.VMEM((MB, 3 * RR, RR), F32),
            pltpu.VMEM((MB, 3 * RW, RR), F32),
            pltpu.VMEM((MB, 3 * RR, RW), F32),
            pltpu.VMEM((MB, C, D), F32),
            pltpu.VMEM((MB, C, D), F32),
            own_rows(3),
            pltpu.VMEM((3, MB, C, 128), F32),
            pltpu.VMEM((9, C, D), F32),
            pltpu.VMEM((6, C, D), F32),
            pltpu.VMEM((2, 1, D), F32),
            pltpu.VMEM((3, 1, 3 * HW), F32),
            pltpu.VMEM((7, 2, 4, 2, 48, D), BF),
            pltpu.VMEM((7, 2, 4, 48, D), BF),
            pltpu.VMEM((4, 4, 48, D), BF),
            pltpu.VMEM((3, 3, 2, 48, D), BF),
            pltpu.VMEM((4, 3, 48, D), BF),
            pltpu.VMEM((3, 48, D), BF),
            pltpu.VMEM((2, 16, 24, D), F32),
            pltpu.VMEM((3, 24, D), F32),
            pltpu.VMEM((TENSOR, 16, D), F32),
            pltpu.VMEM((24, D), F32),
            pltpu.VMEM((24, D), F32),
            pltpu.VMEM((3, 24, D), F32),
            pltpu.VMEM((2, 48, D), F32),
            *[pltpu.SemaphoreType.DMA((MB, TENSOR - 1)) for _ in range(6)],
            pltpu.SemaphoreType.DMA((MB,)),
            pltpu.SemaphoreType.DMA((MB,)),
            pltpu.SemaphoreType.DMA((3, 10)),
            pltpu.SemaphoreType.DMA((3, 10)),
            pltpu.SemaphoreType.DMA((8,)),
            pltpu.SemaphoreType.DMA((8,)),
            pltpu.SemaphoreType.DMA,
            pltpu.SemaphoreType.DMA,
        ],
        compiler_params=pltpu.CompilerParams(
            collective_id=0, has_side_effects=True, vmem_limit_bytes=60 * 2**20
        ),
    )(*inputs)

    dp = lax.axis_index("dp")
    both = lax.axis_index("section") * 16 + dp

    def part(a, index, width):
        return lax.dynamic_slice_in_dim(a, index * width, width, axis=a.ndim - 1)

    def pair(k):
        return jnp.stack([g[k], g[k + 4]])

    qkv_g = pair(0)[:, :, : 3 * HW].reshape(1, 2, 48, 3, HW)
    out_g = jnp.swapaxes(pair(0)[:, :, 3 * HW :], 1, 2)[None]
    in_g = pair(1)[None]
    ffo_g = jnp.swapaxes(pair(2), 1, 2)[None]
    qb = s[18:20, : 3 * HW].reshape(2, 3, LOCAL_HEADS, HEAD_DIM)[:, 0::2]
    qv_bias_g = part(qb, dp, 4)[None]
    b1_g = part(s[16:18].reshape(2, 6, 128), dp, 8)[None]
    small = part(s[:12].reshape(2, 3, 2, D), dp, 48)
    gain_g, shift_g, obias_g = (jnp.swapaxes(small[:, k], 0, 1)[None] for k in range(3))

    cqb = sc[20, : 3 * HW].reshape(3, LOCAL_HEADS, HEAD_DIM)[0::2]
    c_small = part(sc[12:15], both, 24)
    word_rows = y[:, : ITEMS_MB * WORDS].reshape(1, ITEMS_LOCAL, WORDS, D).astype(F32)
    region_rows = y[:, RW : RW + ITEMS_MB * REGIONS].reshape(1, ITEMS_LOCAL, REGIONS, D).astype(F32)
    return (
        word_rows, region_rows, qkv_g, qv_bias_g, out_g, in_g, b1_g, ffo_g, obias_g, gain_g, shift_g,
        dc[:, : 3 * HW].reshape(24, 3, HW), part(cqb, both, 2), dc[:, 3 * HW :].T,
        c_small[2], c_small[0], c_small[1],
    )


def solution(mesh):
    in_specs = (
        P("section", "dp", None, None),
        P("section", "dp", None, None),
        P("dp"),
        P("dp"),
        P("section", None, None, None, "tensor"),
        P("section", None, None, "tensor", None),
        P("section", None, "tensor", None),
        P("section", None, None, "tensor"),
        P("section", None, "tensor", None),
        P("section", None, "tensor", None),
        P("section", None, None, None),
        P("section", None, None, None),
        P("section", None, None, None),
        P(None, None, "tensor"),
        P(None, "tensor", None),
        P("tensor", None),
        P(),
        P(),
        P(),
    )
    out_specs = (
        P("section", "dp", None, None),
        P("section", "dp", None, None),
        P("section", None, "dp", None, "tensor"),
        P("section", None, None, "tensor", "dp"),
        P("section", None, "tensor", "dp"),
        P("section", None, "dp", "tensor"),
        P("section", None, "tensor", "dp"),
        P("section", None, "tensor", "dp"),
        P("section", None, None, "dp"),
        P("section", None, None, "dp"),
        P("section", None, None, "dp"),
        P(("section", "dp"), None, "tensor"),
        P(None, "tensor", ("section", "dp")),
        P("tensor", ("section", "dp")),
        P(("section", "dp")),
        P(("section", "dp")),
        P(("section", "dp")),
    )
    return jax.shard_map(local, mesh=mesh, in_specs=in_specs, out_specs=out_specs, check_vma=False)
```

```python
import functools

import jax
import jax.numpy as jnp
from jax import lax
from jax.experimental import pallas as pl
from jax.experimental.pallas import tpu as pltpu
from jax.sharding import PartitionSpec as P

MESH = pl.DeviceIdType.MESH
BF = jnp.bfloat16
F32 = jnp.float32
HEAD_DIM = 64
LOCAL_HEADS = 3
HW = HEAD_DIM * LOCAL_HEADS
WORDS = 20
REGIONS = 36
D = 768
ITEMS_LOCAL = 8
TENSOR = 4

ITEMS_MB = 2
MB = ITEMS_LOCAL // ITEMS_MB
RW = 48
RR = 80
R = RW + RR
C = R // TENSOR
SPANS = ((0, RW), (RW, R))

EPSILON = 1e-06
MASKED = -1000000000.0
SCALING = HEAD_DIM ** (-0.5)


def dot(a, b):
    return lax.dot_general(a, b, (((1,), (0,)), ((), ())), preferred_element_type=F32)


def dot_nt(a, b):
    return lax.dot_general(a, b, (((1,), (1,)), ((), ())), preferred_element_type=F32)


def dot_tn(a, b):
    return lax.dot_general(a, b, (((0,), (0,)), ((), ())), preferred_element_type=F32)


def head_masks():
    lane = lax.broadcasted_iota(jnp.int32, (1, HW), 1)
    return [
        ((lane >= h * HEAD_DIM) & (lane < (h + 1) * HEAD_DIM)).astype(F32) for h in range(LOCAL_HEADS)
    ]


def by_head(a):
    masks = [m.astype(BF) for m in head_masks()]
    return jnp.concatenate([a * m for m in masks], axis=0)


def join_heads(stacked):
    rows = stacked.shape[0] // LOCAL_HEADS
    masks = head_masks()
    total = stacked[:rows] * masks[0]
    for h in range(1, LOCAL_HEADS):
        total = total + stacked[h * rows : (h + 1) * rows] * masks[h]
    return total


def item_of(shape, axis, length):
    index = lax.broadcasted_iota(jnp.int32, shape, axis)
    item = jnp.zeros(shape, jnp.int32)
    for k in range(1, ITEMS_MB + 1):
        item = item + (index >= k * length).astype(jnp.int32)
    return item


def spread(rows, length, transposed=False):
    count = ITEMS_LOCAL * length
    shape = (count, MB * rows) if transposed else (MB * rows, count)
    at = lax.broadcasted_iota(jnp.int32, shape, 0 if transposed else 1)
    padded = lax.broadcasted_iota(jnp.int32, shape, 1 if transposed else 0)
    item, position = at & (ITEMS_LOCAL - 1), at >> 3
    block, within = item >> (ITEMS_MB.bit_length() - 1), item & (ITEMS_MB - 1)
    target = block * rows + within * length + position
    return (target == padded).astype(F32).astype(BF)


def key_mask(q_rows, q_len, k_rows, k_len, lengths=None):
    shape = (q_rows, k_rows)
    item = item_of(shape, 1, k_len)
    key = lax.broadcasted_iota(jnp.int32, shape, 1)
    mask = (item_of(shape, 0, q_len) == item) & (key < ITEMS_MB * k_len)
    if lengths is not None:
        for k, length in enumerate(lengths):
            mask = mask & ((item != k) | (key < k * k_len + length))
    return mask


def attend(q, k, v, mask):
    scores = dot_nt(by_head(q), k) * SCALING
    mask = jnp.concatenate([mask] * LOCAL_HEADS, axis=0)
    scores = jnp.where(mask, scores, MASKED)
    e = jnp.exp(scores - jnp.max(scores, axis=-1, keepdims=True))
    probs = e / jnp.sum(e, axis=-1, keepdims=True)
    mixed = join_heads(dot(probs.astype(BF), v)).astype(BF)
    return probs, mixed


def attend_back(dmix, probs, q, k, v):
    d3 = by_head(dmix)
    dp = dot_nt(d3, v)
    ds = (probs * (dp - jnp.sum(probs * dp, axis=-1, keepdims=True))).astype(BF)
    dv = dot_tn(probs.astype(BF), d3).astype(BF)
    dq = (join_heads(dot(ds, k)) * SCALING).astype(BF)
    dk = (dot_tn(ds, by_head(q)) * SCALING).astype(BF)
    return dq, dk, dv


def norm_forward(r, gain, shift):
    center = r - jnp.mean(r, axis=-1, keepdims=True)
    spread = jnp.mean(center * center, axis=-1, keepdims=True)
    rstd = lax.rsqrt(spread + EPSILON)
    n = center * rstd
    return n, rstd, n * gain + shift


def norm_back(dh, n, rstd, gain):
    dn = dh * gain
    return rstd * (
        dn - jnp.mean(dn, axis=-1, keepdims=True) - n * jnp.mean(dn * n, axis=-1, keepdims=True)
    )


def kernel(
    words_ref, regions_ref, lengths_ref, flags_ref, wqkv_ref, qv_bias_ref, wo_ref, w1_ref, b1_in_ref,
    w2_ref, out_bias_ref, gain_ref, shift_ref, cwqkv_ref, cqv_bias_ref, cwo_ref, cout_bias_ref,
    cgain_ref, cshift_ref,
    y_ref, dw_ref, s_ref, dc_ref, sc_ref,
    x_ref, bqkv_ref, b1_ref, cvec_ref, send, recv, xlow, midf, alow, dyf, dya, dyc, ybuf, back,
    qkv, mixed, dqkv, cqkv, cmixed, cdqkv, act, dup, dgelu,
    p_w, p_r, cp_w, cp_r, cur, res, nrm, rstd, acc, rowp, bsum, bqsum,
    g_ref, from_core, from_y, from_zs, from_z, from_ys, wide, sums, sums_t, sums_c, sums_y, sums_z, pack,
    rs_send, rs_recv, ag_send, ag_recv, y_send, y_recv, sec_send, sec_recv,
    dw_send, dw_recv, sm_send, sm_recv, pk_send, pk_recv,
):
    sec = lax.axis_index("section")
    me = lax.axis_index("tensor")
    head = sec == 0
    cross = sec == 1
    own = pl.ds(pl.multiple_of(me * C, C), C)

    def peer(o):
        return {"tensor": lax.rem(me + o, TENSOR)}

    def rows_of(t):
        return pl.ds(pl.multiple_of(t * C, C), C)

    partner = {"section": 1 - sec}
    place = lax.axis_index("dp")
    y_at, z_at, core = place // 8, lax.rem(place // 2, 4), lax.rem(place, 2)

    def dp_device(y, z, c):
        return {"dp": (y * 4 + z) * 2 + c}

    other_core = dp_device(y_at, z_at, 1 - core)
    other_y = dp_device(1 - y_at, z_at, core)

    def z_next(o):
        return lax.rem(z_at + o, 4)

    barrier = pltpu.get_barrier_semaphore()
    for o in range(1, TENSOR):
        pl.semaphore_signal(barrier, inc=1, device_id=peer(o), device_id_type=MESH)
    for device in (partner, other_core, other_y, *(dp_device(y_at, z_next(o), core) for o in (1, 2, 3))):
        pl.semaphore_signal(barrier, inc=1, device_id=device, device_id_type=MESH)

    row = lax.broadcasted_iota(jnp.int32, (C, 1), 0) + me * C
    is_word = row < RW
    for k, ref in enumerate((out_bias_ref, gain_ref, shift_ref)):
        for l in range(2):
            rowp[2 * k + l] = jnp.where(is_word, ref[0, 0, l : l + 1, :], ref[0, 1, l : l + 1, :])

    def side_by_side(rows):
        return jnp.concatenate(rows, axis=1)

    for mod in range(2):
        b1_ref[mod] = side_by_side(
            [b1_in_ref[0, k, mod : mod + 1, :] for k in range(D // 128)]
        )
    for k, ref in enumerate((qv_bias_ref.at[0, 0], qv_bias_ref.at[0, 1], cqv_bias_ref)):
        heads = lambda j: [ref[h, j : j + 1, :] for h in range(LOCAL_HEADS)]
        bqkv_ref[k] = side_by_side([*heads(0), jnp.zeros((1, HW), F32), *heads(1)])
    for k, ref in enumerate((cout_bias_ref, cgain_ref, cshift_ref)):
        cvec_ref[k : k + 1, :] = ref[...].reshape(1, D)

    for ref, (lo, hi), length in zip((words_ref, regions_ref), SPANS, (WORDS, REGIONS)):
        given = ref[0].astype(F32).reshape(ITEMS_LOCAL * length, D).astype(BF)
        placed = dot(spread(hi - lo, length), given).astype(BF)
        x_ref[:, lo:hi, :] = placed.reshape(MB, hi - lo, D)
    acc[...] = jnp.zeros_like(acc)
    bsum[...] = jnp.zeros_like(bsum)
    bqsum[...] = jnp.zeros_like(bqsum)

    pl.semaphore_wait(barrier, 9)

    def rs_copies(m):
        return [
            pltpu.make_async_remote_copy(
                src_ref=send.at[m, rows_of(lax.rem(me + o, TENSOR))],
                dst_ref=recv.at[m, o - 1],
                send_sem=rs_send.at[m, o - 1],
                recv_sem=rs_recv.at[m, o - 1],
                device_id=peer(o),
                device_id_type=MESH,
            )
            for o in range(1, TENSOR)
        ]

    def rs_start(m):
        for copy in rs_copies(m):
            copy.start()

    def rs_finish(m):
        for copy in rs_copies(m):
            copy.wait()
        total = send[m, own].astype(F32)
        for o in range(TENSOR - 1):
            total = total + recv[m, o].astype(F32)
        return total

    def ag_copies(buf, m, ss, rs):
        return [
            pltpu.make_async_remote_copy(
                src_ref=buf.at[m, own],
                dst_ref=buf.at[m, own],
                send_sem=ss.at[m, o - 1],
                recv_sem=rs.at[m, o - 1],
                device_id=peer(o),
                device_id_type=MESH,
            )
            for o in range(1, TENSOR)
        ]

    def ag_start(buf, m, ss=ag_send, rs=ag_recv):
        for copy in ag_copies(buf, m, ss, rs):
            copy.start()

    def ag_finish(buf, m, ss=ag_send, rs=ag_recv):
        for copy in ag_copies(buf, m, ss, rs):
            copy.wait()

    def sec_copy(buf, m):
        return pltpu.make_async_remote_copy(
            src_ref=buf.at[m, own],
            dst_ref=buf.at[m, own],
            send_sem=sec_send.at[m],
            recv_sem=sec_recv.at[m],
            device_id=partner,
            device_id_type=MESH,
        )

    def save_norm(l, m, n, r):
        nrm[l, m] = n
        rstd[l, m] = jnp.broadcast_to(r, (C, 128))

    def norm_step_back(l, m, dh, gain):
        n = nrm[l, m]
        dr = norm_back(dh, n, rstd[l, m][:, :1], gain)
        low = dr.astype(BF)
        acc[3 * l] += dh * n
        acc[3 * l + 1] += dh
        acc[3 * l + 2] += low.astype(F32)
        res[m] = dr
        return low

    def word_keys(m, q_rows, q_len):
        return key_mask(
            q_rows, q_len, RW, WORDS, [lengths_ref[ITEMS_MB * m + k] for k in range(ITEMS_MB)]
        )

    def region_keys(q_rows, q_len):
        return key_mask(q_rows, q_len, RR, REGIONS)

    def cross_a(m):
        sec_copy(midf, m).wait_recv()
        ag_start(midf, m)

    def cross_b(m):
        ag_finish(midf, m)
        out = dot_nt(midf[m], cwqkv_ref[...]) + bqkv_ref[2]
        out = out.astype(BF)
        q, k, v = out[:, :HW], out[:, HW : 2 * HW], out[:, 2 * HW :]
        cqkv[0, m], cqkv[1, m], cqkv[2, m] = q, k, v
        probs, mix = attend(q[:RW], k[RW:], v[RW:], region_keys(RW, WORDS))
        cp_w[m] = probs
        cmixed[m, :RW] = mix
        probs, mix = attend(q[RW:], k[:RW], v[:RW], word_keys(m, RR, REGIONS))
        cp_r[m] = probs
        cmixed[m, RW:] = mix
        send[m] = dot(cmixed[m], cwo_ref[...]).astype(BF)
        rs_start(m)

    def cross_c(m):
        r = midf[m, own].astype(F32) + rs_finish(m) + cvec_ref[0:1, :]
        n, rs, h = norm_forward(r, cvec_ref[1:2, :], cvec_ref[2:3, :])
        save_norm(2, m, n, rs)
        cur[m] = h
        xlow[m, own] = h.astype(BF)
        ag_start(xlow, m)

    def layer_a(m):
        @pl.when(head)
        def _():
            xlow[m] = x_ref[m]
            cur[m] = x_ref[m, own].astype(F32)

        @pl.when(cross)
        def _():
            ag_finish(xlow, m)

        for mod, (lo, hi) in enumerate(SPANS):
            out = (dot_nt(xlow[m, lo:hi], wqkv_ref[mod]) + bqkv_ref[mod]).astype(BF)
            q, k, v = out[:, :HW], out[:, HW : 2 * HW], out[:, 2 * HW :]
            qkv[0, m, lo:hi], qkv[1, m, lo:hi], qkv[2, m, lo:hi] = q, k, v
            if mod == 0:
                probs, mix = attend(q, k, v, word_keys(m, RW, WORDS))
                p_w[m] = probs
            else:
                probs, mix = attend(q, k, v, region_keys(RR, REGIONS))
                p_r[m] = probs
            mixed[m, lo:hi] = mix
            send[m, lo:hi] = dot(mix, wo_ref[mod]).astype(BF)
        rs_start(m)

    def layer_b(m):
        r = cur[m] + rs_finish(m) + rowp[0]
        n, rs, h = norm_forward(r, rowp[2], rowp[4])
        save_norm(0, m, n, rs)
        cur[m] = h
        alow[m, own] = h.astype(BF)
        ag_start(alow, m)

    def layer_c(m):
        ag_finish(alow, m)
        for mod, (lo, hi) in enumerate(SPANS):
            up = dot(alow[m, lo:hi], w1_ref[mod]) + b1_ref[mod]
            cdf = 0.5 * (1.0 + lax.erf(up * (0.5**0.5)))
            dgelu[m, lo:hi] = cdf + up * jnp.exp(-0.5 * up * up) * 0.3989422804014327
            active = (up * cdf).astype(BF)
            act[m, lo:hi] = active
            send[m, lo:hi] = dot(active, w2_ref[mod]).astype(BF)
        rs_start(m)

    def layer_d(m):
        r = cur[m] + rs_finish(m) + rowp[1]
        n, rs, h = norm_forward(r, rowp[3], rowp[5])
        save_norm(1, m, n, rs)
        return h

    def back_e(m, dh):
        low = norm_step_back(1, m, dh, rowp[3])
        dyf[m, own] = low
        ag_start(dyf, m)

    def back_f(m):
        ag_finish(dyf, m)
        for mod, (lo, hi) in enumerate(SPANS):
            d = (dot_nt(dyf[m, lo:hi], w2_ref[mod]) * dgelu[m, lo:hi]).astype(BF)
            dup[m, lo:hi] = d
            bsum[mod] += jnp.sum(d.astype(F32), axis=0, keepdims=True)
            send[m, lo:hi] = dot_nt(d, w1_ref[mod]).astype(BF)
        rs_start(m)

    def back_g(m):
        dh = res[m] + rs_finish(m)
        low = norm_step_back(0, m, dh, rowp[2])
        dya[m, own] = low
        ag_start(dya, m)

    def back_h(m):
        ag_finish(dya, m)
        for mod, (lo, hi) in enumerate(SPANS):
            dmix = dot_nt(dya[m, lo:hi], wo_ref[mod]).astype(BF)
            probs = p_w[m] if mod == 0 else p_r[m]
            parts = attend_back(
                dmix, probs, qkv[0, m, lo:hi], qkv[1, m, lo:hi], qkv[2, m, lo:hi]
            )
            d = jnp.concatenate(parts, axis=1)
            dqkv[m, lo:hi] = d
            bqsum[mod] += jnp.sum(d.astype(F32), axis=0, keepdims=True)
            send[m, lo:hi] = dot(d, wqkv_ref[mod]).astype(BF)
        rs_start(m)

    def cross_back_a(m):
        dh = res[m] + rs_finish(m)
        low = norm_step_back(2, m, dh, cvec_ref[1:2, :])
        dyc[m, own] = low
        ag_start(dyc, m)

    def cross_back_b(m):
        ag_finish(dyc, m)
        dmix = dot_nt(dyc[m], cwo_ref[...]).astype(BF)
        q, k, v = cqkv[0, m], cqkv[1, m], cqkv[2, m]
        dq_w, dk_r, dv_r = attend_back(dmix[:RW], cp_w[m], q[:RW], k[RW:], v[RW:])
        dq_r, dk_w, dv_w = attend_back(dmix[RW:], cp_r[m], q[RW:], k[:RW], v[:RW])
        cdqkv[m, :RW] = jnp.concatenate([dq_w, dk_w, dv_w], axis=1)
        cdqkv[m, RW:] = jnp.concatenate([dq_r, dk_r, dv_r], axis=1)
        d = cdqkv[m]
        bqsum[2] += jnp.sum(d.astype(F32), axis=0, keepdims=True)
        send[m] = dot(d, cwqkv_ref[...]).astype(BF)
        rs_start(m)

    def cross_back_c(m):
        back[m, own] = (res[m] + rs_finish(m)).astype(BF)
        sec_copy(back, m).start()

    def outer(left, right, lo, hi, store):
        def tile(j):
            columns = pl.ds(pl.multiple_of(j * (D // 2), D // 2), D // 2)
            a = left[:, lo:hi, columns].reshape(MB * (hi - lo), D // 2)
            b = right[:, lo:hi, :].reshape(MB * (hi - lo), right.shape[-1])
            store(j, dot_tn(a, b))

        pl.loop(0, 2)(tile)

    def store_at(block, lo, hi):
        def store(j, value):
            g_ref[block, j, :, :, :, lo:hi] = value.astype(BF).reshape(4, 2, 48, hi - lo)

        return store

    def ffn_outer():
        for mod, (lo, hi) in enumerate(SPANS):
            outer(alow, dup, lo, hi, store_at(1 + 4 * mod, 0, D))
            outer(dyf, act, lo, hi, store_at(2 + 4 * mod, 0, D))

    def attn_outer():
        for mod, (lo, hi) in enumerate(SPANS):
            outer(xlow, dqkv, lo, hi, store_at(4 * mod, 0, 3 * HW))
            outer(dya, mixed, lo, hi, store_at(4 * mod, 3 * HW, D))

    def cross_outer():
        def store(lo, hi):
            def put(j, value):
                wide[j, :, :, lo:hi] = value.reshape(16, 24, hi - lo)

            return put

        outer(midf, cdqkv, 0, R, store(0, 3 * HW))
        outer(dyc, cmixed, 0, R, store(3 * HW, D))
        for y in range(2):
            for z in range(4):
                for c in range(2):
                    at = (y * 4 + z) * 2 + c
                    both = jnp.concatenate([wide[0, at], wide[1, at]], axis=0)
                    g_ref[3, y, z, c] = both.astype(BF)

    def moved(src, dst, send_sem, recv_sem, device):
        return pltpu.make_async_remote_copy(
            src_ref=src, dst_ref=dst, send_sem=send_sem, recv_sem=recv_sem, device_id=device,
            device_id_type=MESH,
        )

    def dw_copies(group, phase):
        (a0, a1), (b0, b1) = group[1:]
        sems = lambda k: (dw_send.at[group[0], k], dw_recv.at[group[0], k])
        na, nb = slice(a0, a1), slice(b0, b1)
        nbr = slice(b0 - 4, b1 - 4)
        copies = []
        if phase == 0:
            copies.append(
                moved(g_ref.at[na, :, :, 1 - core], from_core.at[na], *sems(0), other_core)
            )
            if b1 > b0:
                copies.append(
                    moved(g_ref.at[nb, :, :, 1 - core], from_core.at[nb], *sems(1), other_core)
                )
        if phase == 1:
            copies.append(moved(g_ref.at[na, 1 - y_at, :, core], from_y.at[na], *sems(2), other_y))
            if b1 > b0:
                for o in (1, 2, 3):
                    copies.append(
                        moved(
                            g_ref.at[nb, :, z_next(o), core], from_zs.at[nbr, o - 1], *sems(2 + o),
                            dp_device(y_at, z_next(o), core),
                        )
                    )
        if phase == 2:
            for o in (1, 2, 3):
                copies.append(
                    moved(
                        g_ref.at[na, y_at, z_next(o), core], from_z.at[na, o - 1], *sems(5 + o),
                        dp_device(y_at, z_next(o), core),
                    )
                )
            if b1 > b0:
                copies.append(
                    moved(g_ref.at[nb, 1 - y_at, z_at, core], from_ys.at[nbr], *sems(9), other_y)
                )
        return copies

    def dw_start(group, phase):
        for copy in dw_copies(group, phase):
            copy.start()

    def dw_finish(group, phase):
        for copy in dw_copies(group, phase):
            copy.wait()
        (a0, a1), (b0, b1) = group[1:]
        if phase == 0:
            for lo, hi in ((a0, a1), (b0, b1)):

                def add(k, lo=lo):
                    b, y = lo + k // 2, lax.rem(k, 2)
                    mine = g_ref[b, y, :, core].astype(F32)
                    g_ref[b, y, :, core] = (mine + from_core[b, y].astype(F32)).astype(BF)

                pl.loop(0, 2 * (hi - lo))(add)
        if phase == 1:

            def add_a(b):
                mine = g_ref[b, y_at, :, core].astype(F32)
                g_ref[b, y_at, :, core] = (mine + from_y[b].astype(F32)).astype(BF)

            def add_b(b):
                total = g_ref[b, :, z_at, core].astype(F32)
                for o in range(3):
                    total = total + from_zs[b - 4, o].astype(F32)
                g_ref[b, :, z_at, core] = total.astype(BF)

            pl.loop(a0, a1)(add_a)
            pl.loop(b0, b1)(add_b)
        if phase == 2:

            def last_a(b):
                total = g_ref[b, y_at, z_at, core].astype(F32)
                for o in range(3):
                    total = total + from_z[b, o].astype(F32)
                dw_ref[b] = total

            def last_b(b):
                dw_ref[b] = g_ref[b, y_at, z_at, core].astype(F32) + from_ys[b - 4].astype(F32)

            pl.loop(a0, a1)(last_a)
            pl.loop(b0, b1)(last_b)

    FFN = (0, (1, 3), (5, 7))
    ATTN = (1, (0, 1), (4, 5))
    CROSS = (2, (3, 4), (4, 4))

    def sm_copies(step):
        sems = lambda k: (sm_send.at[k], sm_recv.at[k])
        if step == 0:
            return [
                moved(sums_t.at[me], sums_t.at[me], *sems(o - 1), peer(o)) for o in range(1, TENSOR)
            ]
        if step == 1:
            return [moved(sums.at[0], sums_c, *sems(3), other_core)]
        if step == 2:
            return [moved(sums.at[1], sums_y, *sems(4), other_y)]
        return [
            moved(
                sums.at[2], sums_z.at[o - 1], *sems(4 + o), dp_device(y_at, z_next(o), core)
            )
            for o in (1, 2, 3)
        ]

    def sm_start(step):
        for copy in sm_copies(step):
            copy.start()

    def sm_wait(step):
        for copy in sm_copies(step):
            copy.wait()

    def small_norms():
        sums_t[me] = jnp.zeros((16, D), F32)
        for l in range(2):
            for k in range(3):
                a = acc[3 * l + k]
                at = 2 * (3 * l + k)
                sums_t[me, at : at + 1, :] = jnp.sum(jnp.where(is_word, a, 0.0), axis=0, keepdims=True)
                sums_t[me, at + 1 : at + 2, :] = jnp.sum(
                    jnp.where(is_word, 0.0, a), axis=0, keepdims=True
                )
        for k in range(3):
            sums_t[me, 12 + k : 13 + k, :] = jnp.sum(acc[6 + k], axis=0, keepdims=True)
        sm_start(0)

    def small_biases():
        sm_wait(0)
        sums[0] = jnp.zeros((24, D), F32)
        sums[0, :16] = sums_t[0] + sums_t[1] + sums_t[2] + sums_t[3]
        for mod in range(2):
            sums[0, 16 + mod : 17 + mod, :] = bsum[mod]
        for k in range(3):
            sums[0, 18 + k : 19 + k, : 3 * HW] = bqsum[k]
        sm_start(1)

    def small_y():
        sm_wait(1)
        sums[1] = sums[0] + sums_c[...]
        sm_start(2)

    def small_z():
        sm_wait(2)
        sums[2] = sums[1] + sums_y[...]
        sm_start(3)

    def small_last():
        sm_wait(3)
        s_ref[...] = sums[2] + sums_z[0] + sums_z[1] + sums_z[2]

    def packet():
        return moved(pack.at[0], pack.at[1], pk_send, pk_recv, partner)

    def each(*steps):
        def body(m):
            for step in steps:
                step(m)

        pl.loop(0, MB)(body)

    @pl.when(cross)
    def _():
        each(cross_a)
        each(cross_b)
        each(cross_c)

    each(layer_a)
    each(layer_b)
    each(layer_c)

    @pl.when(head)
    def _():
        def to_partner(m):
            midf[m, own] = layer_d(m).astype(BF)
            sec_copy(midf, m).start()

        def from_partner(m):
            sec_copy(midf, m).wait_send()
            sec_copy(back, m).wait_recv()
            back_e(m, back[m, own].astype(F32))

        each(to_partner)
        each(from_partner)

    @pl.when(cross)
    def _():
        def scales(m, flag, first, later):
            value = jnp.where(flags_ref[ITEMS_MB * m] == flag, 0.25, 1.0)
            scale = jnp.full((C, 1), value, F32)
            for k in range(1, ITEMS_MB):
                value = jnp.where(flags_ref[ITEMS_MB * m + k] == flag, 0.25, 1.0)
                scale = jnp.where(row >= first + k * later, value, scale)
            return scale

        def turn(m):
            h = layer_d(m)
            scale = jnp.where(is_word, scales(m, 1, 0, WORDS), scales(m, 0, RW, REGIONS))
            back_e(m, x_ref[m, own].astype(F32) * scale)
            ybuf[m, own] = h.astype(BF)

        each(turn)

    each(back_f)

    @pl.when(head)
    def _():
        ffn_outer()
        dw_start(FFN, 0)

    each(back_g)

    @pl.when(head)
    def _():
        dw_finish(FFN, 0)
        dw_start(FFN, 1)

    each(back_h)

    @pl.when(head)
    def _():
        def last(m):
            ybuf[m, own] = (res[m] + rs_finish(m)).astype(BF)
            ag_start(ybuf, m, y_send, y_recv)

        attn_outer()
        dw_start(ATTN, 0)
        small_norms()
        each(last)
        small_biases()
        dw_finish(FFN, 1)
        small_y()
        dw_start(FFN, 2)
        dw_finish(ATTN, 0)
        dw_start(ATTN, 1)
        small_z()

    @pl.when(cross)
    def _():
        each(cross_back_a)
        each(cross_back_b)
        each(cross_back_c)
        each(lambda m: ag_start(ybuf, m, y_send, y_recv))
        ffn_outer()
        dw_start(FFN, 0)
        small_norms()
        attn_outer()
        dw_start(ATTN, 0)
        dw_finish(FFN, 0)
        dw_start(FFN, 1)
        small_biases()
        cross_outer()
        dw_start(CROSS, 0)
        dw_finish(ATTN, 0)
        dw_start(ATTN, 1)
        small_y()
        dw_finish(CROSS, 0)
        dw_start(CROSS, 1)
        small_z()
        dw_finish(FFN, 1)
        dw_start(FFN, 2)

    def write(m):
        ag_finish(ybuf, m, y_send, y_recv)
        y_ref[m] = ybuf[m]

    each(write)
    dw_finish(FFN, 2)
    dw_finish(ATTN, 1)
    dw_start(ATTN, 2)
    small_last()

    @pl.when(cross)
    def _():
        each(lambda m: sec_copy(back, m).wait_send())
        dw_finish(CROSS, 1)
        dw_start(CROSS, 2)
        dw_finish(CROSS, 2)
        pack[0, :24] = dw_ref[3, :24]
        pack[0, 24:] = s_ref[...]
        packet().start()
        dc_ref[...] = dw_ref[3, 24:]
        sc_ref[...] = s_ref[...]
        packet().wait_send()

    dw_finish(ATTN, 2)

    @pl.when(head)
    def _():
        packet().wait_recv()
        dc_ref[...] = pack[1, :24]
        sc_ref[...] = pack[1, 24:]


def arrange(
    y_ref, dw_ref, s_ref, dc_ref, sc_ref,
    words, regions, qkv_g, qv_bias_g, out_g, in_g, b1_g, ffo_g, obias_g, gain_g, shift_g,
    cqkv_g, cqv_bias_g, cout_g, cobias_g, cgain_g, cshift_g,
):
    place = lax.axis_index("dp")
    both = lax.axis_index("section") * 16 + place

    def from_column(rows, column):
        return pltpu.roll(rows, lax.rem(D - column, D), 1)

    for ref, (lo, hi), length in zip((words, regions), SPANS, (WORDS, REGIONS)):
        padded = y_ref[:, lo:hi, :].reshape(MB * (hi - lo), D)
        rows = dot(spread(hi - lo, length, True), padded)
        ref[0] = rows.reshape(length, ITEMS_LOCAL, D)
    small = s_ref[...]
    for mod in range(2):
        attn = dw_ref[4 * mod]
        for j in range(3):
            qkv_g[0, mod, j] = attn[:, j * HW : (j + 1) * HW]
        out_g[0, mod] = attn[:, 3 * HW :]
        in_g[0, mod] = dw_ref[4 * mod + 1]
        ffo_g[0, mod] = dw_ref[4 * mod + 2]
    columns = from_column(small, 48 * place)[:, :48]
    for mod in range(2):
        for l in range(2):
            for k, ref in enumerate((gain_g, shift_g, obias_g)):
                at = 2 * (3 * l + k) + mod
                ref[0, mod, l : l + 1, :] = columns[at : at + 1]
    columns = from_column(small, 8 * place)
    for mod in range(2):
        for k in range(6):
            b1_g[0, k, mod : mod + 1, :] = columns[16 + mod : 17 + mod, 128 * k : 128 * k + 8]
    columns = from_column(small, 4 * place)
    for mod in range(2):
        for j in range(2):
            for h in range(LOCAL_HEADS):
                lo = 2 * j * HW + h * HEAD_DIM
                qv_bias_g[0, mod, h, j : j + 1, :] = columns[18 + mod : 19 + mod, lo : lo + 4]
    wide = dc_ref[...]
    for j in range(3):
        cqkv_g[j] = wide[:, j * HW : (j + 1) * HW]
    cout_g[...] = wide[:, 3 * HW :]
    small = sc_ref[...]
    columns = from_column(small, 24 * both)
    for k, ref in enumerate((cgain_g, cshift_g, cobias_g)):
        ref[...] = columns[12 + k, :24]
    columns = from_column(small, 2 * both)[20:21]
    for j in range(2):
        heads = []
        for h in range(LOCAL_HEADS):
            lo = 2 * j * HW + h * HEAD_DIM
            heads.append(columns[:, lo : lo + 2])
        cqv_bias_g[j] = jnp.concatenate(heads, axis=0).T


def local(
    words, regions, word_lengths, task_flags, attn_qkv, attn_qv_bias, attn_out, ffn_in, ffn_in_bias,
    ffn_out, out_bias, norm_gain, norm_bias, cross_qkv, cross_qv_bias, cross_out, cross_out_bias,
    cross_norm_gain, cross_norm_bias,
):
    inputs = (
        words.transpose(0, 2, 1, 3), regions.transpose(0, 2, 1, 3), word_lengths, task_flags,
        attn_qkv.transpose(0, 1, 3, 4, 2).reshape(2, 3 * HW, D), attn_qv_bias.transpose(0, 1, 3, 2, 4), attn_out[0],
        ffn_in[0], ffn_in_bias.transpose(0, 2, 1, 3), ffn_out[0], out_bias, norm_gain, norm_bias,
        cross_qkv.transpose(1, 2, 0).reshape(3 * HW, D), cross_qv_bias.transpose(1, 0, 2), cross_out,
        cross_out_bias, cross_norm_gain, cross_norm_bias,
    )

    vmem = pl.BlockSpec(memory_space=pltpu.VMEM)
    smem = pl.BlockSpec(memory_space=pltpu.SMEM)
    mb_rows = lambda width, dtype: pltpu.VMEM((MB, R, width), dtype)
    own_rows = lambda count: pltpu.VMEM((count, MB, C, D), F32)
    y, g, s, dc, sc = pl.pallas_call(
        kernel,
        out_shape=(
            jax.ShapeDtypeStruct((MB, R, D), BF),
            jax.ShapeDtypeStruct((7, 48, D), F32),
            jax.ShapeDtypeStruct((24, D), F32),
            jax.ShapeDtypeStruct((24, D), F32),
            jax.ShapeDtypeStruct((24, D), F32),
        ),
        in_specs=[smem if k in (2, 3) else vmem for k in range(len(inputs))],
        out_specs=[vmem] * 5,
        scratch_shapes=[
            mb_rows(D, BF),
            pltpu.VMEM((3, 1, 3 * HW), F32),
            pltpu.VMEM((2, 1, D), F32),
            pltpu.VMEM((3, D), F32),
            mb_rows(D, BF),
            pltpu.VMEM((MB, TENSOR - 1, C, D), BF),
            *[mb_rows(D, BF) for _ in range(8)],
            pltpu.VMEM((3, MB, R, HW), BF),
            mb_rows(HW, BF),
            mb_rows(3 * HW, BF),
            pltpu.VMEM((3, MB, R, HW), BF),
            mb_rows(HW, BF),
            mb_rows(3 * HW, BF),
            mb_rows(D, BF),
            mb_rows(D, BF),
            mb_rows(D, F32),
            pltpu.VMEM((MB, 3 * RW, RW), F32),
            pltpu.VMEM((MB, 3 * RR, RR), F32),
            pltpu.VMEM((MB, 3 * RW, RR), F32),
            pltpu.VMEM((MB, 3 * RR, RW), F32),
            pltpu.VMEM((MB, C, D), F32),
            pltpu.VMEM((MB, C, D), F32),
            own_rows(3),
            pltpu.VMEM((3, MB, C, 128), F32),
            pltpu.VMEM((9, C, D), F32),
            pltpu.VMEM((6, C, D), F32),
            pltpu.VMEM((2, 1, D), F32),
            pltpu.VMEM((3, 1, 3 * HW), F32),
            pltpu.VMEM((7, 2, 4, 2, 48, D), BF),
            pltpu.VMEM((7, 2, 4, 48, D), BF),
            pltpu.VMEM((4, 4, 48, D), BF),
            pltpu.VMEM((3, 3, 2, 48, D), BF),
            pltpu.VMEM((4, 3, 48, D), BF),
            pltpu.VMEM((3, 48, D), BF),
            pltpu.VMEM((2, 16, 24, D), F32),
            pltpu.VMEM((3, 24, D), F32),
            pltpu.VMEM((TENSOR, 16, D), F32),
            pltpu.VMEM((24, D), F32),
            pltpu.VMEM((24, D), F32),
            pltpu.VMEM((3, 24, D), F32),
            pltpu.VMEM((2, 48, D), F32),
            *[pltpu.SemaphoreType.DMA((MB, TENSOR - 1)) for _ in range(6)],
            pltpu.SemaphoreType.DMA((MB,)),
            pltpu.SemaphoreType.DMA((MB,)),
            pltpu.SemaphoreType.DMA((3, 10)),
            pltpu.SemaphoreType.DMA((3, 10)),
            pltpu.SemaphoreType.DMA((8,)),
            pltpu.SemaphoreType.DMA((8,)),
            pltpu.SemaphoreType.DMA,
            pltpu.SemaphoreType.DMA,
        ],
        compiler_params=pltpu.CompilerParams(
            collective_id=0, has_side_effects=True, vmem_limit_bytes=60 * 2**20
        ),
    )(*inputs)

    shapes = (
        (1, WORDS, ITEMS_LOCAL, D), (1, REGIONS, ITEMS_LOCAL, D), (1, 2, 3, 48, HW),
        (1, 2, LOCAL_HEADS, 2, 4), (1, 2, 48, HW), (1, 2, 48, D), (1, 6, 2, 8), (1, 2, 48, D),
        (1, 2, 2, 48), (1, 2, 2, 48), (1, 2, 2, 48), (3, 24, HW), (2, 2, LOCAL_HEADS), (24, HW),
        (24,), (24,), (24,),
    )
    orders = {
        0: (0, 2, 1, 3), 1: (0, 2, 1, 3), 2: (0, 1, 3, 2, 4), 3: (0, 1, 3, 2, 4), 4: (0, 1, 3, 2),
        6: (0, 2, 1, 3), 7: (0, 1, 3, 2), 11: (1, 0, 2), 12: (0, 2, 1), 13: (1, 0),
    }
    outs = pl.pallas_call(
        arrange,
        out_shape=tuple(jax.ShapeDtypeStruct(shape, F32) for shape in shapes),
        in_specs=[vmem] * 5,
        out_specs=[vmem] * len(shapes),
        compiler_params=pltpu.CompilerParams(vmem_limit_bytes=60 * 2**20),
    )(y, g, s, dc, sc)
    return tuple(out.transpose(orders[k]) if k in orders else out for k, out in enumerate(outs))


def solution(mesh):
    in_specs = (
        P("section", "dp", None, None),
        P("section", "dp", None, None),
        P("dp"),
        P("dp"),
        P("section", None, None, None, "tensor"),
        P("section", None, None, "tensor", None),
        P("section", None, "tensor", None),
        P("section", None, None, "tensor"),
        P("section", None, "tensor", None),
        P("section", None, "tensor", None),
        P("section", None, None, None),
        P("section", None, None, None),
        P("section", None, None, None),
        P(None, None, "tensor"),
        P(None, "tensor", None),
        P("tensor", None),
        P(),
        P(),
        P(),
    )
    out_specs = (
        P("section", "dp", None, None),
        P("section", "dp", None, None),
        P("section", None, "dp", None, "tensor"),
        P("section", None, None, "tensor", "dp"),
        P("section", None, "tensor", "dp"),
        P("section", None, "dp", "tensor"),
        P("section", None, "tensor", "dp"),
        P("section", None, "tensor", "dp"),
        P("section", None, None, "dp"),
        P("section", None, None, "dp"),
        P("section", None, None, "dp"),
        P(("section", "dp"), None, "tensor"),
        P(None, "tensor", ("section", "dp")),
        P("tensor", ("section", "dp")),
        P(("section", "dp")),
        P(("section", "dp")),
        P(("section", "dp")),
    )
    return jax.shard_map(local, mesh=mesh, in_specs=in_specs, out_specs=out_specs, check_vma=False)
```

```python
import functools

import jax
import jax.numpy as jnp
from jax import lax
from jax.experimental import pallas as pl
from jax.experimental.pallas import tpu as pltpu
from jax.sharding import PartitionSpec as P

MESH = pl.DeviceIdType.MESH
BF = jnp.bfloat16
F32 = jnp.float32
HEAD_DIM = 64
LOCAL_HEADS = 3
HW = HEAD_DIM * LOCAL_HEADS
WORDS = 20
REGIONS = 36
D = 768
ITEMS_LOCAL = 8
TENSOR = 4

ITEMS_MB = 2
MB = ITEMS_LOCAL // ITEMS_MB
RW = 48
RR = 80
R = RW + RR
C = R // TENSOR
SPANS = ((0, RW), (RW, R))

EPSILON = 1e-06
MASKED = -1000000000.0
SCALING = HEAD_DIM ** (-0.5)


def dot(a, b):
    return lax.dot_general(a, b, (((1,), (0,)), ((), ())), preferred_element_type=F32)


def dot_nt(a, b):
    return lax.dot_general(a, b, (((1,), (1,)), ((), ())), preferred_element_type=F32)


def dot_tn(a, b):
    return lax.dot_general(a, b, (((0,), (0,)), ((), ())), preferred_element_type=F32)


def head_masks():
    lane = lax.broadcasted_iota(jnp.int32, (1, HW), 1)
    return [
        ((lane >= h * HEAD_DIM) & (lane < (h + 1) * HEAD_DIM)).astype(F32) for h in range(LOCAL_HEADS)
    ]


def by_head(a):
    masks = [m.astype(BF) for m in head_masks()]
    return jnp.concatenate([a * m for m in masks], axis=0)


def join_heads(stacked):
    rows = stacked.shape[0] // LOCAL_HEADS
    masks = head_masks()
    total = stacked[:rows] * masks[0]
    for h in range(1, LOCAL_HEADS):
        total = total + stacked[h * rows : (h + 1) * rows] * masks[h]
    return total


def item_of(shape, axis, length):
    index = lax.broadcasted_iota(jnp.int32, shape, axis)
    item = jnp.zeros(shape, jnp.int32)
    for k in range(1, ITEMS_MB + 1):
        item = item + (index >= k * length).astype(jnp.int32)
    return item


def spread(rows, length, transposed=False):
    count = ITEMS_LOCAL * length
    shape = (count, MB * rows) if transposed else (MB * rows, count)
    at = lax.broadcasted_iota(jnp.int32, shape, 0 if transposed else 1)
    padded = lax.broadcasted_iota(jnp.int32, shape, 1 if transposed else 0)
    item, position = at & (ITEMS_LOCAL - 1), at >> 3
    block, within = item >> (ITEMS_MB.bit_length() - 1), item & (ITEMS_MB - 1)
    target = block * rows + within * length + position
    return (target == padded).astype(F32).astype(BF)


def key_mask(q_rows, q_len, k_rows, k_len, lengths=None):
    shape = (q_rows, k_rows)
    item = item_of(shape, 1, k_len)
    key = lax.broadcasted_iota(jnp.int32, shape, 1)
    mask = (item_of(shape, 0, q_len) == item) & (key < ITEMS_MB * k_len)
    if lengths is not None:
        for k, length in enumerate(lengths):
            mask = mask & ((item != k) | (key < k * k_len + length))
    return mask


def attend(q, k, v, mask):
    scores = dot_nt(by_head(q), k) * SCALING
    mask = jnp.concatenate([mask] * LOCAL_HEADS, axis=0)
    scores = jnp.where(mask, scores, MASKED)
    e = jnp.exp(scores - jnp.max(scores, axis=-1, keepdims=True))
    probs = e / jnp.sum(e, axis=-1, keepdims=True)
    mixed = join_heads(dot(probs.astype(BF), v)).astype(BF)
    return probs, mixed


def attend_back(dmix, probs, q, k, v):
    d3 = by_head(dmix)
    dp = dot_nt(d3, v)
    ds = (probs * (dp - jnp.sum(probs * dp, axis=-1, keepdims=True))).astype(BF)
    dv = dot_tn(probs.astype(BF), d3).astype(BF)
    dq = (join_heads(dot(ds, k)) * SCALING).astype(BF)
    dk = (dot_tn(ds, by_head(q)) * SCALING).astype(BF)
    return dq, dk, dv


def norm_forward(r, gain, shift):
    center = r - jnp.mean(r, axis=-1, keepdims=True)
    spread = jnp.mean(center * center, axis=-1, keepdims=True)
    rstd = lax.rsqrt(spread + EPSILON)
    n = center * rstd
    return n, rstd, n * gain + shift


def norm_back(dh, n, rstd, gain):
    dn = dh * gain
    return rstd * (
        dn - jnp.mean(dn, axis=-1, keepdims=True) - n * jnp.mean(dn * n, axis=-1, keepdims=True)
    )


def kernel(
    words_ref, regions_ref, lengths_ref, flags_ref, wqkv_in, qv_bias_ref, wo_in, w1_in, b1_in_ref,
    w2_in, out_bias_ref, gain_ref, shift_ref, cwqkv_in, cqv_bias_ref, cwo_in, cout_bias_ref,
    cgain_ref, cshift_ref,
    y_ref, dw_ref, s_ref, dc_ref, sc_ref,
    x_ref, bqkv_ref, b1_ref, cvec_ref, send, recv, xlow, midf, alow, dyf, dya, dyc, ybuf, back,
    qkv, mixed, dqkv, cqkv, cmixed, cdqkv, act, dup, dgelu,
    p_w, p_r, cp_w, cp_r, cur, res, nrm, rstd, acc, rowp, bsum, bqsum,
    wqkv_ref, wo_ref, w1_ref, w2_ref, cwqkv_ref, cwo_ref, wqkv_m, wo_m, w1_m, w2_m, cwqkv_m, cwo_m, bqkv_m, b1_m,
    got, act_m, dup_m, mixed_m, dqkv_m, cmixed_m, cdqkv_m, cur_f, res_f, nrm_f, rstd_f, row_sums,
    g_ref, from_core, from_y, from_zs, from_z, from_ys, sums, sums_t, sums_c, sums_y, sums_z, pack,
    rs_send, rs_recv, ag_send, ag_recv, y_send, y_recv, sec_send, sec_recv,
    dw_send, dw_recv, sm_send, sm_recv, pk_send, pk_recv,
    back_send, back_recv, ar_send, ar_recv, mt_send, mt_recv, ga_send, ga_recv, ps_send, ps_recv, loads,
):
    p = functools.partial
    sec = lax.axis_index("section")
    me = lax.axis_index("tensor")
    head = sec == 0
    cross = sec == 1
    own = pl.ds(pl.multiple_of(me * C, C), C)

    def peer(o):
        return {"tensor": lax.rem(me + o, TENSOR)}

    def rows_of(t):
        return pl.ds(pl.multiple_of(t * C, C), C)

    partner = {"section": 1 - sec}
    place = lax.axis_index("dp")
    y_at, z_at, core = place // 8, lax.rem(place // 2, 4), lax.rem(place, 2)

    def dp_device(y, z, c):
        return {"dp": (y * 4 + z) * 2 + c}

    other_core = dp_device(y_at, z_at, 1 - core)
    other_y = dp_device(1 - y_at, z_at, core)

    def z_next(o):
        return lax.rem(z_at + o, 4)

    weights = tuple(
        pltpu.make_async_copy(src, dst, loads.at[k])
        for k, (src, dst) in enumerate((
            (wqkv_in, wqkv_ref), (wo_in, wo_ref), (w1_in, w1_ref), (w2_in, w2_ref),
            (cwqkv_in, cwqkv_ref), (cwo_in, cwo_ref),
        ))
    )

    def load_weights(*which):
        for k in which:
            weights[k].start()

    def wait_weights(*which):
        for k in which:
            weights[k].wait()

    barrier = pltpu.get_barrier_semaphore()
    for o in range(1, TENSOR):
        pl.semaphore_signal(barrier, inc=1, device_id=peer(o), device_id_type=MESH)
    mate, halver = {"tensor": me + 1 - 2 * lax.rem(me, 2)}, {"tensor": 3 - me}
    set_of = lax.rem((me + 1) // 2, 2)
    for t in range(TENSOR):
        pl.semaphore_signal(
            barrier, inc=1, device_id={"section": 1 - sec, "tensor": t}, device_id_type=MESH
        )
    for device in (other_core, other_y, *(dp_device(y_at, z_next(o), core) for o in (1, 2, 3))):
        pl.semaphore_signal(barrier, inc=1, device_id=device, device_id_type=MESH)

    load_weights(0, 1, 2, 3)
    pl.when(cross)(lambda: load_weights(4, 5))

    row = lax.broadcasted_iota(jnp.int32, (C, 1), 0) + me * C
    is_word = row < RW
    for k, ref in enumerate((out_bias_ref, gain_ref, shift_ref)):
        for l in range(2):
            rowp[2 * k + l] = jnp.where(is_word, ref[0, 0, l : l + 1, :], ref[0, 1, l : l + 1, :])

    def side_by_side(rows):
        return jnp.concatenate(rows, axis=1)

    for mod in range(2):
        b1_ref[mod] = side_by_side(
            [b1_in_ref[0, k, mod : mod + 1, :] for k in range(D // 128)]
        )
    for k, ref in enumerate((qv_bias_ref.at[0, 0], qv_bias_ref.at[0, 1], cqv_bias_ref)):
        heads = lambda j: [ref[h, j : j + 1, :] for h in range(LOCAL_HEADS)]
        bqkv_ref[k] = side_by_side([*heads(0), jnp.zeros((1, HW), F32), *heads(1)])
    for k, ref in enumerate((cout_bias_ref, cgain_ref, cshift_ref)):
        cvec_ref[k : k + 1, :] = ref[...].reshape(1, D)

    for ref, (lo, hi), length in zip((words_ref, regions_ref), SPANS, (WORDS, REGIONS)):
        given = ref[0].astype(F32).reshape(ITEMS_LOCAL * length, D).astype(BF)
        placed = dot(spread(hi - lo, length), given).astype(BF)
        x_ref[:, lo:hi, :] = placed.reshape(MB, hi - lo, D)
    acc[...] = jnp.zeros_like(acc)
    bsum[...] = jnp.zeros_like(bsum)
    bqsum[...] = jnp.zeros_like(bqsum)
    row_sums[...] = jnp.zeros_like(row_sums)

    pl.semaphore_wait(barrier, 12)

    def moved(src, dst, send_sem, recv_sem, device):
        return pltpu.make_async_remote_copy(
            src_ref=src, dst_ref=dst, send_sem=send_sem, recv_sem=recv_sem, device_id=device,
            device_id_type=MESH,
        )

    def rs_copies(m):
        return [
            pltpu.make_async_remote_copy(
                src_ref=send.at[m, rows_of(lax.rem(me + o, TENSOR))],
                dst_ref=recv.at[m, o - 1],
                send_sem=rs_send.at[m, o - 1],
                recv_sem=rs_recv.at[m, o - 1],
                device_id=peer(o),
                device_id_type=MESH,
            )
            for o in range(1, TENSOR)
        ]

    def rs_start(m):
        for copy in rs_copies(m):
            copy.start()

    def rs_finish(m):
        for copy in rs_copies(m):
            copy.wait()
        total = send[m, own].astype(F32)
        for o in range(TENSOR - 1):
            total = total + recv[m, o].astype(F32)
        return total

    def ag_copies(buf, m, ss, rs):
        return [
            pltpu.make_async_remote_copy(
                src_ref=buf.at[m, own],
                dst_ref=buf.at[m, own],
                send_sem=ss.at[m, o - 1],
                recv_sem=rs.at[m, o - 1],
                device_id=peer(o),
                device_id_type=MESH,
            )
            for o in range(1, TENSOR)
        ]

    def ag_start(buf, m, ss=ag_send, rs=ag_recv):
        for copy in ag_copies(buf, m, ss, rs):
            copy.start()

    def ag_finish(buf, m, ss=ag_send, rs=ag_recv):
        for copy in ag_copies(buf, m, ss, rs):
            copy.wait()

    def mid_copy(m, k, t):
        return moved(
            midf.at[m, own], midf.at[m, own], sec_send.at[m, k], sec_recv.at[m, me],
            {"section": 1 - sec, "tensor": t},
        )

    def mid_arrive(m):
        for t in range(TENSOR):
            rows = midf.at[m, pl.ds(t * C, C)]
            moved(rows, rows, sec_send.at[m, 0], sec_recv.at[m, t], partner).wait_recv()

    def back_copies(j):
        m = 2 * set_of + j
        first = 2 * (me // 2)
        return [
            moved(
                back.at[m, rows_of(first + k)], back.at[m, rows_of(first + k)],
                back_send.at[j, k], back_recv.at[m], {"section": 1 - sec, "tensor": first + k},
            )
            for k in range(2)
        ]

    def back_arrive(m):
        rows = back.at[m, own]
        moved(rows, rows, back_send.at[0, 0], back_recv.at[m], partner).wait_recv()

    def save_norm(l, m, n, r):
        nrm[l, m] = n
        rstd[l, m] = jnp.broadcast_to(r, (C, 128))

    def norm_step_back(l, m, dh, gain):
        n = nrm[l, m]
        dr = norm_back(dh, n, rstd[l, m][:, :1], gain)
        low = dr.astype(BF)
        acc[3 * l] += dh * n
        acc[3 * l + 1] += dh
        acc[3 * l + 2] += low.astype(F32)
        res[m] = dr
        return low

    def word_keys(m, q_rows, q_len):
        return key_mask(
            q_rows, q_len, RW, WORDS, [lengths_ref[ITEMS_MB * m + k] for k in range(ITEMS_MB)]
        )

    def region_keys(q_rows, q_len):
        return key_mask(q_rows, q_len, RR, REGIONS)

    def layer_a(m):
        xlow[m] = x_ref[m]
        cur[m] = x_ref[m, own].astype(F32)
        for mod, (lo, hi) in enumerate(SPANS):
            out = (dot_nt(xlow[m, lo:hi], wqkv_ref[mod]) + bqkv_ref[mod]).astype(BF)
            q, k, v = out[:, :HW], out[:, HW : 2 * HW], out[:, 2 * HW :]
            qkv[0, m, lo:hi], qkv[1, m, lo:hi], qkv[2, m, lo:hi] = q, k, v
            if mod == 0:
                probs, mix = attend(q, k, v, word_keys(m, RW, WORDS))
                p_w[m] = probs
            else:
                probs, mix = attend(q, k, v, region_keys(RR, REGIONS))
                p_r[m] = probs
            mixed[m, lo:hi] = mix
            send[m, lo:hi] = dot(mix, wo_ref[mod]).astype(BF)
        rs_start(m)

    def layer_b(m):
        r = cur[m] + rs_finish(m) + rowp[0]
        n, rs, h = norm_forward(r, rowp[2], rowp[4])
        save_norm(0, m, n, rs)
        cur[m] = h
        alow[m, own] = h.astype(BF)
        ag_start(alow, m)

    def layer_c(m):
        ag_finish(alow, m)
        for mod, (lo, hi) in enumerate(SPANS):
            up = dot(alow[m, lo:hi], w1_ref[mod]) + b1_ref[mod]
            cdf = 0.5 * (1.0 + lax.erf(up * (0.5**0.5)))
            dgelu[m, lo:hi] = cdf + up * jnp.exp(-0.5 * up * up) * 0.3989422804014327
            active = (up * cdf).astype(BF)
            act[m, lo:hi] = active
            send[m, lo:hi] = dot(active, w2_ref[mod]).astype(BF)
        rs_start(m)

    def layer_d(m):
        r = cur[m] + rs_finish(m) + rowp[1]
        n, rs, h = norm_forward(r, rowp[3], rowp[5])
        save_norm(1, m, n, rs)
        return h

    def back_e(m, dh):
        low = norm_step_back(1, m, dh, rowp[3])
        dyf[m, own] = low
        ag_start(dyf, m)

    def back_f(m):
        ag_finish(dyf, m)
        for mod, (lo, hi) in enumerate(SPANS):
            d = (dot_nt(dyf[m, lo:hi], w2_ref[mod]) * dgelu[m, lo:hi]).astype(BF)
            dup[m, lo:hi] = d
            bsum[mod] += jnp.sum(d.astype(F32), axis=0, keepdims=True)
            send[m, lo:hi] = dot_nt(d, w1_ref[mod]).astype(BF)
        rs_start(m)

    def back_g(m):
        dh = res[m] + rs_finish(m)
        low = norm_step_back(0, m, dh, rowp[2])
        dya[m, own] = low
        ag_start(dya, m)

    def back_h(m):
        ag_finish(dya, m)
        for mod, (lo, hi) in enumerate(SPANS):
            dmix = dot_nt(dya[m, lo:hi], wo_ref[mod]).astype(BF)
            probs = p_w[m] if mod == 0 else p_r[m]
            parts = attend_back(
                dmix, probs, qkv[0, m, lo:hi], qkv[1, m, lo:hi], qkv[2, m, lo:hi]
            )
            d = jnp.concatenate(parts, axis=1)
            dqkv[m, lo:hi] = d
            bqsum[mod] += jnp.sum(d.astype(F32), axis=0, keepdims=True)
            send[m, lo:hi] = dot(d, wqkv_ref[mod]).astype(BF)
        rs_start(m)

    def block_of(j):
        return 2 * set_of + j

    def ar_copy(j, mod, turn):
        lo, hi = SPANS[mod]
        return moved(
            send.at[j, lo:hi], got.at[turn, j, lo:hi], ar_send.at[turn, j, mod], ar_recv.at[turn, j, mod],
            halver,
        )

    def ar_start(j, mod, turn, part):
        lo, hi = SPANS[mod]
        send[j, lo:hi] = part.astype(BF)
        ar_copy(j, mod, turn).start()

    def ar_finish(j, mod, turn):
        lo, hi = SPANS[mod]
        ar_copy(j, mod, turn).wait()
        return send[j, lo:hi].astype(F32) + got[turn, j, lo:hi].astype(F32)

    shared = (xlow, alow, dyf, dya, dyc, ybuf)
    for_mate = ((act_m, act), (dup_m, dup), (mixed_m, mixed), (dqkv_m, dqkv), (cmixed_m, cmixed), (cdqkv_m, cdqkv))
    XLOW, ALOW, DYF, DYA, DYC, YBUF, ACT, DUP, MIXED, DQKV, CMIXED, CDQKV = range(12)

    halves = (DYA, DYC, YBUF)

    def half_rows(which):
        return pl.ds(pl.multiple_of(which * (R // 2), R // 2), R // 2)

    def mate_copy(k, j, arriving=False):
        if k < 6:
            src = dst = shared[k]
            src = src.at[block_of(j)]
        else:
            src, dst = for_mate[k - 6]
            src = src.at[j]
        dst = dst.at[2 * (1 - set_of) + j if arriving else block_of(j)]
        if k in halves:
            src, dst = src.at[half_rows(me // 2)], dst.at[half_rows(me // 2)]
        return moved(src, dst, mt_send.at[k, j], mt_recv.at[k, j], mate)

    def mate_start(j, *kinds):
        for k in kinds:
            mate_copy(k, j).start()

    def mate_start_all(*kinds):
        for k in kinds:
            for j in range(2):
                mate_copy(k, j).start()

    def mate_wait(*kinds):
        for k in kinds:
            for j in range(2):
                mate_copy(k, j, True).wait_recv()
                mate_copy(k, j).wait_send()

    def pass_copy(k, j, arriving=False):
        rows = half_rows(1 - me // 2 if arriving else me // 2)
        place = shared[k].at[2 * (1 - set_of) + j, rows]
        return moved(place, place, ps_send.at[k, j], ps_recv.at[k, j], halver)

    def pass_start(k):
        for j in range(2):
            pass_copy(k, j).start()

    def pass_wait(k):
        for j in range(2):
            pass_copy(k, j, True).wait_recv()
            pass_copy(k, j).wait_send()

    both_mods = slice(0, 2)
    half_columns = pl.ds(pl.multiple_of(core * (D // 2), D // 2), D // 2)

    def z_rows(z, count):
        return pl.ds(pl.multiple_of(z * count, count), count)

    gathered = (
        (cwqkv_in, cwqkv_m, 3 * HW // 4, False), (cwo_in, cwo_m, HW // 4, False),
        (wqkv_in, wqkv_m, 3 * HW // 4, True), (wo_in, wo_m, HW // 4, True),
        (w1_in, w1_m, D // 4, True), (w2_in, w2_m, D // 4, True),
    )
    Y_FIRST = (W1,) = (4,)
    CWQKV, CWO, WQKV, WO, W2 = 0, 1, 2, 3, 5

    def gather_copies(k, step):
        src, dst, count, by_mod = gathered[k]
        sems = lambda i: (ga_send.at[k, i], ga_recv.at[k, i])
        at = lambda mods, rows: (mods, rows, half_columns) if by_mod else (rows, half_columns)
        mine = at(y_at, z_rows(z_at, count))
        if step == "x":
            return [moved(src.at[mine], dst.at[mine], *sems(0), mate)]
        if step == "y":
            place = dst.at[mine] if k in Y_FIRST else dst.at[at(y_at, slice(0, 4 * count))]
            return [moved(place, place, *sems(1), other_y)]
        if step == "z":
            place = dst.at[at(both_mods if k in Y_FIRST else y_at, z_rows(z_at, count))]
            return [
                moved(place, place, *sems(1 + o), dp_device(y_at, z_next(o), core)) for o in (1, 2, 3)
            ]
        place = dst.at[at(both_mods, slice(0, 4 * count))]
        return [moved(place, place, *sems(5), other_core)]

    def gather_start(step, *arrays):
        for k in arrays:
            for copy in gather_copies(k, step):
                copy.start()

    def gather_wait(step, *arrays):
        for k in arrays:
            for copy in gather_copies(k, step):
                copy.wait()

    def bias_copies():
        return [
            moved(bqkv_ref, bqkv_m, ga_send.at[6, 0], ga_recv.at[6, 0], mate),
            moved(b1_ref, b1_m, ga_send.at[7, 0], ga_recv.at[7, 0], mate),
        ]

    def save_norm_f(l, j, lo, hi, n, r):
        nrm_f[l, j, lo:hi] = n
        rstd_f[l, j, lo:hi] = jnp.broadcast_to(r, (hi - lo, 128))

    def count_rows(l, mod, dh, n, low):
        for k, value in enumerate((dh * n, dh, low.astype(F32))):
            at = 12 + k if l == 2 else 2 * (3 * l + k) + mod
            row_sums[at] += jnp.sum(value, axis=0, keepdims=True)

    def cross_forward(j):
        m = block_of(j)
        mid_arrive(m)
        mid = midf[m]
        part = None
        shards = ((cwqkv_ref, bqkv_ref, cwo_ref, cmixed, m), (cwqkv_m, bqkv_m, cwo_m, cmixed_m, j))
        for sh, (w, bias, w_out, keep, at) in enumerate(shards):
            slot = 2 * sh + j
            out = (dot_nt(mid, w[...]) + bias[2]).astype(BF)
            q, k, v = out[:, :HW], out[:, HW : 2 * HW], out[:, 2 * HW :]
            cqkv[0, slot], cqkv[1, slot], cqkv[2, slot] = q, k, v
            probs, mix = attend(q[:RW], k[RW:], v[RW:], region_keys(RW, WORDS))
            cp_w[slot] = probs
            keep[at, :RW] = mix
            probs, mix = attend(q[RW:], k[:RW], v[:RW], word_keys(m, RR, REGIONS))
            cp_r[slot] = probs
            keep[at, RW:] = mix
            one = dot(keep[at], w_out[...])
            part = one if part is None else part + one
        for mod, (lo, hi) in enumerate(SPANS):
            ar_start(j, mod, 0, part[lo:hi])
        mate_start(j, CMIXED)

    def attn_forward(j):
        m = block_of(j)
        shards = (
            (wqkv_ref, bqkv_ref, wo_ref, mixed, m), (wqkv_m, bqkv_m, wo_m, mixed_m, j),
        )
        for mod, (lo, hi) in enumerate(SPANS):
            r = midf[m, lo:hi].astype(F32) + ar_finish(j, mod, 0) + cvec_ref[0:1, :]
            n, rs, h = norm_forward(r, cvec_ref[1:2, :], cvec_ref[2:3, :])
            save_norm_f(1, j, lo, hi, n, rs)
            cur_f[j, lo:hi] = h
            low = h.astype(BF)
            xlow[m, lo:hi] = low
            part = None
            for sh, (w, bias, w_out, keep, at) in enumerate(shards):
                slot = 2 * sh + j
                out = (dot_nt(low, w[mod]) + bias[mod]).astype(BF)
                q, k, v = out[:, :HW], out[:, HW : 2 * HW], out[:, 2 * HW :]
                qkv[0, slot, lo:hi], qkv[1, slot, lo:hi], qkv[2, slot, lo:hi] = q, k, v
                if mod == 0:
                    probs, mix = attend(q, k, v, word_keys(m, RW, WORDS))
                    p_w[slot] = probs
                else:
                    probs, mix = attend(q, k, v, region_keys(RR, REGIONS))
                    p_r[slot] = probs
                keep[at, lo:hi] = mix
                one = dot(mix, w_out[mod])
                part = one if part is None else part + one
            ar_start(j, mod, 1, part)
        mate_start(j, XLOW, MIXED)

    def ffn_forward(j):
        m = block_of(j)
        shards = ((w1_ref, b1_ref, w2_ref, act, m), (w1_m, b1_m, w2_m, act_m, j))
        for mod, (lo, hi) in enumerate(SPANS):
            r = cur_f[j, lo:hi] + ar_finish(j, mod, 1) + out_bias_ref[0, mod, 0:1, :]
            n, rs, h = norm_forward(r, gain_ref[0, mod, 0:1, :], shift_ref[0, mod, 0:1, :])
            save_norm_f(0, j, lo, hi, n, rs)
            cur_f[j, lo:hi] = h
            low = h.astype(BF)
            alow[m, lo:hi] = low
            part = None
            for sh, (w, bias, w_out, keep, at) in enumerate(shards):
                up = dot(low, w[mod]) + bias[mod]
                cdf = 0.5 * (1.0 + lax.erf(up * (0.5**0.5)))
                dgelu[2 * sh + j, lo:hi] = cdf + up * jnp.exp(-0.5 * up * up) * 0.3989422804014327
                active = (up * cdf).astype(BF)
                keep[at, lo:hi] = active
                one = dot(active, w_out[mod])
                part = one if part is None else part + one
            ar_start(j, mod, 0, part)
        mate_start(j, ALOW, ACT)

    def ffn_turn(j):
        m = block_of(j)
        shards = ((w1_ref, w2_ref, dup, m), (w1_m, w2_m, dup_m, j))
        for mod, (lo, hi) in enumerate(SPANS):
            r = cur_f[j, lo:hi] + ar_finish(j, mod, 0) + out_bias_ref[0, mod, 1:2, :]
            gain = gain_ref[0, mod, 1:2, :]
            n, rs, h = norm_forward(r, gain, shift_ref[0, mod, 1:2, :])
            ybuf[m, lo:hi] = h.astype(BF)
            scale = scales(m, 1 - mod, hi - lo, (WORDS, REGIONS)[mod])
            dh = x_ref[m, lo:hi].astype(F32) * scale
            dr = norm_back(dh, n, rs, gain)
            res_f[j, lo:hi] = dr
            low = dr.astype(BF)
            dyf[m, lo:hi] = low
            count_rows(1, mod, dh, n, low)
            part = None
            for sh, (w_in, w_out, keep, at) in enumerate(shards):
                d = (dot_nt(low, w_out[mod]) * dgelu[2 * sh + j, lo:hi]).astype(BF)
                keep[at, lo:hi] = d
                one = dot_nt(d, w_in[mod])
                part = one if part is None else part + one
            ar_start(j, mod, 1, part)
        mate_start(j, DYF)
        pl.when(j == 0)(lambda: mate_start(0, DUP))

    def attn_backward(j):
        m = block_of(j)
        shards = ((wqkv_ref, wo_ref, dqkv, m), (wqkv_m, wo_m, dqkv_m, j))
        for mod, (lo, hi) in enumerate(SPANS):
            dh = res_f[j, lo:hi] + ar_finish(j, mod, 1)
            n = nrm_f[0, j, lo:hi]
            dr = norm_back(dh, n, rstd_f[0, j, lo:hi][:, :1], gain_ref[0, mod, 0:1, :])
            res_f[j, lo:hi] = dr
            low = dr.astype(BF)
            dya[m, lo:hi] = low
            count_rows(0, mod, dh, n, low)
            part = None
            for sh, (w, w_out, keep, at) in enumerate(shards):
                slot = 2 * sh + j
                dmix = dot_nt(low, w_out[mod]).astype(BF)
                probs = p_w[slot] if mod == 0 else p_r[slot]
                parts = attend_back(
                    dmix, probs, qkv[0, slot, lo:hi], qkv[1, slot, lo:hi], qkv[2, slot, lo:hi]
                )
                d = jnp.concatenate(parts, axis=1)
                keep[at, lo:hi] = d
                one = dot(d, w[mod])
                part = one if part is None else part + one
            ar_start(j, mod, 0, part)

    def cross_backward(j):
        m = block_of(j)
        for mod, (lo, hi) in enumerate(SPANS):
            dh = res_f[j, lo:hi] + ar_finish(j, mod, 0)
            n = nrm_f[1, j, lo:hi]
            dr = norm_back(dh, n, rstd_f[1, j, lo:hi][:, :1], cvec_ref[1:2, :])
            res_f[j, lo:hi] = dr
            low = dr.astype(BF)
            dyc[m, lo:hi] = low
            count_rows(2, mod, dh, n, low)
        part = None
        shards = ((cwqkv_ref, cwo_ref, cdqkv, m), (cwqkv_m, cwo_m, cdqkv_m, j))
        for sh, (w, w_out, keep, at) in enumerate(shards):
            slot = 2 * sh + j
            dmix = dot_nt(dyc[m], w_out[...]).astype(BF)
            q, k, v = cqkv[0, slot], cqkv[1, slot], cqkv[2, slot]
            dq_w, dk_r, dv_r = attend_back(dmix[:RW], cp_w[slot], q[:RW], k[RW:], v[RW:])
            dq_r, dk_w, dv_w = attend_back(dmix[RW:], cp_r[slot], q[RW:], k[:RW], v[:RW])
            keep[at, :RW] = jnp.concatenate([dq_w, dk_w, dv_w], axis=1)
            keep[at, RW:] = jnp.concatenate([dq_r, dk_r, dv_r], axis=1)
            one = dot(keep[at], w[...])
            part = one if part is None else part + one
        for mod, (lo, hi) in enumerate(SPANS):
            ar_start(j, mod, 1, part[lo:hi])

    def to_section_0(j):
        m = block_of(j)
        for mod, (lo, hi) in enumerate(SPANS):
            back[m, lo:hi] = (res_f[j, lo:hi] + ar_finish(j, mod, 1)).astype(BF)
        for copy in back_copies(j):
            copy.start()

    def column_sums(buf, lo, hi):
        rows = buf[:, lo:hi, :].astype(F32).reshape(MB * (hi - lo), buf.shape[-1])
        return jnp.sum(rows, axis=0, keepdims=True)

    def scales(m, flag, count, length):
        index = lax.broadcasted_iota(jnp.int32, (count, 1), 0)
        scale = jnp.ones((count, 1), F32)
        for k in range(ITEMS_MB):
            value = jnp.where(flags_ref[ITEMS_MB * m + k] == flag, 0.25, 1.0)
            scale = jnp.where(index >= k * length, value, scale)
        return scale

    def outer_tile(left, right, lo, hi, j, store):
        start = j * (D // 2)
        columns = pl.ds(start if isinstance(j, int) else pl.multiple_of(start, D // 2), D // 2)
        a = left[:, lo:hi, columns].reshape(MB * (hi - lo), D // 2)
        b = right[:, lo:hi, :].reshape(MB * (hi - lo), right.shape[-1])
        store(dot_tn(a, b))

    def outer(left, right, lo, hi, store):
        pl.loop(0, 2)(
            lambda j: outer_tile(left, right, lo, hi, j, p(store, j))
        )

    def store_at(block, lo, hi):
        def store(j, value):
            g_ref[block, j, :, :, :, lo:hi] = value.astype(BF).reshape(4, 2, 48, hi - lo)

        return store

    def ffn_piece(k):
        mod, second = k // 2, k % 2
        left, right = ((alow, dup), (dyf, act))[second]
        outer(left, right, *SPANS[mod], store_at(1 + 4 * mod + second, 0, D))

    def attn_piece(k):
        mod, second = k // 2, k % 2
        left, right = ((xlow, dqkv), (dya, mixed))[second]
        outer(left, right, *SPANS[mod], store_at(4 * mod, *((0, 3 * HW), (3 * HW, D))[second]))

    def cross_outer():
        def store(j, lo, hi):
            def put(value):
                value = value.astype(BF).reshape(2, 4, 2, 24, hi - lo)
                g_ref[3, :, :, :, 24 * j : 24 * j + 24, lo:hi] = value

            return put

        for j in range(2):
            outer_tile(midf, cdqkv, 0, R, j, store(j, 0, 3 * HW))
            outer_tile(dyc, cmixed, 0, R, j, store(j, 3 * HW, D))

    def dw_copies(group, phase):
        index, y_first, lo, hi = group
        sems = lambda k: (dw_send.at[index, k], dw_recv.at[index, k])
        blocks = slice(lo, hi)
        if phase == 0:
            src = g_ref.at[blocks, :, :, 1 - core]
            return [moved(src, from_core.at[blocks], *sems(0), other_core)]
        if y_first and phase == 1:
            src = g_ref.at[blocks, 1 - y_at, :, core]
            return [moved(src, from_y.at[blocks], *sems(1), other_y)]
        if y_first:
            return [
                moved(
                    g_ref.at[blocks, y_at, z_next(o), core], from_z.at[blocks, o - 1],
                    *sems(1 + o), dp_device(y_at, z_next(o), core),
                )
                for o in (1, 2, 3)
            ]
        late = slice(lo - 4, hi - 4)
        if phase == 1:
            return [
                moved(
                    g_ref.at[blocks, :, z_next(o), core], from_zs.at[late, o - 1],
                    *sems(1 + o), dp_device(y_at, z_next(o), core),
                )
                for o in (1, 2, 3)
            ]
        src = g_ref.at[blocks, 1 - y_at, z_at, core]
        return [moved(src, from_ys.at[late], *sems(1), other_y)]

    def dw_start(group, phase):
        for copy in dw_copies(group, phase):
            copy.start()

    def dw_finish(group, phase):
        for copy in dw_copies(group, phase):
            copy.wait()
        index, y_first, lo, hi = group

        def add(b):
            if phase == 0:
                for y in range(2):
                    mine = g_ref[b, y, :, core].astype(F32)
                    g_ref[b, y, :, core] = (mine + from_core[b, y].astype(F32)).astype(BF)
            elif phase == 1 and y_first:
                mine = g_ref[b, y_at, :, core].astype(F32)
                g_ref[b, y_at, :, core] = (mine + from_y[b].astype(F32)).astype(BF)
            elif phase == 1:
                total = g_ref[b, :, z_at, core].astype(F32)
                for o in range(3):
                    total = total + from_zs[b - 4, o].astype(F32)
                g_ref[b, :, z_at, core] = total.astype(BF)
            else:
                total = g_ref[b, y_at, z_at, core].astype(F32)
                for o in range(3 if y_first else 0):
                    total = total + from_z[b, o].astype(F32)
                if not y_first:
                    total = total + from_ys[b - 4].astype(F32)
                dw_ref[b] = total

        pl.loop(lo, hi)(add)

    def dw_turn(group, phase):
        dw_finish(group, phase)
        dw_start(group, phase + 1)

    FFN_W = (0, True, 1, 3)
    FFN_R = (1, False, 5, 7)
    ATTN_W = (2, True, 0, 1)
    ATTN_R = (3, False, 4, 5)
    CROSS = (4, True, 3, 4)

    def sm_copies(step):
        sems = lambda k: (sm_send.at[k], sm_recv.at[k])
        if step == 0:
            return [
                moved(sums_t.at[me], sums_t.at[me], *sems(o - 1), peer(o)) for o in range(1, TENSOR)
            ]
        if step == 1:
            return [moved(sums.at[0], sums_c, *sems(3), other_core)]
        if step == 2:
            return [moved(sums.at[1], sums_y, *sems(4), other_y)]
        return [
            moved(
                sums.at[2], sums_z.at[o - 1], *sems(4 + o), dp_device(y_at, z_next(o), core)
            )
            for o in (1, 2, 3)
        ]

    def sm_start(step):
        for copy in sm_copies(step):
            copy.start()

    def sm_wait(step):
        for copy in sm_copies(step):
            copy.wait()

    def small_norms_all():
        for k in range(15):
            sums_t[me, k : k + 1, :] = jnp.where(me < 2, row_sums[k], 0.0)
        sums_t[me, 15:16, :] = jnp.zeros((1, D), F32)
        sm_start(0)

    def small_norms():
        sums_t[me] = jnp.zeros((16, D), F32)
        for l in range(2):
            for k in range(3):
                a = acc[3 * l + k]
                at = 2 * (3 * l + k)
                sums_t[me, at : at + 1, :] = jnp.sum(jnp.where(is_word, a, 0.0), axis=0, keepdims=True)
                sums_t[me, at + 1 : at + 2, :] = jnp.sum(
                    jnp.where(is_word, 0.0, a), axis=0, keepdims=True
                )
        sm_start(0)

    def small_biases():
        sm_wait(0)
        sums[0] = jnp.zeros((24, D), F32)
        sums[0, :16] = sums_t[0] + sums_t[1] + sums_t[2] + sums_t[3]
        for mod in range(2):
            sums[0, 16 + mod : 17 + mod, :] = bsum[mod]
        for k in range(3):
            sums[0, 18 + k : 19 + k, : 3 * HW] = bqsum[k]
        sm_start(1)

    def small_y():
        sm_wait(1)
        sums[1] = sums[0] + sums_c[...]
        sm_start(2)

    def small_z():
        sm_wait(2)
        sums[2] = sums[1] + sums_y[...]
        sm_start(3)

    def small_last():
        sm_wait(3)
        s_ref[...] = sums[2] + sums_z[0] + sums_z[1] + sums_z[2]

    def packet():
        return moved(pack.at[0], pack.at[1], pk_send, pk_recv, partner)

    def each(*steps, after=()):
        def body(m):
            for step in steps:
                step(m)
            for k, extra in enumerate(after):
                if extra is not None:
                    pl.when(m == k)(extra)

        pl.loop(0, MB)(body)

    def then(*steps):
        def run():
            for step in steps:
                step()

        return run

    def pair(step):
        pl.loop(0, 2)(step)

    @pl.when(head)
    def _():
        def to_partner(m):
            midf[m, own] = layer_d(m).astype(BF)
            first = m // 2
            for k, t in enumerate((first, 3 - first)):
                mid_copy(m, k, t).start()

        def to_others(m):
            first = m // 2
            for k, t in enumerate((1 - first, 2 + first)):
                mid_copy(m, 2 + k, t).start()

        def from_partner(m):
            for k in range(TENSOR):
                mid_copy(m, k, 0).wait_send()
            back_arrive(m)
            back_e(m, back[m, own].astype(F32))

        def last(m):
            ybuf[m, own] = (res[m] + rs_finish(m)).astype(BF)
            ag_start(ybuf, m, y_send, y_recv)

        wait_weights(0, 1)
        each(layer_a)
        wait_weights(2, 3)
        each(layer_b)
        each(layer_c)
        each(to_partner)
        each(to_others)
        each(from_partner)
        each(back_f)
        ffn_piece(2)
        ffn_piece(3)
        dw_start(FFN_R, 0)
        each(
            back_g,
            after=(
                p(ffn_piece, 0),
                then(p(dw_turn, FFN_R, 0), p(ffn_piece, 1), p(dw_start, FFN_W, 0)),
            ),
        )
        small_norms()
        each(back_h, after=(p(dw_turn, FFN_W, 0),))
        attn_piece(2)
        attn_piece(3)
        dw_start(ATTN_R, 0)
        attn_piece(0)
        attn_piece(1)
        dw_start(ATTN_W, 0)
        small_biases()
        each(last, after=(p(dw_turn, ATTN_R, 0), p(dw_turn, FFN_R, 1), p(dw_turn, ATTN_W, 0)))
        small_y()
        dw_turn(FFN_W, 1)
        small_z()

    @pl.when(cross)
    def _():
        gather_start("x", CWQKV, CWO, WQKV, WO)
        for copy in bias_copies():
            copy.start()
        gather_start("x", W2, W1)
        gather_wait("x", CWQKV, CWO)
        gather_start("z", CWQKV, CWO)
        gather_wait("x", WQKV, WO)
        gather_start("z", WQKV, WO)
        gather_wait("x", W2, W1)
        gather_start("y", W1)
        gather_start("z", W2)
        gather_wait("z", CWQKV, CWO)
        gather_start("core", CWQKV, CWO)
        gather_wait("y", W1)
        gather_start("z", W1)
        gather_wait("z", WQKV, WO)
        gather_start("y", WQKV, WO)
        for copy in bias_copies():
            copy.wait()
        gather_wait("core", CWQKV, CWO)
        wait_weights(0, 1, 2, 3, 4, 5)
        cross_forward(0)
        gather_wait("z", W2)
        gather_start("y", W2)
        gather_wait("y", WQKV, WO)
        gather_start("core", WQKV, WO)
        cross_forward(1)
        gather_wait("core", WQKV, WO)
        attn_forward(0)
        gather_wait("z", W1)
        gather_wait("y", W2)
        gather_start("core", W1, W2)
        attn_forward(1)
        gather_wait("core", W1, W2)
        pair(ffn_forward)
        pair(ffn_turn)
        pair(attn_backward)
        pair(cross_backward)
        pair(to_section_0)
        mate_start_all(DYC)
        mate_start(1, DUP)
        mate_start_all(CDQKV)
        small_norms_all()
        mate_wait(CMIXED, XLOW, MIXED, ALOW, ACT, DYF)
        mate_wait(DYC)
        pass_start(DYC)
        mate_start_all(DYA)
        mate_wait(DUP)
        mate_start_all(DQKV)
        ffn_piece(2)
        ffn_piece(3)
        dw_start(FFN_R, 0)
        ffn_piece(0)
        ffn_piece(1)
        dw_start(FFN_W, 0)
        for mod, (lo, hi) in enumerate(SPANS):
            bsum[mod] = column_sums(dup, lo, hi)
        dw_turn(FFN_R, 0)
        dw_turn(FFN_W, 0)
        mate_wait(DYA)
        pass_start(DYA)
        for k in range(2):
            mid_arrive(2 * (1 - set_of) + k)
        mate_wait(CDQKV)
        mate_start_all(YBUF)
        pass_wait(DYC)
        cross_outer()
        dw_start(CROSS, 0)
        bqsum[2] = column_sums(cdqkv, 0, R)
        dw_turn(CROSS, 0)
        mate_wait(DQKV)
        pass_wait(DYA)
        attn_piece(2)
        attn_piece(3)
        dw_start(ATTN_R, 0)
        attn_piece(0)
        attn_piece(1)
        dw_start(ATTN_W, 0)
        for mod, (lo, hi) in enumerate(SPANS):
            bqsum[mod] = column_sums(dqkv, lo, hi)
        small_biases()
        mate_wait(YBUF)
        pass_start(YBUF)
        dw_turn(FFN_R, 1)
        dw_turn(CROSS, 1)
        dw_turn(ATTN_R, 0)
        dw_turn(ATTN_W, 0)
        small_y()
        dw_turn(FFN_W, 1)
        small_z()
        pass_wait(YBUF)
        pair(lambda j: [copy.wait_send() for copy in back_copies(j)] and None)

    def write(m):
        @pl.when(head)
        def _():
            ag_finish(ybuf, m, y_send, y_recv)

        y_ref[m] = ybuf[m]

    each(write)
    dw_finish(FFN_R, 2)
    dw_turn(ATTN_R, 1)
    dw_turn(ATTN_W, 1)
    dw_finish(FFN_W, 2)
    small_last()

    @pl.when(cross)
    def _():
        dw_finish(CROSS, 2)
        pack[0, :24] = dw_ref[3, :24]
        pack[0, 24:] = s_ref[...]
        packet().start()
        dc_ref[...] = dw_ref[3, 24:]
        sc_ref[...] = s_ref[...]

    dw_finish(ATTN_W, 2)
    dw_finish(ATTN_R, 2)
    pl.when(cross)(lambda: packet().wait_send())

    @pl.when(head)
    def _():
        packet().wait_recv()
        dc_ref[...] = pack[1, :24]
        sc_ref[...] = pack[1, 24:]


def arrange(
    y_ref, dw_ref, s_ref, dc_ref, sc_ref,
    words, regions, qkv_g, qv_bias_g, out_g, in_g, b1_g, ffo_g, obias_g, gain_g, shift_g,
    cqkv_g, cqv_bias_g, cout_g, cobias_g, cgain_g, cshift_g,
):
    place = lax.axis_index("dp")
    both = lax.axis_index("section") * 16 + place

    def from_column(rows, column):
        return pltpu.roll(rows, lax.rem(D - column, D), 1)

    for ref, (lo, hi), length in zip((words, regions), SPANS, (WORDS, REGIONS)):
        padded = y_ref[:, lo:hi, :].reshape(MB * (hi - lo), D)
        rows = dot(spread(hi - lo, length, True), padded)
        ref[0] = rows.reshape(length, ITEMS_LOCAL, D)
    small = s_ref[...]
    for mod in range(2):
        attn = dw_ref[4 * mod]
        for j in range(3):
            qkv_g[0, mod, j] = attn[:, j * HW : (j + 1) * HW]
        out_g[0, mod] = attn[:, 3 * HW :]
        in_g[0, mod] = dw_ref[4 * mod + 1]
        ffo_g[0, mod] = dw_ref[4 * mod + 2]
    columns = from_column(small, 48 * place)[:, :48]
    for mod in range(2):
        for l in range(2):
            for k, ref in enumerate((gain_g, shift_g, obias_g)):
                at = 2 * (3 * l + k) + mod
                ref[0, mod, l : l + 1, :] = columns[at : at + 1]
    columns = from_column(small, 8 * place)
    for mod in range(2):
        for k in range(6):
            b1_g[0, k, mod : mod + 1, :] = columns[16 + mod : 17 + mod, 128 * k : 128 * k + 8]
    columns = from_column(small, 4 * place)
    for mod in range(2):
        for j in range(2):
            for h in range(LOCAL_HEADS):
                lo = 2 * j * HW + h * HEAD_DIM
                qv_bias_g[0, mod, h, j : j + 1, :] = columns[18 + mod : 19 + mod, lo : lo + 4]
    wide = dc_ref[...]
    for j in range(3):
        cqkv_g[j] = wide[:, j * HW : (j + 1) * HW]
    cout_g[...] = wide[:, 3 * HW :]
    small = sc_ref[...]
    columns = from_column(small, 24 * both)
    for k, ref in enumerate((cgain_g, cshift_g, cobias_g)):
        ref[...] = columns[12 + k, :24]
    columns = from_column(small, 2 * both)[20:21]
    for j in range(2):
        heads = []
        for h in range(LOCAL_HEADS):
            lo = 2 * j * HW + h * HEAD_DIM
            heads.append(columns[:, lo : lo + 2])
        cqv_bias_g[j] = jnp.concatenate(heads, axis=0).T


def local(
    words, regions, word_lengths, task_flags, attn_qkv, attn_qv_bias, attn_out, ffn_in, ffn_in_bias,
    ffn_out, out_bias, norm_gain, norm_bias, cross_qkv, cross_qv_bias, cross_out, cross_out_bias,
    cross_norm_gain, cross_norm_bias,
):
    inputs = (
        words.transpose(0, 2, 1, 3), regions.transpose(0, 2, 1, 3), word_lengths, task_flags,
        attn_qkv.transpose(0, 1, 3, 4, 2).reshape(2, 3 * HW, D), attn_qv_bias.transpose(0, 1, 3, 2, 4), attn_out[0],
        ffn_in[0], ffn_in_bias.transpose(0, 2, 1, 3), ffn_out[0], out_bias, norm_gain, norm_bias,
        cross_qkv.transpose(1, 2, 0).reshape(3 * HW, D), cross_qv_bias.transpose(1, 0, 2), cross_out,
        cross_out_bias, cross_norm_gain, cross_norm_bias,
    )

    vmem = pl.BlockSpec(memory_space=pltpu.VMEM)
    smem = pl.BlockSpec(memory_space=pltpu.SMEM)
    hbm = pl.BlockSpec(memory_space=pl.ANY)
    mb_rows = lambda width, dtype: pltpu.VMEM((MB, R, width), dtype)
    own_rows = lambda count: pltpu.VMEM((count, MB, C, D), F32)
    y, g, s, dc, sc = pl.pallas_call(
        kernel,
        out_shape=(
            jax.ShapeDtypeStruct((MB, R, D), BF),
            jax.ShapeDtypeStruct((7, 48, D), F32),
            jax.ShapeDtypeStruct((24, D), F32),
            jax.ShapeDtypeStruct((24, D), F32),
            jax.ShapeDtypeStruct((24, D), F32),
        ),
        in_specs=[smem if k in (2, 3) else hbm if k in (4, 6, 7, 9, 13, 15) else vmem for k in range(len(inputs))],
        out_specs=[vmem] * 5,
        scratch_shapes=[
            mb_rows(D, BF),
            pltpu.VMEM((3, 1, 3 * HW), F32),
            pltpu.VMEM((2, 1, D), F32),
            pltpu.VMEM((3, D), F32),
            mb_rows(D, BF),
            pltpu.VMEM((MB, TENSOR - 1, C, D), BF),
            *[mb_rows(D, BF) for _ in range(8)],
            pltpu.VMEM((3, MB, R, HW), BF),
            mb_rows(HW, BF),
            mb_rows(3 * HW, BF),
            pltpu.VMEM((3, MB, R, HW), BF),
            mb_rows(HW, BF),
            mb_rows(3 * HW, BF),
            mb_rows(D, BF),
            mb_rows(D, BF),
            mb_rows(D, F32),
            pltpu.VMEM((MB, 3 * RW, RW), F32),
            pltpu.VMEM((MB, 3 * RR, RR), F32),
            pltpu.VMEM((MB, 3 * RW, RR), F32),
            pltpu.VMEM((MB, 3 * RR, RW), F32),
            pltpu.VMEM((MB, C, D), F32),
            pltpu.VMEM((MB, C, D), F32),
            pltpu.VMEM((2, MB, C, D), F32),
            pltpu.VMEM((2, MB, C, 128), F32),
            pltpu.VMEM((6, C, D), F32),
            pltpu.VMEM((6, C, D), F32),
            pltpu.VMEM((2, 1, D), F32),
            pltpu.VMEM((3, 1, 3 * HW), F32),
            pltpu.VMEM((2, 3 * HW, D), BF),
            pltpu.VMEM((2, HW, D), BF),
            pltpu.VMEM((2, D, D), BF),
            pltpu.VMEM((2, D, D), BF),
            pltpu.VMEM((3 * HW, D), BF),
            pltpu.VMEM((HW, D), BF),
            pltpu.VMEM((2, 3 * HW, D), BF),
            pltpu.VMEM((2, HW, D), BF),
            pltpu.VMEM((2, D, D), BF),
            pltpu.VMEM((2, D, D), BF),
            pltpu.VMEM((3 * HW, D), BF),
            pltpu.VMEM((HW, D), BF),
            pltpu.VMEM((3, 1, 3 * HW), F32),
            pltpu.VMEM((2, 1, D), F32),
            pltpu.VMEM((2, 2, R, D), BF),
            *[pltpu.VMEM((2, R, w), BF) for w in (D, D, HW, 3 * HW, HW, 3 * HW)],
            pltpu.VMEM((2, R, D), F32),
            pltpu.VMEM((2, R, D), F32),
            pltpu.VMEM((2, 2, R, D), F32),
            pltpu.VMEM((2, 2, R, 128), F32),
            pltpu.VMEM((16, 1, D), F32),
            pltpu.VMEM((7, 2, 4, 2, 48, D), BF),
            pltpu.VMEM((7, 2, 4, 48, D), BF),
            pltpu.VMEM((4, 4, 48, D), BF),
            pltpu.VMEM((3, 3, 2, 48, D), BF),
            pltpu.VMEM((4, 3, 48, D), BF),
            pltpu.VMEM((3, 48, D), BF),
            pltpu.VMEM((3, 24, D), F32),
            pltpu.VMEM((TENSOR, 16, D), F32),
            pltpu.VMEM((24, D), F32),
            pltpu.VMEM((24, D), F32),
            pltpu.VMEM((3, 24, D), F32),
            pltpu.VMEM((2, 48, D), F32),
            *[pltpu.SemaphoreType.DMA((MB, TENSOR - 1)) for _ in range(6)],
            pltpu.SemaphoreType.DMA((MB, TENSOR)),
            pltpu.SemaphoreType.DMA((MB, TENSOR)),
            pltpu.SemaphoreType.DMA((5, 5)),
            pltpu.SemaphoreType.DMA((5, 5)),
            pltpu.SemaphoreType.DMA((8,)),
            pltpu.SemaphoreType.DMA((8,)),
            pltpu.SemaphoreType.DMA,
            pltpu.SemaphoreType.DMA,
            pltpu.SemaphoreType.DMA((2, 2)),
            pltpu.SemaphoreType.DMA((MB,)),
            *[pltpu.SemaphoreType.DMA((2, 2, 2)) for _ in range(2)],
            *[pltpu.SemaphoreType.DMA((12, 2)) for _ in range(2)],
            *[pltpu.SemaphoreType.DMA((8, 6)) for _ in range(2)],
            *[pltpu.SemaphoreType.DMA((6, 2)) for _ in range(2)],
            pltpu.SemaphoreType.DMA((6,)),
        ],
        compiler_params=pltpu.CompilerParams(
            collective_id=0, has_side_effects=True, vmem_limit_bytes=63 * 2**20
        ),
    )(*inputs)

    shapes = (
        (1, WORDS, ITEMS_LOCAL, D), (1, REGIONS, ITEMS_LOCAL, D), (1, 2, 3, 48, HW),
        (1, 2, LOCAL_HEADS, 2, 4), (1, 2, 48, HW), (1, 2, 48, D), (1, 6, 2, 8), (1, 2, 48, D),
        (1, 2, 2, 48), (1, 2, 2, 48), (1, 2, 2, 48), (3, 24, HW), (2, 2, LOCAL_HEADS), (24, HW),
        (24,), (24,), (24,),
    )
    orders = {
        0: (0, 2, 1, 3), 1: (0, 2, 1, 3), 2: (0, 1, 3, 2, 4), 3: (0, 1, 3, 2, 4), 4: (0, 1, 3, 2),
        6: (0, 2, 1, 3), 7: (0, 1, 3, 2), 11: (1, 0, 2), 12: (0, 2, 1), 13: (1, 0),
    }
    outs = pl.pallas_call(
        arrange,
        out_shape=tuple(jax.ShapeDtypeStruct(shape, F32) for shape in shapes),
        in_specs=[vmem] * 5,
        out_specs=[vmem] * len(shapes),
        compiler_params=pltpu.CompilerParams(vmem_limit_bytes=60 * 2**20),
    )(y, g, s, dc, sc)
    return tuple(out.transpose(orders[k]) if k in orders else out for k, out in enumerate(outs))


def solution(mesh):
    in_specs = (
        P("section", "dp", None, None),
        P("section", "dp", None, None),
        P("dp"),
        P("dp"),
        P("section", None, None, None, "tensor"),
        P("section", None, None, "tensor", None),
        P("section", None, "tensor", None),
        P("section", None, None, "tensor"),
        P("section", None, "tensor", None),
        P("section", None, "tensor", None),
        P("section", None, None, None),
        P("section", None, None, None),
        P("section", None, None, None),
        P(None, None, "tensor"),
        P(None, "tensor", None),
        P("tensor", None),
        P(),
        P(),
        P(),
    )
    out_specs = (
        P("section", "dp", None, None),
        P("section", "dp", None, None),
        P("section", None, "dp", None, "tensor"),
        P("section", None, None, "tensor", "dp"),
        P("section", None, "tensor", "dp"),
        P("section", None, "dp", "tensor"),
        P("section", None, "tensor", "dp"),
        P("section", None, "tensor", "dp"),
        P("section", None, None, "dp"),
        P("section", None, None, "dp"),
        P("section", None, None, "dp"),
        P(("section", "dp"), None, "tensor"),
        P(None, "tensor", ("section", "dp")),
        P("tensor", ("section", "dp")),
        P(("section", "dp")),
        P(("section", "dp")),
        P(("section", "dp")),
    )
    return jax.shard_map(local, mesh=mesh, in_specs=in_specs, out_specs=out_specs, check_vma=False)
```

```python
import functools

import jax
import jax.numpy as jnp
from jax import lax
from jax.experimental import pallas as pl
from jax.experimental.pallas import tpu as pltpu
from jax.sharding import PartitionSpec as P

MESH = pl.DeviceIdType.MESH
BF = jnp.bfloat16
F32 = jnp.float32
HEAD_DIM = 64
LOCAL_HEADS = 3
HW = HEAD_DIM * LOCAL_HEADS
WORDS = 20
REGIONS = 36
D = 768
ITEMS_LOCAL = 8
TENSOR = 4

ITEMS_MB = 2
MB = ITEMS_LOCAL // ITEMS_MB
RW = 48
RR = 80
R = RW + RR
C = R // TENSOR
SPANS = ((0, RW), (RW, R))

EPSILON = 1e-06
MASKED = -1000000000.0
SCALING = HEAD_DIM ** (-0.5)


def dot(a, b):
    return lax.dot_general(a, b, (((1,), (0,)), ((), ())), preferred_element_type=F32)


def dot_nt(a, b):
    return lax.dot_general(a, b, (((1,), (1,)), ((), ())), preferred_element_type=F32)


def dot_tn(a, b):
    return lax.dot_general(a, b, (((0,), (0,)), ((), ())), preferred_element_type=F32)


def head_masks():
    lane = lax.broadcasted_iota(jnp.int32, (1, HW), 1)
    return [
        ((lane >= h * HEAD_DIM) & (lane < (h + 1) * HEAD_DIM)).astype(F32) for h in range(LOCAL_HEADS)
    ]


def by_head(a):
    masks = [m.astype(BF) for m in head_masks()]
    return jnp.concatenate([a * m for m in masks], axis=0)


def join_heads(stacked):
    rows = stacked.shape[0] // LOCAL_HEADS
    masks = head_masks()
    total = stacked[:rows] * masks[0]
    for h in range(1, LOCAL_HEADS):
        total = total + stacked[h * rows : (h + 1) * rows] * masks[h]
    return total


def item_of(shape, axis, length):
    index = lax.broadcasted_iota(jnp.int32, shape, axis)
    item = jnp.zeros(shape, jnp.int32)
    for k in range(1, ITEMS_MB + 1):
        item = item + (index >= k * length).astype(jnp.int32)
    return item


def spread(rows, length, transposed=False):
    count = ITEMS_LOCAL * length
    shape = (count, MB * rows) if transposed else (MB * rows, count)
    at = lax.broadcasted_iota(jnp.int32, shape, 0 if transposed else 1)
    padded = lax.broadcasted_iota(jnp.int32, shape, 1 if transposed else 0)
    item, position = at & (ITEMS_LOCAL - 1), at >> 3
    block, within = item >> (ITEMS_MB.bit_length() - 1), item & (ITEMS_MB - 1)
    target = block * rows + within * length + position
    return (target == padded).astype(F32).astype(BF)


def key_mask(q_rows, q_len, k_rows, k_len, lengths=None):
    shape = (q_rows, k_rows)
    item = item_of(shape, 1, k_len)
    key = lax.broadcasted_iota(jnp.int32, shape, 1)
    mask = (item_of(shape, 0, q_len) == item) & (key < ITEMS_MB * k_len)
    if lengths is not None:
        for k, length in enumerate(lengths):
            mask = mask & ((item != k) | (key < k * k_len + length))
    return mask


def attend(q, k, v, mask):
    scores = dot_nt(by_head(q), k) * SCALING
    mask = jnp.concatenate([mask] * LOCAL_HEADS, axis=0)
    scores = jnp.where(mask, scores, MASKED)
    e = jnp.exp(scores - jnp.max(scores, axis=-1, keepdims=True))
    probs = e / jnp.sum(e, axis=-1, keepdims=True)
    mixed = join_heads(dot(probs.astype(BF), v)).astype(BF)
    return probs, mixed


def attend_back(dmix, probs, q, k, v):
    d3 = by_head(dmix)
    dp = dot_nt(d3, v)
    ds = (probs * (dp - jnp.sum(probs * dp, axis=-1, keepdims=True))).astype(BF)
    dv = dot_tn(probs.astype(BF), d3).astype(BF)
    dq = (join_heads(dot(ds, k)) * SCALING).astype(BF)
    dk = (dot_tn(ds, by_head(q)) * SCALING).astype(BF)
    return dq, dk, dv


def norm_forward(r, gain, shift):
    center = r - jnp.mean(r, axis=-1, keepdims=True)
    spread = jnp.mean(center * center, axis=-1, keepdims=True)
    rstd = lax.rsqrt(spread + EPSILON)
    n = center * rstd
    return n, rstd, n * gain + shift


def norm_back(dh, n, rstd, gain):
    dn = dh * gain
    return rstd * (
        dn - jnp.mean(dn, axis=-1, keepdims=True) - n * jnp.mean(dn * n, axis=-1, keepdims=True)
    )


def kernel(
    words_ref, regions_ref, lengths_ref, flags_ref, wqkv_in, qv_bias_ref, wo_in, w1_in, b1_in_ref,
    w2_in, out_bias_ref, gain_ref, shift_ref, cwqkv_in, cqv_bias_ref, cwo_in, cout_bias_ref,
    cgain_ref, cshift_ref,
    y_ref, dw_ref, s_ref, dc_ref, sc_ref,
    x_ref, bqkv_ref, b1_ref, cvec_ref, send, recv, xlow, midf, alow, dyf, dya, dyc, ybuf, back,
    qkv, mixed, dqkv, cqkv, cmixed, cdqkv, act, dup, dgelu,
    p_w, p_r, cp_w, cp_r, cur, res, nrm, rstd, acc, rowp, bsum, bqsum,
    wqkv_ref, wo_ref, w1_ref, w2_ref, cwqkv_ref, cwo_ref, wqkv_m, wo_m, w1_m, w2_m, cwqkv_m, cwo_m, bqkv_m, b1_m,
    got, act_m, dup_m, mixed_m, dqkv_m, cmixed_m, cdqkv_m, cur_f, res_f, nrm_f, rstd_f, row_sums,
    g_ref, from_core, from_y, from_zs, from_z, from_ys, sums, sums_t, sums_c, sums_y, sums_z, pack,
    rs_send, rs_recv, ag_send, ag_recv, y_send, y_recv, sec_send, sec_recv,
    dw_send, dw_recv, sm_send, sm_recv, pk_send, pk_recv,
    back_send, back_recv, ar_send, ar_recv, mt_send, mt_recv, ga_send, ga_recv, ps_send, ps_recv, loads,
):
    p = functools.partial
    sec = lax.axis_index("section")
    me = lax.axis_index("tensor")
    head = sec == 0
    cross = sec == 1
    own = pl.ds(pl.multiple_of(me * C, C), C)

    def peer(o):
        return {"tensor": lax.rem(me + o, TENSOR)}

    def rows_of(t):
        return pl.ds(pl.multiple_of(t * C, C), C)

    partner = {"section": 1 - sec}
    place = lax.axis_index("dp")
    y_at, z_at, core = place // 8, lax.rem(place // 2, 4), lax.rem(place, 2)

    def dp_device(y, z, c):
        return {"dp": (y * 4 + z) * 2 + c}

    other_core = dp_device(y_at, z_at, 1 - core)
    other_y = dp_device(1 - y_at, z_at, core)

    def z_next(o):
        return lax.rem(z_at + o, 4)

    weights = tuple(
        pltpu.make_async_copy(src, dst, loads.at[k])
        for k, (src, dst) in enumerate((
            (wqkv_in, wqkv_ref), (wo_in, wo_ref), (w1_in, w1_ref), (w2_in, w2_ref),
            (cwqkv_in, cwqkv_ref), (cwo_in, cwo_ref),
        ))
    )

    def load_weights(*which):
        for k in which:
            weights[k].start()

    def wait_weights(*which):
        for k in which:
            weights[k].wait()

    barrier = pltpu.get_barrier_semaphore()
    for o in range(1, TENSOR):
        pl.semaphore_signal(barrier, inc=1, device_id=peer(o), device_id_type=MESH)
    mate, halver = {"tensor": me + 1 - 2 * lax.rem(me, 2)}, {"tensor": 3 - me}
    set_of = lax.rem((me + 1) // 2, 2)
    for t in range(TENSOR):
        pl.semaphore_signal(
            barrier, inc=1, device_id={"section": 1 - sec, "tensor": t}, device_id_type=MESH
        )
    for device in (other_core, other_y, *(dp_device(y_at, z_next(o), core) for o in (1, 2, 3))):
        pl.semaphore_signal(barrier, inc=1, device_id=device, device_id_type=MESH)

    load_weights(0, 1, 2, 3)
    pl.when(cross)(lambda: load_weights(4, 5))

    def moved(src, dst, send_sem, recv_sem, device):
        return pltpu.make_async_remote_copy(
            src_ref=src, dst_ref=dst, send_sem=send_sem, recv_sem=recv_sem, device_id=device,
            device_id_type=MESH,
        )

    both_mods = slice(0, 2)
    half_columns = pl.ds(pl.multiple_of(core * (D // 2), D // 2), D // 2)

    def z_rows(z, count):
        return pl.ds(pl.multiple_of(z * count, count), count)

    gathered = (
        (cwqkv_in, cwqkv_m, 3 * HW // 4, False), (cwo_in, cwo_m, HW // 4, False),
        (wqkv_in, wqkv_m, 3 * HW // 4, True), (wo_in, wo_m, HW // 4, True),
        (w1_in, w1_m, D // 4, True), (w2_in, w2_m, D // 4, True),
    )
    CWQKV, CWO, WQKV, WO, W1, W2 = range(6)
    Y_FIRST = (WQKV, W1)

    def gather_copies(k, step):
        src, dst, count, by_mod = gathered[k]
        sems = lambda i: (ga_send.at[k, i], ga_recv.at[k, i])
        at = lambda mods, rows: (mods, rows, half_columns) if by_mod else (rows, half_columns)
        mine = at(y_at, z_rows(z_at, count))
        if step == "x":
            return [moved(src.at[mine], dst.at[mine], *sems(0), mate)]
        if step == "y":
            place = dst.at[mine] if k in Y_FIRST else dst.at[at(y_at, slice(0, 4 * count))]
            return [moved(place, place, *sems(1), other_y)]
        if step == "z":
            place = dst.at[at(both_mods if k in Y_FIRST else y_at, z_rows(z_at, count))]
            return [
                moved(place, place, *sems(1 + o), dp_device(y_at, z_next(o), core)) for o in (1, 2, 3)
            ]
        place = dst.at[at(both_mods, slice(0, 4 * count))]
        return [moved(place, place, *sems(5), other_core)]

    def gather_start(step, *arrays):
        for k in arrays:
            for copy in gather_copies(k, step):
                copy.start()

    def gather_wait(step, *arrays):
        for k in arrays:
            for copy in gather_copies(k, step):
                copy.wait()

    @pl.when(cross)
    def _():
        pl.semaphore_wait(barrier, 12)
        gather_start("x", CWQKV, CWO, WQKV, WO, W2, W1)

    row = lax.broadcasted_iota(jnp.int32, (C, 1), 0) + me * C
    is_word = row < RW
    for k, ref in enumerate((out_bias_ref, gain_ref, shift_ref)):
        for l in range(2):
            rowp[2 * k + l] = jnp.where(is_word, ref[0, 0, l : l + 1, :], ref[0, 1, l : l + 1, :])

    def side_by_side(rows):
        return jnp.concatenate(rows, axis=1)

    for mod in range(2):
        b1_ref[mod] = side_by_side(
            [b1_in_ref[0, k, mod : mod + 1, :] for k in range(D // 128)]
        )
    for k, ref in enumerate((qv_bias_ref.at[0, 0], qv_bias_ref.at[0, 1], cqv_bias_ref)):
        heads = lambda j: [ref[h, j : j + 1, :] for h in range(LOCAL_HEADS)]
        bqkv_ref[k] = side_by_side([*heads(0), jnp.zeros((1, HW), F32), *heads(1)])
    for k, ref in enumerate((cout_bias_ref, cgain_ref, cshift_ref)):
        cvec_ref[k : k + 1, :] = ref[...].reshape(1, D)

    for ref, (lo, hi), length in zip((words_ref, regions_ref), SPANS, (WORDS, REGIONS)):
        given = ref[0].astype(F32).reshape(ITEMS_LOCAL * length, D).astype(BF)
        placed = dot(spread(hi - lo, length), given).astype(BF)
        x_ref[:, lo:hi, :] = placed.reshape(MB, hi - lo, D)
    acc[...] = jnp.zeros_like(acc)
    bsum[...] = jnp.zeros_like(bsum)
    bqsum[...] = jnp.zeros_like(bqsum)
    row_sums[...] = jnp.zeros_like(row_sums)


    def rs_copies(m):
        return [
            pltpu.make_async_remote_copy(
                src_ref=send.at[m, rows_of(lax.rem(me + o, TENSOR))],
                dst_ref=recv.at[m, o - 1],
                send_sem=rs_send.at[m, o - 1],
                recv_sem=rs_recv.at[m, o - 1],
                device_id=peer(o),
                device_id_type=MESH,
            )
            for o in range(1, TENSOR)
        ]

    def rs_start(m):
        for copy in rs_copies(m):
            copy.start()

    def rs_finish(m):
        for copy in rs_copies(m):
            copy.wait()
        total = send[m, own].astype(F32)
        for o in range(TENSOR - 1):
            total = total + recv[m, o].astype(F32)
        return total

    def ag_copies(buf, m, ss, rs):
        return [
            pltpu.make_async_remote_copy(
                src_ref=buf.at[m, own],
                dst_ref=buf.at[m, own],
                send_sem=ss.at[m, o - 1],
                recv_sem=rs.at[m, o - 1],
                device_id=peer(o),
                device_id_type=MESH,
            )
            for o in range(1, TENSOR)
        ]

    def ag_start(buf, m, ss=ag_send, rs=ag_recv):
        for copy in ag_copies(buf, m, ss, rs):
            copy.start()

    def ag_finish(buf, m, ss=ag_send, rs=ag_recv):
        for copy in ag_copies(buf, m, ss, rs):
            copy.wait()

    def mid_copy(m):
        rows = midf.at[m, own]
        return moved(rows, rows, sec_send.at[m], sec_recv.at[m], partner)

    def mid_relay(m):
        mid_copy(m).wait_recv()
        ag_start(midf, m)

    def back_copies(j):
        m = 2 * set_of + j
        first = 2 * (me // 2)
        return [
            moved(
                back.at[m, rows_of(first + k)], back.at[m, rows_of(first + k)],
                back_send.at[j, k], back_recv.at[m], {"section": 1 - sec, "tensor": first + k},
            )
            for k in range(2)
        ]

    def back_arrive(m):
        rows = back.at[m, own]
        moved(rows, rows, back_send.at[0, 0], back_recv.at[m], partner).wait_recv()

    def save_norm(l, m, n, r):
        nrm[l, m] = n
        rstd[l, m] = jnp.broadcast_to(r, (C, 128))

    def norm_step_back(l, m, dh, gain):
        n = nrm[l, m]
        dr = norm_back(dh, n, rstd[l, m][:, :1], gain)
        low = dr.astype(BF)
        acc[3 * l] += dh * n
        acc[3 * l + 1] += dh
        acc[3 * l + 2] += low.astype(F32)
        res[m] = dr
        return low

    def word_keys(m, q_rows, q_len):
        return key_mask(
            q_rows, q_len, RW, WORDS, [lengths_ref[ITEMS_MB * m + k] for k in range(ITEMS_MB)]
        )

    def region_keys(q_rows, q_len):
        return key_mask(q_rows, q_len, RR, REGIONS)

    def layer_a(m):
        xlow[m] = x_ref[m]
        cur[m] = x_ref[m, own].astype(F32)
        for mod, (lo, hi) in enumerate(SPANS):
            out = (dot_nt(xlow[m, lo:hi], wqkv_ref[mod]) + bqkv_ref[mod]).astype(BF)
            q, k, v = out[:, :HW], out[:, HW : 2 * HW], out[:, 2 * HW :]
            qkv[0, m, lo:hi], qkv[1, m, lo:hi], qkv[2, m, lo:hi] = q, k, v
            if mod == 0:
                probs, mix = attend(q, k, v, word_keys(m, RW, WORDS))
                p_w[m] = probs
            else:
                probs, mix = attend(q, k, v, region_keys(RR, REGIONS))
                p_r[m] = probs
            mixed[m, lo:hi] = mix
            send[m, lo:hi] = dot(mix, wo_ref[mod]).astype(BF)

        @pl.when(m == 1)
        def _():
            pl.semaphore_wait(barrier, 12)
            rs_start(0)

        @pl.when(m >= 1)
        def _():
            rs_start(m)


    def layer_b(m):
        r = cur[m] + rs_finish(m) + rowp[0]
        n, rs, h = norm_forward(r, rowp[2], rowp[4])
        save_norm(0, m, n, rs)
        cur[m] = h
        alow[m, own] = h.astype(BF)
        ag_start(alow, m)

    def layer_c(m):
        ag_finish(alow, m)
        for mod, (lo, hi) in enumerate(SPANS):
            up = dot(alow[m, lo:hi], w1_ref[mod]) + b1_ref[mod]
            cdf = 0.5 * (1.0 + lax.erf(up * (0.5**0.5)))
            dgelu[m, lo:hi] = cdf + up * jnp.exp(-0.5 * up * up) * 0.3989422804014327
            active = (up * cdf).astype(BF)
            act[m, lo:hi] = active
            send[m, lo:hi] = dot(active, w2_ref[mod]).astype(BF)
        rs_start(m)

    def layer_d(m):
        r = cur[m] + rs_finish(m) + rowp[1]
        n, rs, h = norm_forward(r, rowp[3], rowp[5])
        save_norm(1, m, n, rs)
        return h

    def back_e(m, dh):
        low = norm_step_back(1, m, dh, rowp[3])
        dyf[m, own] = low
        ag_start(dyf, m)

    def back_f(m):
        ag_finish(dyf, m)
        for mod, (lo, hi) in enumerate(SPANS):
            d = (dot_nt(dyf[m, lo:hi], w2_ref[mod]) * dgelu[m, lo:hi]).astype(BF)
            dup[m, lo:hi] = d
            bsum[mod] += jnp.sum(d.astype(F32), axis=0, keepdims=True)
            send[m, lo:hi] = dot_nt(d, w1_ref[mod]).astype(BF)
        rs_start(m)

    def back_g(m):
        dh = res[m] + rs_finish(m)
        low = norm_step_back(0, m, dh, rowp[2])
        dya[m, own] = low
        ag_start(dya, m)

    def back_h(m):
        ag_finish(dya, m)
        for mod, (lo, hi) in enumerate(SPANS):
            dmix = dot_nt(dya[m, lo:hi], wo_ref[mod]).astype(BF)
            probs = p_w[m] if mod == 0 else p_r[m]
            parts = attend_back(
                dmix, probs, qkv[0, m, lo:hi], qkv[1, m, lo:hi], qkv[2, m, lo:hi]
            )
            d = jnp.concatenate(parts, axis=1)
            dqkv[m, lo:hi] = d
            bqsum[mod] += jnp.sum(d.astype(F32), axis=0, keepdims=True)
            send[m, lo:hi] = dot(d, wqkv_ref[mod]).astype(BF)
        rs_start(m)

    def block_of(j):
        return 2 * set_of + j

    def ar_copy(j, mod, turn):
        lo, hi = SPANS[mod]
        return moved(
            send.at[j, lo:hi], got.at[turn, j, lo:hi], ar_send.at[turn, j, mod], ar_recv.at[turn, j, mod],
            halver,
        )

    def ar_start(j, mod, turn, part):
        lo, hi = SPANS[mod]
        send[j, lo:hi] = part.astype(BF)
        ar_copy(j, mod, turn).start()

    def ar_finish(j, mod, turn):
        lo, hi = SPANS[mod]
        ar_copy(j, mod, turn).wait()
        return send[j, lo:hi].astype(F32) + got[turn, j, lo:hi].astype(F32)

    shared = (xlow, alow, dyf, dya, dyc, ybuf)
    for_mate = ((act_m, act), (dup_m, dup), (mixed_m, mixed), (dqkv_m, dqkv), (cmixed_m, cmixed), (cdqkv_m, cdqkv))
    XLOW, ALOW, DYF, DYA, DYC, YBUF, ACT, DUP, MIXED, DQKV, CMIXED, CDQKV = range(12)

    halves = (XLOW, DYA, DYC, YBUF)

    def half_rows(which):
        return pl.ds(pl.multiple_of(which * (R // 2), R // 2), R // 2)

    def mate_copy(k, j, arriving=False):
        if k < 6:
            src = dst = shared[k]
            src = src.at[block_of(j)]
        else:
            src, dst = for_mate[k - 6]
            src = src.at[j]
        dst = dst.at[2 * (1 - set_of) + j if arriving else block_of(j)]
        if k in halves:
            src, dst = src.at[half_rows(me // 2)], dst.at[half_rows(me // 2)]
        return moved(src, dst, mt_send.at[k, j], mt_recv.at[k, j], mate)

    def mate_start(j, *kinds):
        for k in kinds:
            mate_copy(k, j).start()

    def mate_start_all(*kinds):
        for k in kinds:
            for j in range(2):
                mate_copy(k, j).start()

    def mate_wait(*kinds):
        for k in kinds:
            for j in range(2):
                mate_copy(k, j, True).wait_recv()
                mate_copy(k, j).wait_send()

    def pass_copy(k, j, arriving=False):
        rows = half_rows(1 - me // 2 if arriving else me // 2)
        place = shared[k].at[2 * (1 - set_of) + j, rows]
        return moved(place, place, ps_send.at[k, j], ps_recv.at[k, j], halver)

    def pass_start(k):
        for j in range(2):
            pass_copy(k, j).start()

    def pass_wait(k):
        for j in range(2):
            pass_copy(k, j, True).wait_recv()
            pass_copy(k, j).wait_send()

    def bias_copies():
        return [
            moved(bqkv_ref, bqkv_m, ga_send.at[6, 0], ga_recv.at[6, 0], mate),
            moved(b1_ref, b1_m, ga_send.at[7, 0], ga_recv.at[7, 0], mate),
        ]

    def save_norm_f(l, j, lo, hi, n, r):
        nrm_f[l, j, lo:hi] = n
        rstd_f[l, j, lo:hi] = jnp.broadcast_to(r, (hi - lo, 128))

    def count_rows(l, mod, dh, n, low):
        for k, value in enumerate((dh * n, dh, low.astype(F32))):
            at = 12 + k if l == 2 else 2 * (3 * l + k) + mod
            row_sums[at] += jnp.sum(value, axis=0, keepdims=True)

    def cross_forward(j):
        m = block_of(j)
        ag_finish(midf, m)
        mid = midf[m]
        shards = ((cwqkv_ref, bqkv_ref, cwo_ref, cmixed, m), (cwqkv_m, bqkv_m, cwo_m, cmixed_m, j))
        qkvs = []
        for sh, (w, bias, w_out, keep, at) in enumerate(shards):
            out = (dot_nt(mid, w[...]) + bias[2]).astype(BF)
            q, k, v = out[:, :HW], out[:, HW : 2 * HW], out[:, 2 * HW :]
            cqkv[0, 2 * sh + j], cqkv[1, 2 * sh + j], cqkv[2, 2 * sh + j] = q, k, v
            qkvs.append((q, k, v))
        for mod, (lo, hi) in enumerate(SPANS):
            others = slice(*SPANS[1 - mod])
            part = None
            for sh, (w, bias, w_out, keep, at) in enumerate(shards):
                q, k, v = qkvs[sh]
                mask = region_keys(RW, WORDS) if mod == 0 else word_keys(m, RR, REGIONS)
                probs, mix = attend(q[lo:hi], k[others], v[others], mask)
                (cp_w, cp_r)[mod][2 * sh + j] = probs
                keep[at, lo:hi] = mix
                one = dot(mix, w_out[...])
                part = one if part is None else part + one
            ar_start(j, mod, 0, part)

    def attn_forward(j):
        m = block_of(j)
        shards = (
            (wqkv_ref, bqkv_ref, wo_ref, mixed, m), (wqkv_m, bqkv_m, wo_m, mixed_m, j),
        )
        for mod, (lo, hi) in enumerate(SPANS):
            r = midf[m, lo:hi].astype(F32) + ar_finish(j, mod, 0) + cvec_ref[0:1, :]
            n, rs, h = norm_forward(r, cvec_ref[1:2, :], cvec_ref[2:3, :])
            save_norm_f(1, j, lo, hi, n, rs)
            cur_f[j, lo:hi] = h
            low = h.astype(BF)
            xlow[m, lo:hi] = low
            part = None
            for sh, (w, bias, w_out, keep, at) in enumerate(shards):
                slot = 2 * sh + j
                out = (dot_nt(low, w[mod]) + bias[mod]).astype(BF)
                q, k, v = out[:, :HW], out[:, HW : 2 * HW], out[:, 2 * HW :]
                qkv[0, slot, lo:hi], qkv[1, slot, lo:hi], qkv[2, slot, lo:hi] = q, k, v
                if mod == 0:
                    probs, mix = attend(q, k, v, word_keys(m, RW, WORDS))
                    p_w[slot] = probs
                else:
                    probs, mix = attend(q, k, v, region_keys(RR, REGIONS))
                    p_r[slot] = probs
                keep[at, lo:hi] = mix
                one = dot(mix, w_out[mod])
                part = one if part is None else part + one
            ar_start(j, mod, 1, part)
        mate_start(j, XLOW)

    def ffn_forward(j):
        m = block_of(j)
        shards = ((w1_ref, b1_ref, w2_ref, act, m), (w1_m, b1_m, w2_m, act_m, j))
        for mod, (lo, hi) in enumerate(SPANS):
            r = cur_f[j, lo:hi] + ar_finish(j, mod, 1) + out_bias_ref[0, mod, 0:1, :]
            n, rs, h = norm_forward(r, gain_ref[0, mod, 0:1, :], shift_ref[0, mod, 0:1, :])
            save_norm_f(0, j, lo, hi, n, rs)
            cur_f[j, lo:hi] = h
            low = h.astype(BF)
            alow[m, lo:hi] = low
            part = None
            for sh, (w, bias, w_out, keep, at) in enumerate(shards):
                if mod == 0 and sh == 1:
                    pl.when(j == 0)(lambda: gather_wait("core", W1))
                up = dot(low, w[mod]) + bias[mod]
                cdf = 0.5 * (1.0 + lax.erf(up * (0.5**0.5)))
                dgelu[2 * sh + j, lo:hi] = cdf + up * jnp.exp(-0.5 * up * up) * 0.3989422804014327
                active = (up * cdf).astype(BF)
                keep[at, lo:hi] = active
                if mod == 0 and sh == 1:
                    pl.when(j == 0)(lambda: gather_wait("core", W2))
                one = dot(active, w_out[mod])
                part = one if part is None else part + one
            ar_start(j, mod, 0, part)
        mate_start(j, ALOW, ACT)

    def ffn_turn(j):
        m = block_of(j)
        shards = ((w1_ref, w2_ref, dup, m), (w1_m, w2_m, dup_m, j))
        for mod, (lo, hi) in enumerate(SPANS):
            r = cur_f[j, lo:hi] + ar_finish(j, mod, 0) + out_bias_ref[0, mod, 1:2, :]
            gain = gain_ref[0, mod, 1:2, :]
            n, rs, h = norm_forward(r, gain, shift_ref[0, mod, 1:2, :])
            ybuf[m, lo:hi] = h.astype(BF)
            scale = scales(m, 1 - mod, hi - lo, (WORDS, REGIONS)[mod])
            dh = x_ref[m, lo:hi].astype(F32) * scale
            dr = norm_back(dh, n, rs, gain)
            res_f[j, lo:hi] = dr
            low = dr.astype(BF)
            dyf[m, lo:hi] = low
            count_rows(1, mod, dh, n, low)
            part = None
            for sh, (w_in, w_out, keep, at) in enumerate(shards):
                d = (dot_nt(low, w_out[mod]) * dgelu[2 * sh + j, lo:hi]).astype(BF)
                keep[at, lo:hi] = d
                one = dot_nt(d, w_in[mod])
                part = one if part is None else part + one
            ar_start(j, mod, 1, part)
        mate_start(j, DYF, DUP)

    def attn_backward(j):
        m = block_of(j)
        shards = ((wqkv_ref, wo_ref, dqkv, m), (wqkv_m, wo_m, dqkv_m, j))
        for mod, (lo, hi) in enumerate(SPANS):
            dh = res_f[j, lo:hi] + ar_finish(j, mod, 1)
            n = nrm_f[0, j, lo:hi]
            dr = norm_back(dh, n, rstd_f[0, j, lo:hi][:, :1], gain_ref[0, mod, 0:1, :])
            res_f[j, lo:hi] = dr
            low = dr.astype(BF)
            dya[m, lo:hi] = low
            count_rows(0, mod, dh, n, low)
            part = None
            for sh, (w, w_out, keep, at) in enumerate(shards):
                slot = 2 * sh + j
                dmix = dot_nt(low, w_out[mod]).astype(BF)
                probs = p_w[slot] if mod == 0 else p_r[slot]
                parts = attend_back(
                    dmix, probs, qkv[0, slot, lo:hi], qkv[1, slot, lo:hi], qkv[2, slot, lo:hi]
                )
                d = jnp.concatenate(parts, axis=1)
                keep[at, lo:hi] = d
                one = dot(d, w[mod])
                part = one if part is None else part + one
            ar_start(j, mod, 0, part)

    def cross_backward(j):
        m = block_of(j)
        for mod, (lo, hi) in enumerate(SPANS):
            dh = res_f[j, lo:hi] + ar_finish(j, mod, 0)
            n = nrm_f[1, j, lo:hi]
            dr = norm_back(dh, n, rstd_f[1, j, lo:hi][:, :1], cvec_ref[1:2, :])
            res_f[j, lo:hi] = dr
            low = dr.astype(BF)
            dyc[m, lo:hi] = low
            count_rows(2, mod, dh, n, low)
        part = None
        shards = ((cwqkv_ref, cwo_ref, cdqkv, m), (cwqkv_m, cwo_m, cdqkv_m, j))
        for sh, (w, w_out, keep, at) in enumerate(shards):
            slot = 2 * sh + j
            dmix = dot_nt(dyc[m], w_out[...]).astype(BF)
            q, k, v = cqkv[0, slot], cqkv[1, slot], cqkv[2, slot]
            dq_w, dk_r, dv_r = attend_back(dmix[:RW], cp_w[slot], q[:RW], k[RW:], v[RW:])
            dq_r, dk_w, dv_w = attend_back(dmix[RW:], cp_r[slot], q[RW:], k[:RW], v[:RW])
            keep[at, :RW] = jnp.concatenate([dq_w, dk_w, dv_w], axis=1)
            keep[at, RW:] = jnp.concatenate([dq_r, dk_r, dv_r], axis=1)
            one = dot(keep[at], w[...])
            part = one if part is None else part + one
        for mod, (lo, hi) in enumerate(SPANS):
            ar_start(j, mod, 1, part[lo:hi])

    def to_section_0(j):
        m = block_of(j)
        for mod, (lo, hi) in enumerate(SPANS):
            back[m, lo:hi] = (res_f[j, lo:hi] + ar_finish(j, mod, 1)).astype(BF)
        for copy in back_copies(j):
            copy.start()

    def column_sums(buf, lo, hi):
        rows = buf[:, lo:hi, :].astype(F32).reshape(MB * (hi - lo), buf.shape[-1])
        return jnp.sum(rows, axis=0, keepdims=True)

    def scales(m, flag, count, length):
        index = lax.broadcasted_iota(jnp.int32, (count, 1), 0)
        scale = jnp.ones((count, 1), F32)
        for k in range(ITEMS_MB):
            value = jnp.where(flags_ref[ITEMS_MB * m + k] == flag, 0.25, 1.0)
            scale = jnp.where(index >= k * length, value, scale)
        return scale

    def outer_tile(left, right, lo, hi, j, store):
        start = j * (D // 2)
        columns = pl.ds(start if isinstance(j, int) else pl.multiple_of(start, D // 2), D // 2)
        a = left[:, lo:hi, columns].reshape(MB * (hi - lo), D // 2)
        b = right[:, lo:hi, :].reshape(MB * (hi - lo), right.shape[-1])
        store(dot_tn(a, b))

    def outer(left, right, lo, hi, store):
        pl.loop(0, 2)(
            lambda j: outer_tile(left, right, lo, hi, j, p(store, j))
        )

    def store_at(block, lo, hi):
        def store(j, value):
            g_ref[block, j, :, :, :, lo:hi] = value.astype(BF).reshape(4, 2, 48, hi - lo)

        return store

    def ffn_piece(k):
        mod, second = k // 2, k % 2
        left, right = ((alow, dup), (dyf, act))[second]
        outer(left, right, *SPANS[mod], store_at((5, 1)[second] + mod, 0, D))

    def attn_piece(k):
        mod, second = k // 2, k % 2
        left, right = ((xlow, dqkv), (dya, mixed))[second]
        outer(left, right, *SPANS[mod], store_at(4 * mod, *((0, 3 * HW), (3 * HW, D))[second]))

    def cross_outer():
        def store(j, lo, hi):
            def put(value):
                value = value.astype(BF).reshape(2, 4, 2, 24, hi - lo)
                g_ref[3, :, :, :, 24 * j : 24 * j + 24, lo:hi] = value

            return put

        for j in range(2):
            outer_tile(midf, cdqkv, 0, R, j, store(j, 0, 3 * HW))
            outer_tile(dyc, cmixed, 0, R, j, store(j, 3 * HW, D))

    def dw_copies(group, phase):
        index, y_first, lo, hi = group
        sems = lambda k: (dw_send.at[index, k], dw_recv.at[index, k])
        blocks = slice(lo, hi)
        if phase == 0:
            src = g_ref.at[blocks, :, :, 1 - core]
            return [moved(src, from_core.at[blocks], *sems(0), other_core)]
        if y_first and phase == 1:
            src = g_ref.at[blocks, 1 - y_at, :, core]
            return [moved(src, from_y.at[blocks], *sems(1), other_y)]
        if y_first:
            return [
                moved(
                    g_ref.at[blocks, y_at, z_next(o), core], from_z.at[blocks, o - 1],
                    *sems(1 + o), dp_device(y_at, z_next(o), core),
                )
                for o in (1, 2, 3)
            ]
        late = slice(lo - 4, hi - 4)
        if phase == 1:
            return [
                moved(
                    g_ref.at[blocks, :, z_next(o), core], from_zs.at[late, o - 1],
                    *sems(1 + o), dp_device(y_at, z_next(o), core),
                )
                for o in (1, 2, 3)
            ]
        src = g_ref.at[blocks, 1 - y_at, z_at, core]
        return [moved(src, from_ys.at[late], *sems(1), other_y)]

    def dw_start(group, phase):
        for copy in dw_copies(group, phase):
            copy.start()

    def dw_finish(group, phase):
        for copy in dw_copies(group, phase):
            copy.wait()
        index, y_first, lo, hi = group

        def add(b):
            if phase == 0:
                for y in range(2):
                    mine = g_ref[b, y, :, core].astype(F32)
                    g_ref[b, y, :, core] = (mine + from_core[b, y].astype(F32)).astype(BF)
            elif phase == 1 and y_first:
                mine = g_ref[b, y_at, :, core].astype(F32)
                g_ref[b, y_at, :, core] = (mine + from_y[b].astype(F32)).astype(BF)
            elif phase == 1:
                total = g_ref[b, :, z_at, core].astype(F32)
                for o in range(3):
                    total = total + from_zs[b - 4, o].astype(F32)
                g_ref[b, :, z_at, core] = total.astype(BF)
            else:
                total = g_ref[b, y_at, z_at, core].astype(F32)
                for o in range(3 if y_first else 0):
                    total = total + from_z[b, o].astype(F32)
                if not y_first:
                    total = total + from_ys[b - 4].astype(F32)
                dw_ref[b] = total

        pl.loop(lo, hi)(add)

    def dw_turn(group, phase):
        dw_finish(group, phase)
        dw_start(group, phase + 1)

    OUT_W, OUT_R, IN_W, IN_R = (0, True, 1, 2), (1, True, 2, 3), (2, False, 5, 6), (3, False, 6, 7)
    ATTN_W, ATTN_R, CROSS = (4, True, 0, 1), (5, False, 4, 5), (6, True, 3, 4)

    def sm_copies(step):
        sems = lambda k: (sm_send.at[k], sm_recv.at[k])
        if step == 0:
            return [
                moved(sums_t.at[me], sums_t.at[me], *sems(o - 1), peer(o)) for o in range(1, TENSOR)
            ]
        if step == 1:
            return [moved(sums.at[0], sums_c, *sems(3), other_core)]
        if step == 2:
            return [moved(sums.at[1], sums_y, *sems(4), other_y)]
        return [
            moved(
                sums.at[2], sums_z.at[o - 1], *sems(4 + o), dp_device(y_at, z_next(o), core)
            )
            for o in (1, 2, 3)
        ]

    def sm_start(step):
        for copy in sm_copies(step):
            copy.start()

    def sm_wait(step):
        for copy in sm_copies(step):
            copy.wait()

    def small_norms_all():
        for k in range(15):
            sums_t[me, k : k + 1, :] = jnp.where(me < 2, row_sums[k], 0.0)
        sums_t[me, 15:16, :] = jnp.zeros((1, D), F32)
        sm_start(0)

    def small_norms():
        sums_t[me] = jnp.zeros((16, D), F32)
        for l in range(2):
            for k in range(3):
                a = acc[3 * l + k]
                at = 2 * (3 * l + k)
                sums_t[me, at : at + 1, :] = jnp.sum(jnp.where(is_word, a, 0.0), axis=0, keepdims=True)
                sums_t[me, at + 1 : at + 2, :] = jnp.sum(
                    jnp.where(is_word, 0.0, a), axis=0, keepdims=True
                )
        sm_start(0)

    def small_biases():
        sm_wait(0)
        sums[0] = jnp.zeros((24, D), F32)
        sums[0, :16] = sums_t[0] + sums_t[1] + sums_t[2] + sums_t[3]
        for mod in range(2):
            sums[0, 16 + mod : 17 + mod, :] = bsum[mod]
        for k in range(3):
            sums[0, 18 + k : 19 + k, : 3 * HW] = bqsum[k]
        sm_start(1)

    def small_y():
        sm_wait(1)
        sums[1] = sums[0] + sums_c[...]
        sm_start(2)

    def small_z():
        sm_wait(2)
        sums[2] = sums[1] + sums_y[...]
        sm_start(3)

    def small_last():
        sm_wait(3)
        s_ref[...] = sums[2] + sums_z[0] + sums_z[1] + sums_z[2]

    def packet():
        return moved(pack.at[0], pack.at[1], pk_send, pk_recv, partner)

    def each(*steps, after=()):
        def body(m):
            for step in steps:
                step(m)
            for k, extra in enumerate(after):
                if extra is not None:
                    pl.when(m == k)(extra)

        pl.loop(0, MB)(body)

    def then(*steps):
        def run():
            for step in steps:
                step()

        return run

    def pair(step):
        pl.loop(0, 2)(step)

    @pl.when(head)
    def _():
        def to_partner(m):
            midf[m, own] = layer_d(m).astype(BF)
            mid_copy(m).start()

        def from_partner(m):
            mid_copy(m).wait_send()
            back_arrive(m)
            back_e(m, back[m, own].astype(F32))

        def last(m):
            ybuf[m, own] = (res[m] + rs_finish(m)).astype(BF)
            ag_start(ybuf, m, y_send, y_recv)

        wait_weights(0, 1)
        each(layer_a)
        wait_weights(2, 3)
        each(layer_b)
        each(layer_c)
        each(to_partner)
        each(from_partner)
        each(back_f)
        each(
            back_g,
            after=(
                then(p(ffn_piece, 2), p(dw_start, IN_R, 0)),
                then(p(ffn_piece, 3), p(dw_start, OUT_R, 0)),
                then(p(dw_turn, IN_R, 0), p(ffn_piece, 0), p(dw_start, IN_W, 0)),
                then(p(dw_turn, OUT_R, 0), p(ffn_piece, 1), p(dw_start, OUT_W, 0)),
            ),
        )
        small_norms()
        each(
            back_h,
            after=(
                then(p(dw_turn, IN_W, 0), p(dw_turn, OUT_W, 0)), None, p(dw_turn, IN_R, 1),
                p(dw_turn, OUT_R, 1),
            ),
        )
        small_biases()
        attn_piece(2)
        attn_piece(3)
        dw_start(ATTN_R, 0)
        small_y()
        attn_piece(0)
        attn_piece(1)
        dw_start(ATTN_W, 0)
        dw_turn(ATTN_R, 0)
        dw_turn(IN_W, 1)
        dw_turn(ATTN_W, 0)
        dw_turn(OUT_W, 1)
        each(last)
        small_z()

    @pl.when(cross)
    def _():
        for copy in bias_copies():
            copy.start()
        gather_wait("x", CWQKV, CWO)
        gather_start("z", CWQKV, CWO)
        gather_wait("x", WQKV, WO)
        gather_start("y", WQKV)
        gather_start("z", WO)
        gather_wait("x", W2, W1)
        gather_start("y", W1)
        gather_wait("y", WQKV)
        gather_start("z", WQKV)
        gather_wait("z", CWQKV, CWO)
        gather_start("core", CWQKV, CWO)
        gather_start("z", W2)
        gather_wait("z", WO)
        gather_start("y", WO)
        gather_wait("y", W1)
        gather_start("z", W1)
        for copy in bias_copies():
            copy.wait()
        gather_wait("core", CWQKV, CWO)
        gather_wait("y", WO)
        gather_wait("z", WQKV)
        gather_start("core", WQKV, WO)
        wait_weights(0, 1, 2, 3, 4, 5)
        pl.loop(0, 3)(mid_relay)
        pl.when(set_of == 1)(lambda: mid_relay(3))
        cross_forward(0)
        pl.when(set_of == 0)(lambda: mid_relay(3))
        gather_wait("z", W2)
        gather_start("y", W2)
        cross_forward(1)
        gather_wait("core", WQKV, WO)
        attn_forward(0)
        gather_wait("z", W1)
        gather_start("core", W1)
        attn_forward(1)
        gather_wait("y", W2)
        gather_start("core", W2)
        pair(ffn_forward)
        pair(ffn_turn)
        pair(attn_backward)
        pair(cross_backward)
        pair(to_section_0)
        mate_wait(XLOW, ALOW, ACT, DYF, DUP)
        mate_start_all(DYC, CDQKV, CMIXED)
        pass_start(XLOW)
        ffn_piece(2)
        dw_start(IN_R, 0)
        ffn_piece(3)
        dw_start(OUT_R, 0)
        ffn_piece(0)
        dw_start(IN_W, 0)
        dw_turn(IN_R, 0)
        ffn_piece(1)
        dw_start(OUT_W, 0)
        dw_turn(OUT_R, 0)
        small_norms_all()
        for mod, (lo, hi) in enumerate(SPANS):
            bsum[mod] = column_sums(dup, lo, hi)
        dw_turn(IN_W, 0)
        dw_turn(OUT_W, 0)
        mate_wait(DYC)
        pass_start(DYC)
        mate_start_all(DYA, DQKV, MIXED)
        for k in range(2):
            ag_finish(midf, 2 * (1 - set_of) + k)
        mate_wait(CDQKV, CMIXED)
        pass_wait(DYC)
        cross_outer()
        dw_start(CROSS, 0)
        bqsum[2] = column_sums(cdqkv, 0, R)
        dw_turn(CROSS, 0)
        mate_wait(DYA)
        pass_start(DYA)
        dw_turn(IN_R, 1)
        dw_turn(OUT_R, 1)
        dw_turn(IN_W, 1)
        dw_turn(OUT_W, 1)
        mate_wait(DQKV, MIXED)
        mate_start_all(YBUF)
        pass_wait(XLOW)
        pass_wait(DYA)
        for mod, (lo, hi) in enumerate(SPANS):
            bqsum[mod] = column_sums(dqkv, lo, hi)
        small_biases()
        attn_piece(2)
        attn_piece(3)
        dw_start(ATTN_R, 0)
        small_y()
        attn_piece(0)
        attn_piece(1)
        dw_start(ATTN_W, 0)
        dw_turn(CROSS, 1)
        dw_turn(ATTN_R, 0)
        small_z()
        dw_turn(ATTN_W, 0)
        mate_wait(YBUF)
        pass_start(YBUF)
        dw_finish(CROSS, 2)
        pass_wait(YBUF)
        pair(lambda j: [copy.wait_send() for copy in back_copies(j)] and None)

    def write(m):
        @pl.when(head)
        def _():
            ag_finish(ybuf, m, y_send, y_recv)

        y_ref[m] = ybuf[m]

    dw_finish(IN_R, 2)
    dw_finish(OUT_R, 2)
    dw_turn(ATTN_R, 1)
    dw_finish(IN_W, 2)
    dw_finish(OUT_W, 2)
    dw_turn(ATTN_W, 1)
    small_last()
    each(write)

    @pl.when(cross)
    def _():
        pack[0, :24] = dw_ref[3, :24]
        pack[0, 24:] = s_ref[...]
        packet().start()
        dc_ref[...] = dw_ref[3, 24:]
        sc_ref[...] = s_ref[...]

    dw_finish(ATTN_W, 2)
    dw_finish(ATTN_R, 2)
    pl.when(cross)(lambda: packet().wait_send())

    @pl.when(head)
    def _():
        packet().wait_recv()
        dc_ref[...] = pack[1, :24]
        sc_ref[...] = pack[1, 24:]


def arrange(
    y_ref, dw_ref, s_ref, dc_ref, sc_ref,
    words, regions, qkv_g, qv_bias_g, out_g, in_g, b1_g, ffo_g, obias_g, gain_g, shift_g,
    cqkv_g, cqv_bias_g, cout_g, cobias_g, cgain_g, cshift_g,
):
    place = lax.axis_index("dp")
    both = lax.axis_index("section") * 16 + place

    def from_column(rows, column):
        return pltpu.roll(rows, lax.rem(D - column, D), 1)

    for ref, (lo, hi), length in zip((words, regions), SPANS, (WORDS, REGIONS)):
        padded = y_ref[:, lo:hi, :].reshape(MB * (hi - lo), D)
        rows = dot(spread(hi - lo, length, True), padded)
        ref[0] = rows.reshape(length, ITEMS_LOCAL, D)
    small = s_ref[...]
    for mod in range(2):
        attn = dw_ref[4 * mod]
        for j in range(3):
            qkv_g[0, mod, j] = attn[:, j * HW : (j + 1) * HW]
        out_g[0, mod] = attn[:, 3 * HW :]
        in_g[0, mod] = dw_ref[5 + mod]
        ffo_g[0, mod] = dw_ref[1 + mod]
    columns = from_column(small, 48 * place)[:, :48]
    for mod in range(2):
        for l in range(2):
            for k, ref in enumerate((gain_g, shift_g, obias_g)):
                at = 2 * (3 * l + k) + mod
                ref[0, mod, l : l + 1, :] = columns[at : at + 1]
    columns = from_column(small, 8 * place)
    for mod in range(2):
        for k in range(6):
            b1_g[0, k, mod : mod + 1, :] = columns[16 + mod : 17 + mod, 128 * k : 128 * k + 8]
    columns = from_column(small, 4 * place)
    for mod in range(2):
        for j in range(2):
            for h in range(LOCAL_HEADS):
                lo = 2 * j * HW + h * HEAD_DIM
                qv_bias_g[0, mod, h, j : j + 1, :] = columns[18 + mod : 19 + mod, lo : lo + 4]
    wide = dc_ref[...]
    for j in range(3):
        cqkv_g[j] = wide[:, j * HW : (j + 1) * HW]
    cout_g[...] = wide[:, 3 * HW :]
    small = sc_ref[...]
    columns = from_column(small, 24 * both)
    for k, ref in enumerate((cgain_g, cshift_g, cobias_g)):
        ref[...] = columns[12 + k, :24]
    columns = from_column(small, 2 * both)[20:21]
    for j in range(2):
        heads = []
        for h in range(LOCAL_HEADS):
            lo = 2 * j * HW + h * HEAD_DIM
            heads.append(columns[:, lo : lo + 2])
        cqv_bias_g[j] = jnp.concatenate(heads, axis=0).T


def local(
    words, regions, word_lengths, task_flags, attn_qkv, attn_qv_bias, attn_out, ffn_in, ffn_in_bias,
    ffn_out, out_bias, norm_gain, norm_bias, cross_qkv, cross_qv_bias, cross_out, cross_out_bias,
    cross_norm_gain, cross_norm_bias,
):
    inputs = (
        words.transpose(0, 2, 1, 3), regions.transpose(0, 2, 1, 3), word_lengths, task_flags,
        attn_qkv.transpose(0, 1, 3, 4, 2).reshape(2, 3 * HW, D), attn_qv_bias.transpose(0, 1, 3, 2, 4), attn_out[0],
        ffn_in[0], ffn_in_bias.transpose(0, 2, 1, 3), ffn_out[0], out_bias, norm_gain, norm_bias,
        cross_qkv.transpose(1, 2, 0).reshape(3 * HW, D), cross_qv_bias.transpose(1, 0, 2), cross_out,
        cross_out_bias, cross_norm_gain, cross_norm_bias,
    )

    vmem = pl.BlockSpec(memory_space=pltpu.VMEM)
    smem = pl.BlockSpec(memory_space=pltpu.SMEM)
    hbm = pl.BlockSpec(memory_space=pl.ANY)
    mb_rows = lambda width, dtype: pltpu.VMEM((MB, R, width), dtype)
    own_rows = lambda count: pltpu.VMEM((count, MB, C, D), F32)
    y, g, s, dc, sc = pl.pallas_call(
        kernel,
        out_shape=(
            jax.ShapeDtypeStruct((MB, R, D), BF),
            jax.ShapeDtypeStruct((7, 48, D), F32),
            jax.ShapeDtypeStruct((24, D), F32),
            jax.ShapeDtypeStruct((24, D), F32),
            jax.ShapeDtypeStruct((24, D), F32),
        ),
        in_specs=[smem if k in (2, 3) else hbm if k in (4, 6, 7, 9, 13, 15) else vmem for k in range(len(inputs))],
        out_specs=[vmem] * 5,
        scratch_shapes=[
            mb_rows(D, BF),
            pltpu.VMEM((3, 1, 3 * HW), F32),
            pltpu.VMEM((2, 1, D), F32),
            pltpu.VMEM((3, D), F32),
            mb_rows(D, BF),
            pltpu.VMEM((MB, TENSOR - 1, C, D), BF),
            *[mb_rows(D, BF) for _ in range(8)],
            pltpu.VMEM((3, MB, R, HW), BF),
            mb_rows(HW, BF),
            mb_rows(3 * HW, BF),
            pltpu.VMEM((3, MB, R, HW), BF),
            mb_rows(HW, BF),
            mb_rows(3 * HW, BF),
            mb_rows(D, BF),
            mb_rows(D, BF),
            mb_rows(D, F32),
            pltpu.VMEM((MB, 3 * RW, RW), F32),
            pltpu.VMEM((MB, 3 * RR, RR), F32),
            pltpu.VMEM((MB, 3 * RW, RR), F32),
            pltpu.VMEM((MB, 3 * RR, RW), F32),
            pltpu.VMEM((MB, C, D), F32),
            pltpu.VMEM((MB, C, D), F32),
            pltpu.VMEM((2, MB, C, D), F32),
            pltpu.VMEM((2, MB, C, 128), F32),
            pltpu.VMEM((6, C, D), F32),
            pltpu.VMEM((6, C, D), F32),
            pltpu.VMEM((2, 1, D), F32),
            pltpu.VMEM((3, 1, 3 * HW), F32),
            pltpu.VMEM((2, 3 * HW, D), BF),
            pltpu.VMEM((2, HW, D), BF),
            pltpu.VMEM((2, D, D), BF),
            pltpu.VMEM((2, D, D), BF),
            pltpu.VMEM((3 * HW, D), BF),
            pltpu.VMEM((HW, D), BF),
            pltpu.VMEM((2, 3 * HW, D), BF),
            pltpu.VMEM((2, HW, D), BF),
            pltpu.VMEM((2, D, D), BF),
            pltpu.VMEM((2, D, D), BF),
            pltpu.VMEM((3 * HW, D), BF),
            pltpu.VMEM((HW, D), BF),
            pltpu.VMEM((3, 1, 3 * HW), F32),
            pltpu.VMEM((2, 1, D), F32),
            pltpu.VMEM((2, 2, R, D), BF),
            *[pltpu.VMEM((2, R, w), BF) for w in (D, D, HW, 3 * HW, HW, 3 * HW)],
            pltpu.VMEM((2, R, D), F32),
            pltpu.VMEM((2, R, D), F32),
            pltpu.VMEM((2, 2, R, D), F32),
            pltpu.VMEM((2, 2, R, 128), F32),
            pltpu.VMEM((16, 1, D), F32),
            pltpu.VMEM((7, 2, 4, 2, 48, D), BF),
            pltpu.VMEM((7, 2, 4, 48, D), BF),
            pltpu.VMEM((4, 4, 48, D), BF),
            pltpu.VMEM((3, 3, 2, 48, D), BF),
            pltpu.VMEM((4, 3, 48, D), BF),
            pltpu.VMEM((3, 48, D), BF),
            pltpu.VMEM((3, 24, D), F32),
            pltpu.VMEM((TENSOR, 16, D), F32),
            pltpu.VMEM((24, D), F32),
            pltpu.VMEM((24, D), F32),
            pltpu.VMEM((3, 24, D), F32),
            pltpu.VMEM((2, 48, D), F32),
            *[pltpu.SemaphoreType.DMA((MB, TENSOR - 1)) for _ in range(6)],
            pltpu.SemaphoreType.DMA((MB,)),
            pltpu.SemaphoreType.DMA((MB,)),
            pltpu.SemaphoreType.DMA((7, 5)),
            pltpu.SemaphoreType.DMA((7, 5)),
            pltpu.SemaphoreType.DMA((8,)),
            pltpu.SemaphoreType.DMA((8,)),
            pltpu.SemaphoreType.DMA,
            pltpu.SemaphoreType.DMA,
            pltpu.SemaphoreType.DMA((2, 2)),
            pltpu.SemaphoreType.DMA((MB,)),
            *[pltpu.SemaphoreType.DMA((2, 2, 2)) for _ in range(2)],
            *[pltpu.SemaphoreType.DMA((12, 2)) for _ in range(2)],
            *[pltpu.SemaphoreType.DMA((8, 6)) for _ in range(2)],
            *[pltpu.SemaphoreType.DMA((6, 2)) for _ in range(2)],
            pltpu.SemaphoreType.DMA((6,)),
        ],
        compiler_params=pltpu.CompilerParams(
            collective_id=0, has_side_effects=True, vmem_limit_bytes=63 * 2**20
        ),
    )(*inputs)

    shapes = (
        (1, WORDS, ITEMS_LOCAL, D), (1, REGIONS, ITEMS_LOCAL, D), (1, 2, 3, 48, HW),
        (1, 2, LOCAL_HEADS, 2, 4), (1, 2, 48, HW), (1, 2, 48, D), (1, 6, 2, 8), (1, 2, 48, D),
        (1, 2, 2, 48), (1, 2, 2, 48), (1, 2, 2, 48), (3, 24, HW), (2, 2, LOCAL_HEADS), (24, HW),
        (24,), (24,), (24,),
    )
    orders = {
        0: (0, 2, 1, 3), 1: (0, 2, 1, 3), 2: (0, 1, 3, 2, 4), 3: (0, 1, 3, 2, 4), 4: (0, 1, 3, 2),
        6: (0, 2, 1, 3), 7: (0, 1, 3, 2), 11: (1, 0, 2), 12: (0, 2, 1), 13: (1, 0),
    }
    outs = pl.pallas_call(
        arrange,
        out_shape=tuple(jax.ShapeDtypeStruct(shape, F32) for shape in shapes),
        in_specs=[vmem] * 5,
        out_specs=[vmem] * len(shapes),
        compiler_params=pltpu.CompilerParams(vmem_limit_bytes=60 * 2**20),
    )(y, g, s, dc, sc)
    return tuple(out.transpose(orders[k]) if k in orders else out for k, out in enumerate(outs))


def solution(mesh):
    in_specs = (
        P("section", "dp", None, None),
        P("section", "dp", None, None),
        P("dp"),
        P("dp"),
        P("section", None, None, None, "tensor"),
        P("section", None, None, "tensor", None),
        P("section", None, "tensor", None),
        P("section", None, None, "tensor"),
        P("section", None, "tensor", None),
        P("section", None, "tensor", None),
        P("section", None, None, None),
        P("section", None, None, None),
        P("section", None, None, None),
        P(None, None, "tensor"),
        P(None, "tensor", None),
        P("tensor", None),
        P(),
        P(),
        P(),
    )
    out_specs = (
        P("section", "dp", None, None),
        P("section", "dp", None, None),
        P("section", None, "dp", None, "tensor"),
        P("section", None, None, "tensor", "dp"),
        P("section", None, "tensor", "dp"),
        P("section", None, "dp", "tensor"),
        P("section", None, "tensor", "dp"),
        P("section", None, "tensor", "dp"),
        P("section", None, None, "dp"),
        P("section", None, None, "dp"),
        P("section", None, None, "dp"),
        P(("section", "dp"), None, "tensor"),
        P(None, "tensor", ("section", "dp")),
        P("tensor", ("section", "dp")),
        P(("section", "dp")),
        P(("section", "dp")),
        P(("section", "dp")),
    )
    return jax.shard_map(local, mesh=mesh, in_specs=in_specs, out_specs=out_specs, check_vma=False)
```

```python
import functools

import jax
import jax.numpy as jnp
from jax import lax
from jax.experimental import pallas as pl
from jax.experimental.pallas import tpu as pltpu
from jax.sharding import PartitionSpec as P

MESH = pl.DeviceIdType.MESH
BF = jnp.bfloat16
F32 = jnp.float32
HEAD_DIM = 64
LOCAL_HEADS = 3
HW = HEAD_DIM * LOCAL_HEADS
WORDS = 20
REGIONS = 36
D = 768
ITEMS_LOCAL = 8
TENSOR = 4

ITEMS_MB = 2
MB = ITEMS_LOCAL // ITEMS_MB
RW = 48
RR = 80
R = RW + RR
C = R // TENSOR
SPANS = ((0, RW), (RW, R))

EPSILON = 1e-06
MASKED = -1000000000.0
SCALING = HEAD_DIM ** (-0.5)


def dot(a, b):
    return lax.dot_general(a, b, (((1,), (0,)), ((), ())), preferred_element_type=F32)


def dot_nt(a, b):
    return lax.dot_general(a, b, (((1,), (1,)), ((), ())), preferred_element_type=F32)


def dot_tn(a, b):
    return lax.dot_general(a, b, (((0,), (0,)), ((), ())), preferred_element_type=F32)


def head_masks():
    lane = lax.broadcasted_iota(jnp.int32, (1, HW), 1)
    return [
        ((lane >= h * HEAD_DIM) & (lane < (h + 1) * HEAD_DIM)).astype(F32) for h in range(LOCAL_HEADS)
    ]


def by_head(a):
    masks = [m.astype(BF) for m in head_masks()]
    return jnp.concatenate([a * m for m in masks], axis=0)


def join_heads(stacked):
    rows = stacked.shape[0] // LOCAL_HEADS
    masks = head_masks()
    total = stacked[:rows] * masks[0]
    for h in range(1, LOCAL_HEADS):
        total = total + stacked[h * rows : (h + 1) * rows] * masks[h]
    return total


def item_of(shape, axis, length):
    index = lax.broadcasted_iota(jnp.int32, shape, axis)
    item = jnp.zeros(shape, jnp.int32)
    for k in range(1, ITEMS_MB + 1):
        item = item + (index >= k * length).astype(jnp.int32)
    return item


def spread(rows, length, transposed=False):
    count = ITEMS_LOCAL * length
    shape = (count, MB * rows) if transposed else (MB * rows, count)
    at = lax.broadcasted_iota(jnp.int32, shape, 0 if transposed else 1)
    padded = lax.broadcasted_iota(jnp.int32, shape, 1 if transposed else 0)
    item, position = at & (ITEMS_LOCAL - 1), at >> 3
    block, within = item >> (ITEMS_MB.bit_length() - 1), item & (ITEMS_MB - 1)
    target = block * rows + within * length + position
    return (target == padded).astype(F32).astype(BF)


def key_mask(q_rows, q_len, k_rows, k_len, lengths=None):
    shape = (q_rows, k_rows)
    item = item_of(shape, 1, k_len)
    key = lax.broadcasted_iota(jnp.int32, shape, 1)
    mask = (item_of(shape, 0, q_len) == item) & (key < ITEMS_MB * k_len)
    if lengths is not None:
        for k, length in enumerate(lengths):
            mask = mask & ((item != k) | (key < k * k_len + length))
    return mask


def attend(q, k, v, mask):
    scores = dot_nt(by_head(q), k) * SCALING
    mask = jnp.concatenate([mask] * LOCAL_HEADS, axis=0)
    scores = jnp.where(mask, scores, MASKED)
    e = jnp.exp(scores - jnp.max(scores, axis=-1, keepdims=True))
    probs = e / jnp.sum(e, axis=-1, keepdims=True)
    mixed = join_heads(dot(probs.astype(BF), v)).astype(BF)
    return probs, mixed


def attend_back(dmix, probs, q, k, v):
    d3 = by_head(dmix)
    dp = dot_nt(d3, v)
    ds = (probs * (dp - jnp.sum(probs * dp, axis=-1, keepdims=True))).astype(BF)
    dv = dot_tn(probs.astype(BF), d3).astype(BF)
    dq = (join_heads(dot(ds, k)) * SCALING).astype(BF)
    dk = (dot_tn(ds, by_head(q)) * SCALING).astype(BF)
    return dq, dk, dv


def norm_forward(r, gain, shift):
    center = r - jnp.mean(r, axis=-1, keepdims=True)
    spread = jnp.mean(center * center, axis=-1, keepdims=True)
    rstd = lax.rsqrt(spread + EPSILON)
    n = center * rstd
    return n, rstd, n * gain + shift


def norm_back(dh, n, rstd, gain):
    dn = dh * gain
    return rstd * (
        dn - jnp.mean(dn, axis=-1, keepdims=True) - n * jnp.mean(dn * n, axis=-1, keepdims=True)
    )


def kernel(
    words_ref, regions_ref, lengths_ref, flags_ref, wqkv_in, qv_bias_ref, wo_in, w1_in, b1_in_ref,
    w2_in, out_bias_ref, gain_ref, shift_ref, cwqkv_in, cqv_bias_ref, cwo_in, cout_bias_ref,
    cgain_ref, cshift_ref,
    y_ref, dw_ref, s_ref, dc_ref, sc_ref,
    x_ref, bqkv_ref, b1_ref, cvec_ref, send, recv, xlow, midf, alow, dyf, dya, dyc, ybuf, back,
    qkv, mixed, dqkv, cqkv, cmixed, cdqkv, act, dup, dgelu,
    p_w, p_r, cp_w, cp_r, cur, res, nrm, rstd, acc, rowp, bsum, bqsum,
    wqkv_ref, wo_ref, w1_ref, w2_ref, cwqkv_ref, cwo_ref, wqkv_m, wo_m, w1_m, w2_m, cwqkv_m, cwo_m, bqkv_m, b1_m,
    got, act_m, dup_m, mixed_m, dqkv_m, cmixed_m, cdqkv_m, cur_f, res_f, nrm_f, rstd_f, row_sums,
    g_ref, from_core, from_y, from_zs, from_z, from_ys, sums, sums_t, sums_c, sums_y, sums_z, pack,
    rs_send, rs_recv, ag_send, ag_recv, y_send, y_recv, sec_send, sec_recv,
    dw_send, dw_recv, sm_send, sm_recv, pk_send, pk_recv,
    back_send, back_recv, ar_send, ar_recv, mt_send, mt_recv, ga_send, ga_recv, ps_send, ps_recv, loads,
):
    p = functools.partial
    sec = lax.axis_index("section")
    me = lax.axis_index("tensor")
    head = sec == 0
    cross = sec == 1
    own = pl.ds(pl.multiple_of(me * C, C), C)

    def peer(o):
        return {"tensor": lax.rem(me + o, TENSOR)}

    def rows_of(t):
        return pl.ds(pl.multiple_of(t * C, C), C)

    partner = {"section": 1 - sec}
    place = lax.axis_index("dp")
    y_at, z_at, core = place // 8, lax.rem(place // 2, 4), lax.rem(place, 2)

    def dp_device(y, z, c):
        return {"dp": (y * 4 + z) * 2 + c}

    other_core = dp_device(y_at, z_at, 1 - core)
    other_y = dp_device(1 - y_at, z_at, core)

    def z_next(o):
        return lax.rem(z_at + o, 4)

    weights = tuple(
        pltpu.make_async_copy(src, dst, loads.at[k])
        for k, (src, dst) in enumerate((
            (wqkv_in, wqkv_ref), (wo_in, wo_ref), (w1_in, w1_ref), (w2_in, w2_ref),
            (cwqkv_in, cwqkv_ref), (cwo_in, cwo_ref),
        ))
    )

    def load_weights(*which):
        for k in which:
            weights[k].start()

    def wait_weights(*which):
        for k in which:
            weights[k].wait()

    barrier = pltpu.get_barrier_semaphore()
    for o in range(1, TENSOR):
        pl.semaphore_signal(barrier, inc=1, device_id=peer(o), device_id_type=MESH)
    mate, halver = {"tensor": me + 1 - 2 * lax.rem(me, 2)}, {"tensor": 3 - me}
    set_of = lax.rem((me + 1) // 2, 2)
    for t in range(TENSOR):
        pl.semaphore_signal(
            barrier, inc=1, device_id={"section": 1 - sec, "tensor": t}, device_id_type=MESH
        )
    for device in (other_core, other_y, *(dp_device(y_at, z_next(o), core) for o in (1, 2, 3))):
        pl.semaphore_signal(barrier, inc=1, device_id=device, device_id_type=MESH)

    load_weights(0, 1, 2, 3)
    pl.when(cross)(lambda: load_weights(4, 5))

    def moved(src, dst, send_sem, recv_sem, device):
        return pltpu.make_async_remote_copy(
            src_ref=src, dst_ref=dst, send_sem=send_sem, recv_sem=recv_sem, device_id=device,
            device_id_type=MESH,
        )

    both_mods = slice(0, 2)
    half_columns = pl.ds(pl.multiple_of(core * (D // 2), D // 2), D // 2)

    def z_rows(z, count):
        return pl.ds(pl.multiple_of(z * count, count), count)

    gathered = (
        (cwqkv_in, cwqkv_m, 3 * HW // 4, False), (cwo_in, cwo_m, HW // 4, False),
        (wqkv_in, wqkv_m, 3 * HW // 4, True), (wo_in, wo_m, HW // 4, True),
        (w1_in, w1_m, D // 4, True), (w2_in, w2_m, D // 4, True),
    )
    CWQKV, CWO, WQKV, WO, W1, W2 = range(6)
    Y_FIRST = (WQKV, W1)

    def gather_copies(k, step):
        src, dst, count, by_mod = gathered[k]
        sems = lambda i: (ga_send.at[k, i], ga_recv.at[k, i])
        at = lambda mods, rows: (mods, rows, half_columns) if by_mod else (rows, half_columns)
        mine = at(y_at, z_rows(z_at, count))
        column = at(y_at, slice(0, 4 * count)) if by_mod else None
        if step == "x":
            part = column if k == W2 else mine
            return [moved(src.at[part], dst.at[part], *sems(0), mate)]
        if step == "y":
            place = dst.at[mine] if k in Y_FIRST else dst.at[column]
            return [moved(place, place, *sems(1), other_y)]
        if step == "z":
            place = dst.at[at(both_mods if k in Y_FIRST else y_at, z_rows(z_at, count))]
            return [
                moved(place, place, *sems(2), dp_device(y_at, z_next(o), core)) for o in (1, 2, 3)
            ]
        place = dst.at[at(both_mods, slice(0, 4 * count))]
        return [moved(place, place, *sems(3), other_core)]

    def gather_start(step, *arrays):
        for k in arrays:
            for copy in gather_copies(k, step):
                copy.start()

    def gather_wait(step, *arrays):
        for k in arrays:
            if step != "z":
                gather_copies(k, step)[0].wait()
                continue
            _, dst, count, by_mod = gathered[k]
            rows = slice(0, 3 * count)
            mods = both_mods if k in Y_FIRST else y_at
            place = dst.at[(mods, rows, half_columns) if by_mod else (rows, half_columns)]
            moved(place, place, ga_send.at[k, 2], ga_recv.at[k, 2], mate).wait()

    @pl.when(cross)
    def _():
        pl.semaphore_wait(barrier, 12)
        gather_start("x", CWQKV, CWO, WQKV, WO, W1, W2)

    row = lax.broadcasted_iota(jnp.int32, (C, 1), 0) + me * C
    is_word = row < RW
    for k, ref in enumerate((out_bias_ref, gain_ref, shift_ref)):
        for l in range(2):
            rowp[2 * k + l] = jnp.where(is_word, ref[0, 0, l : l + 1, :], ref[0, 1, l : l + 1, :])

    def side_by_side(rows):
        return jnp.concatenate(rows, axis=1)

    for mod in range(2):
        b1_ref[mod] = side_by_side(
            [b1_in_ref[0, k, mod : mod + 1, :] for k in range(D // 128)]
        )
    for k, ref in enumerate((qv_bias_ref.at[0, 0], qv_bias_ref.at[0, 1], cqv_bias_ref)):
        heads = lambda j: [ref[h, j : j + 1, :] for h in range(LOCAL_HEADS)]
        bqkv_ref[k] = side_by_side([*heads(0), jnp.zeros((1, HW), F32), *heads(1)])
    for k, ref in enumerate((cout_bias_ref, cgain_ref, cshift_ref)):
        cvec_ref[k : k + 1, :] = ref[...].reshape(1, D)

    for ref, (lo, hi), length in zip((words_ref, regions_ref), SPANS, (WORDS, REGIONS)):
        given = ref[0].astype(F32).reshape(ITEMS_LOCAL * length, D).astype(BF)
        placed = dot(spread(hi - lo, length), given).astype(BF)
        x_ref[:, lo:hi, :] = placed.reshape(MB, hi - lo, D)
    acc[...] = jnp.zeros_like(acc)
    bsum[...] = jnp.zeros_like(bsum)
    bqsum[...] = jnp.zeros_like(bqsum)
    row_sums[...] = jnp.zeros_like(row_sums)


    def rs_copies(m):
        return [
            pltpu.make_async_remote_copy(
                src_ref=send.at[m, rows_of(lax.rem(me + o, TENSOR))],
                dst_ref=recv.at[m, o - 1],
                send_sem=rs_send.at[m],
                recv_sem=rs_recv.at[m],
                device_id=peer(o),
                device_id_type=MESH,
            )
            for o in range(1, TENSOR)
        ]

    def rs_start(m):
        for copy in rs_copies(m):
            copy.start()

    def rs_finish(m):
        moved(recv.at[m], recv.at[m], rs_send.at[m], rs_recv.at[m], peer(1)).wait()
        total = send[m, own].astype(F32)
        for o in range(TENSOR - 1):
            total = total + recv[m, o].astype(F32)
        return total

    def ag_copies(buf, m, ss, rs):
        return [
            pltpu.make_async_remote_copy(
                src_ref=buf.at[m, own],
                dst_ref=buf.at[m, own],
                send_sem=ss.at[m],
                recv_sem=rs.at[m],
                device_id=peer(o),
                device_id_type=MESH,
            )
            for o in range(1, TENSOR)
        ]

    def ag_start(buf, m, ss=ag_send, rs=ag_recv):
        for copy in ag_copies(buf, m, ss, rs):
            copy.start()

    def ag_finish(buf, m, ss=ag_send, rs=ag_recv):
        three = buf.at[m, pl.ds(0, (TENSOR - 1) * C)]
        moved(three, three, ss.at[m], rs.at[m], peer(1)).wait()

    def mid_copy(m):
        rows = midf.at[m, own]
        return moved(rows, rows, sec_send.at[m], sec_recv.at[m], partner)

    def mid_relay(m):
        mid_copy(m).wait_recv()
        ag_start(midf, m)

    def back_copies(j):
        m = 2 * set_of + j
        first = 2 * (me // 2)
        return [
            moved(
                back.at[m, rows_of(first + k)], back.at[m, rows_of(first + k)],
                back_send.at[j], back_recv.at[m], {"section": 1 - sec, "tensor": first + k},
            )
            for k in range(2)
        ]

    def back_arrive(m):
        rows = back.at[m, own]
        moved(rows, rows, back_send.at[0], back_recv.at[m], partner).wait_recv()

    def save_norm(l, m, n, r):
        nrm[l, m] = n
        rstd[l, m] = jnp.broadcast_to(r, (C, 128))

    def norm_step_back(l, m, dh, gain):
        n = nrm[l, m]
        dr = norm_back(dh, n, rstd[l, m][:, :1], gain)
        low = dr.astype(BF)
        acc[3 * l] += dh * n
        acc[3 * l + 1] += dh
        acc[3 * l + 2] += low.astype(F32)
        res[m] = dr
        return low

    def word_keys(m, q_rows, q_len):
        return key_mask(
            q_rows, q_len, RW, WORDS, [lengths_ref[ITEMS_MB * m + k] for k in range(ITEMS_MB)]
        )

    def region_keys(q_rows, q_len):
        return key_mask(q_rows, q_len, RR, REGIONS)

    def layer_a(m):
        xlow[m] = x_ref[m]
        cur[m] = x_ref[m, own].astype(F32)
        for mod, (lo, hi) in enumerate(SPANS):
            out = (dot_nt(xlow[m, lo:hi], wqkv_ref[mod]) + bqkv_ref[mod]).astype(BF)
            q, k, v = out[:, :HW], out[:, HW : 2 * HW], out[:, 2 * HW :]
            qkv[0, m, lo:hi], qkv[1, m, lo:hi], qkv[2, m, lo:hi] = q, k, v
            if mod == 0:
                probs, mix = attend(q, k, v, word_keys(m, RW, WORDS))
                p_w[m] = probs
            else:
                probs, mix = attend(q, k, v, region_keys(RR, REGIONS))
                p_r[m] = probs
            mixed[m, lo:hi] = mix
            send[m, lo:hi] = dot(mix, wo_ref[mod]).astype(BF)

    def layer_b(m):
        r = cur[m] + rs_finish(m) + rowp[0]
        n, rs, h = norm_forward(r, rowp[2], rowp[4])
        save_norm(0, m, n, rs)
        cur[m] = h
        alow[m, own] = h.astype(BF)
        ag_start(alow, m)

    def layer_c(m):
        ag_finish(alow, m)
        for mod, (lo, hi) in enumerate(SPANS):
            up = dot(alow[m, lo:hi], w1_ref[mod]) + b1_ref[mod]
            cdf = 0.5 * (1.0 + lax.erf(up * (0.5**0.5)))
            dgelu[m, lo:hi] = cdf + up * jnp.exp(-0.5 * up * up) * 0.3989422804014327
            active = (up * cdf).astype(BF)
            act[m, lo:hi] = active
            send[m, lo:hi] = dot(active, w2_ref[mod]).astype(BF)
        rs_start(m)

    def layer_d(m):
        r = cur[m] + rs_finish(m) + rowp[1]
        n, rs, h = norm_forward(r, rowp[3], rowp[5])
        save_norm(1, m, n, rs)
        return h

    def back_e(m, dh):
        low = norm_step_back(1, m, dh, rowp[3])
        dyf[m, own] = low
        ag_start(dyf, m)

    def back_f(m):
        ag_finish(dyf, m)
        for mod, (lo, hi) in enumerate(SPANS):
            d = (dot_nt(dyf[m, lo:hi], w2_ref[mod]) * dgelu[m, lo:hi]).astype(BF)
            dup[m, lo:hi] = d
            bsum[mod] += jnp.sum(d.astype(F32), axis=0, keepdims=True)
            send[m, lo:hi] = dot_nt(d, w1_ref[mod]).astype(BF)
        rs_start(m)

    def back_g(m):
        dh = res[m] + rs_finish(m)
        low = norm_step_back(0, m, dh, rowp[2])
        dya[m, own] = low
        ag_start(dya, m)

    def back_h(m):
        ag_finish(dya, m)
        for mod, (lo, hi) in enumerate(SPANS):
            dmix = dot_nt(dya[m, lo:hi], wo_ref[mod]).astype(BF)
            probs = p_w[m] if mod == 0 else p_r[m]
            parts = attend_back(
                dmix, probs, qkv[0, m, lo:hi], qkv[1, m, lo:hi], qkv[2, m, lo:hi]
            )
            d = jnp.concatenate(parts, axis=1)
            dqkv[m, lo:hi] = d
            bqsum[mod] += jnp.sum(d.astype(F32), axis=0, keepdims=True)
            send[m, lo:hi] = dot(d, wqkv_ref[mod]).astype(BF)
        rs_start(m)

    def block_of(j):
        return 2 * set_of + j

    def ar_copy(j, mod, turn):
        lo, hi = SPANS[mod]
        return moved(
            send.at[j, lo:hi], got.at[turn, j, lo:hi], ar_send.at[turn, j, mod], ar_recv.at[turn, j, mod],
            halver,
        )

    def ar_start(j, mod, turn, part):
        lo, hi = SPANS[mod]
        send[j, lo:hi] = part.astype(BF)
        ar_copy(j, mod, turn).start()

    def ar_finish(j, mod, turn):
        lo, hi = SPANS[mod]
        ar_copy(j, mod, turn).wait()
        return send[j, lo:hi].astype(F32) + got[turn, j, lo:hi].astype(F32)

    shared = (xlow, alow, dyf, dya, dyc, ybuf)
    for_mate = ((act_m, act), (dup_m, dup), (mixed_m, mixed), (dqkv_m, dqkv), (cmixed_m, cmixed), (cdqkv_m, cdqkv))
    XLOW, ALOW, DYF, DYA, DYC, YBUF, ACT, DUP, MIXED, DQKV, CMIXED, CDQKV = range(12)

    halves = (XLOW, DYF, DYA, DYC, YBUF)

    def half_rows(which):
        return pl.ds(pl.multiple_of(which * (R // 2), R // 2), R // 2)

    def mate_copy(k, j):
        if k < 6:
            src = dst = shared[k]
            src = src.at[block_of(j)]
        else:
            src, dst = for_mate[k - 6]
            src = src.at[j]
        dst = dst.at[block_of(j)]
        if k in halves:
            src, dst = src.at[half_rows(me // 2)], dst.at[half_rows(me // 2)]
        return moved(src, dst, mt_send.at[k], mt_recv.at[k], mate)

    def mate_start(j, *kinds):
        for k in kinds:
            mate_copy(k, j).start()

    def mate_start_all(*kinds):
        for k in kinds:
            for j in range(2):
                mate_copy(k, j).start()

    def mate_wait(*kinds):
        for k in kinds:
            place = (shared[k] if k < 6 else for_mate[k - 6][1]).at[pl.ds(2 * (1 - set_of), 2)]
            if k in halves:
                place = place.at[:, half_rows(me // 2)]
            moved(place, place, mt_send.at[k], mt_recv.at[k], mate).wait()

    def pass_copy(k):
        place = shared[k].at[pl.ds(2 * (1 - set_of), 2), half_rows(me // 2)]
        return moved(place, place, ps_send.at[k], ps_recv.at[k], halver)

    def pass_start(k):
        pass_copy(k).start()

    def pass_wait(k):
        pass_copy(k).wait()

    def bias_copies():
        return [
            moved(bqkv_ref, bqkv_m, ga_send.at[6, 0], ga_recv.at[6, 0], mate),
            moved(b1_ref, b1_m, ga_send.at[6, 1], ga_recv.at[6, 1], mate),
        ]

    def save_norm_f(l, j, lo, hi, n, r):
        nrm_f[l, j, lo:hi] = n
        rstd_f[l, j, lo:hi] = jnp.broadcast_to(r, (hi - lo, 128))

    def count_rows(l, mod, dh, n, low):
        for k, value in enumerate((dh * n, dh, low.astype(F32))):
            at = 12 + k if l == 2 else 2 * (3 * l + k) + mod
            row_sums[at] += jnp.sum(value, axis=0, keepdims=True)

    def cross_forward(j):
        m = block_of(j)
        ag_finish(midf, m)
        mid = midf[m]
        shards = ((cwqkv_ref, bqkv_ref, cwo_ref, cmixed, m), (cwqkv_m, bqkv_m, cwo_m, cmixed_m, j))
        qkvs = []
        for sh, (w, bias, w_out, keep, at) in enumerate(shards):
            out = (dot_nt(mid, w[...]) + bias[2]).astype(BF)
            q, k, v = out[:, :HW], out[:, HW : 2 * HW], out[:, 2 * HW :]
            cqkv[0, 2 * sh + j], cqkv[1, 2 * sh + j], cqkv[2, 2 * sh + j] = q, k, v
            qkvs.append((q, k, v))
        for mod, (lo, hi) in enumerate(SPANS):
            others = slice(*SPANS[1 - mod])
            part = None
            for sh, (w, bias, w_out, keep, at) in enumerate(shards):
                q, k, v = qkvs[sh]
                mask = region_keys(RW, WORDS) if mod == 0 else word_keys(m, RR, REGIONS)
                probs, mix = attend(q[lo:hi], k[others], v[others], mask)
                (cp_w, cp_r)[mod][2 * sh + j] = probs
                keep[at, lo:hi] = mix
                one = dot(mix, w_out[...])
                part = one if part is None else part + one
            ar_start(j, mod, 0, part)
        mate_start(j, CMIXED)

    def attn_forward(j):
        m = block_of(j)
        shards = (
            (wqkv_ref, bqkv_ref, wo_ref, mixed, m), (wqkv_m, bqkv_m, wo_m, mixed_m, j),
        )
        for mod, (lo, hi) in enumerate(SPANS):
            r = midf[m, lo:hi].astype(F32) + ar_finish(j, mod, 0) + cvec_ref[0:1, :]
            n, rs, h = norm_forward(r, cvec_ref[1:2, :], cvec_ref[2:3, :])
            save_norm_f(1, j, lo, hi, n, rs)
            cur_f[j, lo:hi] = h
            low = h.astype(BF)
            xlow[m, lo:hi] = low
            part = None
            for sh, (w, bias, w_out, keep, at) in enumerate(shards):
                slot = 2 * sh + j
                out = (dot_nt(low, w[mod]) + bias[mod]).astype(BF)
                q, k, v = out[:, :HW], out[:, HW : 2 * HW], out[:, 2 * HW :]
                qkv[0, slot, lo:hi], qkv[1, slot, lo:hi], qkv[2, slot, lo:hi] = q, k, v
                if mod == 0:
                    probs, mix = attend(q, k, v, word_keys(m, RW, WORDS))
                    p_w[slot] = probs
                else:
                    probs, mix = attend(q, k, v, region_keys(RR, REGIONS))
                    p_r[slot] = probs
                keep[at, lo:hi] = mix
                one = dot(mix, w_out[mod])
                part = one if part is None else part + one
            ar_start(j, mod, 1, part)
        mate_start(j, XLOW, MIXED)

    def ffn_forward(j):
        m = block_of(j)
        shards = ((w1_ref, b1_ref, w2_ref, act, m), (w1_m, b1_m, w2_m, act_m, j))
        for mod, (lo, hi) in enumerate(SPANS):
            r = cur_f[j, lo:hi] + ar_finish(j, mod, 1) + out_bias_ref[0, mod, 0:1, :]
            n, rs, h = norm_forward(r, gain_ref[0, mod, 0:1, :], shift_ref[0, mod, 0:1, :])
            save_norm_f(0, j, lo, hi, n, rs)
            cur_f[j, lo:hi] = h
            low = h.astype(BF)
            alow[m, lo:hi] = low
            part = None
            for sh, (w, bias, w_out, keep, at) in enumerate(shards):
                if mod == 0 and sh == 1:
                    pl.when(j == 0)(lambda: gather_wait("core", W1))
                up = dot(low, w[mod]) + bias[mod]
                cdf = 0.5 * (1.0 + lax.erf(up * (0.5**0.5)))
                dgelu[2 * sh + j, lo:hi] = cdf + up * jnp.exp(-0.5 * up * up) * 0.3989422804014327
                active = (up * cdf).astype(BF)
                keep[at, lo:hi] = active
                if mod == 0 and sh == 1:
                    pl.when(j == 0)(lambda: gather_wait("core", W2))
                one = dot(active, w_out[mod])
                part = one if part is None else part + one
            ar_start(j, mod, 0, part)
        mate_start(j, ALOW, ACT)

    def ffn_turn(j):
        m = block_of(j)
        shards = ((w1_ref, w2_ref, dup, m), (w1_m, w2_m, dup_m, j))
        for mod, (lo, hi) in enumerate(SPANS):
            r = cur_f[j, lo:hi] + ar_finish(j, mod, 0) + out_bias_ref[0, mod, 1:2, :]
            gain = gain_ref[0, mod, 1:2, :]
            n, rs, h = norm_forward(r, gain, shift_ref[0, mod, 1:2, :])
            ybuf[m, lo:hi] = h.astype(BF)
            scale = scales(m, 1 - mod, hi - lo, (WORDS, REGIONS)[mod])
            dh = x_ref[m, lo:hi].astype(F32) * scale
            dr = norm_back(dh, n, rs, gain)
            res_f[j, lo:hi] = dr
            low = dr.astype(BF)
            dyf[m, lo:hi] = low
            count_rows(1, mod, dh, n, low)
            part = None
            for sh, (w_in, w_out, keep, at) in enumerate(shards):
                d = (dot_nt(low, w_out[mod]) * dgelu[2 * sh + j, lo:hi]).astype(BF)
                keep[at, lo:hi] = d
                one = dot_nt(d, w_in[mod])
                part = one if part is None else part + one
            ar_start(j, mod, 1, part)
        mate_start(j, DYF, DUP)

    def attn_backward(j):
        m = block_of(j)
        shards = ((wqkv_ref, wo_ref, dqkv, m), (wqkv_m, wo_m, dqkv_m, j))
        for mod, (lo, hi) in enumerate(SPANS):
            dh = res_f[j, lo:hi] + ar_finish(j, mod, 1)
            n = nrm_f[0, j, lo:hi]
            dr = norm_back(dh, n, rstd_f[0, j, lo:hi][:, :1], gain_ref[0, mod, 0:1, :])
            res_f[j, lo:hi] = dr
            low = dr.astype(BF)
            dya[m, lo:hi] = low
            count_rows(0, mod, dh, n, low)
            part = None
            for sh, (w, w_out, keep, at) in enumerate(shards):
                slot = 2 * sh + j
                dmix = dot_nt(low, w_out[mod]).astype(BF)
                probs = p_w[slot] if mod == 0 else p_r[slot]
                parts = attend_back(
                    dmix, probs, qkv[0, slot, lo:hi], qkv[1, slot, lo:hi], qkv[2, slot, lo:hi]
                )
                d = jnp.concatenate(parts, axis=1)
                keep[at, lo:hi] = d
                one = dot(d, w[mod])
                part = one if part is None else part + one
            ar_start(j, mod, 0, part)

    def cross_backward(j):
        m = block_of(j)
        for mod, (lo, hi) in enumerate(SPANS):
            dh = res_f[j, lo:hi] + ar_finish(j, mod, 0)
            n = nrm_f[1, j, lo:hi]
            dr = norm_back(dh, n, rstd_f[1, j, lo:hi][:, :1], cvec_ref[1:2, :])
            res_f[j, lo:hi] = dr
            low = dr.astype(BF)
            dyc[m, lo:hi] = low
            count_rows(2, mod, dh, n, low)
        part = None
        shards = ((cwqkv_ref, cwo_ref, cdqkv, m), (cwqkv_m, cwo_m, cdqkv_m, j))
        for sh, (w, w_out, keep, at) in enumerate(shards):
            slot = 2 * sh + j
            dmix = dot_nt(dyc[m], w_out[...]).astype(BF)
            q, k, v = cqkv[0, slot], cqkv[1, slot], cqkv[2, slot]
            dq_w, dk_r, dv_r = attend_back(dmix[:RW], cp_w[slot], q[:RW], k[RW:], v[RW:])
            dq_r, dk_w, dv_w = attend_back(dmix[RW:], cp_r[slot], q[RW:], k[:RW], v[:RW])
            keep[at, :RW] = jnp.concatenate([dq_w, dk_w, dv_w], axis=1)
            keep[at, RW:] = jnp.concatenate([dq_r, dk_r, dv_r], axis=1)
            one = dot(keep[at], w[...])
            part = one if part is None else part + one
        for mod, (lo, hi) in enumerate(SPANS):
            ar_start(j, mod, 1, part[lo:hi])

    def to_section_0(j):
        m = block_of(j)
        for mod, (lo, hi) in enumerate(SPANS):
            back[m, lo:hi] = (res_f[j, lo:hi] + ar_finish(j, mod, 1)).astype(BF)
        for copy in back_copies(j):
            copy.start()

    def column_sums(buf, lo, hi):
        rows = buf[:, lo:hi, :].astype(F32).reshape(MB * (hi - lo), buf.shape[-1])
        return jnp.sum(rows, axis=0, keepdims=True)

    def scales(m, flag, count, length):
        index = lax.broadcasted_iota(jnp.int32, (count, 1), 0)
        scale = jnp.ones((count, 1), F32)
        for k in range(ITEMS_MB):
            value = jnp.where(flags_ref[ITEMS_MB * m + k] == flag, 0.25, 1.0)
            scale = jnp.where(index >= k * length, value, scale)
        return scale

    def outer_tile(left, right, lo, hi, j, store):
        start = j * (D // 2)
        columns = pl.ds(start if isinstance(j, int) else pl.multiple_of(start, D // 2), D // 2)
        a = left[:, lo:hi, columns].reshape(MB * (hi - lo), D // 2)
        b = right[:, lo:hi, :].reshape(MB * (hi - lo), right.shape[-1])
        store(dot_tn(a, b))

    def outer(left, right, lo, hi, store):
        pl.loop(0, 2)(
            lambda j: outer_tile(left, right, lo, hi, j, p(store, j))
        )

    def store_at(block, lo, hi):
        def store(j, value):
            g_ref[block, j, :, :, :, lo:hi] = value.astype(BF).reshape(4, 2, 48, hi - lo)

        return store

    def ffn_piece(k):
        mod, second = k // 2, k % 2
        left, right = ((alow, dup), (dyf, act))[second]
        outer(left, right, *SPANS[mod], store_at((5, 1)[second] + mod, 0, D))

    def attn_piece(k):
        mod, second = k // 2, k % 2
        left, right = ((xlow, dqkv), (dya, mixed))[second]
        outer(left, right, *SPANS[mod], store_at(4 * mod, *((0, 3 * HW), (3 * HW, D))[second]))

    def cross_outer():
        def store(j, lo, hi):
            def put(value):
                value = value.astype(BF).reshape(2, 4, 2, 24, hi - lo)
                g_ref[3, :, :, :, 24 * j : 24 * j + 24, lo:hi] = value

            return put

        for j in range(2):
            outer_tile(midf, cdqkv, 0, R, j, store(j, 0, 3 * HW))
            outer_tile(dyc, cmixed, 0, R, j, store(j, 3 * HW, D))

    def dw_copies(group, phase):
        index, y_first, lo, hi = group
        sems = lambda k: (dw_send.at[index, k], dw_recv.at[index, k])
        blocks = slice(lo, hi)
        if phase == 0:
            src = g_ref.at[blocks, :, :, 1 - core]
            return [moved(src, from_core.at[blocks], *sems(0), other_core)]
        if y_first and phase == 1:
            src = g_ref.at[blocks, 1 - y_at, :, core]
            return [moved(src, from_y.at[blocks], *sems(1), other_y)]
        if y_first:
            return [
                moved(
                    g_ref.at[blocks, y_at, z_next(o), core], from_z.at[blocks, o - 1],
                    *sems(2), dp_device(y_at, z_next(o), core),
                )
                for o in (1, 2, 3)
            ]
        late = slice(lo - 4, hi - 4)
        if phase == 1:
            return [
                moved(
                    g_ref.at[blocks, :, z_next(o), core], from_zs.at[late, o - 1],
                    *sems(2), dp_device(y_at, z_next(o), core),
                )
                for o in (1, 2, 3)
            ]
        src = g_ref.at[blocks, 1 - y_at, z_at, core]
        return [moved(src, from_ys.at[late], *sems(1), other_y)]

    def dw_start(group, phase):
        for copy in dw_copies(group, phase):
            copy.start()

    def dw_finish(group, phase):
        index, y_first, lo, hi = group
        if phase == (2 if y_first else 1):
            place = from_z.at[slice(lo, hi)] if y_first else from_zs.at[slice(lo - 4, hi - 4)]
            moved(place, place, dw_send.at[index, 2], dw_recv.at[index, 2], other_core).wait()
        else:
            dw_copies(group, phase)[0].wait()

        def add(b):
            if phase == 0:
                for y in range(2):
                    mine = g_ref[b, y, :, core].astype(F32)
                    g_ref[b, y, :, core] = (mine + from_core[b, y].astype(F32)).astype(BF)
            elif phase == 1 and y_first:
                mine = g_ref[b, y_at, :, core].astype(F32)
                g_ref[b, y_at, :, core] = (mine + from_y[b].astype(F32)).astype(BF)
            elif phase == 1:
                total = g_ref[b, :, z_at, core].astype(F32)
                for o in range(3):
                    total = total + from_zs[b - 4, o].astype(F32)
                g_ref[b, :, z_at, core] = total.astype(BF)
            else:
                total = g_ref[b, y_at, z_at, core].astype(F32)
                for o in range(3 if y_first else 0):
                    total = total + from_z[b, o].astype(F32)
                if not y_first:
                    total = total + from_ys[b - 4].astype(F32)
                dw_ref[b] = total

        pl.loop(lo, hi)(add)

    def dw_turn(group, phase):
        dw_finish(group, phase)
        dw_start(group, phase + 1)

    OUT_W, OUT_R, IN_W, IN_R = (0, True, 1, 2), (1, True, 2, 3), (2, False, 5, 6), (3, False, 6, 7)
    ATTN_W, ATTN_R, CROSS = (4, True, 0, 1), (5, False, 4, 5), (6, True, 3, 4)

    def sm_copies(step):
        sems = lambda k: (sm_send.at[k], sm_recv.at[k])
        if step == 0:
            return [
                moved(sums_t.at[me], sums_t.at[me], *sems(0), peer(o)) for o in range(1, TENSOR)
            ]
        if step == 1:
            return [moved(sums.at[0], sums_c, *sems(1), other_core)]
        if step == 2:
            return [moved(sums.at[1], sums_y, *sems(2), other_y)]
        return [
            moved(
                sums.at[2], sums_z.at[o - 1], *sems(3), dp_device(y_at, z_next(o), core)
            )
            for o in (1, 2, 3)
        ]

    def sm_start(step):
        for copy in sm_copies(step):
            copy.start()

    def sm_wait(step):
        if step in (0, 3):
            place = sums_z if step == 3 else sums_t.at[pl.ds(0, TENSOR - 1)]
            moved(place, place, sm_send.at[step], sm_recv.at[step], other_core).wait()
        else:
            sm_copies(step)[0].wait()

    def small_norms_all():
        for k in range(15):
            sums_t[me, k : k + 1, :] = jnp.where(me < 2, row_sums[k], 0.0)
        sums_t[me, 15:16, :] = jnp.zeros((1, D), F32)
        sm_start(0)

    def small_norms():
        sums_t[me] = jnp.zeros((16, D), F32)
        for l in range(2):
            for k in range(3):
                a = acc[3 * l + k]
                at = 2 * (3 * l + k)
                sums_t[me, at : at + 1, :] = jnp.sum(jnp.where(is_word, a, 0.0), axis=0, keepdims=True)
                sums_t[me, at + 1 : at + 2, :] = jnp.sum(
                    jnp.where(is_word, 0.0, a), axis=0, keepdims=True
                )
        sm_start(0)

    def small_biases():
        sm_wait(0)
        sums[0] = jnp.zeros((24, D), F32)
        sums[0, :16] = sums_t[0] + sums_t[1] + sums_t[2] + sums_t[3]
        for mod in range(2):
            sums[0, 16 + mod : 17 + mod, :] = bsum[mod]
        for k in range(3):
            sums[0, 18 + k : 19 + k, : 3 * HW] = bqsum[k]
        sm_start(1)

    def small_y():
        sm_wait(1)
        sums[1] = sums[0] + sums_c[...]
        sm_start(2)

    def small_z():
        sm_wait(2)
        sums[2] = sums[1] + sums_y[...]
        sm_start(3)

    def small_last():
        sm_wait(3)
        s_ref[...] = sums[2] + sums_z[0] + sums_z[1] + sums_z[2]

    def packet():
        return moved(pack.at[0], pack.at[1], pk_send, pk_recv, partner)

    def each(*steps, first=0, last=MB, after=()):
        def body(m):
            for step in steps:
                step(m)
            for k, extra in enumerate(after):
                if extra is not None:
                    pl.when(m == first + k)(extra)

        pl.loop(first, last)(body)

    def then(*steps):
        def run():
            for step in steps:
                step()

        return run

    def pair(step):
        pl.loop(0, 2)(step)

    @pl.when(head)
    def _():
        def to_partner(m):
            midf[m, own] = layer_d(m).astype(BF)
            mid_copy(m).start()

        def from_partner(m):
            mid_copy(m).wait_send()
            back_arrive(m)
            back_e(m, back[m, own].astype(F32))

        def last(m):
            ybuf[m, own] = (res[m] + rs_finish(m)).astype(BF)
            ag_start(ybuf, m, y_send, y_recv)

        front, rear = dict(first=0, last=2), dict(first=2, last=4)
        wait_weights(0, 1)
        each(
            layer_a,
            after=(
                None, then(p(pl.semaphore_wait, barrier, 12), p(rs_start, 0), p(rs_start, 1)),
                p(rs_start, 2),
            ),
        )
        each(layer_b, **front)
        rs_start(3)
        layer_b(2)
        wait_weights(2, 3)
        each(layer_c, **front)
        layer_b(3)
        layer_c(2)
        each(to_partner, **front)
        layer_c(3)
        each(to_partner, **rear)
        each(from_partner, last=3)
        each(back_f, after=(p(from_partner, 3), None, p(back_g, 0), p(back_g, 1)))
        ffn_piece(2)
        dw_start(IN_R, 0)
        ffn_piece(3)
        dw_start(OUT_R, 0)
        back_g(2)
        ffn_piece(0)
        dw_start(IN_W, 0)
        dw_turn(IN_R, 0)
        ffn_piece(1)
        dw_start(OUT_W, 0)
        dw_turn(OUT_R, 0)
        back_g(3)
        each(
            back_h,
            after=(
                then(p(dw_turn, IN_W, 0), p(dw_turn, OUT_W, 0)), small_norms, None, then(p(dw_turn, IN_R, 1), p(dw_turn, OUT_R, 1)),
            ),
        )
        attn_piece(2)
        attn_piece(3)
        dw_start(ATTN_R, 0)
        small_biases()
        attn_piece(0)
        attn_piece(1)
        dw_start(ATTN_W, 0)
        small_y()
        dw_turn(ATTN_R, 0)
        dw_turn(ATTN_W, 0)
        dw_turn(OUT_W, 1)
        small_z()
        dw_turn(IN_W, 1)
        each(last)

    @pl.when(cross)
    def _():
        for copy in bias_copies():
            copy.start()
        gather_wait("x", CWQKV, CWO)
        gather_start("z", CWQKV, CWO)
        gather_wait("x", WQKV, WO)
        gather_start("y", WQKV)
        gather_start("z", WO)
        gather_wait("x", W1)
        gather_start("y", W1)
        gather_wait("y", WQKV)
        gather_start("z", WQKV)
        gather_wait("z", CWQKV, CWO)
        gather_start("core", CWQKV, CWO)
        gather_wait("z", WO)
        gather_start("y", WO)
        gather_wait("y", W1)
        gather_start("z", W1)
        gather_wait("x", W2)
        gather_start("y", W2)
        for copy in bias_copies():
            copy.wait()
        gather_wait("core", CWQKV, CWO)
        wait_weights(0, 1, 2, 3, 4, 5)
        pl.loop(0, 3)(mid_relay)

        @pl.when(set_of == 1)
        def _():
            gather_wait("y", WO)
            gather_wait("z", WQKV)
            gather_start("core", WQKV, WO)
            mid_relay(3)

        cross_forward(0)

        @pl.when(set_of == 0)
        def _():
            gather_wait("y", WO)
            gather_wait("z", WQKV)
            gather_start("core", WQKV, WO)
            mid_relay(3)

        cross_forward(1)
        gather_wait("core", WQKV, WO)
        attn_forward(0)
        gather_wait("z", W1)
        gather_start("core", W1)
        attn_forward(1)
        gather_wait("y", W2)
        gather_start("core", W2)
        pair(ffn_forward)
        pair(ffn_turn)
        pair(attn_backward)
        pair(cross_backward)
        pair(to_section_0)
        mate_wait(CMIXED, XLOW, MIXED, ALOW, ACT, DYF, DUP)
        pass_start(DYF)
        mate_start_all(DYC, CDQKV)
        ffn_piece(2)
        dw_start(IN_R, 0)
        ffn_piece(0)
        dw_start(IN_W, 0)
        dw_turn(IN_R, 0)
        dw_turn(IN_W, 0)
        pass_wait(DYF)
        pass_start(XLOW)
        ffn_piece(3)
        dw_start(OUT_R, 0)
        ffn_piece(1)
        dw_start(OUT_W, 0)
        dw_turn(OUT_R, 0)
        small_norms_all()
        for mod, (lo, hi) in enumerate(SPANS):
            bsum[mod] = column_sums(dup, lo, hi)
        dw_turn(OUT_W, 0)
        mate_wait(DYC)
        pass_start(DYC)
        mate_start_all(DYA, DQKV)
        for k in range(2):
            ag_finish(midf, 2 * (1 - set_of) + k)
        mate_wait(CDQKV)
        pass_wait(DYC)
        cross_outer()
        dw_start(CROSS, 0)
        bqsum[2] = column_sums(cdqkv, 0, R)
        dw_turn(CROSS, 0)
        mate_wait(DYA)
        pass_start(DYA)
        dw_turn(IN_R, 1)
        dw_turn(OUT_R, 1)
        dw_turn(IN_W, 1)
        dw_turn(OUT_W, 1)
        dw_turn(CROSS, 1)
        mate_wait(DQKV)
        mate_start_all(YBUF)
        pass_wait(XLOW)
        pass_wait(DYA)
        for mod, (lo, hi) in enumerate(SPANS):
            bqsum[mod] = column_sums(dqkv, lo, hi)
        small_biases()
        attn_piece(2)
        attn_piece(3)
        dw_start(ATTN_R, 0)
        small_y()
        attn_piece(0)
        attn_piece(1)
        dw_start(ATTN_W, 0)
        dw_turn(ATTN_R, 0)
        small_z()
        dw_turn(ATTN_W, 0)
        mate_wait(YBUF)
        pass_start(YBUF)
        dw_finish(CROSS, 2)
        pass_wait(YBUF)
        for j in range(2):
            rows = back.at[block_of(j), pl.ds(0, 2 * C)]
            moved(rows, rows, back_send.at[j], back_recv.at[0], partner).wait_send()

    def write(m):
        @pl.when(head)
        def _():
            ag_finish(ybuf, m, y_send, y_recv)

        y_ref[m] = ybuf[m]

    dw_finish(IN_R, 2)
    dw_finish(OUT_R, 2)
    dw_turn(ATTN_R, 1)
    dw_turn(ATTN_W, 1)
    dw_finish(IN_W, 2)
    dw_finish(OUT_W, 2)
    small_last()
    each(write)

    @pl.when(cross)
    def _():
        pack[0, :24] = dw_ref[3, :24]
        pack[0, 24:] = s_ref[...]
        packet().start()
        dc_ref[...] = dw_ref[3, 24:]
        sc_ref[...] = s_ref[...]

    dw_finish(ATTN_W, 2)
    dw_finish(ATTN_R, 2)
    pl.when(cross)(lambda: packet().wait_send())

    @pl.when(head)
    def _():
        packet().wait_recv()
        dc_ref[...] = pack[1, :24]
        sc_ref[...] = pack[1, 24:]


def arrange(
    y_ref, dw_ref, s_ref, dc_ref, sc_ref,
    words, regions, qkv_g, qv_bias_g, out_g, in_g, b1_g, ffo_g, obias_g, gain_g, shift_g,
    cqkv_g, cqv_bias_g, cout_g, cobias_g, cgain_g, cshift_g,
):
    place = lax.axis_index("dp")
    both = lax.axis_index("section") * 16 + place

    def from_column(rows, column):
        return pltpu.roll(rows, lax.rem(D - column, D), 1)

    for ref, (lo, hi), length in zip((words, regions), SPANS, (WORDS, REGIONS)):
        padded = y_ref[:, lo:hi, :].reshape(MB * (hi - lo), D)
        rows = dot(spread(hi - lo, length, True), padded)
        ref[0] = rows.reshape(length, ITEMS_LOCAL, D)
    small = s_ref[...]
    for mod in range(2):
        attn = dw_ref[4 * mod]
        for j in range(3):
            qkv_g[0, mod, j] = attn[:, j * HW : (j + 1) * HW]
        out_g[0, mod] = attn[:, 3 * HW :]
        in_g[0, mod] = dw_ref[5 + mod]
        ffo_g[0, mod] = dw_ref[1 + mod]
    columns = from_column(small, 48 * place)[:, :48]
    for mod in range(2):
        for l in range(2):
            for k, ref in enumerate((gain_g, shift_g, obias_g)):
                at = 2 * (3 * l + k) + mod
                ref[0, mod, l : l + 1, :] = columns[at : at + 1]
    columns = from_column(small, 8 * place)
    for mod in range(2):
        for k in range(6):
            b1_g[0, k, mod : mod + 1, :] = columns[16 + mod : 17 + mod, 128 * k : 128 * k + 8]
    columns = from_column(small, 4 * place)
    for mod in range(2):
        for j in range(2):
            for h in range(LOCAL_HEADS):
                lo = 2 * j * HW + h * HEAD_DIM
                qv_bias_g[0, mod, h, j : j + 1, :] = columns[18 + mod : 19 + mod, lo : lo + 4]
    wide = dc_ref[...]
    for j in range(3):
        cqkv_g[j] = wide[:, j * HW : (j + 1) * HW]
    cout_g[...] = wide[:, 3 * HW :]
    small = sc_ref[...]
    columns = from_column(small, 24 * both)
    for k, ref in enumerate((cgain_g, cshift_g, cobias_g)):
        ref[...] = columns[12 + k, :24]
    columns = from_column(small, 2 * both)[20:21]
    for j in range(2):
        heads = []
        for h in range(LOCAL_HEADS):
            lo = 2 * j * HW + h * HEAD_DIM
            heads.append(columns[:, lo : lo + 2])
        cqv_bias_g[j] = jnp.concatenate(heads, axis=0).T


def local(
    words, regions, word_lengths, task_flags, attn_qkv, attn_qv_bias, attn_out, ffn_in, ffn_in_bias,
    ffn_out, out_bias, norm_gain, norm_bias, cross_qkv, cross_qv_bias, cross_out, cross_out_bias,
    cross_norm_gain, cross_norm_bias,
):
    inputs = (
        words.transpose(0, 2, 1, 3), regions.transpose(0, 2, 1, 3), word_lengths, task_flags,
        attn_qkv.transpose(0, 1, 3, 4, 2).reshape(2, 3 * HW, D), attn_qv_bias.transpose(0, 1, 3, 2, 4), attn_out[0],
        ffn_in[0], ffn_in_bias.transpose(0, 2, 1, 3), ffn_out[0], out_bias, norm_gain, norm_bias,
        cross_qkv.transpose(1, 2, 0).reshape(3 * HW, D), cross_qv_bias.transpose(1, 0, 2), cross_out,
        cross_out_bias, cross_norm_gain, cross_norm_bias,
    )

    vmem = pl.BlockSpec(memory_space=pltpu.VMEM)
    smem = pl.BlockSpec(memory_space=pltpu.SMEM)
    hbm = pl.BlockSpec(memory_space=pl.ANY)
    mb_rows = lambda width, dtype: pltpu.VMEM((MB, R, width), dtype)
    own_rows = lambda count: pltpu.VMEM((count, MB, C, D), F32)
    y, g, s, dc, sc = pl.pallas_call(
        kernel,
        out_shape=(
            jax.ShapeDtypeStruct((MB, R, D), BF),
            jax.ShapeDtypeStruct((7, 48, D), F32),
            jax.ShapeDtypeStruct((24, D), F32),
            jax.ShapeDtypeStruct((24, D), F32),
            jax.ShapeDtypeStruct((24, D), F32),
        ),
        in_specs=[smem if k in (2, 3) else hbm if k in (4, 6, 7, 9, 13, 15) else vmem for k in range(len(inputs))],
        out_specs=[vmem] * 5,
        scratch_shapes=[
            mb_rows(D, BF),
            pltpu.VMEM((3, 1, 3 * HW), F32),
            pltpu.VMEM((2, 1, D), F32),
            pltpu.VMEM((3, D), F32),
            mb_rows(D, BF),
            pltpu.VMEM((MB, TENSOR - 1, C, D), BF),
            *[mb_rows(D, BF) for _ in range(8)],
            pltpu.VMEM((3, MB, R, HW), BF),
            mb_rows(HW, BF),
            mb_rows(3 * HW, BF),
            pltpu.VMEM((3, MB, R, HW), BF),
            mb_rows(HW, BF),
            mb_rows(3 * HW, BF),
            mb_rows(D, BF),
            mb_rows(D, BF),
            mb_rows(D, F32),
            pltpu.VMEM((MB, 3 * RW, RW), F32),
            pltpu.VMEM((MB, 3 * RR, RR), F32),
            pltpu.VMEM((MB, 3 * RW, RR), F32),
            pltpu.VMEM((MB, 3 * RR, RW), F32),
            pltpu.VMEM((MB, C, D), F32),
            pltpu.VMEM((MB, C, D), F32),
            pltpu.VMEM((2, MB, C, D), F32),
            pltpu.VMEM((2, MB, C, 128), F32),
            pltpu.VMEM((6, C, D), F32),
            pltpu.VMEM((6, C, D), F32),
            pltpu.VMEM((2, 1, D), F32),
            pltpu.VMEM((3, 1, 3 * HW), F32),
            pltpu.VMEM((2, 3 * HW, D), BF),
            pltpu.VMEM((2, HW, D), BF),
            pltpu.VMEM((2, D, D), BF),
            pltpu.VMEM((2, D, D), BF),
            pltpu.VMEM((3 * HW, D), BF),
            pltpu.VMEM((HW, D), BF),
            pltpu.VMEM((2, 3 * HW, D), BF),
            pltpu.VMEM((2, HW, D), BF),
            pltpu.VMEM((2, D, D), BF),
            pltpu.VMEM((2, D, D), BF),
            pltpu.VMEM((3 * HW, D), BF),
            pltpu.VMEM((HW, D), BF),
            pltpu.VMEM((3, 1, 3 * HW), F32),
            pltpu.VMEM((2, 1, D), F32),
            pltpu.VMEM((2, 2, R, D), BF),
            *[pltpu.VMEM((2, R, w), BF) for w in (D, D, HW, 3 * HW, HW, 3 * HW)],
            pltpu.VMEM((2, R, D), F32),
            pltpu.VMEM((2, R, D), F32),
            pltpu.VMEM((2, 2, R, D), F32),
            pltpu.VMEM((2, 2, R, 128), F32),
            pltpu.VMEM((16, 1, D), F32),
            pltpu.VMEM((7, 2, 4, 2, 48, D), BF),
            pltpu.VMEM((7, 2, 4, 48, D), BF),
            pltpu.VMEM((4, 4, 48, D), BF),
            pltpu.VMEM((3, 3, 2, 48, D), BF),
            pltpu.VMEM((4, 3, 48, D), BF),
            pltpu.VMEM((3, 48, D), BF),
            pltpu.VMEM((3, 24, D), F32),
            pltpu.VMEM((TENSOR, 16, D), F32),
            pltpu.VMEM((24, D), F32),
            pltpu.VMEM((24, D), F32),
            pltpu.VMEM((3, 24, D), F32),
            pltpu.VMEM((2, 48, D), F32),
            *[pltpu.SemaphoreType.DMA((MB,)) for _ in range(6)],
            pltpu.SemaphoreType.DMA((MB,)),
            pltpu.SemaphoreType.DMA((MB,)),
            pltpu.SemaphoreType.DMA((7, 3)),
            pltpu.SemaphoreType.DMA((7, 3)),
            pltpu.SemaphoreType.DMA((4,)),
            pltpu.SemaphoreType.DMA((4,)),
            pltpu.SemaphoreType.DMA,
            pltpu.SemaphoreType.DMA,
            pltpu.SemaphoreType.DMA((2,)),
            pltpu.SemaphoreType.DMA((MB,)),
            *[pltpu.SemaphoreType.DMA((2, 2, 2)) for _ in range(2)],
            *[pltpu.SemaphoreType.DMA((12,)) for _ in range(2)],
            *[pltpu.SemaphoreType.DMA((7, 4)) for _ in range(2)],
            *[pltpu.SemaphoreType.DMA((6,)) for _ in range(2)],
            pltpu.SemaphoreType.DMA((6,)),
        ],
        compiler_params=pltpu.CompilerParams(
            collective_id=0, has_side_effects=True, vmem_limit_bytes=63 * 2**20
        ),
    )(*inputs)

    shapes = (
        (1, WORDS, ITEMS_LOCAL, D), (1, REGIONS, ITEMS_LOCAL, D), (1, 2, 3, 48, HW),
        (1, 2, LOCAL_HEADS, 2, 4), (1, 2, 48, HW), (1, 2, 48, D), (1, 6, 2, 8), (1, 2, 48, D),
        (1, 2, 2, 48), (1, 2, 2, 48), (1, 2, 2, 48), (3, 24, HW), (2, 2, LOCAL_HEADS), (24, HW),
        (24,), (24,), (24,),
    )
    orders = {
        0: (0, 2, 1, 3), 1: (0, 2, 1, 3), 2: (0, 1, 3, 2, 4), 3: (0, 1, 3, 2, 4), 4: (0, 1, 3, 2),
        6: (0, 2, 1, 3), 7: (0, 1, 3, 2), 11: (1, 0, 2), 12: (0, 2, 1), 13: (1, 0),
    }
    outs = pl.pallas_call(
        arrange,
        out_shape=tuple(jax.ShapeDtypeStruct(shape, F32) for shape in shapes),
        in_specs=[vmem] * 5,
        out_specs=[vmem] * len(shapes),
        compiler_params=pltpu.CompilerParams(vmem_limit_bytes=60 * 2**20),
    )(y, g, s, dc, sc)
    return tuple(out.transpose(orders[k]) if k in orders else out for k, out in enumerate(outs))


def solution(mesh):
    in_specs = (
        P("section", "dp", None, None),
        P("section", "dp", None, None),
        P("dp"),
        P("dp"),
        P("section", None, None, None, "tensor"),
        P("section", None, None, "tensor", None),
        P("section", None, "tensor", None),
        P("section", None, None, "tensor"),
        P("section", None, "tensor", None),
        P("section", None, "tensor", None),
        P("section", None, None, None),
        P("section", None, None, None),
        P("section", None, None, None),
        P(None, None, "tensor"),
        P(None, "tensor", None),
        P("tensor", None),
        P(),
        P(),
        P(),
    )
    out_specs = (
        P("section", "dp", None, None),
        P("section", "dp", None, None),
        P("section", None, "dp", None, "tensor"),
        P("section", None, None, "tensor", "dp"),
        P("section", None, "tensor", "dp"),
        P("section", None, "dp", "tensor"),
        P("section", None, "tensor", "dp"),
        P("section", None, "tensor", "dp"),
        P("section", None, None, "dp"),
        P("section", None, None, "dp"),
        P("section", None, None, "dp"),
        P(("section", "dp"), None, "tensor"),
        P(None, "tensor", ("section", "dp")),
        P("tensor", ("section", "dp")),
        P(("section", "dp")),
        P(("section", "dp")),
        P(("section", "dp")),
    )
    return jax.shard_map(local, mesh=mesh, in_specs=in_specs, out_specs=out_specs, check_vma=False)
```

```python
import functools

import jax
import jax.numpy as jnp
from jax import lax
from jax.experimental import pallas as pl
from jax.experimental.pallas import tpu as pltpu
from jax.sharding import PartitionSpec as P

MESH = pl.DeviceIdType.MESH
BF = jnp.bfloat16
F32 = jnp.float32
HEAD_DIM = 64
LOCAL_HEADS = 3
HW = HEAD_DIM * LOCAL_HEADS
WORDS = 20
REGIONS = 36
D = 768
ITEMS_LOCAL = 8
TENSOR = 4

ITEMS_MB = 2
MB = ITEMS_LOCAL // ITEMS_MB
RW = 48
RR = 80
R = RW + RR
C = R // TENSOR
SPANS = ((0, RW), (RW, R))

EPSILON = 1e-06
MASKED = -1000000000.0
SCALING = HEAD_DIM ** (-0.5)


def dot(a, b):
    return lax.dot_general(a, b, (((1,), (0,)), ((), ())), preferred_element_type=F32)


def dot_nt(a, b):
    return lax.dot_general(a, b, (((1,), (1,)), ((), ())), preferred_element_type=F32)


def dot_tn(a, b):
    return lax.dot_general(a, b, (((0,), (0,)), ((), ())), preferred_element_type=F32)


def head_masks():
    lane = lax.broadcasted_iota(jnp.int32, (1, HW), 1)
    return [
        ((lane >= h * HEAD_DIM) & (lane < (h + 1) * HEAD_DIM)).astype(F32) for h in range(LOCAL_HEADS)
    ]


def by_head(a):
    masks = [m.astype(BF) for m in head_masks()]
    return jnp.concatenate([a * m for m in masks], axis=0)


def join_heads(stacked):
    rows = stacked.shape[0] // LOCAL_HEADS
    masks = head_masks()
    total = stacked[:rows] * masks[0]
    for h in range(1, LOCAL_HEADS):
        total = total + stacked[h * rows : (h + 1) * rows] * masks[h]
    return total


def item_of(shape, axis, length):
    index = lax.broadcasted_iota(jnp.int32, shape, axis)
    item = jnp.zeros(shape, jnp.int32)
    for k in range(1, ITEMS_MB + 1):
        item = item + (index >= k * length).astype(jnp.int32)
    return item


def spread(rows, length, transposed=False):
    count = ITEMS_LOCAL * length
    shape = (count, MB * rows) if transposed else (MB * rows, count)
    at = lax.broadcasted_iota(jnp.int32, shape, 0 if transposed else 1)
    padded = lax.broadcasted_iota(jnp.int32, shape, 1 if transposed else 0)
    item, position = at & (ITEMS_LOCAL - 1), at >> 3
    block, within = item >> (ITEMS_MB.bit_length() - 1), item & (ITEMS_MB - 1)
    target = block * rows + within * length + position
    return (target == padded).astype(F32).astype(BF)


def key_mask(q_rows, q_len, k_rows, k_len, lengths=None):
    shape = (q_rows, k_rows)
    item = item_of(shape, 1, k_len)
    key = lax.broadcasted_iota(jnp.int32, shape, 1)
    mask = (item_of(shape, 0, q_len) == item) & (key < ITEMS_MB * k_len)
    if lengths is not None:
        for k, length in enumerate(lengths):
            mask = mask & ((item != k) | (key < k * k_len + length))
    return mask


def attend(cases):
    masks = [jnp.concatenate([mask] * LOCAL_HEADS, axis=0) for _, _, _, mask in cases]
    scores = [dot_nt(by_head(q), k) * SCALING for q, k, _, _ in cases]
    scores = [jnp.where(mask, score, MASKED) for mask, score in zip(masks, scores)]
    es = [jnp.exp(score - jnp.max(score, axis=-1, keepdims=True)) for score in scores]
    probs = [e / jnp.sum(e, axis=-1, keepdims=True) for e in es]
    mixed = [dot(p.astype(BF), v) for p, (_, _, v, _) in zip(probs, cases)]
    return [(p, join_heads(mix).astype(BF)) for p, mix in zip(probs, mixed)]


def attend_back(cases):
    d3s = [by_head(dmix) for dmix, _, _, _, _ in cases]
    dps = [dot_nt(d3, v) for d3, (_, _, _, _, v) in zip(d3s, cases)]
    dss = [
        (probs * (dp - jnp.sum(probs * dp, axis=-1, keepdims=True))).astype(BF)
        for dp, (_, probs, _, _, _) in zip(dps, cases)
    ]
    dqs = [dot(ds, k) for ds, (_, _, _, k, _) in zip(dss, cases)]
    dks = [dot_tn(ds, by_head(q)) for ds, (_, _, q, _, _) in zip(dss, cases)]
    dvs = [dot_tn(probs.astype(BF), d3) for d3, (_, probs, _, _, _) in zip(d3s, cases)]
    return [
        ((join_heads(dq) * SCALING).astype(BF), (dk * SCALING).astype(BF), dv.astype(BF))
        for dq, dk, dv in zip(dqs, dks, dvs)
    ]


def split_qkv(out):
    return out[:, :HW], out[:, HW : 2 * HW], out[:, 2 * HW :]


def gelu(up):
    cdf = 0.5 * (1.0 + lax.erf(up * (0.5**0.5)))
    return (up * cdf).astype(BF), cdf + up * jnp.exp(-0.5 * up * up) * 0.3989422804014327


def norm_forward(r, gain, shift):
    center = r - jnp.mean(r, axis=-1, keepdims=True)
    spread = jnp.mean(center * center, axis=-1, keepdims=True)
    rstd = lax.rsqrt(spread + EPSILON)
    n = center * rstd
    return n, rstd, n * gain + shift


def norm_back(dh, n, rstd, gain):
    dn = dh * gain
    return rstd * (
        dn - jnp.mean(dn, axis=-1, keepdims=True) - n * jnp.mean(dn * n, axis=-1, keepdims=True)
    )


def kernel(
    words_ref, regions_ref, lengths_ref, flags_ref, wqkv_in, qv_bias_ref, wo_in, w1_in, b1_in_ref,
    w2_in, out_bias_ref, gain_ref, shift_ref, cwqkv_in, cqv_bias_ref, cwo_in, cout_bias_ref,
    cgain_ref, cshift_ref,
    y_ref, dw_ref, s_ref, dc_ref, sc_ref,
    x_ref, bqkv_ref, b1_ref, cvec_ref, send, recv, xlow, midf, alow, dyf, dya, dyc, ybuf, back,
    qkv, mixed, dqkv, cqkv, cmixed, cdqkv, act, dup, dgelu,
    p_w, p_r, cp_w, cp_r, cur, res, nrm, rstd, packed, gathered_end, total_ref, low_ref, bsum, bqsum,
    wqkv_ref, wo_ref, w1_ref, w2_ref, cwqkv_ref, cwo_ref, wqkv_m, wo_m, w1_m, w2_m, cwqkv_m, cwo_m, bqkv_m, b1_m,
    got, tails, got_tails, act_m, dup_m, mixed_m, dqkv_m, cmixed_m, cdqkv_m, cur_f, res_f, nrm_f, rstd_f, row_sums,
    g_ref, from_core, from_y, from_zs, from_h, from_z, from_ys, sums, total, sums_t, sums_c, sums_y, sums_z, pack,
    rs_send, rs_recv, ag_send, ag_recv, y_send, y_recv, sec_send, sec_recv,
    dw_send, dw_recv, sm_send, sm_recv, pk_send, pk_recv,
    back_send, back_recv, ar_send, ar_recv, mt_send, mt_recv, ga_send, ga_recv, ps_send, ps_recv, loads,
):
    p = functools.partial
    sec = lax.axis_index("section")
    me = lax.axis_index("tensor")
    head = sec == 0
    cross = sec == 1

    def peer(o):
        return {"tensor": lax.rem(me + o, TENSOR)}

    partner = {"section": 1 - sec}
    place = lax.axis_index("dp")
    y_at, z_at, core = place // 8, lax.rem(place // 2, 4), lax.rem(place, 2)

    def dp_device(y, z, c):
        return {"dp": (y * 4 + z) * 2 + c}

    other_core = dp_device(y_at, z_at, 1 - core)
    other_y = dp_device(1 - y_at, z_at, core)

    def z_next(o):
        return lax.rem(z_at + o, 4)

    weights = tuple(
        pltpu.make_async_copy(src, dst, loads.at[k])
        for k, (src, dst) in enumerate((
            (wqkv_in, wqkv_ref), (wo_in, wo_ref), (w1_in, w1_ref), (w2_in, w2_ref),
            (cwqkv_in, cwqkv_ref), (cwo_in, cwo_ref),
        ))
    )

    def load_weights(*which):
        for k in which:
            weights[k].start()

    def wait_weights(*which):
        for k in which:
            weights[k].wait()

    barrier = pltpu.get_barrier_semaphore()
    for o in range(1, TENSOR):
        pl.semaphore_signal(barrier, inc=1, device_id=peer(o), device_id_type=MESH)
    mate, halver = {"tensor": me + 1 - 2 * lax.rem(me, 2)}, {"tensor": 3 - me}
    set_of = lax.rem((me + 1) // 2, 2)
    for t in range(TENSOR):
        pl.semaphore_signal(
            barrier, inc=1, device_id={"section": 1 - sec, "tensor": t}, device_id_type=MESH
        )
    for device in (other_core, other_y, *(dp_device(y_at, z_next(o), core) for o in (1, 2, 3))):
        pl.semaphore_signal(barrier, inc=1, device_id=device, device_id_type=MESH)

    load_weights(0, 1, 2, 3)
    pl.when(cross)(lambda: load_weights(4, 5))

    def moved(src, dst, send_sem, recv_sem, device):
        return pltpu.make_async_remote_copy(
            src_ref=src, dst_ref=dst, send_sem=send_sem, recv_sem=recv_sem, device_id=device,
            device_id_type=MESH,
        )

    both_mods = slice(0, 2)
    half_columns = pl.ds(pl.multiple_of(core * (D // 2), D // 2), D // 2)

    def z_rows(z, count):
        return pl.ds(pl.multiple_of(z * count, count), count)

    gathered = (
        (cwqkv_in, cwqkv_m, 3 * HW // 4, False), (cwo_in, cwo_m, HW // 4, False),
        (wqkv_in, wqkv_m, 3 * HW // 4, True), (wo_in, wo_m, HW // 4, True),
        (w1_in, w1_m, D // 4, True), (w2_in, w2_m, D // 4, True),
    )
    CWQKV, CWO, WQKV, WO, W1, W2 = range(6)
    Y_FIRST = (WQKV, W1)

    def gather_copies(k, step):
        src, dst, count, by_mod = gathered[k]
        sems = lambda i: (ga_send.at[k, i], ga_recv.at[k, i])
        at = lambda mods, rows: (mods, rows, half_columns) if by_mod else (rows, half_columns)
        mine = at(y_at, z_rows(z_at, count))
        column = at(y_at, slice(0, 4 * count)) if by_mod else None
        if step == "x":
            part = column if k == W2 else mine
            return [moved(src.at[part], dst.at[part], *sems(0), mate)]
        if step == "y":
            place = dst.at[mine] if k in Y_FIRST else dst.at[column]
            return [moved(place, place, *sems(1), other_y)]
        if step == "z":
            place = dst.at[at(both_mods if k in Y_FIRST else y_at, z_rows(z_at, count))]
            return [
                moved(place, place, *sems(2), dp_device(y_at, z_next(o), core)) for o in (1, 2, 3)
            ]
        place = dst.at[at(both_mods, slice(0, 4 * count))]
        return [moved(place, place, *sems(3), other_core)]

    def gather_start(step, *arrays):
        for k in arrays:
            for copy in gather_copies(k, step):
                copy.start()

    def gather_wait(step, *arrays):
        for k in arrays:
            if step != "z":
                gather_copies(k, step)[0].wait()
                continue
            _, dst, count, by_mod = gathered[k]
            rows = slice(0, 3 * count)
            mods = both_mods if k in Y_FIRST else y_at
            place = dst.at[(mods, rows, half_columns) if by_mod else (rows, half_columns)]
            moved(place, place, ga_send.at[k, 2], ga_recv.at[k, 2], mate).wait()

    @pl.when(cross)
    def _():
        pl.semaphore_wait(barrier, 12)
        gather_start("x", CWQKV, CWO, WQKV, WO, W1, W2)

    def side_by_side(rows):
        return jnp.concatenate(rows, axis=1)

    for mod in range(2):
        b1_ref[mod] = side_by_side(
            [b1_in_ref[0, k, mod : mod + 1, :] for k in range(D // 128)]
        )
    for k, ref in enumerate((qv_bias_ref.at[0, 0], qv_bias_ref.at[0, 1], cqv_bias_ref)):
        heads = lambda j: [ref[h, j : j + 1, :] for h in range(LOCAL_HEADS)]
        bqkv_ref[k] = side_by_side([*heads(0), jnp.zeros((1, HW), F32), *heads(1)])
    for k, ref in enumerate((cout_bias_ref, cgain_ref, cshift_ref)):
        cvec_ref[k : k + 1, :] = ref[...].reshape(1, D)

    for ref, (lo, hi), length in zip((words_ref, regions_ref), SPANS, (WORDS, REGIONS)):
        given = ref[0].astype(F32).reshape(ITEMS_LOCAL * length, D).astype(BF)
        placed = dot(spread(hi - lo, length), given).astype(BF)
        x_ref[:, lo:hi, :] = placed.reshape(MB, hi - lo, D)
    bsum[...] = jnp.zeros_like(bsum)
    bqsum[...] = jnp.zeros_like(bqsum)
    row_sums[...] = jnp.zeros_like(row_sums)


    def place_of(t, m):
        return lax.rem(t + m, TENSOR)

    def rows_at(at):
        return pl.ds(pl.multiple_of(48 * at - 16 * (at // 2), 16), C)

    def by_place(at, heavy, light):
        pl.when(at != 3)(heavy)
        pl.when(at == 3)(light)

    WORD_END, REGION_END = pl.ds(32, 16), pl.ds(112, 16)
    no_rows = jnp.zeros((8, D), F32)

    def pack_rows(words_end, regions_end):
        return jnp.concatenate([words_end, regions_end], axis=0).astype(BF)

    def wait_rows(m, ss, rs, sent, received):
        out, come = send.at[m, pl.ds(0, sent)], send.at[m, pl.ds(0, received)]
        moved(out, out, ss.at[m], rs.at[m], peer(1)).wait_send()
        moved(come, come, ss.at[m], rs.at[m], peer(1)).wait_recv()

    def own_rows_of(ref, m):
        at = place_of(me, m)

        def heavy():
            low_ref[...] = ref[m, rows_at(at)]

        def light():
            low_ref[0:16] = ref[m, WORD_END]
            low_ref[16:32] = ref[m, REGION_END]

        by_place(at, heavy, light)
        return low_ref[...]

    def put_own_rows(ref, m, low):
        at = place_of(me, m)

        def heavy():
            ref[m, rows_at(at)] = low

        def light():
            ref[m, WORD_END] = low[:16]
            ref[m, REGION_END] = low[16:]

        by_place(at, heavy, light)

    def put_parts(m, parts):
        for (lo, hi), part in zip(SPANS, parts):
            send[m, lo:hi] = part.astype(BF)
        packed[m] = pack_rows(parts[0][32:40], parts[1][64:72])

    def rs_start(m):
        for o in range(1, TENSOR):
            at = place_of(me + o, m)

            def heavy(o=o, at=at):
                src, dst = send.at[m, rows_at(at)], recv.at[m, o - 1]
                moved(src, dst, rs_send.at[m], rs_recv.at[m], peer(o)).start()

            def light(o=o):
                src, dst = packed.at[m], recv.at[m, o - 1, pl.ds(0, 16)]
                moved(src, dst, rs_send.at[m], rs_recv.at[m], peer(o)).start()

            by_place(at, heavy, light)

    def rs_finish(m):
        at = place_of(me, m)

        def heavy():
            wait_rows(m, rs_send, rs_recv, 80, 96)
            total = send[m, rows_at(at)].astype(F32)
            for o in range(TENSOR - 1):
                total = total + recv[m, o].astype(F32)
            total_ref[...] = total

        def light():
            wait_rows(m, rs_send, rs_recv, 96, 48)
            total = packed[m].astype(F32)
            for o in range(TENSOR - 1):
                total = total + recv[m, o, 0:16].astype(F32)
            total_ref[...] = jnp.concatenate([total[:8], no_rows, total[8:], no_rows], axis=0)

        by_place(at, heavy, light)
        return total_ref[...]

    def ag_start(buf, m, low, ss=ag_send, rs=ag_recv):
        put_own_rows(buf, m, low)
        at = place_of(me, m)

        def heavy():
            rows = buf.at[m, rows_at(at)]
            for o in range(1, TENSOR):
                moved(rows, rows, ss.at[m], rs.at[m], peer(o)).start()

        def light():
            wide = low.astype(F32)
            gathered_end[m] = pack_rows(wide[:8], wide[16:24])
            for o in range(1, TENSOR):
                end = gathered_end.at[m]
                moved(end, end, ss.at[m], rs.at[m], peer(o)).start()

        by_place(at, heavy, light)

    def ag_finish(buf, m, ss=ag_send, rs=ag_recv):
        def heavy():
            wait_rows(m, ss, rs, 96, 80)
            end = gathered_end[m].astype(F32)
            buf[m, WORD_END] = pack_rows(end[:8], no_rows)
            buf[m, REGION_END] = pack_rows(end[8:], no_rows)

        def light():
            wait_rows(m, ss, rs, 48, 96)

        by_place(place_of(me, m), heavy, light)

    def start_rows(ref, m, at, ss, rs, *devices):
        def heavy():
            rows = ref.at[m, rows_at(at)]
            for device in devices:
                moved(rows, rows, ss, rs, device).start()

        def light():
            for end in (WORD_END, REGION_END):
                rows = ref.at[m, end]
                for device in devices:
                    moved(rows, rows, ss, rs, device).start()

        by_place(at, heavy, light)

    def some_rows(ref, m, count, ss, rs):
        rows = ref.at[m, pl.ds(0, count)]
        return moved(rows, rows, ss, rs, partner)

    def mid_start(m):
        start_rows(midf, m, place_of(me, m), sec_send.at[m], sec_recv.at[m], partner)

    def mid_relay(m):
        some_rows(midf, m, C, sec_send.at[m], sec_recv.at[m]).wait_recv()
        start_rows(midf, m, place_of(me, m), ag_send.at[m], ag_recv.at[m], peer(1), peer(2), peer(3))

    def mid_finish(m):
        some_rows(midf, m, 3 * C, ag_send.at[m], ag_recv.at[m]).wait()

    def back_start(j):
        m = 2 * set_of + j
        for k in range(2):
            t = 2 * (me // 2) + k
            device = {"section": 1 - sec, "tensor": t}
            start_rows(back, m, place_of(t, m), back_send.at[j], back_recv.at[m], device)

    def back_arrive(m):
        some_rows(back, m, C, back_send.at[0], back_recv.at[m]).wait_recv()

    def save_norm(l, m, n, r):
        nrm[l, m] = n
        rstd[l, m] = jnp.broadcast_to(r, (C, 128))

    def own_words(m):
        at = place_of(me, m)
        count = jnp.where(at == 0, C, jnp.where(at == 3, C // 2, 0))
        return lax.broadcasted_iota(jnp.int32, (C, 1), 0) < count

    def own_param(ref, l, m):
        return jnp.where(own_words(m), ref[0, 0, l : l + 1, :], ref[0, 1, l : l + 1, :])

    def norm_step_back(l, m, dh):
        n = nrm[l, m]
        dr = norm_back(dh, n, rstd[l, m][:, :1], own_param(gain_ref, l, m))
        low = dr.astype(BF)
        words_only = own_words(m)
        for k, value in enumerate((dh * n, dh, low.astype(F32))):
            part = jnp.where(words_only, value, 0.0)
            at = 2 * (3 * l + k)
            row_sums[at] += jnp.sum(part, axis=0, keepdims=True)
            row_sums[at + 1] += jnp.sum(value - part, axis=0, keepdims=True)
        res[m] = dr
        return low

    def word_keys(m, q_rows, q_len):
        return key_mask(
            q_rows, q_len, RW, WORDS, [lengths_ref[ITEMS_MB * m + k] for k in range(ITEMS_MB)]
        )

    def region_keys(q_rows, q_len):
        return key_mask(q_rows, q_len, RR, REGIONS)

    def layer_a(m):
        xlow[m] = x_ref[m]
        cur[m] = own_rows_of(x_ref, m).astype(F32)
        outs = [
            (dot_nt(xlow[m, lo:hi], wqkv_ref[mod]) + bqkv_ref[mod]).astype(BF)
            for mod, (lo, hi) in enumerate(SPANS)
        ]
        for (lo, hi), out in zip(SPANS, outs):
            for k, part in enumerate(split_qkv(out)):
                qkv[k, m, lo:hi] = part
        masks = (word_keys(m, RW, WORDS), region_keys(RR, REGIONS))
        done = attend([(*split_qkv(out), mask) for out, mask in zip(outs, masks)])
        for (lo, hi), keep, (probs, mix) in zip(SPANS, (p_w, p_r), done):
            keep[m] = probs
            mixed[m, lo:hi] = mix
        put_parts(m, [dot(mix, wo_ref[mod]) for mod, (_, mix) in enumerate(done)])

    def layer_b(m):
        r = cur[m] + rs_finish(m) + own_param(out_bias_ref, 0, m)
        n, rs, h = norm_forward(r, own_param(gain_ref, 0, m), own_param(shift_ref, 0, m))
        save_norm(0, m, n, rs)
        cur[m] = h
        ag_start(alow, m, h.astype(BF))

    def layer_c(m):
        ag_finish(alow, m)
        ups = [dot(alow[m, lo:hi], w1_ref[mod]) + b1_ref[mod] for mod, (lo, hi) in enumerate(SPANS)]
        pairs = [gelu(up) for up in ups]
        put_parts(m, [dot(active, w2_ref[mod]) for mod, (active, _) in enumerate(pairs)])
        rs_start(m)
        for (lo, hi), (active, slope) in zip(SPANS, pairs):
            act[m, lo:hi] = active
            dgelu[m, lo:hi] = slope

    def layer_d(m):
        r = cur[m] + rs_finish(m) + own_param(out_bias_ref, 1, m)
        n, rs, h = norm_forward(r, own_param(gain_ref, 1, m), own_param(shift_ref, 1, m))
        save_norm(1, m, n, rs)
        return h

    def back_e(m, dh):
        ag_start(dyf, m, norm_step_back(1, m, dh))

    def back_f(m):
        ag_finish(dyf, m)
        dacts = [dot_nt(dyf[m, lo:hi], w2_ref[mod]) for mod, (lo, hi) in enumerate(SPANS)]
        ds = [(dact * dgelu[m, lo:hi]).astype(BF) for dact, (lo, hi) in zip(dacts, SPANS)]
        put_parts(m, [dot_nt(d, w1_ref[mod]) for mod, d in enumerate(ds)])
        rs_start(m)
        for mod, (lo, hi) in enumerate(SPANS):
            dup[m, lo:hi] = ds[mod]
            bsum[mod] += jnp.sum(ds[mod].astype(F32), axis=0, keepdims=True)

    def back_g(m):
        dh = res[m] + rs_finish(m)
        ag_start(dya, m, norm_step_back(0, m, dh))

    def back_h(m):
        ag_finish(dya, m)
        dmixs = [
            dot_nt(dya[m, lo:hi], wo_ref[mod]).astype(BF) for mod, (lo, hi) in enumerate(SPANS)
        ]
        grads = attend_back([
            (dmix, keep[m], *(qkv[k, m, lo:hi] for k in range(3)))
            for dmix, keep, (lo, hi) in zip(dmixs, (p_w, p_r), SPANS)
        ])
        ds = [jnp.concatenate(grad, axis=1) for grad in grads]
        put_parts(m, [dot(d, wqkv_ref[mod]) for mod, d in enumerate(ds)])
        rs_start(m)
        for mod, (lo, hi) in enumerate(SPANS):
            dqkv[m, lo:hi] = ds[mod]
            bqsum[mod] += jnp.sum(ds[mod].astype(F32), axis=0, keepdims=True)

    def block_of(j):
        return 2 * set_of + j

    def ar_copies(j, mod, turn):
        lo, hi = SPANS[mod]
        rows = slice(lo, hi - 16)
        sems = lambda k: (ar_send.at[turn, j, 2 * mod + k], ar_recv.at[turn, j, 2 * mod + k])
        return [
            moved(send.at[j, rows], got.at[turn, j, rows], *sems(0), halver),
            moved(tails.at[j, mod], got_tails.at[turn, j, mod], *sems(1), halver),
        ]

    def ar_start(j, mod, turn, part):
        lo, hi = SPANS[mod]
        full = hi - lo - 16
        send[j, lo : hi - 16] = part[:full].astype(BF)
        tail = part[full : full + 8]
        tails[j, mod] = jnp.concatenate([tail[:, : D // 2], tail[:, D // 2 :]], axis=0).astype(BF)
        for copy in ar_copies(j, mod, turn):
            copy.start()

    def ar_finish(j, mod, turn):
        lo, hi = SPANS[mod]
        for copy in ar_copies(j, mod, turn):
            copy.wait()
        rows = send[j, lo : hi - 16].astype(F32) + got[turn, j, lo : hi - 16].astype(F32)
        tail = tails[j, mod].astype(F32) + got_tails[turn, j, mod].astype(F32)
        return jnp.concatenate([rows, jnp.concatenate([tail[:8], tail[8:]], axis=1), no_rows], axis=0)

    shared = (xlow, alow, dyf, dya, dyc, ybuf)
    for_mate = ((act_m, act), (dup_m, dup), (mixed_m, mixed), (dqkv_m, dqkv), (cmixed_m, cmixed), (cdqkv_m, cdqkv))
    XLOW, ALOW, DYF, DYA, DYC, YBUF, ACT, DUP, MIXED, DQKV, CMIXED, CDQKV = range(12)

    halves = (XLOW, DYF, DYA, DYC, YBUF)

    def half_rows(which):
        return pl.ds(pl.multiple_of(which * (R // 2), R // 2), R // 2)

    def mate_copy(k, j):
        if k < 6:
            src = dst = shared[k]
            src = src.at[block_of(j)]
        else:
            src, dst = for_mate[k - 6]
            src = src.at[j]
        dst = dst.at[block_of(j)]
        if k in halves:
            src, dst = src.at[half_rows(me // 2)], dst.at[half_rows(me // 2)]
        return moved(src, dst, mt_send.at[k], mt_recv.at[k], mate)

    def mate_start(j, *kinds):
        for k in kinds:
            mate_copy(k, j).start()

    def mate_start_all(*kinds):
        for k in kinds:
            for j in range(2):
                mate_copy(k, j).start()

    def mate_wait(*kinds):
        for k in kinds:
            place = (shared[k] if k < 6 else for_mate[k - 6][1]).at[pl.ds(2 * (1 - set_of), 2)]
            if k in halves:
                place = place.at[:, half_rows(me // 2)]
            moved(place, place, mt_send.at[k], mt_recv.at[k], mate).wait()

    def pass_copy(k):
        place = shared[k].at[pl.ds(2 * (1 - set_of), 2), half_rows(me // 2)]
        return moved(place, place, ps_send.at[k], ps_recv.at[k], halver)

    def pass_start(k):
        pass_copy(k).start()

    def pass_wait(k):
        pass_copy(k).wait()

    def bias_copies():
        return [
            moved(bqkv_ref, bqkv_m, ga_send.at[6, 0], ga_recv.at[6, 0], mate),
            moved(b1_ref, b1_m, ga_send.at[6, 1], ga_recv.at[6, 1], mate),
        ]

    def save_norm_f(l, j, lo, hi, n, r):
        nrm_f[l, j, lo:hi] = n
        rstd_f[l, j, lo:hi] = jnp.broadcast_to(r, (hi - lo, 128))

    def count_rows(l, mod, dh, n, low):
        for k, value in enumerate((dh * n, dh, low.astype(F32))):
            at = 12 + k if l == 2 else 2 * (3 * l + k) + mod
            row_sums[at] += jnp.sum(value, axis=0, keepdims=True)

    def cross_forward(j):
        m = block_of(j)
        mid_finish(m)
        mid = midf[m]
        shards = ((cwqkv_ref, bqkv_ref, cwo_ref, cmixed, m), (cwqkv_m, bqkv_m, cwo_m, cmixed_m, j))
        qkvs = []
        for sh, (w, bias, w_out, keep, at) in enumerate(shards):
            out = (dot_nt(mid, w[...]) + bias[2]).astype(BF)
            q, k, v = split_qkv(out)
            cqkv[0, 2 * sh + j], cqkv[1, 2 * sh + j], cqkv[2, 2 * sh + j] = q, k, v
            qkvs.append((q, k, v))
        for mod, (lo, hi) in enumerate(SPANS):
            others = slice(*SPANS[1 - mod])
            mask = region_keys(RW, WORDS) if mod == 0 else word_keys(m, RR, REGIONS)
            done = attend([(q[lo:hi], k[others], v[others], mask) for q, k, v in qkvs])
            part = None
            for sh, (w, bias, w_out, keep, at) in enumerate(shards):
                probs, mix = done[sh]
                (cp_w, cp_r)[mod][2 * sh + j] = probs
                keep[at, lo:hi] = mix
                one = dot(mix, w_out[...])
                part = one if part is None else part + one
            ar_start(j, mod, 0, part)
        mate_start(j, CMIXED)

    def attn_forward(j):
        m = block_of(j)
        shards = (
            (wqkv_ref, bqkv_ref, wo_ref, mixed, m), (wqkv_m, bqkv_m, wo_m, mixed_m, j),
        )
        for mod, (lo, hi) in enumerate(SPANS):
            r = midf[m, lo:hi].astype(F32) + ar_finish(j, mod, 0) + cvec_ref[0:1, :]
            n, rs, h = norm_forward(r, cvec_ref[1:2, :], cvec_ref[2:3, :])
            save_norm_f(1, j, lo, hi, n, rs)
            cur_f[j, lo:hi] = h
            low = h.astype(BF)
            xlow[m, lo:hi] = low
            outs = [(dot_nt(low, w[mod]) + bias[mod]).astype(BF) for w, bias, _, _, _ in shards]
            for sh, out in enumerate(outs):
                for k, part in enumerate(split_qkv(out)):
                    qkv[k, 2 * sh + j, lo:hi] = part
            mask = word_keys(m, RW, WORDS) if mod == 0 else region_keys(RR, REGIONS)
            done = attend([(*split_qkv(out), mask) for out in outs])
            part = None
            for sh, (w, bias, w_out, keep, at) in enumerate(shards):
                probs, mix = done[sh]
                (p_w, p_r)[mod][2 * sh + j] = probs
                keep[at, lo:hi] = mix
                one = dot(mix, w_out[mod])
                part = one if part is None else part + one
            ar_start(j, mod, 1, part)
        mate_start(j, XLOW, MIXED)

    def ffn_forward(j):
        m = block_of(j)
        shards = ((w1_ref, b1_ref, w2_ref, act, m), (w1_m, b1_m, w2_m, act_m, j))
        for mod, (lo, hi) in enumerate(SPANS):
            r = cur_f[j, lo:hi] + ar_finish(j, mod, 1) + out_bias_ref[0, mod, 0:1, :]
            n, rs, h = norm_forward(r, gain_ref[0, mod, 0:1, :], shift_ref[0, mod, 0:1, :])
            save_norm_f(0, j, lo, hi, n, rs)
            cur_f[j, lo:hi] = h
            low = h.astype(BF)
            alow[m, lo:hi] = low
            if mod == 0:
                pl.when(j == 0)(lambda: gather_wait("core", W1))
            ups = [dot(low, w[mod]) + bias[mod] for w, bias, _, _, _ in shards]
            pairs = [gelu(up) for up in ups]
            for sh, (_, _, _, keep, at) in enumerate(shards):
                keep[at, lo:hi], dgelu[2 * sh + j, lo:hi] = pairs[sh]
            if mod == 0:
                pl.when(j == 0)(lambda: gather_wait("core", W2))
            ones = [dot(active, w_out[mod]) for (active, _), (_, _, w_out, _, _) in zip(pairs, shards)]
            part = ones[0] + ones[1]
            ar_start(j, mod, 0, part)
        mate_start(j, ALOW, ACT)

    def ffn_turn(j):
        m = block_of(j)
        shards = ((w1_ref, w2_ref, dup, m), (w1_m, w2_m, dup_m, j))
        for mod, (lo, hi) in enumerate(SPANS):
            r = cur_f[j, lo:hi] + ar_finish(j, mod, 0) + out_bias_ref[0, mod, 1:2, :]
            gain = gain_ref[0, mod, 1:2, :]
            n, rs, h = norm_forward(r, gain, shift_ref[0, mod, 1:2, :])
            ybuf[m, lo:hi] = h.astype(BF)
            scale = scales(m, 1 - mod, hi - lo, (WORDS, REGIONS)[mod])
            dh = x_ref[m, lo:hi].astype(F32) * scale
            dr = norm_back(dh, n, rs, gain)
            res_f[j, lo:hi] = dr
            low = dr.astype(BF)
            dyf[m, lo:hi] = low
            dacts = [dot_nt(low, w_out[mod]) for _, w_out, _, _ in shards]
            ds = [(dact * dgelu[2 * sh + j, lo:hi]).astype(BF) for sh, dact in enumerate(dacts)]
            ones = [dot_nt(d, w_in[mod]) for d, (w_in, _, _, _) in zip(ds, shards)]
            part = ones[0] + ones[1]
            for d, (_, _, keep, at) in zip(ds, shards):
                keep[at, lo:hi] = d
            count_rows(1, mod, dh, n, low)
            ar_start(j, mod, 1, part)
        mate_start(j, DYF, DUP)

    def attn_backward(j):
        m = block_of(j)
        shards = ((wqkv_ref, wo_ref, dqkv, m), (wqkv_m, wo_m, dqkv_m, j))
        for mod, (lo, hi) in enumerate(SPANS):
            dh = res_f[j, lo:hi] + ar_finish(j, mod, 1)
            n = nrm_f[0, j, lo:hi]
            dr = norm_back(dh, n, rstd_f[0, j, lo:hi][:, :1], gain_ref[0, mod, 0:1, :])
            res_f[j, lo:hi] = dr
            low = dr.astype(BF)
            dya[m, lo:hi] = low
            count_rows(0, mod, dh, n, low)
            dmixs = [dot_nt(low, w_out[mod]).astype(BF) for _, w_out, _, _ in shards]
            grads = attend_back([
                (dmix, (p_w, p_r)[mod][2 * sh + j], *(qkv[k, 2 * sh + j, lo:hi] for k in range(3)))
                for sh, dmix in enumerate(dmixs)
            ])
            part = None
            for grad, (w, _, keep, at) in zip(grads, shards):
                d = jnp.concatenate(grad, axis=1)
                keep[at, lo:hi] = d
                one = dot(d, w[mod])
                part = one if part is None else part + one
            ar_start(j, mod, 0, part)

    def cross_backward(j):
        m = block_of(j)
        for mod, (lo, hi) in enumerate(SPANS):
            dh = res_f[j, lo:hi] + ar_finish(j, mod, 0)
            n = nrm_f[1, j, lo:hi]
            dr = norm_back(dh, n, rstd_f[1, j, lo:hi][:, :1], cvec_ref[1:2, :])
            res_f[j, lo:hi] = dr
            low = dr.astype(BF)
            dyc[m, lo:hi] = low
            count_rows(2, mod, dh, n, low)
        shards = ((cwqkv_ref, cwo_ref, cdqkv, m), (cwqkv_m, cwo_m, cdqkv_m, j))
        dmixs = [dot_nt(dyc[m], w_out[...]).astype(BF) for _, w_out, _, _ in shards]
        cases = []
        for sh, dmix in enumerate(dmixs):
            slot = 2 * sh + j
            q, k, v = cqkv[0, slot], cqkv[1, slot], cqkv[2, slot]
            cases.append((dmix[:RW], cp_w[slot], q[:RW], k[RW:], v[RW:]))
            cases.append((dmix[RW:], cp_r[slot], q[RW:], k[:RW], v[:RW]))
        grads = attend_back(cases)
        part = None
        for sh, (w, _, keep, at) in enumerate(shards):
            (dq_w, dk_r, dv_r), (dq_r, dk_w, dv_w) = grads[2 * sh : 2 * sh + 2]
            keep[at, :RW] = jnp.concatenate([dq_w, dk_w, dv_w], axis=1)
            keep[at, RW:] = jnp.concatenate([dq_r, dk_r, dv_r], axis=1)
            one = dot(keep[at], w[...])
            part = one if part is None else part + one
        for mod, (lo, hi) in enumerate(SPANS):
            ar_start(j, mod, 1, part[lo:hi])

    def to_section_0(j):
        m = block_of(j)
        for mod, (lo, hi) in enumerate(SPANS):
            back[m, lo:hi] = (res_f[j, lo:hi] + ar_finish(j, mod, 1)).astype(BF)
        back_start(j)

    def column_sums(buf, lo, hi):
        rows = buf[:, lo:hi, :].astype(F32).reshape(MB * (hi - lo), buf.shape[-1])
        return jnp.sum(rows, axis=0, keepdims=True)

    def scales(m, flag, count, length):
        index = lax.broadcasted_iota(jnp.int32, (count, 1), 0)
        scale = jnp.ones((count, 1), F32)
        for k in range(ITEMS_MB):
            value = jnp.where(flags_ref[ITEMS_MB * m + k] == flag, 0.25, 1.0)
            scale = jnp.where(index >= k * length, value, scale)
        return scale

    def outer_tile(left, right, lo, hi, j, store):
        start = j * (D // 2)
        columns = pl.ds(start if isinstance(j, int) else pl.multiple_of(start, D // 2), D // 2)
        a = left[:, lo:hi, columns].reshape(MB * (hi - lo), D // 2)
        b = right[:, lo:hi, :].reshape(MB * (hi - lo), right.shape[-1])
        store(dot_tn(a, b))

    def outer(left, right, lo, hi, store):
        pl.loop(0, 2)(
            lambda j: outer_tile(left, right, lo, hi, j, p(store, j))
        )

    def store_at(block, lo, hi):
        def store(j, value):
            g_ref[block, j, :, :, :, lo:hi] = value.astype(BF).reshape(4, 2, 48, hi - lo)

        return store

    def ffn_piece(k):
        mod, second = k // 2, k % 2
        left, right = ((alow, dup), (dyf, act))[second]
        outer(left, right, *SPANS[mod], store_at((5, 1)[second] + mod, 0, D))

    def attn_piece(k):
        mod, second = k // 2, k % 2
        left, right = ((xlow, dqkv), (dya, mixed))[second]
        outer(left, right, *SPANS[mod], store_at(4 * mod, *((0, 3 * HW), (3 * HW, D))[second]))

    def cross_outer():
        def store(j, lo, hi):
            def put(value):
                value = value.astype(BF).reshape(2, 4, 2, 24, hi - lo)
                g_ref[3, :, :, :, 24 * j : 24 * j + 24, lo:hi] = value

            return put

        for j in range(2):
            outer_tile(midf, cdqkv, 0, R, j, store(j, 0, 3 * HW))
            outer_tile(dyc, cmixed, 0, R, j, store(j, 3 * HW, D))

    Y, Z, EVEN, ODD = range(4)
    even_z, odd_z = z_at + 1 - 2 * lax.rem(z_at, 2), 3 - z_at
    LAST = {Y: 2, Z: 2, EVEN: 3, ODD: 3}

    def dw_copies(group, phase):
        index, kind, b = group
        sems = lambda k: (dw_send.at[index, k], dw_recv.at[index, k])
        if phase == 0:
            return [moved(g_ref.at[b, :, :, 1 - core], from_core.at[b], *sems(0), other_core)]
        if kind == Y:
            if phase == 1:
                return [moved(g_ref.at[b, 1 - y_at, :, core], from_y.at[b], *sems(1), other_y)]
            return [
                moved(
                    g_ref.at[b, y_at, z_next(o), core], from_z.at[b, o - 1], *sems(2),
                    dp_device(y_at, z_next(o), core),
                )
                for o in (1, 2, 3)
            ]
        if phase == LAST[kind]:
            src = g_ref.at[b, 1 - y_at, z_at, core]
            return [moved(src, from_ys.at[b - 4], *sems(1), other_y)]
        if kind == Z:
            return [
                moved(
                    g_ref.at[b, :, z_next(o), core], from_zs.at[o - 1], *sems(2),
                    dp_device(y_at, z_next(o), core),
                )
                for o in (1, 2, 3)
            ]
        near, far = (even_z, odd_z) if kind == EVEN else (odd_z, even_z)
        to = lambda z: dp_device(y_at, z, core)
        if phase == 1:
            beyond = 3 - near if kind == EVEN else near + 1 - 2 * lax.rem(near, 2)
            return [
                moved(g_ref.at[b, :, z, core], from_h.at[b - 5, k], *sems(2), to(near))
                for k, z in enumerate((near, beyond))
            ]
        return [moved(g_ref.at[b, :, far, core], from_h.at[b - 5, 2], *sems(3), to(far))]

    def dw_start(group, phase):
        for copy in dw_copies(group, phase):
            copy.start()

    def dw_finish(group, phase):
        index, kind, b = group
        together = None
        if kind == Y and phase == 2:
            together = from_z.at[b]
        elif kind == Z and phase == 1:
            together = from_zs
        elif kind in (EVEN, ODD) and phase == 1:
            together = from_h.at[b - 5, pl.ds(0, 2)]
        if together is None:
            dw_copies(group, phase)[0].wait()
        else:
            moved(together, together, dw_send.at[index, 2], dw_recv.at[index, 2], other_core).wait()

        def add(place, *others):
            total = g_ref[place].astype(F32)
            for other in others:
                total = total + other.astype(F32)
            return total

        if phase == 0:

            def sum_y(y):
                place = (b, y, slice(None), core)
                g_ref[place] = add(place, from_core[b, y]).astype(BF)

            pl.loop(0, 2)(sum_y)
            return
        mine = (b, y_at, z_at, core)
        if phase == LAST[kind]:
            others = [from_z[b, o] for o in range(3)] if kind == Y else [from_ys[b - 4]]
            dw_ref[b] = add(mine, *others)
            return
        every = slice(None)
        if kind == Y:
            sums_of = [((b, y_at, every, core), [from_y[b]])]
        elif kind == Z:
            sums_of = [((b, every, z_at, core), [from_zs[o] for o in range(3)])]
        elif phase == 1:
            far = odd_z if kind == EVEN else even_z
            sums_of = [((b, every, z, core), [from_h[b - 5, k]]) for k, z in enumerate((z_at, far))]
        else:
            sums_of = [((b, every, z_at, core), [from_h[b - 5, 2]])]
        for place, others in sums_of:
            g_ref[place] = add(place, *others).astype(BF)

    def dw_turn(group, phase):
        dw_finish(group, phase)
        dw_start(group, phase + 1)

    OUT_W, OUT_R, IN_W, IN_R = (0, Y, 1), (1, Y, 2), (2, EVEN, 5), (3, ODD, 6)
    ATTN_W, ATTN_R, CROSS = (4, Y, 0), (5, Z, 4), (6, Y, 3)

    def sm_copies(step, count):
        sems = (sm_send.at[step], sm_recv.at[step])
        if step == 0:
            return [moved(sums_t.at[me], sums_t.at[me], *sems, peer(o)) for o in range(1, TENSOR)]
        rows = pl.ds(0, count)
        src = sums.at[step - 1, rows]
        if step == 1:
            return [moved(src, sums_c.at[rows], *sems, other_core)]
        if step == 2:
            return [moved(src, sums_y.at[rows], *sems, other_y)]
        return [
            moved(src, sums_z.at[o - 1, rows], *sems, dp_device(y_at, z_next(o), core)) for o in (1, 2, 3)
        ]

    def sm_start(step, count=32):
        for copy in sm_copies(step, count):
            copy.start()

    def sm_wait(step, count=32):
        if step in (0, 3):
            place = sums_z.at[:, pl.ds(0, count)] if step == 3 else sums_t.at[pl.ds(0, TENSOR - 1)]
            moved(place, place, sm_send.at[step], sm_recv.at[step], other_core).wait()
        else:
            sm_copies(step, count)[0].wait()

    def small_norms():
        counts = jnp.logical_or(head, me < 2)
        for k in range(15):
            sums_t[me, k : k + 1, :] = jnp.where(counts, row_sums[k], 0.0)
        sums_t[me, 15:16, :] = jnp.zeros((1, D), F32)
        sm_start(0)

    def small_biases(count):
        sm_wait(0)
        total[...] = jnp.zeros((32, D), F32)
        norms = sums_t[0] + sums_t[1] + sums_t[2] + sums_t[3]
        total[0:12] = norms[:12]
        total[16:19] = norms[12:15]
        for mod in range(2):
            total[12 + mod : 13 + mod, :] = bsum[mod]
            total[14 + mod : 15 + mod, : 3 * HW] = bqsum[mod]
        total[19:20, : 3 * HW] = bqsum[2]
        sums[0] = total[...].astype(BF)
        sm_start(1, count)

    def small_y(count):
        sm_wait(1, count)
        total[:count] = total[:count] + sums_c[:count].astype(F32)
        sums[1] = total[...].astype(BF)
        sm_start(2, count)

    def small_z(count):
        sm_wait(2, count)
        total[:count] = total[:count] + sums_y[:count].astype(F32)
        sums[2] = total[...].astype(BF)
        sm_start(3, count)

    def small_last(count):
        sm_wait(3, count)
        for o in range(3):
            total[:count] = total[:count] + sums_z[o, :count].astype(F32)
        s_ref[...] = total[:24]

    def packet():
        return moved(pack.at[0], pack.at[1], pk_send, pk_recv, partner)

    def each(*steps, first=0, last=MB, after=()):
        def body(m):
            for step in steps:
                step(m)
            for k, extra in enumerate(after):
                if extra is not None:
                    pl.when(m == first + k)(extra)

        pl.loop(first, last)(body)

    def then(*steps):
        def run():
            for step in steps:
                step()

        return run

    def pair(step):
        pl.loop(0, 2)(step)

    @pl.when(head)
    def _():
        def to_partner(m):
            put_own_rows(midf, m, layer_d(m).astype(BF))
            mid_start(m)

        def from_partner(m):
            some_rows(midf, m, C, sec_send.at[m], sec_recv.at[m]).wait_send()
            back_arrive(m)
            back_e(m, own_rows_of(back, m).astype(F32))

        def last(m):
            ag_start(ybuf, m, (res[m] + rs_finish(m)).astype(BF), y_send, y_recv)

        front, rear = dict(first=0, last=2), dict(first=2, last=4)
        wait_weights(0, 1)
        each(
            layer_a,
            after=(
                None, then(p(pl.semaphore_wait, barrier, 12), p(rs_start, 0), p(rs_start, 1)),
                p(rs_start, 2),
            ),
        )
        each(layer_b, **front)
        rs_start(3)
        layer_b(2)
        wait_weights(2, 3)
        each(layer_c, **front)
        layer_b(3)
        layer_c(2)
        each(to_partner, **front)
        layer_c(3)
        each(to_partner, **rear)
        each(from_partner, last=3)
        each(back_f, after=(p(from_partner, 3), None, p(back_g, 0), p(back_g, 1)))
        ffn_piece(2)
        dw_start(IN_R, 0)
        ffn_piece(3)
        dw_start(OUT_R, 0)
        back_g(2)
        ffn_piece(0)
        dw_start(IN_W, 0)
        dw_turn(IN_R, 0)
        ffn_piece(1)
        dw_start(OUT_W, 0)
        dw_turn(OUT_R, 0)
        back_g(3)
        each(
            back_h,
            after=(
                then(p(dw_turn, IN_W, 0), p(dw_turn, OUT_W, 0)), small_norms,
            ),
        )
        attn_piece(2)
        attn_piece(3)
        dw_start(ATTN_R, 0)
        dw_turn(IN_R, 1)
        dw_turn(OUT_R, 1)
        attn_piece(0)
        dw_turn(ATTN_R, 0)
        attn_piece(1)
        dw_start(ATTN_W, 0)
        dw_turn(IN_W, 1)
        small_biases(16)
        each(last)
        dw_turn(ATTN_W, 0)
        small_y(16)
        dw_turn(OUT_W, 1)
        dw_turn(IN_R, 2)
        small_z(16)

    @pl.when(cross)
    def _():
        for copy in bias_copies():
            copy.start()
        gather_wait("x", CWQKV, CWO)
        gather_start("z", CWQKV, CWO)
        gather_wait("x", WQKV, WO)
        gather_start("y", WQKV)
        gather_start("z", WO)
        gather_wait("x", W1)
        gather_start("y", W1)
        gather_wait("y", WQKV)
        gather_start("z", WQKV)
        gather_wait("z", CWQKV, CWO)
        gather_start("core", CWQKV, CWO)
        gather_wait("z", WO)
        gather_start("y", WO)
        gather_wait("y", W1)
        gather_start("z", W1)
        gather_wait("x", W2)
        gather_start("y", W2)
        for copy in bias_copies():
            copy.wait()
        gather_wait("core", CWQKV, CWO)
        wait_weights(0, 1, 2, 3, 4, 5)
        pl.loop(0, 3)(mid_relay)

        @pl.when(set_of == 1)
        def _():
            gather_wait("y", WO)
            gather_wait("z", WQKV)
            gather_start("core", WQKV, WO)
            mid_relay(3)

        cross_forward(0)

        @pl.when(set_of == 0)
        def _():
            gather_wait("y", WO)
            gather_wait("z", WQKV)
            gather_start("core", WQKV, WO)
            mid_relay(3)

        cross_forward(1)
        gather_wait("core", WQKV, WO)
        attn_forward(0)
        gather_wait("z", W1)
        gather_start("core", W1)
        attn_forward(1)
        gather_wait("y", W2)
        gather_start("core", W2)
        pair(ffn_forward)
        pair(ffn_turn)
        pair(attn_backward)
        pair(cross_backward)
        pair(to_section_0)
        mate_wait(CMIXED, XLOW, MIXED, ALOW, ACT, DYF, DUP)
        pass_start(DYF)
        mate_start_all(DYC, CDQKV)
        ffn_piece(2)
        dw_start(IN_R, 0)
        ffn_piece(0)
        dw_start(IN_W, 0)
        dw_turn(IN_R, 0)
        dw_turn(IN_W, 0)
        pass_wait(DYF)
        pass_start(XLOW)
        ffn_piece(3)
        dw_start(OUT_R, 0)
        ffn_piece(1)
        dw_start(OUT_W, 0)
        dw_turn(OUT_R, 0)
        small_norms()
        for mod, (lo, hi) in enumerate(SPANS):
            bsum[mod] = column_sums(dup, lo, hi)
        dw_turn(OUT_W, 0)
        mate_wait(DYC)
        pass_start(DYC)
        mate_start_all(DYA, DQKV)
        for k in range(2):
            mid_finish(2 * (1 - set_of) + k)
        mate_wait(CDQKV)
        pass_wait(DYC)
        cross_outer()
        dw_start(CROSS, 0)
        bqsum[2] = column_sums(cdqkv, 0, R)
        dw_turn(CROSS, 0)
        mate_wait(DYA)
        pass_start(DYA)
        dw_turn(IN_R, 1)
        dw_turn(OUT_R, 1)
        dw_turn(IN_W, 1)
        dw_turn(OUT_W, 1)
        dw_turn(IN_R, 2)
        dw_turn(IN_W, 2)
        dw_turn(CROSS, 1)
        mate_wait(DQKV)
        mate_start_all(YBUF)
        pass_wait(XLOW)
        pass_wait(DYA)
        for mod, (lo, hi) in enumerate(SPANS):
            bqsum[mod] = column_sums(dqkv, lo, hi)
        small_biases(32)
        attn_piece(2)
        attn_piece(3)
        dw_start(ATTN_R, 0)
        small_y(32)
        attn_piece(0)
        attn_piece(1)
        dw_start(ATTN_W, 0)
        dw_turn(ATTN_R, 0)
        small_z(32)
        dw_turn(ATTN_W, 0)
        mate_wait(YBUF)
        pass_start(YBUF)
        dw_finish(CROSS, 2)
        pass_wait(YBUF)
        for j in range(2):
            rows = back.at[block_of(j), pl.ds(0, 2 * C)]
            moved(rows, rows, back_send.at[j], back_recv.at[0], partner).wait_send()

    def write(m):
        @pl.when(head)
        def _():
            ag_finish(ybuf, m, y_send, y_recv)

        y_ref[m] = ybuf[m]

    pl.when(head)(p(dw_turn, IN_W, 2))
    dw_turn(ATTN_R, 1)
    dw_turn(ATTN_W, 1)
    dw_finish(OUT_R, 2)
    dw_finish(IN_R, 3)
    dw_finish(IN_W, 3)
    dw_finish(OUT_W, 2)
    pl.when(head)(p(small_last, 16))
    pl.when(cross)(p(small_last, 32))
    each(write)

    @pl.when(cross)
    def _():
        pack[0, :24] = dw_ref[3, :24]
        pack[0, 24:] = s_ref[...]
        packet().start()
        dc_ref[...] = dw_ref[3, 24:]
        sc_ref[...] = s_ref[...]

    dw_finish(ATTN_W, 2)
    dw_finish(ATTN_R, 2)
    pl.when(cross)(lambda: packet().wait_send())

    @pl.when(head)
    def _():
        packet().wait_recv()
        dc_ref[...] = pack[1, :24]
        sc_ref[...] = pack[1, 24:]


def arrange(
    y_ref, dw_ref, s_ref, dc_ref, sc_ref,
    words, regions, qkv_g, qv_bias_g, out_g, in_g, b1_g, ffo_g, obias_g, gain_g, shift_g,
    cqkv_g, cqv_bias_g, cout_g, cobias_g, cgain_g, cshift_g,
):
    place = lax.axis_index("dp")
    both = lax.axis_index("section") * 16 + place

    def from_column(rows, column):
        return pltpu.roll(rows, lax.rem(D - column, D), 1)

    for ref, (lo, hi), length in zip((words, regions), SPANS, (WORDS, REGIONS)):
        padded = y_ref[:, lo:hi, :].reshape(MB * (hi - lo), D)
        rows = dot(spread(hi - lo, length, True), padded)
        ref[0] = rows.reshape(length, ITEMS_LOCAL, D)
    small = s_ref[...]
    for mod in range(2):
        attn = dw_ref[4 * mod]
        for j in range(3):
            qkv_g[0, mod, j] = attn[:, j * HW : (j + 1) * HW]
        out_g[0, mod] = attn[:, 3 * HW :]
        in_g[0, mod] = dw_ref[5 + mod]
        ffo_g[0, mod] = dw_ref[1 + mod]
    columns = from_column(small, 48 * place)[:, :48]
    for mod in range(2):
        for l in range(2):
            for k, ref in enumerate((gain_g, shift_g, obias_g)):
                at = 2 * (3 * l + k) + mod
                ref[0, mod, l : l + 1, :] = columns[at : at + 1]
    columns = from_column(small, 8 * place)
    for mod in range(2):
        for k in range(6):
            b1_g[0, k, mod : mod + 1, :] = columns[12 + mod : 13 + mod, 128 * k : 128 * k + 8]
    columns = from_column(small, 4 * place)
    for mod in range(2):
        for j in range(2):
            for h in range(LOCAL_HEADS):
                lo = 2 * j * HW + h * HEAD_DIM
                qv_bias_g[0, mod, h, j : j + 1, :] = columns[14 + mod : 15 + mod, lo : lo + 4]
    wide = dc_ref[...]
    for j in range(3):
        cqkv_g[j] = wide[:, j * HW : (j + 1) * HW]
    cout_g[...] = wide[:, 3 * HW :]
    small = sc_ref[...]
    columns = from_column(small, 24 * both)
    for k, ref in enumerate((cgain_g, cshift_g, cobias_g)):
        ref[...] = columns[16 + k, :24]
    columns = from_column(small, 2 * both)[19:20]
    for j in range(2):
        heads = []
        for h in range(LOCAL_HEADS):
            lo = 2 * j * HW + h * HEAD_DIM
            heads.append(columns[:, lo : lo + 2])
        cqv_bias_g[j] = jnp.concatenate(heads, axis=0).T


def local(
    words, regions, word_lengths, task_flags, attn_qkv, attn_qv_bias, attn_out, ffn_in, ffn_in_bias,
    ffn_out, out_bias, norm_gain, norm_bias, cross_qkv, cross_qv_bias, cross_out, cross_out_bias,
    cross_norm_gain, cross_norm_bias,
):
    inputs = (
        words.transpose(0, 2, 1, 3), regions.transpose(0, 2, 1, 3), word_lengths, task_flags,
        attn_qkv.transpose(0, 1, 3, 4, 2).reshape(2, 3 * HW, D), attn_qv_bias.transpose(0, 1, 3, 2, 4), attn_out[0],
        ffn_in[0], ffn_in_bias.transpose(0, 2, 1, 3), ffn_out[0], out_bias, norm_gain, norm_bias,
        cross_qkv.transpose(1, 2, 0).reshape(3 * HW, D), cross_qv_bias.transpose(1, 0, 2), cross_out,
        cross_out_bias, cross_norm_gain, cross_norm_bias,
    )

    vmem = pl.BlockSpec(memory_space=pltpu.VMEM)
    smem = pl.BlockSpec(memory_space=pltpu.SMEM)
    hbm = pl.BlockSpec(memory_space=pl.ANY)
    mb_rows = lambda width, dtype: pltpu.VMEM((MB, R, width), dtype)
    own_rows = lambda count: pltpu.VMEM((count, MB, C, D), F32)
    y, g, s, dc, sc = pl.pallas_call(
        kernel,
        out_shape=(
            jax.ShapeDtypeStruct((MB, R, D), BF),
            jax.ShapeDtypeStruct((7, 48, D), F32),
            jax.ShapeDtypeStruct((24, D), F32),
            jax.ShapeDtypeStruct((24, D), F32),
            jax.ShapeDtypeStruct((24, D), F32),
        ),
        in_specs=[smem if k in (2, 3) else hbm if k in (4, 6, 7, 9, 13, 15) else vmem for k in range(len(inputs))],
        out_specs=[vmem] * 5,
        scratch_shapes=[
            mb_rows(D, BF),
            pltpu.VMEM((3, 1, 3 * HW), F32),
            pltpu.VMEM((2, 1, D), F32),
            pltpu.VMEM((3, D), F32),
            mb_rows(D, BF),
            pltpu.VMEM((MB, TENSOR - 1, C, D), BF),
            *[mb_rows(D, BF) for _ in range(8)],
            pltpu.VMEM((3, MB, R, HW), BF),
            mb_rows(HW, BF),
            mb_rows(3 * HW, BF),
            pltpu.VMEM((3, MB, R, HW), BF),
            mb_rows(HW, BF),
            mb_rows(3 * HW, BF),
            mb_rows(D, BF),
            mb_rows(D, BF),
            mb_rows(D, F32),
            pltpu.VMEM((MB, 3 * RW, RW), F32),
            pltpu.VMEM((MB, 3 * RR, RR), F32),
            pltpu.VMEM((MB, 3 * RW, RR), F32),
            pltpu.VMEM((MB, 3 * RR, RW), F32),
            pltpu.VMEM((MB, C, D), F32),
            pltpu.VMEM((MB, C, D), F32),
            pltpu.VMEM((2, MB, C, D), F32),
            pltpu.VMEM((2, MB, C, 128), F32),
            pltpu.VMEM((MB, 16, D), BF),
            pltpu.VMEM((MB, 16, D), BF),
            pltpu.VMEM((C, D), F32),
            pltpu.VMEM((C, D), BF),
            pltpu.VMEM((2, 1, D), F32),
            pltpu.VMEM((3, 1, 3 * HW), F32),
            pltpu.VMEM((2, 3 * HW, D), BF),
            pltpu.VMEM((2, HW, D), BF),
            pltpu.VMEM((2, D, D), BF),
            pltpu.VMEM((2, D, D), BF),
            pltpu.VMEM((3 * HW, D), BF),
            pltpu.VMEM((HW, D), BF),
            pltpu.VMEM((2, 3 * HW, D), BF),
            pltpu.VMEM((2, HW, D), BF),
            pltpu.VMEM((2, D, D), BF),
            pltpu.VMEM((2, D, D), BF),
            pltpu.VMEM((3 * HW, D), BF),
            pltpu.VMEM((HW, D), BF),
            pltpu.VMEM((3, 1, 3 * HW), F32),
            pltpu.VMEM((2, 1, D), F32),
            pltpu.VMEM((2, 2, R, D), BF),
            pltpu.VMEM((2, 2, 16, D // 2), BF),
            pltpu.VMEM((2, 2, 2, 16, D // 2), BF),
            *[pltpu.VMEM((2, R, w), BF) for w in (D, D, HW, 3 * HW, HW, 3 * HW)],
            pltpu.VMEM((2, R, D), F32),
            pltpu.VMEM((2, R, D), F32),
            pltpu.VMEM((2, 2, R, D), F32),
            pltpu.VMEM((2, 2, R, 128), F32),
            pltpu.VMEM((16, 1, D), F32),
            pltpu.VMEM((7, 2, 4, 2, 48, D), BF),
            pltpu.VMEM((7, 2, 4, 48, D), BF),
            pltpu.VMEM((4, 4, 48, D), BF),
            pltpu.VMEM((3, 2, 48, D), BF),
            pltpu.VMEM((2, 3, 2, 48, D), BF),
            pltpu.VMEM((4, 3, 48, D), BF),
            pltpu.VMEM((3, 48, D), BF),
            pltpu.VMEM((3, 32, D), BF),
            pltpu.VMEM((32, D), F32),
            pltpu.VMEM((TENSOR, 16, D), F32),
            pltpu.VMEM((32, D), BF),
            pltpu.VMEM((32, D), BF),
            pltpu.VMEM((3, 32, D), BF),
            pltpu.VMEM((2, 48, D), F32),
            *[pltpu.SemaphoreType.DMA((MB,)) for _ in range(6)],
            pltpu.SemaphoreType.DMA((MB,)),
            pltpu.SemaphoreType.DMA((MB,)),
            pltpu.SemaphoreType.DMA((7, 4)),
            pltpu.SemaphoreType.DMA((7, 4)),
            pltpu.SemaphoreType.DMA((4,)),
            pltpu.SemaphoreType.DMA((4,)),
            pltpu.SemaphoreType.DMA,
            pltpu.SemaphoreType.DMA,
            pltpu.SemaphoreType.DMA((2,)),
            pltpu.SemaphoreType.DMA((MB,)),
            *[pltpu.SemaphoreType.DMA((2, 2, 4)) for _ in range(2)],
            *[pltpu.SemaphoreType.DMA((12,)) for _ in range(2)],
            *[pltpu.SemaphoreType.DMA((7, 4)) for _ in range(2)],
            *[pltpu.SemaphoreType.DMA((6,)) for _ in range(2)],
            pltpu.SemaphoreType.DMA((6,)),
        ],
        compiler_params=pltpu.CompilerParams(
            collective_id=0, has_side_effects=True, vmem_limit_bytes=63 * 2**20
        ),
    )(*inputs)

    shapes = (
        (1, WORDS, ITEMS_LOCAL, D), (1, REGIONS, ITEMS_LOCAL, D), (1, 2, 3, 48, HW),
        (1, 2, LOCAL_HEADS, 2, 4), (1, 2, 48, HW), (1, 2, 48, D), (1, 6, 2, 8), (1, 2, 48, D),
        (1, 2, 2, 48), (1, 2, 2, 48), (1, 2, 2, 48), (3, 24, HW), (2, 2, LOCAL_HEADS), (24, HW),
        (24,), (24,), (24,),
    )
    orders = {
        0: (0, 2, 1, 3), 1: (0, 2, 1, 3), 2: (0, 1, 3, 2, 4), 3: (0, 1, 3, 2, 4), 4: (0, 1, 3, 2),
        6: (0, 2, 1, 3), 7: (0, 1, 3, 2), 11: (1, 0, 2), 12: (0, 2, 1), 13: (1, 0),
    }
    outs = pl.pallas_call(
        arrange,
        out_shape=tuple(jax.ShapeDtypeStruct(shape, F32) for shape in shapes),
        in_specs=[vmem] * 5,
        out_specs=[vmem] * len(shapes),
        compiler_params=pltpu.CompilerParams(vmem_limit_bytes=60 * 2**20),
    )(y, g, s, dc, sc)
    return tuple(out.transpose(orders[k]) if k in orders else out for k, out in enumerate(outs))


def solution(mesh):
    in_specs = (
        P("section", "dp", None, None),
        P("section", "dp", None, None),
        P("dp"),
        P("dp"),
        P("section", None, None, None, "tensor"),
        P("section", None, None, "tensor", None),
        P("section", None, "tensor", None),
        P("section", None, None, "tensor"),
        P("section", None, "tensor", None),
        P("section", None, "tensor", None),
        P("section", None, None, None),
        P("section", None, None, None),
        P("section", None, None, None),
        P(None, None, "tensor"),
        P(None, "tensor", None),
        P("tensor", None),
        P(),
        P(),
        P(),
    )
    out_specs = (
        P("section", "dp", None, None),
        P("section", "dp", None, None),
        P("section", None, "dp", None, "tensor"),
        P("section", None, None, "tensor", "dp"),
        P("section", None, "tensor", "dp"),
        P("section", None, "dp", "tensor"),
        P("section", None, "tensor", "dp"),
        P("section", None, "tensor", "dp"),
        P("section", None, None, "dp"),
        P("section", None, None, "dp"),
        P("section", None, None, "dp"),
        P(("section", "dp"), None, "tensor"),
        P(None, "tensor", ("section", "dp")),
        P("tensor", ("section", "dp")),
        P(("section", "dp")),
        P(("section", "dp")),
        P(("section", "dp")),
    )
    return jax.shard_map(local, mesh=mesh, in_specs=in_specs, out_specs=out_specs, check_vma=False)
```

```python
import functools

import jax
import jax.numpy as jnp
from jax import lax
from jax.experimental import pallas as pl
from jax.experimental.pallas import tpu as pltpu
from jax.sharding import PartitionSpec as P

MESH = pl.DeviceIdType.MESH
BF = jnp.bfloat16
F32 = jnp.float32
HEAD_DIM = 64
LOCAL_HEADS = 3
HW = HEAD_DIM * LOCAL_HEADS
WORDS = 20
REGIONS = 36
D = 768
ITEMS_LOCAL = 8
TENSOR = 4

ITEMS_MB = 2
MB = ITEMS_LOCAL // ITEMS_MB
RW = 48
RR = 80
R = RW + RR
C = R // TENSOR
SPANS = ((0, RW), (RW, R))

EPSILON = 1e-06
MASKED = -1000000000.0
SCALING = HEAD_DIM ** (-0.5)


def dot(a, b):
    return lax.dot_general(a, b, (((1,), (0,)), ((), ())), preferred_element_type=F32)


def dot_nt(a, b):
    return lax.dot_general(a, b, (((1,), (1,)), ((), ())), preferred_element_type=F32)


def dot_tn(a, b):
    return lax.dot_general(a, b, (((0,), (0,)), ((), ())), preferred_element_type=F32)


def head_masks():
    lane = lax.broadcasted_iota(jnp.int32, (1, HW), 1)
    return [
        ((lane >= h * HEAD_DIM) & (lane < (h + 1) * HEAD_DIM)).astype(F32) for h in range(LOCAL_HEADS)
    ]


def by_head(a):
    masks = [m.astype(BF) for m in head_masks()]
    return jnp.concatenate([a * m for m in masks], axis=0)


def join_heads(stacked):
    rows = stacked.shape[0] // LOCAL_HEADS
    masks = head_masks()
    total = stacked[:rows] * masks[0]
    for h in range(1, LOCAL_HEADS):
        total = total + stacked[h * rows : (h + 1) * rows] * masks[h]
    return total


def item_of(shape, axis, length):
    index = lax.broadcasted_iota(jnp.int32, shape, axis)
    item = jnp.zeros(shape, jnp.int32)
    for k in range(1, ITEMS_MB + 1):
        item = item + (index >= k * length).astype(jnp.int32)
    return item


def spread(rows, length, transposed=False):
    count = ITEMS_LOCAL * length
    shape = (count, MB * rows) if transposed else (MB * rows, count)
    at = lax.broadcasted_iota(jnp.int32, shape, 0 if transposed else 1)
    padded = lax.broadcasted_iota(jnp.int32, shape, 1 if transposed else 0)
    item, position = at & (ITEMS_LOCAL - 1), at >> 3
    block, within = item >> (ITEMS_MB.bit_length() - 1), item & (ITEMS_MB - 1)
    target = block * rows + within * length + position
    return (target == padded).astype(F32).astype(BF)


def key_mask(q_rows, q_len, k_rows, k_len, lengths=None):
    shape = (q_rows, k_rows)
    item = item_of(shape, 1, k_len)
    key = lax.broadcasted_iota(jnp.int32, shape, 1)
    mask = (item_of(shape, 0, q_len) == item) & (key < ITEMS_MB * k_len)
    if lengths is not None:
        for k, length in enumerate(lengths):
            mask = mask & ((item != k) | (key < k * k_len + length))
    return mask


def attend(cases):
    masks = [jnp.concatenate([mask] * LOCAL_HEADS, axis=0) for _, _, _, mask in cases]
    scores = [dot_nt(by_head(q), k) * SCALING for q, k, _, _ in cases]
    scores = [jnp.where(mask, score, MASKED) for mask, score in zip(masks, scores)]
    es = [jnp.exp(score - jnp.max(score, axis=-1, keepdims=True)) for score in scores]
    probs = [e / jnp.sum(e, axis=-1, keepdims=True) for e in es]
    mixed = [dot(p.astype(BF), v) for p, (_, _, v, _) in zip(probs, cases)]
    return [(p, join_heads(mix).astype(BF)) for p, mix in zip(probs, mixed)]


def attend_back(cases):
    d3s = [by_head(dmix) for dmix, _, _, _, _ in cases]
    dps = [dot_nt(d3, v) for d3, (_, _, _, _, v) in zip(d3s, cases)]
    dss = [
        (probs * (dp - jnp.sum(probs * dp, axis=-1, keepdims=True))).astype(BF)
        for dp, (_, probs, _, _, _) in zip(dps, cases)
    ]
    dqs = [dot(ds, k) for ds, (_, _, _, k, _) in zip(dss, cases)]
    dks = [dot_tn(ds, by_head(q)) for ds, (_, _, q, _, _) in zip(dss, cases)]
    dvs = [dot_tn(probs.astype(BF), d3) for d3, (_, probs, _, _, _) in zip(d3s, cases)]
    return [
        ((join_heads(dq) * SCALING).astype(BF), (dk * SCALING).astype(BF), dv.astype(BF))
        for dq, dk, dv in zip(dqs, dks, dvs)
    ]


def split_qkv(out):
    return out[:, :HW], out[:, HW : 2 * HW], out[:, 2 * HW :]


def gelu(up):
    cdf = 0.5 * (1.0 + lax.erf(up * (0.5**0.5)))
    return (up * cdf).astype(BF), cdf + up * jnp.exp(-0.5 * up * up) * 0.3989422804014327


def norm_forward(r, gain, shift):
    center = r - jnp.mean(r, axis=-1, keepdims=True)
    spread = jnp.mean(center * center, axis=-1, keepdims=True)
    rstd = lax.rsqrt(spread + EPSILON)
    n = center * rstd
    return n, rstd, n * gain + shift


def norm_back(dh, n, rstd, gain):
    dn = dh * gain
    return rstd * (
        dn - jnp.mean(dn, axis=-1, keepdims=True) - n * jnp.mean(dn * n, axis=-1, keepdims=True)
    )


def kernel(
    words_ref, regions_ref, lengths_ref, flags_ref, wqkv_in, qv_bias_ref, wo_in, w1_in, b1_in_ref,
    w2_in, out_bias_ref, gain_ref, shift_ref, cwqkv_in, cqv_bias_ref, cwo_in, cout_bias_ref,
    cgain_ref, cshift_ref,
    y_out, dw_out, s_ref, dc_ref, sc_ref,
    dw_ref, out_sems, x_ref, bqkv_ref, b1_ref, cvec_ref, send, recv, xlow, midf, alow, dyf, dya, dyc, ybuf, back,
    qkv, mixed, dqkv, cqkv, cmixed, cdqkv, act, dup, dgelu,
    p_w, p_r, cp_w, cp_r, cur, res, nrm, rstd, packed, gathered_end, total_ref, low_ref, bsum, bqsum,
    wqkv_ref, wo_ref, w1_ref, w2_ref, cwqkv_ref, cwo_ref, wqkv_m, wo_m, w1_m, w2_m, cwqkv_m, cwo_m, bqkv_m, b1_m,
    got, tails, got_tails, act_m, dup_m, mixed_m, dqkv_m, cmixed_m, cdqkv_m, cur_f, res_f, nrm_f, rstd_f, row_sums,
    g_ref, from_core, from_y, from_zs, from_h, from_z, from_ys, sums, total, sums_t, sums_c, sums_y, sums_z, pack,
    rs_send, rs_recv, ag_send, ag_recv, y_send, y_recv, sec_send, sec_recv,
    dw_send, dw_recv, sm_send, sm_recv, pk_send, pk_recv,
    back_send, back_recv, ar_send, ar_recv, mt_send, mt_recv, ga_send, ga_recv, ps_send, ps_recv, loads,
):
    p = functools.partial
    sec = lax.axis_index("section")
    me = lax.axis_index("tensor")
    head = sec == 0
    cross = sec == 1

    def peer(o):
        return {"tensor": lax.rem(me + o, TENSOR)}

    partner = {"section": 1 - sec}
    place = lax.axis_index("dp")
    y_at, z_at, core = place // 8, lax.rem(place // 2, 4), lax.rem(place, 2)

    def dp_device(y, z, c):
        return {"dp": (y * 4 + z) * 2 + c}

    other_core = dp_device(y_at, z_at, 1 - core)
    other_y = dp_device(1 - y_at, z_at, core)

    def z_next(o):
        return lax.rem(z_at + o, 4)

    weights = tuple(
        pltpu.make_async_copy(src, dst, loads.at[k])
        for k, (src, dst) in enumerate((
            (wqkv_in, wqkv_ref), (wo_in, wo_ref), (w1_in, w1_ref), (w2_in, w2_ref),
            (cwqkv_in, cwqkv_ref), (cwo_in, cwo_ref),
        ))
    )

    def load_weights(*which):
        for k in which:
            weights[k].start()

    def wait_weights(*which):
        for k in which:
            weights[k].wait()

    barrier = pltpu.get_barrier_semaphore()
    for o in range(1, TENSOR):
        pl.semaphore_signal(barrier, inc=1, device_id=peer(o), device_id_type=MESH)
    mate, halver = {"tensor": me + 1 - 2 * lax.rem(me, 2)}, {"tensor": 3 - me}
    set_of = lax.rem((me + 1) // 2, 2)
    for t in range(TENSOR):
        pl.semaphore_signal(
            barrier, inc=1, device_id={"section": 1 - sec, "tensor": t}, device_id_type=MESH
        )
    for device in (other_core, other_y, *(dp_device(y_at, z_next(o), core) for o in (1, 2, 3))):
        pl.semaphore_signal(barrier, inc=1, device_id=device, device_id_type=MESH)

    load_weights(0, 1, 2, 3)
    pl.when(cross)(lambda: load_weights(4, 5))

    def moved(src, dst, send_sem, recv_sem, device):
        return pltpu.make_async_remote_copy(
            src_ref=src, dst_ref=dst, send_sem=send_sem, recv_sem=recv_sem, device_id=device,
            device_id_type=MESH,
        )

    both_mods = slice(0, 2)
    half_columns = pl.ds(pl.multiple_of(core * (D // 2), D // 2), D // 2)

    def z_rows(z, count):
        return pl.ds(pl.multiple_of(z * count, count), count)

    gathered = (
        (cwqkv_in, cwqkv_m, 3 * HW // 4, False), (cwo_in, cwo_m, HW // 4, False),
        (wqkv_in, wqkv_m, 3 * HW // 4, True), (wo_in, wo_m, HW // 4, True),
        (w1_in, w1_m, D // 4, True), (w2_in, w2_m, D // 4, True),
    )
    CWQKV, CWO, WQKV, WO, W1, W2 = range(6)
    Y_FIRST = (WQKV, W1)

    def gather_copies(k, step):
        src, dst, count, by_mod = gathered[k]
        sems = lambda i: (ga_send.at[k, i], ga_recv.at[k, i])
        at = lambda mods, rows: (mods, rows, half_columns) if by_mod else (rows, half_columns)
        mine = at(y_at, z_rows(z_at, count))
        column = at(y_at, slice(0, 4 * count)) if by_mod else None
        if step == "x":
            part = column if k == W2 else mine
            return [moved(src.at[part], dst.at[part], *sems(0), mate)]
        if step == "y":
            place = dst.at[mine] if k in Y_FIRST else dst.at[column]
            return [moved(place, place, *sems(1), other_y)]
        if step == "z":
            place = dst.at[at(both_mods if k in Y_FIRST else y_at, z_rows(z_at, count))]
            return [
                moved(place, place, *sems(2), dp_device(y_at, z_next(o), core)) for o in (1, 2, 3)
            ]
        place = dst.at[at(both_mods, slice(0, 4 * count))]
        return [moved(place, place, *sems(3), other_core)]

    def gather_start(step, *arrays):
        for k in arrays:
            for copy in gather_copies(k, step):
                copy.start()

    def gather_wait(step, *arrays):
        for k in arrays:
            if step != "z":
                gather_copies(k, step)[0].wait()
                continue
            _, dst, count, by_mod = gathered[k]
            rows = slice(0, 3 * count)
            mods = both_mods if k in Y_FIRST else y_at
            place = dst.at[(mods, rows, half_columns) if by_mod else (rows, half_columns)]
            moved(place, place, ga_send.at[k, 2], ga_recv.at[k, 2], mate).wait()

    @pl.when(cross)
    def _():
        pl.semaphore_wait(barrier, 12)
        gather_start("x", CWQKV, CWO, WQKV, WO, W1)

    def side_by_side(rows):
        return jnp.concatenate(rows, axis=1)

    for mod in range(2):
        b1_ref[mod] = side_by_side(
            [b1_in_ref[0, k, mod : mod + 1, :] for k in range(D // 128)]
        )
    for k, ref in enumerate((qv_bias_ref.at[0, 0], qv_bias_ref.at[0, 1], cqv_bias_ref)):
        heads = lambda j: [ref[h, j : j + 1, :] for h in range(LOCAL_HEADS)]
        bqkv_ref[k] = side_by_side([*heads(0), jnp.zeros((1, HW), F32), *heads(1)])
    for k, ref in enumerate((cout_bias_ref, cgain_ref, cshift_ref)):
        cvec_ref[k : k + 1, :] = ref[...].reshape(1, D)

    for ref, (lo, hi), length in zip((words_ref, regions_ref), SPANS, (WORDS, REGIONS)):
        given = ref[0].astype(F32).reshape(ITEMS_LOCAL * length, D).astype(BF)
        placed = dot(spread(hi - lo, length), given).astype(BF)
        x_ref[:, lo:hi, :] = placed.reshape(MB, hi - lo, D)
    bsum[...] = jnp.zeros_like(bsum)
    bqsum[...] = jnp.zeros_like(bqsum)
    row_sums[...] = jnp.zeros_like(row_sums)


    def place_of(t, m):
        return lax.rem(t + m, TENSOR)

    def rows_at(at):
        return pl.ds(pl.multiple_of(48 * at - 16 * (at // 2), 16), C)

    def by_place(at, heavy, light):
        pl.when(at != 3)(heavy)
        pl.when(at == 3)(light)

    WORD_END, REGION_END = pl.ds(32, 16), pl.ds(112, 16)
    no_rows = jnp.zeros((8, D), F32)

    def pack_rows(words_end, regions_end):
        return jnp.concatenate([words_end, regions_end], axis=0).astype(BF)

    def wait_rows(m, ss, rs, sent, received):
        out, come = send.at[m, pl.ds(0, sent)], send.at[m, pl.ds(0, received)]
        moved(out, out, ss.at[m], rs.at[m], peer(1)).wait_send()
        moved(come, come, ss.at[m], rs.at[m], peer(1)).wait_recv()

    def own_rows_of(ref, m):
        at = place_of(me, m)

        def heavy():
            low_ref[...] = ref[m, rows_at(at)]

        def light():
            low_ref[0:16] = ref[m, WORD_END]
            low_ref[16:32] = ref[m, REGION_END]

        by_place(at, heavy, light)
        return low_ref[...]

    def put_own_rows(ref, m, low):
        at = place_of(me, m)

        def heavy():
            ref[m, rows_at(at)] = low

        def light():
            ref[m, WORD_END] = low[:16]
            ref[m, REGION_END] = low[16:]

        by_place(at, heavy, light)

    def put_parts(m, parts):
        for (lo, hi), part in zip(SPANS, parts):
            send[m, lo:hi] = part.astype(BF)
        packed[m] = pack_rows(parts[0][32:40], parts[1][64:72])

    def rs_start(m):
        for o in range(1, TENSOR):
            at = place_of(me + o, m)

            def heavy(o=o, at=at):
                src, dst = send.at[m, rows_at(at)], recv.at[m, o - 1]
                moved(src, dst, rs_send.at[m], rs_recv.at[m], peer(o)).start()

            def light(o=o):
                src, dst = packed.at[m], recv.at[m, o - 1, pl.ds(0, 16)]
                moved(src, dst, rs_send.at[m], rs_recv.at[m], peer(o)).start()

            by_place(at, heavy, light)

    def rs_finish(m):
        at = place_of(me, m)

        def heavy():
            wait_rows(m, rs_send, rs_recv, 80, 96)
            total = send[m, rows_at(at)].astype(F32)
            for o in range(TENSOR - 1):
                total = total + recv[m, o].astype(F32)
            total_ref[...] = total

        def light():
            wait_rows(m, rs_send, rs_recv, 96, 48)
            total = packed[m].astype(F32)
            for o in range(TENSOR - 1):
                total = total + recv[m, o, 0:16].astype(F32)
            total_ref[...] = jnp.concatenate([total[:8], no_rows, total[8:], no_rows], axis=0)

        by_place(at, heavy, light)
        return total_ref[...]

    def ag_start(buf, m, low, ss=ag_send, rs=ag_recv):
        put_own_rows(buf, m, low)
        at = place_of(me, m)

        def heavy():
            rows = buf.at[m, rows_at(at)]
            for o in range(1, TENSOR):
                moved(rows, rows, ss.at[m], rs.at[m], peer(o)).start()

        def light():
            wide = low.astype(F32)
            gathered_end[m] = pack_rows(wide[:8], wide[16:24])
            for o in range(1, TENSOR):
                end = gathered_end.at[m]
                moved(end, end, ss.at[m], rs.at[m], peer(o)).start()

        by_place(at, heavy, light)

    def ag_finish(buf, m, ss=ag_send, rs=ag_recv):
        def heavy():
            wait_rows(m, ss, rs, 96, 80)
            end = gathered_end[m].astype(F32)
            buf[m, WORD_END] = pack_rows(end[:8], no_rows)
            buf[m, REGION_END] = pack_rows(end[8:], no_rows)

        def light():
            wait_rows(m, ss, rs, 48, 96)

        by_place(place_of(me, m), heavy, light)

    def start_rows(ref, m, at, ss, rs, *devices):
        def heavy():
            rows = ref.at[m, rows_at(at)]
            for device in devices:
                moved(rows, rows, ss, rs, device).start()

        def light():
            for end in (WORD_END, REGION_END):
                rows = ref.at[m, end]
                for device in devices:
                    moved(rows, rows, ss, rs, device).start()

        by_place(at, heavy, light)

    def some_rows(ref, m, count, ss, rs):
        rows = ref.at[m, pl.ds(0, count)]
        return moved(rows, rows, ss, rs, partner)

    def mid_start(m):
        start_rows(midf, m, place_of(me, m), sec_send.at[m], sec_recv.at[m], partner)

    def mid_relay(m):
        some_rows(midf, m, C, sec_send.at[m], sec_recv.at[m]).wait_recv()
        start_rows(midf, m, place_of(me, m), ag_send.at[m], ag_recv.at[m], peer(1), peer(2), peer(3))

    def mid_finish(m):
        some_rows(midf, m, 3 * C, ag_send.at[m], ag_recv.at[m]).wait()

    def back_start(j):
        m = 2 * set_of + j
        for k in range(2):
            t = 2 * (me // 2) + k
            device = {"section": 1 - sec, "tensor": t}
            start_rows(back, m, place_of(t, m), back_send.at[j], back_recv.at[m], device)

    def back_arrive(m):
        some_rows(back, m, C, back_send.at[0], back_recv.at[m]).wait_recv()

    def save_norm(l, m, n, r):
        nrm[l, m] = n
        rstd[l, m] = jnp.broadcast_to(r, (C, 128))

    def own_words(m):
        at = place_of(me, m)
        count = jnp.where(at == 0, C, jnp.where(at == 3, C // 2, 0))
        return lax.broadcasted_iota(jnp.int32, (C, 1), 0) < count

    def own_param(ref, l, m):
        return jnp.where(own_words(m), ref[0, 0, l : l + 1, :], ref[0, 1, l : l + 1, :])

    def norm_step_back(l, m, dh):
        n = nrm[l, m]
        dr = norm_back(dh, n, rstd[l, m][:, :1], own_param(gain_ref, l, m))
        low = dr.astype(BF)
        words_only = own_words(m)
        for k, value in enumerate((dh * n, dh, low.astype(F32))):
            part = jnp.where(words_only, value, 0.0)
            at = 2 * (3 * l + k)
            row_sums[at] += jnp.sum(part, axis=0, keepdims=True)
            row_sums[at + 1] += jnp.sum(value - part, axis=0, keepdims=True)
        res[m] = dr
        return low

    def word_keys(m, q_rows, q_len):
        return key_mask(
            q_rows, q_len, RW, WORDS, [lengths_ref[ITEMS_MB * m + k] for k in range(ITEMS_MB)]
        )

    def region_keys(q_rows, q_len):
        return key_mask(q_rows, q_len, RR, REGIONS)

    def layer_a(m):
        xlow[m] = x_ref[m]
        cur[m] = own_rows_of(x_ref, m).astype(F32)
        outs = [
            (dot_nt(xlow[m, lo:hi], wqkv_ref[mod]) + bqkv_ref[mod]).astype(BF)
            for mod, (lo, hi) in enumerate(SPANS)
        ]
        for (lo, hi), out in zip(SPANS, outs):
            for k, part in enumerate(split_qkv(out)):
                qkv[k, m, lo:hi] = part
        masks = (word_keys(m, RW, WORDS), region_keys(RR, REGIONS))
        done = attend([(*split_qkv(out), mask) for out, mask in zip(outs, masks)])
        for (lo, hi), keep, (probs, mix) in zip(SPANS, (p_w, p_r), done):
            keep[m] = probs
            mixed[m, lo:hi] = mix
        put_parts(m, [dot(mix, wo_ref[mod]) for mod, (_, mix) in enumerate(done)])

    def layer_b(m):
        r = cur[m] + rs_finish(m) + own_param(out_bias_ref, 0, m)
        n, rs, h = norm_forward(r, own_param(gain_ref, 0, m), own_param(shift_ref, 0, m))
        save_norm(0, m, n, rs)
        cur[m] = h
        ag_start(alow, m, h.astype(BF))

    def layer_c(m):
        ag_finish(alow, m)
        ups = [dot(alow[m, lo:hi], w1_ref[mod]) + b1_ref[mod] for mod, (lo, hi) in enumerate(SPANS)]
        pairs = [gelu(up) for up in ups]
        put_parts(m, [dot(active, w2_ref[mod]) for mod, (active, _) in enumerate(pairs)])
        rs_start(m)
        for (lo, hi), (active, slope) in zip(SPANS, pairs):
            act[m, lo:hi] = active
            dgelu[m, lo:hi] = slope

    def layer_d(m):
        r = cur[m] + rs_finish(m) + own_param(out_bias_ref, 1, m)
        n, rs, h = norm_forward(r, own_param(gain_ref, 1, m), own_param(shift_ref, 1, m))
        save_norm(1, m, n, rs)
        return h

    def back_e(m, dh):
        ag_start(dyf, m, norm_step_back(1, m, dh))

    def back_f(m):
        ag_finish(dyf, m)
        dacts = [dot_nt(dyf[m, lo:hi], w2_ref[mod]) for mod, (lo, hi) in enumerate(SPANS)]
        ds = [(dact * dgelu[m, lo:hi]).astype(BF) for dact, (lo, hi) in zip(dacts, SPANS)]
        put_parts(m, [dot_nt(d, w1_ref[mod]) for mod, d in enumerate(ds)])
        rs_start(m)
        for mod, (lo, hi) in enumerate(SPANS):
            dup[m, lo:hi] = ds[mod]
            bsum[mod] += jnp.sum(ds[mod].astype(F32), axis=0, keepdims=True)

    def back_g(m):
        dh = res[m] + rs_finish(m)
        ag_start(dya, m, norm_step_back(0, m, dh))

    def back_h(m):
        ag_finish(dya, m)
        dmixs = [
            dot_nt(dya[m, lo:hi], wo_ref[mod]).astype(BF) for mod, (lo, hi) in enumerate(SPANS)
        ]
        grads = attend_back([
            (dmix, keep[m], *(qkv[k, m, lo:hi] for k in range(3)))
            for dmix, keep, (lo, hi) in zip(dmixs, (p_w, p_r), SPANS)
        ])
        ds = [jnp.concatenate(grad, axis=1) for grad in grads]
        put_parts(m, [dot(d, wqkv_ref[mod]) for mod, d in enumerate(ds)])
        rs_start(m)
        for mod, (lo, hi) in enumerate(SPANS):
            dqkv[m, lo:hi] = ds[mod]
            bqsum[mod] += jnp.sum(ds[mod].astype(F32), axis=0, keepdims=True)

    def block_of(j):
        return 2 * set_of + j

    def ar_copies(j, mod, turn):
        lo, hi = SPANS[mod]
        rows = slice(lo, hi - 16)
        sems = lambda k: (ar_send.at[turn, j, 2 * mod + k], ar_recv.at[turn, j, 2 * mod + k])
        return [
            moved(send.at[j, rows], got.at[turn, j, rows], *sems(0), halver),
            moved(tails.at[j, mod], got_tails.at[turn, j, mod], *sems(1), halver),
        ]

    def ar_start(j, mod, turn, part):
        lo, hi = SPANS[mod]
        full = hi - lo - 16
        send[j, lo : hi - 16] = part[:full].astype(BF)
        tail = part[full : full + 8]
        tails[j, mod] = jnp.concatenate([tail[:, : D // 2], tail[:, D // 2 :]], axis=0).astype(BF)
        for copy in ar_copies(j, mod, turn):
            copy.start()

    def ar_finish(j, mod, turn):
        lo, hi = SPANS[mod]
        for copy in ar_copies(j, mod, turn):
            copy.wait()
        rows = send[j, lo : hi - 16].astype(F32) + got[turn, j, lo : hi - 16].astype(F32)
        tail = tails[j, mod].astype(F32) + got_tails[turn, j, mod].astype(F32)
        return jnp.concatenate([rows, jnp.concatenate([tail[:8], tail[8:]], axis=1), no_rows], axis=0)

    shared = (xlow, alow, dyf, dya, dyc, ybuf)
    for_mate = ((act_m, act), (dup_m, dup), (mixed_m, mixed), (dqkv_m, dqkv), (cmixed_m, cmixed), (cdqkv_m, cdqkv))
    XLOW, ALOW, DYF, DYA, DYC, YBUF, ACT, DUP, MIXED, DQKV, CMIXED, CDQKV = range(12)

    halves = (XLOW, DYF, DYA, DYC, YBUF)

    def half_rows(which):
        return pl.ds(pl.multiple_of(which * (R // 2), R // 2), R // 2)

    def mate_copy(k, j):
        if k < 6:
            src = dst = shared[k]
            src = src.at[block_of(j)]
        else:
            src, dst = for_mate[k - 6]
            src = src.at[j]
        dst = dst.at[block_of(j)]
        if k in halves:
            src, dst = src.at[half_rows(me // 2)], dst.at[half_rows(me // 2)]
        return moved(src, dst, mt_send.at[k], mt_recv.at[k], mate)

    def mate_start(j, *kinds):
        for k in kinds:
            mate_copy(k, j).start()

    def mate_start_all(*kinds):
        for k in kinds:
            for j in range(2):
                mate_copy(k, j).start()

    def mate_wait(*kinds):
        for k in kinds:
            place = (shared[k] if k < 6 else for_mate[k - 6][1]).at[pl.ds(2 * (1 - set_of), 2)]
            if k in halves:
                place = place.at[:, half_rows(me // 2)]
            moved(place, place, mt_send.at[k], mt_recv.at[k], mate).wait()

    def pass_copy(k):
        place = shared[k].at[pl.ds(2 * (1 - set_of), 2), half_rows(me // 2)]
        return moved(place, place, ps_send.at[k], ps_recv.at[k], halver)

    def pass_start(k):
        pass_copy(k).start()

    def pass_wait(k):
        pass_copy(k).wait()

    def bias_copies():
        return [
            moved(bqkv_ref, bqkv_m, ga_send.at[6, 0], ga_recv.at[6, 0], mate),
            moved(b1_ref, b1_m, ga_send.at[6, 1], ga_recv.at[6, 1], mate),
        ]

    def save_norm_f(l, j, lo, hi, n, r):
        nrm_f[l, j, lo:hi] = n
        rstd_f[l, j, lo:hi] = jnp.broadcast_to(r, (hi - lo, 128))

    def count_rows(l, mod, dh, n, low):
        for k, value in enumerate((dh * n, dh, low.astype(F32))):
            at = 12 + k if l == 2 else 2 * (3 * l + k) + mod
            row_sums[at] += jnp.sum(value, axis=0, keepdims=True)

    def cross_forward(j):
        m = block_of(j)
        mid_finish(m)
        mid = midf[m]
        shards = ((cwqkv_ref, bqkv_ref, cwo_ref, cmixed, m), (cwqkv_m, bqkv_m, cwo_m, cmixed_m, j))
        qkvs = []
        for sh, (w, bias, w_out, keep, at) in enumerate(shards):
            out = (dot_nt(mid, w[...]) + bias[2]).astype(BF)
            q, k, v = split_qkv(out)
            cqkv[0, 2 * sh + j], cqkv[1, 2 * sh + j], cqkv[2, 2 * sh + j] = q, k, v
            qkvs.append((q, k, v))
        for mod, (lo, hi) in enumerate(SPANS):
            others = slice(*SPANS[1 - mod])
            mask = region_keys(RW, WORDS) if mod == 0 else word_keys(m, RR, REGIONS)
            done = attend([(q[lo:hi], k[others], v[others], mask) for q, k, v in qkvs])
            part = None
            for sh, (w, bias, w_out, keep, at) in enumerate(shards):
                probs, mix = done[sh]
                (cp_w, cp_r)[mod][2 * sh + j] = probs
                keep[at, lo:hi] = mix
                one = dot(mix, w_out[...])
                part = one if part is None else part + one
            ar_start(j, mod, 0, part)
        mate_start(j, CMIXED)

    def attn_forward(j):
        m = block_of(j)
        shards = (
            (wqkv_ref, bqkv_ref, wo_ref, mixed, m), (wqkv_m, bqkv_m, wo_m, mixed_m, j),
        )
        for mod, (lo, hi) in enumerate(SPANS):
            r = midf[m, lo:hi].astype(F32) + ar_finish(j, mod, 0) + cvec_ref[0:1, :]
            n, rs, h = norm_forward(r, cvec_ref[1:2, :], cvec_ref[2:3, :])
            save_norm_f(1, j, lo, hi, n, rs)
            cur_f[j, lo:hi] = h
            low = h.astype(BF)
            xlow[m, lo:hi] = low
            outs = [(dot_nt(low, w[mod]) + bias[mod]).astype(BF) for w, bias, _, _, _ in shards]
            for sh, out in enumerate(outs):
                for k, part in enumerate(split_qkv(out)):
                    qkv[k, 2 * sh + j, lo:hi] = part
            mask = word_keys(m, RW, WORDS) if mod == 0 else region_keys(RR, REGIONS)
            done = attend([(*split_qkv(out), mask) for out in outs])
            part = None
            for sh, (w, bias, w_out, keep, at) in enumerate(shards):
                probs, mix = done[sh]
                (p_w, p_r)[mod][2 * sh + j] = probs
                keep[at, lo:hi] = mix
                one = dot(mix, w_out[mod])
                part = one if part is None else part + one
            ar_start(j, mod, 1, part)
        mate_start(j, XLOW, MIXED)

    def ffn_forward(j):
        m = block_of(j)
        shards = ((w1_ref, b1_ref, w2_ref, act, m), (w1_m, b1_m, w2_m, act_m, j))
        for mod, (lo, hi) in enumerate(SPANS):
            r = cur_f[j, lo:hi] + ar_finish(j, mod, 1) + out_bias_ref[0, mod, 0:1, :]
            n, rs, h = norm_forward(r, gain_ref[0, mod, 0:1, :], shift_ref[0, mod, 0:1, :])
            save_norm_f(0, j, lo, hi, n, rs)
            cur_f[j, lo:hi] = h
            low = h.astype(BF)
            alow[m, lo:hi] = low
            if mod == 0:
                pl.when(j == 0)(lambda: gather_wait("core", W1))
            ups = [dot(low, w[mod]) + bias[mod] for w, bias, _, _, _ in shards]
            pairs = [gelu(up) for up in ups]
            for sh, (_, _, _, keep, at) in enumerate(shards):
                keep[at, lo:hi], dgelu[2 * sh + j, lo:hi] = pairs[sh]
            if mod == 0:
                pl.when(j == 0)(lambda: gather_wait("core", W2))
            ones = [dot(active, w_out[mod]) for (active, _), (_, _, w_out, _, _) in zip(pairs, shards)]
            part = ones[0] + ones[1]
            ar_start(j, mod, 0, part)
        mate_start(j, ALOW, ACT)

    def ffn_turn(j):
        m = block_of(j)
        shards = ((w1_ref, w2_ref, dup, m), (w1_m, w2_m, dup_m, j))
        for mod, (lo, hi) in enumerate(SPANS):
            r = cur_f[j, lo:hi] + ar_finish(j, mod, 0) + out_bias_ref[0, mod, 1:2, :]
            gain = gain_ref[0, mod, 1:2, :]
            n, rs, h = norm_forward(r, gain, shift_ref[0, mod, 1:2, :])
            ybuf[m, lo:hi] = h.astype(BF)
            scale = scales(m, 1 - mod, hi - lo, (WORDS, REGIONS)[mod])
            dh = x_ref[m, lo:hi].astype(F32) * scale
            dr = norm_back(dh, n, rs, gain)
            res_f[j, lo:hi] = dr
            low = dr.astype(BF)
            dyf[m, lo:hi] = low
            dacts = [dot_nt(low, w_out[mod]) for _, w_out, _, _ in shards]
            ds = [(dact * dgelu[2 * sh + j, lo:hi]).astype(BF) for sh, dact in enumerate(dacts)]
            ones = [dot_nt(d, w_in[mod]) for d, (w_in, _, _, _) in zip(ds, shards)]
            part = ones[0] + ones[1]
            for d, (_, _, keep, at) in zip(ds, shards):
                keep[at, lo:hi] = d
            count_rows(1, mod, dh, n, low)
            ar_start(j, mod, 1, part)
        mate_start(j, DYF, DUP)

    def attn_backward(j):
        m = block_of(j)
        shards = ((wqkv_ref, wo_ref, dqkv, m), (wqkv_m, wo_m, dqkv_m, j))
        for mod, (lo, hi) in enumerate(SPANS):
            dh = res_f[j, lo:hi] + ar_finish(j, mod, 1)
            n = nrm_f[0, j, lo:hi]
            dr = norm_back(dh, n, rstd_f[0, j, lo:hi][:, :1], gain_ref[0, mod, 0:1, :])
            res_f[j, lo:hi] = dr
            low = dr.astype(BF)
            dya[m, lo:hi] = low
            count_rows(0, mod, dh, n, low)
            dmixs = [dot_nt(low, w_out[mod]).astype(BF) for _, w_out, _, _ in shards]
            grads = attend_back([
                (dmix, (p_w, p_r)[mod][2 * sh + j], *(qkv[k, 2 * sh + j, lo:hi] for k in range(3)))
                for sh, dmix in enumerate(dmixs)
            ])
            part = None
            for grad, (w, _, keep, at) in zip(grads, shards):
                d = jnp.concatenate(grad, axis=1)
                keep[at, lo:hi] = d
                one = dot(d, w[mod])
                part = one if part is None else part + one
            ar_start(j, mod, 0, part)

    def cross_backward(j):
        m = block_of(j)
        for mod, (lo, hi) in enumerate(SPANS):
            dh = res_f[j, lo:hi] + ar_finish(j, mod, 0)
            n = nrm_f[1, j, lo:hi]
            dr = norm_back(dh, n, rstd_f[1, j, lo:hi][:, :1], cvec_ref[1:2, :])
            res_f[j, lo:hi] = dr
            low = dr.astype(BF)
            dyc[m, lo:hi] = low
            count_rows(2, mod, dh, n, low)
        shards = ((cwqkv_ref, cwo_ref, cdqkv, m), (cwqkv_m, cwo_m, cdqkv_m, j))
        dmixs = [dot_nt(dyc[m], w_out[...]).astype(BF) for _, w_out, _, _ in shards]
        cases = []
        for sh, dmix in enumerate(dmixs):
            slot = 2 * sh + j
            q, k, v = cqkv[0, slot], cqkv[1, slot], cqkv[2, slot]
            cases.append((dmix[:RW], cp_w[slot], q[:RW], k[RW:], v[RW:]))
            cases.append((dmix[RW:], cp_r[slot], q[RW:], k[:RW], v[:RW]))
        grads = attend_back(cases)
        part = None
        for sh, (w, _, keep, at) in enumerate(shards):
            (dq_w, dk_r, dv_r), (dq_r, dk_w, dv_w) = grads[2 * sh : 2 * sh + 2]
            keep[at, :RW] = jnp.concatenate([dq_w, dk_w, dv_w], axis=1)
            keep[at, RW:] = jnp.concatenate([dq_r, dk_r, dv_r], axis=1)
            one = dot(keep[at], w[...])
            part = one if part is None else part + one
        for mod, (lo, hi) in enumerate(SPANS):
            ar_start(j, mod, 1, part[lo:hi])

    def to_section_0(j):
        m = block_of(j)
        for mod, (lo, hi) in enumerate(SPANS):
            back[m, lo:hi] = (res_f[j, lo:hi] + ar_finish(j, mod, 1)).astype(BF)
        back_start(j)

    def column_sums(buf, lo, hi):
        rows = buf[:, lo:hi, :].astype(F32).reshape(MB * (hi - lo), buf.shape[-1])
        return jnp.sum(rows, axis=0, keepdims=True)

    def scales(m, flag, count, length):
        index = lax.broadcasted_iota(jnp.int32, (count, 1), 0)
        scale = jnp.ones((count, 1), F32)
        for k in range(ITEMS_MB):
            value = jnp.where(flags_ref[ITEMS_MB * m + k] == flag, 0.25, 1.0)
            scale = jnp.where(index >= k * length, value, scale)
        return scale

    def outer_tile(left, right, lo, hi, j, store):
        start = j * (D // 2)
        columns = pl.ds(start if isinstance(j, int) else pl.multiple_of(start, D // 2), D // 2)
        a = left[:, lo:hi, columns].reshape(MB * (hi - lo), D // 2)
        b = right[:, lo:hi, :].reshape(MB * (hi - lo), right.shape[-1])
        store(dot_tn(a, b))

    def outer(left, right, lo, hi, store):
        pl.loop(0, 2)(
            lambda j: outer_tile(left, right, lo, hi, j, p(store, j))
        )

    def store_at(block, lo, hi):
        def store(j, value):
            g_ref[block, j, :, :, :, lo:hi] = value.astype(BF).reshape(4, 2, 48, hi - lo)

        return store

    def ffn_piece(k):
        mod, second = k // 2, k % 2
        left, right = ((alow, dup), (dyf, act))[second]
        outer(left, right, *SPANS[mod], store_at((5, 1)[second] + mod, 0, D))

    def attn_piece(k):
        mod, second = k // 2, k % 2
        left, right = ((xlow, dqkv), (dya, mixed))[second]
        outer(left, right, *SPANS[mod], store_at(4 * mod, *((0, 3 * HW), (3 * HW, D))[second]))

    def cross_outer():
        def store(j, lo, hi):
            def put(value):
                value = value.astype(BF).reshape(2, 4, 2, 24, hi - lo)
                g_ref[3, :, :, :, 24 * j : 24 * j + 24, lo:hi] = value

            return put

        for j in range(2):
            outer_tile(midf, cdqkv, 0, R, j, store(j, 0, 3 * HW))
            outer_tile(dyc, cmixed, 0, R, j, store(j, 3 * HW, D))

    Y, Z, EVEN, ODD, Y_EVEN, Y_ODD = range(6)
    even_z, odd_z = z_at + 1 - 2 * lax.rem(z_at, 2), 3 - z_at
    LAST = {Y: 2, Z: 2, EVEN: 3, ODD: 3, Y_EVEN: 3, Y_ODD: 3}
    Y_FIRST_KINDS = (Y, Y_EVEN, Y_ODD)

    def z_links(kind):
        return (even_z, odd_z) if kind in (EVEN, Y_EVEN) else (odd_z, even_z)

    def beyond(kind, near):
        return 3 - near if kind in (EVEN, Y_EVEN) else near + 1 - 2 * lax.rem(near, 2)

    def dw_copies(group, phase):
        index, kind, b = group
        sems = lambda k: (dw_send.at[index, k], dw_recv.at[index, k])
        if phase == 0:
            return [moved(g_ref.at[b, :, :, 1 - core], from_core.at[b], *sems(0), other_core)]
        to = lambda z: dp_device(y_at, z, core)
        if kind in Y_FIRST_KINDS and phase == 1:
            return [moved(g_ref.at[b, 1 - y_at, :, core], from_y.at[b], *sems(1), other_y)]
        if kind in (Y_EVEN, Y_ODD):
            near, far = z_links(kind)
            if phase == 3:
                return [moved(g_ref.at[b, y_at, far, core], from_z.at[b, 2], *sems(3), to(far))]
            return [
                moved(g_ref.at[b, y_at, z, core], from_z.at[b, k], *sems(2), to(near))
                for k, z in enumerate((near, beyond(kind, near)))
            ]
        if kind == Y:
            return [
                moved(
                    g_ref.at[b, y_at, z_next(o), core], from_z.at[b, o - 1], *sems(2),
                    dp_device(y_at, z_next(o), core),
                )
                for o in (1, 2, 3)
            ]
        if phase == LAST[kind]:
            src = g_ref.at[b, 1 - y_at, z_at, core]
            return [moved(src, from_ys.at[b - 4], *sems(1), other_y)]
        if kind == Z:
            return [
                moved(
                    g_ref.at[b, :, z_next(o), core], from_zs.at[o - 1], *sems(2),
                    dp_device(y_at, z_next(o), core),
                )
                for o in (1, 2, 3)
            ]
        near, far = z_links(kind)
        if phase == 1:
            return [
                moved(g_ref.at[b, :, z, core], from_h.at[b - 5, k], *sems(2), to(near))
                for k, z in enumerate((near, beyond(kind, near)))
            ]
        return [moved(g_ref.at[b, :, far, core], from_h.at[b - 5, 2], *sems(3), to(far))]

    def dw_start(group, phase):
        for copy in dw_copies(group, phase):
            copy.start()

    def dw_finish(group, phase):
        index, kind, b = group
        together = None
        if kind == Y and phase == 2:
            together = from_z.at[b]
        elif kind == Z and phase == 1:
            together = from_zs
        elif kind in (EVEN, ODD) and phase == 1:
            together = from_h.at[b - 5, pl.ds(0, 2)]
        elif kind in (Y_EVEN, Y_ODD) and phase == 2:
            together = from_z.at[b, pl.ds(0, 2)]
        if together is None:
            dw_copies(group, phase)[0].wait()
        else:
            moved(together, together, dw_send.at[index, 2], dw_recv.at[index, 2], other_core).wait()

        def add(place, *others):
            total = g_ref[place].astype(F32)
            for other in others:
                total = total + other.astype(F32)
            return total

        if phase == 0:

            def sum_y(y):
                place = (b, y, slice(None), core)
                g_ref[place] = add(place, from_core[b, y]).astype(BF)

            pl.loop(0, 2)(sum_y)
            return
        mine = (b, y_at, z_at, core)
        if phase == LAST[kind]:
            if kind == Y:
                others = [from_z[b, o] for o in range(3)]
            elif kind in Y_FIRST_KINDS:
                others = [from_z[b, 2]]
            else:
                others = [from_ys[b - 4]]
            dw_ref[b] = add(mine, *others)
            if b != 3:
                pltpu.make_async_copy(dw_ref.at[b], dw_out.at[b], out_sems.at[b]).start()
            return
        every = slice(None)
        if kind in Y_FIRST_KINDS and phase == 1:
            sums_of = [((b, y_at, every, core), [from_y[b]])]
        elif kind in (Y_EVEN, Y_ODD):
            sums_of = [((b, y_at, z, core), [from_z[b, k]]) for k, z in enumerate((z_at, z_links(kind)[1]))]
        elif kind == Z:
            sums_of = [((b, every, z_at, core), [from_zs[o] for o in range(3)])]
        elif phase == 1:
            places = (z_at, z_links(kind)[1])
            sums_of = [((b, every, z, core), [from_h[b - 5, k]]) for k, z in enumerate(places)]
        else:
            sums_of = [((b, every, z_at, core), [from_h[b - 5, 2]])]
        for place, others in sums_of:
            g_ref[place] = add(place, *others).astype(BF)

    def dw_turn(group, phase):
        dw_finish(group, phase)
        dw_start(group, phase + 1)

    OUT_W, OUT_R, IN_W, IN_R = (0, Y_EVEN, 1), (1, Y_ODD, 2), (2, EVEN, 5), (3, ODD, 6)
    ATTN_W, ATTN_R, CROSS = (4, Y, 0), (5, Z, 4), (6, Y, 3)

    def sm_copies(step, count):
        sems = (sm_send.at[step], sm_recv.at[step])
        if step == 0:
            return [moved(sums_t.at[me], sums_t.at[me], *sems, peer(o)) for o in range(1, TENSOR)]
        rows = pl.ds(0, count)
        src = sums.at[step - 1, rows]
        if step == 1:
            return [moved(src, sums_c.at[rows], *sems, other_core)]
        if step == 2:
            return [moved(src, sums_y.at[rows], *sems, other_y)]
        return [
            moved(src, sums_z.at[o - 1, rows], *sems, dp_device(y_at, z_next(o), core)) for o in (1, 2, 3)
        ]

    def sm_start(step, count=32):
        for copy in sm_copies(step, count):
            copy.start()

    def sm_wait(step, count=32):
        if step in (0, 3):
            place = sums_z.at[:, pl.ds(0, count)] if step == 3 else sums_t.at[pl.ds(0, TENSOR - 1)]
            moved(place, place, sm_send.at[step], sm_recv.at[step], other_core).wait()
        else:
            sm_copies(step, count)[0].wait()

    def small_norms():
        counts = jnp.logical_or(head, me < 2)
        for k in range(15):
            sums_t[me, k : k + 1, :] = jnp.where(counts, row_sums[k], 0.0)
        sums_t[me, 15:16, :] = jnp.zeros((1, D), F32)
        sm_start(0)

    def small_biases(count):
        sm_wait(0)
        total[...] = jnp.zeros((32, D), F32)
        norms = sums_t[0] + sums_t[1] + sums_t[2] + sums_t[3]
        total[0:12] = norms[:12]
        total[16:19] = norms[12:15]
        for mod in range(2):
            total[12 + mod : 13 + mod, :] = bsum[mod]
            total[14 + mod : 15 + mod, : 3 * HW] = bqsum[mod]
        total[19:20, : 3 * HW] = bqsum[2]
        sums[0] = total[...].astype(BF)
        sm_start(1, count)

    def small_y(count):
        sm_wait(1, count)
        total[:count] = total[:count] + sums_c[:count].astype(F32)
        sums[1] = total[...].astype(BF)
        sm_start(2, count)

    def small_z(count):
        sm_wait(2, count)
        total[:count] = total[:count] + sums_y[:count].astype(F32)
        sums[2] = total[...].astype(BF)
        sm_start(3, count)

    def small_last(count):
        sm_wait(3, count)
        for o in range(3):
            total[:count] = total[:count] + sums_z[o, :count].astype(F32)
        s_ref[...] = total[:24]

    def packet():
        return moved(pack.at[0], pack.at[1], pk_send, pk_recv, partner)

    def each(*steps, first=0, last=MB, after=()):
        def body(m):
            for step in steps:
                step(m)
            for k, extra in enumerate(after):
                if extra is not None:
                    pl.when(m == first + k)(extra)

        pl.loop(first, last)(body)

    def then(*steps):
        def run():
            for step in steps:
                step()

        return run

    def pair(step):
        pl.loop(0, 2)(step)

    @pl.when(head)
    def _():
        def to_partner(m):
            put_own_rows(midf, m, layer_d(m).astype(BF))
            mid_start(m)

        def from_partner(m):
            some_rows(midf, m, C, sec_send.at[m], sec_recv.at[m]).wait_send()
            back_arrive(m)
            back_e(m, own_rows_of(back, m).astype(F32))

        def last(m):
            ag_start(ybuf, m, (res[m] + rs_finish(m)).astype(BF), y_send, y_recv)

        front, rear = dict(first=0, last=2), dict(first=2, last=4)
        wait_weights(0, 1)
        each(
            layer_a,
            after=(
                None, then(p(pl.semaphore_wait, barrier, 12), p(rs_start, 0), p(rs_start, 1)),
                p(rs_start, 2),
            ),
        )
        each(layer_b, **front)
        rs_start(3)
        layer_b(2)
        wait_weights(2, 3)
        each(layer_c, **front)
        layer_b(3)
        layer_c(2)
        each(to_partner, **front)
        layer_c(3)
        each(to_partner, **rear)
        each(from_partner, last=3)
        each(back_f, after=(p(from_partner, 3), None, p(back_g, 0), p(back_g, 1)))
        ffn_piece(2)
        dw_start(IN_R, 0)
        ffn_piece(3)
        dw_start(OUT_R, 0)
        back_g(2)
        ffn_piece(0)
        dw_start(IN_W, 0)
        dw_turn(IN_R, 0)
        ffn_piece(1)
        dw_start(OUT_W, 0)
        dw_turn(OUT_R, 0)
        back_g(3)
        each(
            back_h,
            after=(
                then(p(dw_turn, IN_W, 0), p(dw_turn, OUT_W, 0)), small_norms,
            ),
        )
        attn_piece(2)
        attn_piece(3)
        dw_start(ATTN_R, 0)
        dw_turn(OUT_R, 1)
        dw_turn(IN_R, 1)
        attn_piece(0)
        dw_turn(ATTN_R, 0)
        attn_piece(1)
        dw_start(ATTN_W, 0)
        dw_turn(IN_W, 1)
        small_biases(16)
        dw_turn(ATTN_W, 0)
        small_y(16)
        each(last)
        dw_turn(OUT_W, 1)
        dw_turn(OUT_R, 2)
        dw_turn(IN_R, 2)
        dw_turn(IN_W, 2)
        dw_turn(OUT_W, 2)
        dw_turn(ATTN_R, 1)
        small_z(16)
        dw_turn(ATTN_W, 1)

    @pl.when(cross)
    def _():
        for copy in bias_copies():
            copy.start()
        gather_start("x", W2)
        gather_wait("x", CWQKV, CWO)
        gather_start("z", CWQKV, CWO)
        gather_wait("x", WQKV, WO)
        gather_start("y", WQKV)
        gather_start("z", WO)
        gather_wait("x", W1)
        gather_start("y", W1)
        gather_wait("y", WQKV)
        gather_start("z", WQKV)
        gather_wait("z", CWQKV, CWO)
        gather_start("core", CWQKV, CWO)
        gather_wait("z", WO)
        gather_start("y", WO)
        gather_wait("y", W1)
        gather_start("z", W1)
        for copy in bias_copies():
            copy.wait()
        gather_wait("core", CWQKV, CWO)
        wait_weights(0, 1, 2, 3, 4, 5)
        pl.loop(0, 2)(mid_relay)
        gather_wait("x", W2)
        gather_start("y", W2)
        mid_relay(2)

        @pl.when(set_of == 1)
        def _():
            gather_wait("y", WO)
            gather_wait("z", WQKV)
            gather_start("core", WQKV, WO)
            mid_relay(3)

        cross_forward(0)

        @pl.when(set_of == 0)
        def _():
            gather_wait("y", WO)
            gather_wait("z", WQKV)
            gather_start("core", WQKV, WO)
            mid_relay(3)

        cross_forward(1)
        gather_wait("core", WQKV, WO)
        attn_forward(0)
        gather_wait("z", W1)
        gather_start("core", W1)
        gather_wait("y", W2)
        gather_start("core", W2)
        attn_forward(1)
        pair(ffn_forward)
        pair(ffn_turn)
        pair(attn_backward)
        pair(cross_backward)
        pair(to_section_0)
        mate_wait(CMIXED, XLOW, MIXED, ALOW, ACT, DYF, DUP)
        pass_start(DYF)
        mate_start_all(DYC, CDQKV)
        ffn_piece(2)
        dw_start(IN_R, 0)
        ffn_piece(0)
        dw_start(IN_W, 0)
        dw_turn(IN_R, 0)
        dw_turn(IN_W, 0)
        pass_wait(DYF)
        pass_start(XLOW)
        ffn_piece(3)
        dw_start(OUT_R, 0)
        ffn_piece(1)
        dw_start(OUT_W, 0)
        dw_turn(OUT_R, 0)
        small_norms()
        for mod, (lo, hi) in enumerate(SPANS):
            bsum[mod] = column_sums(dup, lo, hi)
        dw_turn(OUT_W, 0)
        mate_wait(DYC)
        pass_start(DYC)
        mate_start_all(DYA, DQKV)
        for k in range(2):
            mid_finish(2 * (1 - set_of) + k)
        mate_wait(CDQKV)
        pass_wait(DYC)
        cross_outer()
        dw_start(CROSS, 0)
        bqsum[2] = column_sums(cdqkv, 0, R)
        dw_turn(CROSS, 0)
        mate_wait(DYA)
        pass_start(DYA)
        dw_turn(IN_R, 1)
        dw_turn(OUT_R, 1)
        dw_turn(IN_W, 1)
        mate_wait(DQKV)
        mate_start_all(YBUF)
        pass_wait(XLOW)
        pass_wait(DYA)
        for mod, (lo, hi) in enumerate(SPANS):
            bqsum[mod] = column_sums(dqkv, lo, hi)
        small_biases(32)
        attn_piece(2)
        attn_piece(3)
        dw_start(ATTN_R, 0)
        small_y(32)
        dw_turn(OUT_W, 1)
        attn_piece(0)
        attn_piece(1)
        dw_start(ATTN_W, 0)
        dw_turn(CROSS, 1)
        small_z(32)
        dw_turn(ATTN_R, 0)
        dw_turn(ATTN_W, 0)
        dw_turn(IN_R, 2)
        dw_turn(IN_W, 2)
        dw_turn(OUT_R, 2)
        dw_turn(OUT_W, 2)
        mate_wait(YBUF)
        pass_start(YBUF)
        dw_finish(CROSS, 2)
        small_last(32)
        pack[0, :24] = dw_ref[3, :24]
        pack[0, 24:] = s_ref[...]
        packet().start()
        dc_ref[...] = dw_ref[3, 24:]
        sc_ref[...] = s_ref[...]
        dw_turn(ATTN_R, 1)
        dw_turn(ATTN_W, 1)
        pass_wait(YBUF)
        for j in range(2):
            rows = back.at[block_of(j), pl.ds(0, 2 * C)]
            moved(rows, rows, back_send.at[j], back_recv.at[0], partner).wait_send()

    def write(m):
        @pl.when(head)
        def _():
            ag_finish(ybuf, m, y_send, y_recv)

        pltpu.make_async_copy(ybuf.at[m], y_out.at[m], out_sems.at[7 + m]).start()

    each(write)
    dw_finish(OUT_R, 3)
    dw_finish(IN_R, 3)
    dw_finish(IN_W, 3)
    dw_finish(OUT_W, 3)
    pl.when(head)(p(small_last, 16))
    dw_finish(ATTN_W, 2)
    dw_finish(ATTN_R, 2)
    for b in (0, 1, 2, 4, 5, 6):
        pltpu.make_async_copy(dw_ref.at[b], dw_out.at[b], out_sems.at[b]).wait()
    for m in range(MB):
        pltpu.make_async_copy(ybuf.at[m], y_out.at[m], out_sems.at[7 + m]).wait()
    pl.when(cross)(lambda: packet().wait_send())

    @pl.when(head)
    def _():
        packet().wait_recv()
        dc_ref[...] = pack[1, :24]
        sc_ref[...] = pack[1, 24:]


def arrange(
    y_ref, dw_ref, s_ref, dc_ref, sc_ref,
    words, regions, qkv_g, qv_bias_g, out_g, in_g, b1_g, ffo_g, obias_g, gain_g, shift_g,
    cqkv_g, cqv_bias_g, cout_g, cobias_g, cgain_g, cshift_g,
):
    place = lax.axis_index("dp")
    both = lax.axis_index("section") * 16 + place

    def from_column(rows, column):
        return pltpu.roll(rows, lax.rem(D - column, D), 1)

    for ref, (lo, hi), length in zip((words, regions), SPANS, (WORDS, REGIONS)):
        padded = y_ref[:, lo:hi, :].reshape(MB * (hi - lo), D)
        rows = dot(spread(hi - lo, length, True), padded)
        ref[0] = rows.reshape(length, ITEMS_LOCAL, D)
    small = s_ref[...]
    for mod in range(2):
        attn = dw_ref[4 * mod]
        for j in range(3):
            qkv_g[0, mod, j] = attn[:, j * HW : (j + 1) * HW]
        out_g[0, mod] = attn[:, 3 * HW :]
        in_g[0, mod] = dw_ref[5 + mod]
        ffo_g[0, mod] = dw_ref[1 + mod]
    columns = from_column(small, 48 * place)[:, :48]
    for mod in range(2):
        for l in range(2):
            for k, ref in enumerate((gain_g, shift_g, obias_g)):
                at = 2 * (3 * l + k) + mod
                ref[0, mod, l : l + 1, :] = columns[at : at + 1]
    columns = from_column(small, 8 * place)
    for mod in range(2):
        for k in range(6):
            b1_g[0, k, mod : mod + 1, :] = columns[12 + mod : 13 + mod, 128 * k : 128 * k + 8]
    columns = from_column(small, 4 * place)
    for mod in range(2):
        for j in range(2):
            for h in range(LOCAL_HEADS):
                lo = 2 * j * HW + h * HEAD_DIM
                qv_bias_g[0, mod, h, j : j + 1, :] = columns[14 + mod : 15 + mod, lo : lo + 4]
    wide = dc_ref[...]
    for j in range(3):
        cqkv_g[j] = wide[:, j * HW : (j + 1) * HW]
    cout_g[...] = wide[:, 3 * HW :]
    small = sc_ref[...]
    columns = from_column(small, 24 * both)
    for k, ref in enumerate((cgain_g, cshift_g, cobias_g)):
        ref[...] = columns[16 + k, :24]
    columns = from_column(small, 2 * both)[19:20]
    for j in range(2):
        heads = []
        for h in range(LOCAL_HEADS):
            lo = 2 * j * HW + h * HEAD_DIM
            heads.append(columns[:, lo : lo + 2])
        cqv_bias_g[j] = jnp.concatenate(heads, axis=0).T


def local(
    words, regions, word_lengths, task_flags, attn_qkv, attn_qv_bias, attn_out, ffn_in, ffn_in_bias,
    ffn_out, out_bias, norm_gain, norm_bias, cross_qkv, cross_qv_bias, cross_out, cross_out_bias,
    cross_norm_gain, cross_norm_bias,
):
    inputs = (
        words.transpose(0, 2, 1, 3), regions.transpose(0, 2, 1, 3), word_lengths, task_flags,
        attn_qkv.transpose(0, 1, 3, 4, 2).reshape(2, 3 * HW, D), attn_qv_bias.transpose(0, 1, 3, 2, 4), attn_out[0],
        ffn_in[0], ffn_in_bias.transpose(0, 2, 1, 3), ffn_out[0], out_bias, norm_gain, norm_bias,
        cross_qkv.transpose(1, 2, 0).reshape(3 * HW, D), cross_qv_bias.transpose(1, 0, 2), cross_out,
        cross_out_bias, cross_norm_gain, cross_norm_bias,
    )

    vmem = pl.BlockSpec(memory_space=pltpu.VMEM)
    smem = pl.BlockSpec(memory_space=pltpu.SMEM)
    hbm = pl.BlockSpec(memory_space=pl.ANY)
    mb_rows = lambda width, dtype: pltpu.VMEM((MB, R, width), dtype)
    own_rows = lambda count: pltpu.VMEM((count, MB, C, D), F32)
    y, g, s, dc, sc = pl.pallas_call(
        kernel,
        out_shape=(
            jax.ShapeDtypeStruct((MB, R, D), BF),
            jax.ShapeDtypeStruct((7, 48, D), F32),
            jax.ShapeDtypeStruct((24, D), F32),
            jax.ShapeDtypeStruct((24, D), F32),
            jax.ShapeDtypeStruct((24, D), F32),
        ),
        in_specs=[smem if k in (2, 3) else hbm if k in (4, 6, 7, 9, 13, 15) else vmem for k in range(len(inputs))],
        out_specs=[hbm] * 2 + [vmem] * 3,
        scratch_shapes=[
            pltpu.VMEM((7, 48, D), F32),
            pltpu.SemaphoreType.DMA((7 + MB,)),
            mb_rows(D, BF),
            pltpu.VMEM((3, 1, 3 * HW), F32),
            pltpu.VMEM((2, 1, D), F32),
            pltpu.VMEM((3, D), F32),
            mb_rows(D, BF),
            pltpu.VMEM((MB, TENSOR - 1, C, D), BF),
            *[mb_rows(D, BF) for _ in range(8)],
            pltpu.VMEM((3, MB, R, HW), BF),
            mb_rows(HW, BF),
            mb_rows(3 * HW, BF),
            pltpu.VMEM((3, MB, R, HW), BF),
            mb_rows(HW, BF),
            mb_rows(3 * HW, BF),
            mb_rows(D, BF),
            mb_rows(D, BF),
            mb_rows(D, F32),
            pltpu.VMEM((MB, 3 * RW, RW), F32),
            pltpu.VMEM((MB, 3 * RR, RR), F32),
            pltpu.VMEM((MB, 3 * RW, RR), F32),
            pltpu.VMEM((MB, 3 * RR, RW), F32),
            pltpu.VMEM((MB, C, D), F32),
            pltpu.VMEM((MB, C, D), F32),
            pltpu.VMEM((2, MB, C, D), F32),
            pltpu.VMEM((2, MB, C, 128), F32),
            pltpu.VMEM((MB, 16, D), BF),
            pltpu.VMEM((MB, 16, D), BF),
            pltpu.VMEM((C, D), F32),
            pltpu.VMEM((C, D), BF),
            pltpu.VMEM((2, 1, D), F32),
            pltpu.VMEM((3, 1, 3 * HW), F32),
            pltpu.VMEM((2, 3 * HW, D), BF),
            pltpu.VMEM((2, HW, D), BF),
            pltpu.VMEM((2, D, D), BF),
            pltpu.VMEM((2, D, D), BF),
            pltpu.VMEM((3 * HW, D), BF),
            pltpu.VMEM((HW, D), BF),
            pltpu.VMEM((2, 3 * HW, D), BF),
            pltpu.VMEM((2, HW, D), BF),
            pltpu.VMEM((2, D, D), BF),
            pltpu.VMEM((2, D, D), BF),
            pltpu.VMEM((3 * HW, D), BF),
            pltpu.VMEM((HW, D), BF),
            pltpu.VMEM((3, 1, 3 * HW), F32),
            pltpu.VMEM((2, 1, D), F32),
            pltpu.VMEM((2, 2, R, D), BF),
            pltpu.VMEM((2, 2, 16, D // 2), BF),
            pltpu.VMEM((2, 2, 2, 16, D // 2), BF),
            *[pltpu.VMEM((2, R, w), BF) for w in (D, D, HW, 3 * HW, HW, 3 * HW)],
            pltpu.VMEM((2, R, D), F32),
            pltpu.VMEM((2, R, D), F32),
            pltpu.VMEM((2, 2, R, D), F32),
            pltpu.VMEM((2, 2, R, 128), F32),
            pltpu.VMEM((16, 1, D), F32),
            pltpu.VMEM((7, 2, 4, 2, 48, D), BF),
            pltpu.VMEM((7, 2, 4, 48, D), BF),
            pltpu.VMEM((4, 4, 48, D), BF),
            pltpu.VMEM((3, 2, 48, D), BF),
            pltpu.VMEM((2, 3, 2, 48, D), BF),
            pltpu.VMEM((4, 3, 48, D), BF),
            pltpu.VMEM((3, 48, D), BF),
            pltpu.VMEM((3, 32, D), BF),
            pltpu.VMEM((32, D), F32),
            pltpu.VMEM((TENSOR, 16, D), F32),
            pltpu.VMEM((32, D), BF),
            pltpu.VMEM((32, D), BF),
            pltpu.VMEM((3, 32, D), BF),
            pltpu.VMEM((2, 48, D), F32),
            *[pltpu.SemaphoreType.DMA((MB,)) for _ in range(6)],
            pltpu.SemaphoreType.DMA((MB,)),
            pltpu.SemaphoreType.DMA((MB,)),
            pltpu.SemaphoreType.DMA((7, 4)),
            pltpu.SemaphoreType.DMA((7, 4)),
            pltpu.SemaphoreType.DMA((4,)),
            pltpu.SemaphoreType.DMA((4,)),
            pltpu.SemaphoreType.DMA,
            pltpu.SemaphoreType.DMA,
            pltpu.SemaphoreType.DMA((2,)),
            pltpu.SemaphoreType.DMA((MB,)),
            *[pltpu.SemaphoreType.DMA((2, 2, 4)) for _ in range(2)],
            *[pltpu.SemaphoreType.DMA((12,)) for _ in range(2)],
            *[pltpu.SemaphoreType.DMA((7, 4)) for _ in range(2)],
            *[pltpu.SemaphoreType.DMA((6,)) for _ in range(2)],
            pltpu.SemaphoreType.DMA((6,)),
        ],
        compiler_params=pltpu.CompilerParams(
            collective_id=0, has_side_effects=True, vmem_limit_bytes=63 * 2**20
        ),
    )(*inputs)

    shapes = (
        (1, WORDS, ITEMS_LOCAL, D), (1, REGIONS, ITEMS_LOCAL, D), (1, 2, 3, 48, HW),
        (1, 2, LOCAL_HEADS, 2, 4), (1, 2, 48, HW), (1, 2, 48, D), (1, 6, 2, 8), (1, 2, 48, D),
        (1, 2, 2, 48), (1, 2, 2, 48), (1, 2, 2, 48), (3, 24, HW), (2, 2, LOCAL_HEADS), (24, HW),
        (24,), (24,), (24,),
    )
    orders = {
        0: (0, 2, 1, 3), 1: (0, 2, 1, 3), 2: (0, 1, 3, 2, 4), 3: (0, 1, 3, 2, 4), 4: (0, 1, 3, 2),
        6: (0, 2, 1, 3), 7: (0, 1, 3, 2), 11: (1, 0, 2), 12: (0, 2, 1), 13: (1, 0),
    }
    outs = pl.pallas_call(
        arrange,
        out_shape=tuple(jax.ShapeDtypeStruct(shape, F32) for shape in shapes),
        in_specs=[vmem] * 5,
        out_specs=[vmem] * len(shapes),
        compiler_params=pltpu.CompilerParams(vmem_limit_bytes=60 * 2**20),
    )(y, g, s, dc, sc)
    return tuple(out.transpose(orders[k]) if k in orders else out for k, out in enumerate(outs))


def solution(mesh):
    in_specs = (
        P("section", "dp", None, None),
        P("section", "dp", None, None),
        P("dp"),
        P("dp"),
        P("section", None, None, None, "tensor"),
        P("section", None, None, "tensor", None),
        P("section", None, "tensor", None),
        P("section", None, None, "tensor"),
        P("section", None, "tensor", None),
        P("section", None, "tensor", None),
        P("section", None, None, None),
        P("section", None, None, None),
        P("section", None, None, None),
        P(None, None, "tensor"),
        P(None, "tensor", None),
        P("tensor", None),
        P(),
        P(),
        P(),
    )
    out_specs = (
        P("section", "dp", None, None),
        P("section", "dp", None, None),
        P("section", None, "dp", None, "tensor"),
        P("section", None, None, "tensor", "dp"),
        P("section", None, "tensor", "dp"),
        P("section", None, "dp", "tensor"),
        P("section", None, "tensor", "dp"),
        P("section", None, "tensor", "dp"),
        P("section", None, None, "dp"),
        P("section", None, None, "dp"),
        P("section", None, None, "dp"),
        P(("section", "dp"), None, "tensor"),
        P(None, "tensor", ("section", "dp")),
        P("tensor", ("section", "dp")),
        P(("section", "dp")),
        P(("section", "dp")),
        P(("section", "dp")),
    )
    return jax.shard_map(local, mesh=mesh, in_specs=in_specs, out_specs=out_specs, check_vma=False)
```

```python
import functools

import jax
import jax.numpy as jnp
from jax import lax
from jax.experimental import pallas as pl
from jax.experimental.pallas import tpu as pltpu
from jax.sharding import PartitionSpec as P

MESH = pl.DeviceIdType.MESH
BF = jnp.bfloat16
F32 = jnp.float32
HEAD_DIM = 64
LOCAL_HEADS = 3
HW = HEAD_DIM * LOCAL_HEADS
WORDS = 20
REGIONS = 36
D = 768
ITEMS_LOCAL = 8
TENSOR = 4

ITEMS_MB = 2
MB = ITEMS_LOCAL // ITEMS_MB
RW = 48
RR = 80
R = RW + RR
C = R // TENSOR
SPANS = ((0, RW), (RW, R))

EPSILON = 1e-06
MASKED = -1000000000.0
SCALING = HEAD_DIM ** (-0.5)


def dot(a, b):
    return lax.dot_general(a, b, (((1,), (0,)), ((), ())), preferred_element_type=F32)


def dot_nt(a, b):
    return lax.dot_general(a, b, (((1,), (1,)), ((), ())), preferred_element_type=F32)


def dot_tn(a, b):
    return lax.dot_general(a, b, (((0,), (0,)), ((), ())), preferred_element_type=F32)


def head_masks():
    lane = lax.broadcasted_iota(jnp.int32, (1, HW), 1)
    return [
        ((lane >= h * HEAD_DIM) & (lane < (h + 1) * HEAD_DIM)).astype(F32) for h in range(LOCAL_HEADS)
    ]


def by_head(a):
    masks = [m.astype(BF) for m in head_masks()]
    return jnp.concatenate([a * m for m in masks], axis=0)


def join_heads(stacked):
    rows = stacked.shape[0] // LOCAL_HEADS
    masks = head_masks()
    total = stacked[:rows] * masks[0]
    for h in range(1, LOCAL_HEADS):
        total = total + stacked[h * rows : (h + 1) * rows] * masks[h]
    return total


def item_of(shape, axis, length):
    index = lax.broadcasted_iota(jnp.int32, shape, axis)
    item = jnp.zeros(shape, jnp.int32)
    for k in range(1, ITEMS_MB + 1):
        item = item + (index >= k * length).astype(jnp.int32)
    return item


def spread(rows, length, transposed=False):
    count = ITEMS_LOCAL * length
    shape = (count, MB * rows) if transposed else (MB * rows, count)
    at = lax.broadcasted_iota(jnp.int32, shape, 0 if transposed else 1)
    padded = lax.broadcasted_iota(jnp.int32, shape, 1 if transposed else 0)
    item, position = at & (ITEMS_LOCAL - 1), at >> 3
    block, within = item >> (ITEMS_MB.bit_length() - 1), item & (ITEMS_MB - 1)
    target = block * rows + within * length + position
    return (target == padded).astype(F32).astype(BF)


def key_mask(q_rows, q_len, k_rows, k_len, lengths=None):
    shape = (q_rows, k_rows)
    item = item_of(shape, 1, k_len)
    key = lax.broadcasted_iota(jnp.int32, shape, 1)
    mask = (item_of(shape, 0, q_len) == item) & (key < ITEMS_MB * k_len)
    if lengths is not None:
        for k, length in enumerate(lengths):
            mask = mask & ((item != k) | (key < k * k_len + length))
    return mask


def attend(cases):
    masks = [jnp.concatenate([mask] * LOCAL_HEADS, axis=0) for _, _, _, mask in cases]
    scores = [dot_nt(by_head(q), k) * SCALING for q, k, _, _ in cases]
    scores = [jnp.where(mask, score, MASKED) for mask, score in zip(masks, scores)]
    es = [jnp.exp(score - jnp.max(score, axis=-1, keepdims=True)) for score in scores]
    probs = [e / jnp.sum(e, axis=-1, keepdims=True) for e in es]
    mixed = [dot(p.astype(BF), v) for p, (_, _, v, _) in zip(probs, cases)]
    return [(p, join_heads(mix).astype(BF)) for p, mix in zip(probs, mixed)]


def attend_back(cases):
    d3s = [by_head(dmix) for dmix, _, _, _, _ in cases]
    dps = [dot_nt(d3, v) for d3, (_, _, _, _, v) in zip(d3s, cases)]
    dss = [
        (probs * (dp - jnp.sum(probs * dp, axis=-1, keepdims=True))).astype(BF)
        for dp, (_, probs, _, _, _) in zip(dps, cases)
    ]
    dqs = [dot(ds, k) for ds, (_, _, _, k, _) in zip(dss, cases)]
    dks = [dot_tn(ds, by_head(q)) for ds, (_, _, q, _, _) in zip(dss, cases)]
    dvs = [dot_tn(probs.astype(BF), d3) for d3, (_, probs, _, _, _) in zip(d3s, cases)]
    return [
        ((join_heads(dq) * SCALING).astype(BF), (dk * SCALING).astype(BF), dv.astype(BF))
        for dq, dk, dv in zip(dqs, dks, dvs)
    ]


def split_qkv(out):
    return out[:, :HW], out[:, HW : 2 * HW], out[:, 2 * HW :]


def gelu(up):
    cdf = 0.5 * (1.0 + lax.erf(up * (0.5**0.5)))
    return (up * cdf).astype(BF), cdf + up * jnp.exp(-0.5 * up * up) * 0.3989422804014327


def norm_forward(r, gain, shift):
    center = r - jnp.mean(r, axis=-1, keepdims=True)
    spread = jnp.mean(center * center, axis=-1, keepdims=True)
    rstd = lax.rsqrt(spread + EPSILON)
    n = center * rstd
    return n, rstd, n * gain + shift


def norm_back(dh, n, rstd, gain):
    dn = dh * gain
    return rstd * (
        dn - jnp.mean(dn, axis=-1, keepdims=True) - n * jnp.mean(dn * n, axis=-1, keepdims=True)
    )


def kernel(
    words_hbm, regions_hbm, lengths_hbm, flags_hbm, wqkv_in, qv_bias_hbm, wo_in, w1_in, b1_in_hbm,
    w2_in, out_bias_hbm, gain_hbm, shift_hbm, cwqkv_in, cqv_bias_hbm, cwo_in, cout_bias_hbm,
    cgain_hbm, cshift_hbm,
    y_out, dw_out, s_ref, dc_ref, sc_ref,
    words_ref, regions_ref, lengths_ref, flags_ref, qv_bias_ref, b1_in_ref, out_bias_ref, gain_ref, shift_ref, cqv_bias_ref, cout_bias_ref, cgain_ref, cshift_ref,
    small_loads, dw_ref, out_sems, x_ref, bqkv_ref, b1_ref, cvec_ref, send, recv, xlow, midf, alow, dyf, dya, dyc, ybuf, back,
    qkv, mixed, dqkv, cqkv, cmixed, cdqkv, act, dup, dgelu,
    p_w, p_r, cp_w, cp_r, cur, res, nrm, rstd, packed, gathered_end, total_ref, low_ref, bsum, bqsum,
    wqkv_ref, wo_ref, w1_ref, w2_ref, cwqkv_ref, cwo_ref, wqkv_m, wo_m, w1_m, w2_m, cwqkv_m, cwo_m, bqkv_m, b1_m,
    got, tails, got_tails, act_m, dup_m, mixed_m, dqkv_m, cmixed_m, cdqkv_m, cur_f, res_f, nrm_f, rstd_f, row_sums,
    g_ref, from_core, from_y, from_zs, from_h, from_z, from_ys, sums, total, sums_t, sums_c, sums_y, sums_z, pack,
    x_send, rs_recv, ag_recv, y_recv, sec_recv,
    dw_send, dw_recv, sm_send, sm_recv, pk_send, pk_recv,
    back_send, back_recv, ar_send, ar_recv, mt_send, mt_recv, ga_send, ga_recv, ps_send, ps_recv, loads,
):
    p = functools.partial
    sec = lax.axis_index("section")
    me = lax.axis_index("tensor")
    head = sec == 0
    cross = sec == 1

    def peer(o):
        return {"tensor": lax.rem(me + o, TENSOR)}

    partner = {"section": 1 - sec}
    place = lax.axis_index("dp")
    y_at, z_at, core = place // 8, lax.rem(place // 2, 4), lax.rem(place, 2)

    def dp_device(y, z, c):
        return {"dp": (y * 4 + z) * 2 + c}

    other_core = dp_device(y_at, z_at, 1 - core)
    other_y = dp_device(1 - y_at, z_at, core)

    def z_next(o):
        return lax.rem(z_at + o, 4)

    weights = tuple(
        pltpu.make_async_copy(src, dst, loads.at[k])
        for k, (src, dst) in enumerate((
            (wqkv_in, wqkv_ref), (wo_in, wo_ref), (w1_in, w1_ref), (w2_in, w2_ref),
            (cwqkv_in, cwqkv_ref), (cwo_in, cwo_ref),
        ))
    )

    def load_weights(*which):
        for k in which:
            weights[k].start()

    def wait_weights(*which):
        for k in which:
            weights[k].wait()

    barrier = pltpu.get_barrier_semaphore()
    for o in range(1, TENSOR):
        pl.semaphore_signal(barrier, inc=1, device_id=peer(o), device_id_type=MESH)
    mate, halver = {"tensor": me + 1 - 2 * lax.rem(me, 2)}, {"tensor": 3 - me}
    set_of = lax.rem((me + 1) // 2, 2)
    for t in range(TENSOR):
        pl.semaphore_signal(
            barrier, inc=1, device_id={"section": 1 - sec, "tensor": t}, device_id_type=MESH
        )
    for device in (other_core, other_y, *(dp_device(y_at, z_next(o), core) for o in (1, 2, 3))):
        pl.semaphore_signal(barrier, inc=1, device_id=device, device_id_type=MESH)

    small_inputs = tuple(
        pltpu.make_async_copy(src, dst, small_loads.at[k])
        for k, (src, dst) in enumerate((
            (words_hbm, words_ref), (regions_hbm, regions_ref), (lengths_hbm, lengths_ref), (flags_hbm, flags_ref), (qv_bias_hbm, qv_bias_ref), (b1_in_hbm, b1_in_ref), (out_bias_hbm, out_bias_ref), (gain_hbm, gain_ref), (shift_hbm, shift_ref), (cqv_bias_hbm, cqv_bias_ref), (cout_bias_hbm, cout_bias_ref), (cgain_hbm, cgain_ref), (cshift_hbm, cshift_ref),
        ))
    )
    for copy in small_inputs:
        copy.start()
    load_weights(0, 1)

    def moved(src, dst, send_sem, recv_sem, device):
        return pltpu.make_async_remote_copy(
            src_ref=src, dst_ref=dst, send_sem=send_sem, recv_sem=recv_sem, device_id=device,
            device_id_type=MESH,
        )

    both_mods = slice(0, 2)
    half_columns = pl.ds(pl.multiple_of(core * (D // 2), D // 2), D // 2)

    def z_rows(z, count):
        return pl.ds(pl.multiple_of(z * count, count), count)

    gathered = (
        (cwqkv_in, cwqkv_m, 3 * HW // 4, False), (cwo_in, cwo_m, HW // 4, False),
        (wqkv_in, wqkv_m, 3 * HW // 4, True), (wo_in, wo_m, HW // 4, True),
        (w1_in, w1_m, D // 4, True), (w2_in, w2_m, D // 4, True),
    )
    CWQKV, CWO, WQKV, WO, W1, W2 = range(6)
    Y_FIRST = (WQKV, W1)

    def gather_copies(k, step):
        src, dst, count, by_mod = gathered[k]
        sems = lambda i: (ga_send.at[k], ga_recv.at[k, i])
        at = lambda mods, rows: (mods, rows, half_columns) if by_mod else (rows, half_columns)
        mine = at(y_at, z_rows(z_at, count))
        column = at(y_at, slice(0, 4 * count)) if by_mod else None
        if step == "x":
            part = column if k == W2 else mine
            return [moved(src.at[part], dst.at[part], *sems(0), mate)]
        if step == "y":
            place = dst.at[mine] if k in Y_FIRST else dst.at[column]
            return [moved(place, place, *sems(1), other_y)]
        if step == "z":
            place = dst.at[at(both_mods if k in Y_FIRST else y_at, z_rows(z_at, count))]
            return [
                moved(place, place, *sems(2), dp_device(y_at, z_next(o), core)) for o in (1, 2, 3)
            ]
        place = dst.at[at(both_mods, slice(0, 4 * count))]
        return [moved(place, place, *sems(3), other_core)]

    def gather_start(step, *arrays):
        for k in arrays:
            for copy in gather_copies(k, step):
                copy.start()

    def gather_wait(step, *arrays):
        for k in arrays:
            if step != "z":
                gather_copies(k, step)[0].wait()
                continue
            _, dst, count, by_mod = gathered[k]
            rows = slice(0, 3 * count)
            mods = both_mods if k in Y_FIRST else y_at
            place = dst.at[(mods, rows, half_columns) if by_mod else (rows, half_columns)]
            moved(place, place, ga_send.at[k], ga_recv.at[k, 2], mate).wait()

    @pl.when(cross)
    def _():
        pl.semaphore_wait(barrier, 12)
        gather_start("x", CWQKV, CWO, WQKV, WO, W1)

    for copy in small_inputs:
        copy.wait()
    load_weights(2, 3)
    pl.when(cross)(lambda: load_weights(4, 5))
    def side_by_side(rows):
        return jnp.concatenate(rows, axis=1)

    for mod in range(2):
        b1_ref[mod] = side_by_side(
            [b1_in_ref[0, k, mod : mod + 1, :] for k in range(D // 128)]
        )
    for k, ref in enumerate((qv_bias_ref.at[0, 0], qv_bias_ref.at[0, 1], cqv_bias_ref)):
        heads = lambda j: [ref[h, j : j + 1, :] for h in range(LOCAL_HEADS)]
        bqkv_ref[k] = side_by_side([*heads(0), jnp.zeros((1, HW), F32), *heads(1)])
    for k, ref in enumerate((cout_bias_ref, cgain_ref, cshift_ref)):
        cvec_ref[k : k + 1, :] = ref[...].reshape(1, D)

    for ref, (lo, hi), length in zip((words_ref, regions_ref), SPANS, (WORDS, REGIONS)):
        given = ref[0].astype(F32).reshape(ITEMS_LOCAL * length, D).astype(BF)
        placed = dot(spread(hi - lo, length), given).astype(BF)
        x_ref[:, lo:hi, :] = placed.reshape(MB, hi - lo, D)
    bsum[...] = jnp.zeros_like(bsum)
    bqsum[...] = jnp.zeros_like(bqsum)
    row_sums[...] = jnp.zeros_like(row_sums)


    def place_of(t, m):
        return lax.rem(t + m, TENSOR)

    def rows_at(at):
        return pl.ds(pl.multiple_of(48 * at - 16 * (at // 2), 16), C)

    def by_place(at, heavy, light):
        pl.when(at != 3)(heavy)
        pl.when(at == 3)(light)

    WORD_END, REGION_END = pl.ds(32, 16), pl.ds(112, 16)
    no_rows = jnp.zeros((8, D), F32)

    def pack_rows(words_end, regions_end):
        return jnp.concatenate([words_end, regions_end], axis=0).astype(BF)

    def wait_rows(m, ss, rs, sent, received):
        out, come = send.at[m, pl.ds(0, sent)], send.at[m, pl.ds(0, received)]
        moved(out, out, ss.at[m], rs.at[m], peer(1)).wait_send()
        moved(come, come, ss.at[m], rs.at[m], peer(1)).wait_recv()

    def own_rows_of(ref, m):
        at = place_of(me, m)

        def heavy():
            low_ref[...] = ref[m, rows_at(at)]

        def light():
            low_ref[0:16] = ref[m, WORD_END]
            low_ref[16:32] = ref[m, REGION_END]

        by_place(at, heavy, light)
        return low_ref[...]

    def put_own_rows(ref, m, low):
        at = place_of(me, m)

        def heavy():
            ref[m, rows_at(at)] = low

        def light():
            ref[m, WORD_END] = low[:16]
            ref[m, REGION_END] = low[16:]

        by_place(at, heavy, light)

    def put_parts(m, parts):
        for (lo, hi), part in zip(SPANS, parts):
            send[m, lo:hi] = part.astype(BF)
        packed[m] = pack_rows(parts[0][32:40], parts[1][64:72])

    def rs_start(m):
        for o in range(1, TENSOR):
            at = place_of(me + o, m)

            def heavy(o=o, at=at):
                src, dst = send.at[m, rows_at(at)], recv.at[m, o - 1]
                moved(src, dst, x_send.at[m], rs_recv.at[m], peer(o)).start()

            def light(o=o):
                src, dst = packed.at[m], recv.at[m, o - 1, pl.ds(0, 16)]
                moved(src, dst, x_send.at[m], rs_recv.at[m], peer(o)).start()

            by_place(at, heavy, light)

    def rs_finish(m):
        at = place_of(me, m)

        def heavy():
            wait_rows(m, x_send, rs_recv, 80, 96)
            total = send[m, rows_at(at)].astype(F32)
            for o in range(TENSOR - 1):
                total = total + recv[m, o].astype(F32)
            total_ref[...] = total

        def light():
            wait_rows(m, x_send, rs_recv, 96, 48)
            total = packed[m].astype(F32)
            for o in range(TENSOR - 1):
                total = total + recv[m, o, 0:16].astype(F32)
            total_ref[...] = jnp.concatenate([total[:8], no_rows, total[8:], no_rows], axis=0)

        by_place(at, heavy, light)
        return total_ref[...]

    def ag_start(buf, m, low, ss=x_send, rs=ag_recv):
        put_own_rows(buf, m, low)
        at = place_of(me, m)

        def heavy():
            rows = buf.at[m, rows_at(at)]
            for o in range(1, TENSOR):
                moved(rows, rows, ss.at[m], rs.at[m], peer(o)).start()

        def light():
            wide = low.astype(F32)
            gathered_end[m] = pack_rows(wide[:8], wide[16:24])
            for o in range(1, TENSOR):
                end = gathered_end.at[m]
                moved(end, end, ss.at[m], rs.at[m], peer(o)).start()

        by_place(at, heavy, light)

    def ag_finish(buf, m, ss=x_send, rs=ag_recv):
        def heavy():
            wait_rows(m, ss, rs, 96, 80)
            end = gathered_end[m].astype(F32)
            buf[m, WORD_END] = pack_rows(end[:8], no_rows)
            buf[m, REGION_END] = pack_rows(end[8:], no_rows)

        def light():
            wait_rows(m, ss, rs, 48, 96)

        by_place(place_of(me, m), heavy, light)

    def start_rows(ref, m, at, ss, rs, *devices):
        def heavy():
            rows = ref.at[m, rows_at(at)]
            for device in devices:
                moved(rows, rows, ss, rs, device).start()

        def light():
            for end in (WORD_END, REGION_END):
                rows = ref.at[m, end]
                for device in devices:
                    moved(rows, rows, ss, rs, device).start()

        by_place(at, heavy, light)

    def some_rows(ref, m, count, ss, rs):
        rows = ref.at[m, pl.ds(0, count)]
        return moved(rows, rows, ss, rs, partner)

    def mid_start(m):
        start_rows(midf, m, place_of(me, m), x_send.at[m], sec_recv.at[m], partner)

    def mid_relay(m):
        some_rows(midf, m, C, x_send.at[m], sec_recv.at[m]).wait_recv()
        start_rows(midf, m, place_of(me, m), x_send.at[m], ag_recv.at[m], peer(1), peer(2), peer(3))

    def mid_finish(m):
        some_rows(midf, m, 3 * C, x_send.at[m], ag_recv.at[m]).wait()

    def back_start(j):
        m = 2 * set_of + j
        for k in range(2):
            t = 2 * (me // 2) + k
            device = {"section": 1 - sec, "tensor": t}
            start_rows(back, m, place_of(t, m), back_send.at[j], back_recv.at[m], device)

    def back_arrive(m):
        some_rows(back, m, C, back_send.at[0], back_recv.at[m]).wait_recv()

    def save_norm(l, m, n, r):
        nrm[l, m] = n
        rstd[l, m] = jnp.broadcast_to(r, (C, 128))

    def own_words(m):
        at = place_of(me, m)
        count = jnp.where(at == 0, C, jnp.where(at == 3, C // 2, 0))
        return lax.broadcasted_iota(jnp.int32, (C, 1), 0) < count

    def own_param(ref, l, m):
        return jnp.where(own_words(m), ref[0, 0, l : l + 1, :], ref[0, 1, l : l + 1, :])

    def norm_step_back(l, m, dh):
        n = nrm[l, m]
        dr = norm_back(dh, n, rstd[l, m][:, :1], own_param(gain_ref, l, m))
        low = dr.astype(BF)
        words_only = own_words(m)
        for k, value in enumerate((dh * n, dh, low.astype(F32))):
            part = jnp.where(words_only, value, 0.0)
            at = 2 * (3 * l + k)
            row_sums[at] += jnp.sum(part, axis=0, keepdims=True)
            row_sums[at + 1] += jnp.sum(value - part, axis=0, keepdims=True)
        res[m] = dr
        return low

    def word_keys(m, q_rows, q_len):
        return key_mask(
            q_rows, q_len, RW, WORDS, [lengths_ref[ITEMS_MB * m + k] for k in range(ITEMS_MB)]
        )

    def region_keys(q_rows, q_len):
        return key_mask(q_rows, q_len, RR, REGIONS)

    def layer_a(m):
        xlow[m] = x_ref[m]
        cur[m] = own_rows_of(x_ref, m).astype(F32)
        outs = [
            (dot_nt(xlow[m, lo:hi], wqkv_ref[mod]) + bqkv_ref[mod]).astype(BF)
            for mod, (lo, hi) in enumerate(SPANS)
        ]
        for (lo, hi), out in zip(SPANS, outs):
            for k, part in enumerate(split_qkv(out)):
                qkv[k, m, lo:hi] = part
        masks = (word_keys(m, RW, WORDS), region_keys(RR, REGIONS))
        done = attend([(*split_qkv(out), mask) for out, mask in zip(outs, masks)])
        for (lo, hi), keep, (probs, mix) in zip(SPANS, (p_w, p_r), done):
            keep[m] = probs
            mixed[m, lo:hi] = mix
        put_parts(m, [dot(mix, wo_ref[mod]) for mod, (_, mix) in enumerate(done)])

    def layer_b(m):
        r = cur[m] + rs_finish(m) + own_param(out_bias_ref, 0, m)
        n, rs, h = norm_forward(r, own_param(gain_ref, 0, m), own_param(shift_ref, 0, m))
        save_norm(0, m, n, rs)
        cur[m] = h
        ag_start(alow, m, h.astype(BF))

    def layer_c(m):
        ag_finish(alow, m)
        ups = [dot(alow[m, lo:hi], w1_ref[mod]) + b1_ref[mod] for mod, (lo, hi) in enumerate(SPANS)]
        pairs = [gelu(up) for up in ups]
        put_parts(m, [dot(active, w2_ref[mod]) for mod, (active, _) in enumerate(pairs)])
        rs_start(m)
        for (lo, hi), (active, slope) in zip(SPANS, pairs):
            act[m, lo:hi] = active
            dgelu[m, lo:hi] = slope

    def layer_d(m):
        r = cur[m] + rs_finish(m) + own_param(out_bias_ref, 1, m)
        n, rs, h = norm_forward(r, own_param(gain_ref, 1, m), own_param(shift_ref, 1, m))
        save_norm(1, m, n, rs)
        return h

    def back_e(m, dh):
        ag_start(dyf, m, norm_step_back(1, m, dh))

    def back_f(m):
        ag_finish(dyf, m)
        dacts = [dot_nt(dyf[m, lo:hi], w2_ref[mod]) for mod, (lo, hi) in enumerate(SPANS)]
        ds = [(dact * dgelu[m, lo:hi]).astype(BF) for dact, (lo, hi) in zip(dacts, SPANS)]
        put_parts(m, [dot_nt(d, w1_ref[mod]) for mod, d in enumerate(ds)])
        rs_start(m)
        for mod, (lo, hi) in enumerate(SPANS):
            dup[m, lo:hi] = ds[mod]
            bsum[mod] += jnp.sum(ds[mod].astype(F32), axis=0, keepdims=True)

    def back_g(m):
        dh = res[m] + rs_finish(m)
        ag_start(dya, m, norm_step_back(0, m, dh))

    def back_h(m):
        ag_finish(dya, m)
        dmixs = [
            dot_nt(dya[m, lo:hi], wo_ref[mod]).astype(BF) for mod, (lo, hi) in enumerate(SPANS)
        ]
        grads = attend_back([
            (dmix, keep[m], *(qkv[k, m, lo:hi] for k in range(3)))
            for dmix, keep, (lo, hi) in zip(dmixs, (p_w, p_r), SPANS)
        ])
        ds = [jnp.concatenate(grad, axis=1) for grad in grads]
        put_parts(m, [dot(d, wqkv_ref[mod]) for mod, d in enumerate(ds)])
        rs_start(m)
        for mod, (lo, hi) in enumerate(SPANS):
            dqkv[m, lo:hi] = ds[mod]
            bqsum[mod] += jnp.sum(ds[mod].astype(F32), axis=0, keepdims=True)

    def block_of(j):
        return 2 * set_of + j

    def ar_copies(j, mod, turn):
        lo, hi = SPANS[mod]
        rows = slice(lo, hi - 16)
        sems = lambda k: (ar_send.at[j, 2 * mod + k], ar_recv.at[turn, j, 2 * mod + k])
        return [
            moved(send.at[j, rows], got.at[turn, j, rows], *sems(0), halver),
            moved(tails.at[j, mod], got_tails.at[turn, j, mod], *sems(1), halver),
        ]

    def ar_start(j, mod, turn, part):
        lo, hi = SPANS[mod]
        full = hi - lo - 16
        send[j, lo : hi - 16] = part[:full].astype(BF)
        tail = part[full : full + 8]
        tails[j, mod] = jnp.concatenate([tail[:, : D // 2], tail[:, D // 2 :]], axis=0).astype(BF)
        for copy in ar_copies(j, mod, turn):
            copy.start()

    def ar_finish(j, mod, turn):
        lo, hi = SPANS[mod]
        for copy in ar_copies(j, mod, turn):
            copy.wait()
        rows = send[j, lo : hi - 16].astype(F32) + got[turn, j, lo : hi - 16].astype(F32)
        tail = tails[j, mod].astype(F32) + got_tails[turn, j, mod].astype(F32)
        return jnp.concatenate([rows, jnp.concatenate([tail[:8], tail[8:]], axis=1), no_rows], axis=0)

    shared = (xlow, alow, dyf, dya, dyc, ybuf)
    for_mate = ((act_m, act), (dup_m, dup), (mixed_m, mixed), (dqkv_m, dqkv), (cmixed_m, cmixed), (cdqkv_m, cdqkv))
    XLOW, ALOW, DYF, DYA, DYC, YBUF, ACT, DUP, MIXED, DQKV, CMIXED, CDQKV = range(12)

    halves = (XLOW, DYF, DYA, DYC, YBUF)

    def half_rows(which):
        return pl.ds(pl.multiple_of(which * (R // 2), R // 2), R // 2)

    def mate_copy(k, j):
        if k < 6:
            src = dst = shared[k]
            src = src.at[block_of(j)]
        else:
            src, dst = for_mate[k - 6]
            src = src.at[j]
        dst = dst.at[block_of(j)]
        if k in halves:
            src, dst = src.at[half_rows(me // 2)], dst.at[half_rows(me // 2)]
        return moved(src, dst, mt_send.at[k], mt_recv.at[k], mate)

    def mate_start(j, *kinds):
        for k in kinds:
            mate_copy(k, j).start()

    def mate_start_all(*kinds):
        for k in kinds:
            for j in range(2):
                mate_copy(k, j).start()

    def mate_wait(*kinds):
        for k in kinds:
            place = (shared[k] if k < 6 else for_mate[k - 6][1]).at[pl.ds(2 * (1 - set_of), 2)]
            if k in halves:
                place = place.at[:, half_rows(me // 2)]
            moved(place, place, mt_send.at[k], mt_recv.at[k], mate).wait()

    def pass_copy(k):
        place = shared[k].at[pl.ds(2 * (1 - set_of), 2), half_rows(me // 2)]
        return moved(place, place, ps_send.at[k], ps_recv.at[k], halver)

    def pass_start(k):
        pass_copy(k).start()

    def pass_wait(k):
        pass_copy(k).wait()

    def bias_copies():
        return [
            moved(bqkv_ref, bqkv_m, ga_send.at[6], ga_recv.at[6, 0], mate),
            moved(b1_ref, b1_m, ga_send.at[7], ga_recv.at[6, 1], mate),
        ]

    def save_norm_f(l, j, lo, hi, n, r):
        nrm_f[l, j, lo:hi] = n
        rstd_f[l, j, lo:hi] = jnp.broadcast_to(r, (hi - lo, 128))

    def count_rows(l, mod, dh, n, low):
        for k, value in enumerate((dh * n, dh, low.astype(F32))):
            at = 12 + k if l == 2 else 2 * (3 * l + k) + mod
            row_sums[at] += jnp.sum(value, axis=0, keepdims=True)

    def cross_forward(j):
        m = block_of(j)
        mid_finish(m)
        mid = midf[m]
        shards = ((cwqkv_ref, bqkv_ref, cwo_ref, cmixed, m), (cwqkv_m, bqkv_m, cwo_m, cmixed_m, j))
        qkvs = []
        for sh, (w, bias, w_out, keep, at) in enumerate(shards):
            out = (dot_nt(mid, w[...]) + bias[2]).astype(BF)
            q, k, v = split_qkv(out)
            cqkv[0, 2 * sh + j], cqkv[1, 2 * sh + j], cqkv[2, 2 * sh + j] = q, k, v
            qkvs.append((q, k, v))
        for mod, (lo, hi) in enumerate(SPANS):
            others = slice(*SPANS[1 - mod])
            mask = region_keys(RW, WORDS) if mod == 0 else word_keys(m, RR, REGIONS)
            done = attend([(q[lo:hi], k[others], v[others], mask) for q, k, v in qkvs])
            part = None
            for sh, (w, bias, w_out, keep, at) in enumerate(shards):
                probs, mix = done[sh]
                (cp_w, cp_r)[mod][2 * sh + j] = probs
                keep[at, lo:hi] = mix
                one = dot(mix, w_out[...])
                part = one if part is None else part + one
            ar_start(j, mod, 0, part)
        mate_start(j, CMIXED)

    def attn_forward(j):
        m = block_of(j)
        shards = (
            (wqkv_ref, bqkv_ref, wo_ref, mixed, m), (wqkv_m, bqkv_m, wo_m, mixed_m, j),
        )
        for mod, (lo, hi) in enumerate(SPANS):
            r = midf[m, lo:hi].astype(F32) + ar_finish(j, mod, 0) + cvec_ref[0:1, :]
            n, rs, h = norm_forward(r, cvec_ref[1:2, :], cvec_ref[2:3, :])
            save_norm_f(1, j, lo, hi, n, rs)
            cur_f[j, lo:hi] = h
            low = h.astype(BF)
            xlow[m, lo:hi] = low
            outs = [(dot_nt(low, w[mod]) + bias[mod]).astype(BF) for w, bias, _, _, _ in shards]
            for sh, out in enumerate(outs):
                for k, part in enumerate(split_qkv(out)):
                    qkv[k, 2 * sh + j, lo:hi] = part
            mask = word_keys(m, RW, WORDS) if mod == 0 else region_keys(RR, REGIONS)
            done = attend([(*split_qkv(out), mask) for out in outs])
            part = None
            for sh, (w, bias, w_out, keep, at) in enumerate(shards):
                probs, mix = done[sh]
                (p_w, p_r)[mod][2 * sh + j] = probs
                keep[at, lo:hi] = mix
                one = dot(mix, w_out[mod])
                part = one if part is None else part + one
            ar_start(j, mod, 1, part)
        mate_start(j, XLOW, MIXED)

    def ffn_forward(j):
        m = block_of(j)
        shards = ((w1_ref, b1_ref, w2_ref, act, m), (w1_m, b1_m, w2_m, act_m, j))
        for mod, (lo, hi) in enumerate(SPANS):
            r = cur_f[j, lo:hi] + ar_finish(j, mod, 1) + out_bias_ref[0, mod, 0:1, :]
            n, rs, h = norm_forward(r, gain_ref[0, mod, 0:1, :], shift_ref[0, mod, 0:1, :])
            save_norm_f(0, j, lo, hi, n, rs)
            cur_f[j, lo:hi] = h
            low = h.astype(BF)
            alow[m, lo:hi] = low
            if mod == 0:
                pl.when(j == 0)(lambda: gather_wait("core", W1))
            ups = [dot(low, w[mod]) + bias[mod] for w, bias, _, _, _ in shards]
            pairs = [gelu(up) for up in ups]
            for sh, (_, _, _, keep, at) in enumerate(shards):
                keep[at, lo:hi], dgelu[2 * sh + j, lo:hi] = pairs[sh]
            if mod == 0:
                pl.when(j == 0)(lambda: gather_wait("core", W2))
            ones = [dot(active, w_out[mod]) for (active, _), (_, _, w_out, _, _) in zip(pairs, shards)]
            part = ones[0] + ones[1]
            ar_start(j, mod, 0, part)
        mate_start(j, ALOW, ACT)

    def ffn_turn(j):
        m = block_of(j)
        shards = ((w1_ref, w2_ref, dup, m), (w1_m, w2_m, dup_m, j))
        for mod, (lo, hi) in enumerate(SPANS):
            r = cur_f[j, lo:hi] + ar_finish(j, mod, 0) + out_bias_ref[0, mod, 1:2, :]
            gain = gain_ref[0, mod, 1:2, :]
            n, rs, h = norm_forward(r, gain, shift_ref[0, mod, 1:2, :])
            ybuf[m, lo:hi] = h.astype(BF)
            scale = scales(m, 1 - mod, hi - lo, (WORDS, REGIONS)[mod])
            dh = x_ref[m, lo:hi].astype(F32) * scale
            dr = norm_back(dh, n, rs, gain)
            res_f[j, lo:hi] = dr
            low = dr.astype(BF)
            dyf[m, lo:hi] = low
            dacts = [dot_nt(low, w_out[mod]) for _, w_out, _, _ in shards]
            ds = [(dact * dgelu[2 * sh + j, lo:hi]).astype(BF) for sh, dact in enumerate(dacts)]
            ones = [dot_nt(d, w_in[mod]) for d, (w_in, _, _, _) in zip(ds, shards)]
            part = ones[0] + ones[1]
            for d, (_, _, keep, at) in zip(ds, shards):
                keep[at, lo:hi] = d
            count_rows(1, mod, dh, n, low)
            ar_start(j, mod, 1, part)
        mate_start(j, DYF, DUP)

    def attn_backward(j):
        m = block_of(j)
        shards = ((wqkv_ref, wo_ref, dqkv, m), (wqkv_m, wo_m, dqkv_m, j))
        for mod, (lo, hi) in enumerate(SPANS):
            dh = res_f[j, lo:hi] + ar_finish(j, mod, 1)
            n = nrm_f[0, j, lo:hi]
            dr = norm_back(dh, n, rstd_f[0, j, lo:hi][:, :1], gain_ref[0, mod, 0:1, :])
            res_f[j, lo:hi] = dr
            low = dr.astype(BF)
            dya[m, lo:hi] = low
            count_rows(0, mod, dh, n, low)
            dmixs = [dot_nt(low, w_out[mod]).astype(BF) for _, w_out, _, _ in shards]
            grads = attend_back([
                (dmix, (p_w, p_r)[mod][2 * sh + j], *(qkv[k, 2 * sh + j, lo:hi] for k in range(3)))
                for sh, dmix in enumerate(dmixs)
            ])
            part = None
            for grad, (w, _, keep, at) in zip(grads, shards):
                d = jnp.concatenate(grad, axis=1)
                keep[at, lo:hi] = d
                one = dot(d, w[mod])
                part = one if part is None else part + one
            ar_start(j, mod, 0, part)

    def cross_backward(j):
        m = block_of(j)
        for mod, (lo, hi) in enumerate(SPANS):
            dh = res_f[j, lo:hi] + ar_finish(j, mod, 0)
            n = nrm_f[1, j, lo:hi]
            dr = norm_back(dh, n, rstd_f[1, j, lo:hi][:, :1], cvec_ref[1:2, :])
            res_f[j, lo:hi] = dr
            low = dr.astype(BF)
            dyc[m, lo:hi] = low
            count_rows(2, mod, dh, n, low)
        shards = ((cwqkv_ref, cwo_ref, cdqkv, m), (cwqkv_m, cwo_m, cdqkv_m, j))
        dmixs = [dot_nt(dyc[m], w_out[...]).astype(BF) for _, w_out, _, _ in shards]
        cases = []
        for sh, dmix in enumerate(dmixs):
            slot = 2 * sh + j
            q, k, v = cqkv[0, slot], cqkv[1, slot], cqkv[2, slot]
            cases.append((dmix[:RW], cp_w[slot], q[:RW], k[RW:], v[RW:]))
            cases.append((dmix[RW:], cp_r[slot], q[RW:], k[:RW], v[:RW]))
        grads = attend_back(cases)
        part = None
        for sh, (w, _, keep, at) in enumerate(shards):
            (dq_w, dk_r, dv_r), (dq_r, dk_w, dv_w) = grads[2 * sh : 2 * sh + 2]
            keep[at, :RW] = jnp.concatenate([dq_w, dk_w, dv_w], axis=1)
            keep[at, RW:] = jnp.concatenate([dq_r, dk_r, dv_r], axis=1)
            one = dot(keep[at], w[...])
            part = one if part is None else part + one
        for mod, (lo, hi) in enumerate(SPANS):
            ar_start(j, mod, 1, part[lo:hi])

    def to_section_0(j):
        m = block_of(j)
        for mod, (lo, hi) in enumerate(SPANS):
            back[m, lo:hi] = (res_f[j, lo:hi] + ar_finish(j, mod, 1)).astype(BF)
        back_start(j)

    def column_sums(buf, lo, hi):
        rows = buf[:, lo:hi, :].astype(F32).reshape(MB * (hi - lo), buf.shape[-1])
        return jnp.sum(rows, axis=0, keepdims=True)

    def scales(m, flag, count, length):
        index = lax.broadcasted_iota(jnp.int32, (count, 1), 0)
        scale = jnp.ones((count, 1), F32)
        for k in range(ITEMS_MB):
            value = jnp.where(flags_ref[ITEMS_MB * m + k] == flag, 0.25, 1.0)
            scale = jnp.where(index >= k * length, value, scale)
        return scale

    def outer_tile(left, right, lo, hi, j, store):
        start = j * (D // 2)
        columns = pl.ds(start if isinstance(j, int) else pl.multiple_of(start, D // 2), D // 2)
        a = left[:, lo:hi, columns].reshape(MB * (hi - lo), D // 2)
        b = right[:, lo:hi, :].reshape(MB * (hi - lo), right.shape[-1])
        store(dot_tn(a, b))

    def outer(left, right, lo, hi, store):
        pl.loop(0, 2)(
            lambda j: outer_tile(left, right, lo, hi, j, p(store, j))
        )

    def store_at(block, lo, hi):
        def store(j, value):
            g_ref[block, j, :, :, :, lo:hi] = value.astype(BF).reshape(4, 2, 48, hi - lo)

        return store

    def ffn_piece(k):
        mod, second = k // 2, k % 2
        left, right = ((alow, dup), (dyf, act))[second]
        outer(left, right, *SPANS[mod], store_at((5, 1)[second] + mod, 0, D))

    def attn_piece(k):
        mod, second = k // 2, k % 2
        left, right = ((xlow, dqkv), (dya, mixed))[second]
        outer(left, right, *SPANS[mod], store_at(4 * mod, *((0, 3 * HW), (3 * HW, D))[second]))

    def cross_outer():
        def store(j, lo, hi):
            def put(value):
                value = value.astype(BF).reshape(2, 4, 2, 24, hi - lo)
                g_ref[3, :, :, :, 24 * j : 24 * j + 24, lo:hi] = value

            return put

        for j in range(2):
            outer_tile(midf, cdqkv, 0, R, j, store(j, 0, 3 * HW))
            outer_tile(dyc, cmixed, 0, R, j, store(j, 3 * HW, D))

    Y, Z, EVEN, ODD, Y_EVEN, Y_ODD = range(6)
    even_z, odd_z = z_at + 1 - 2 * lax.rem(z_at, 2), 3 - z_at
    LAST = {Y: 2, Z: 2, EVEN: 3, ODD: 3, Y_EVEN: 3, Y_ODD: 3}
    Y_FIRST_KINDS = (Y, Y_EVEN, Y_ODD)

    def z_links(kind):
        return (even_z, odd_z) if kind in (EVEN, Y_EVEN) else (odd_z, even_z)

    def beyond(kind, near):
        return 3 - near if kind in (EVEN, Y_EVEN) else near + 1 - 2 * lax.rem(near, 2)

    def dw_copies(group, phase):
        index, kind, b = group
        sems = lambda k: (dw_send.at[index], dw_recv.at[index, k])
        if phase == 0:
            return [moved(g_ref.at[b, :, :, 1 - core], from_core.at[b], *sems(0), other_core)]
        to = lambda z: dp_device(y_at, z, core)
        if kind in Y_FIRST_KINDS and phase == 1:
            return [moved(g_ref.at[b, 1 - y_at, :, core], from_y.at[b], *sems(1), other_y)]
        if kind in (Y_EVEN, Y_ODD):
            near, far = z_links(kind)
            if phase == 3:
                return [moved(g_ref.at[b, y_at, far, core], from_z.at[b, 2], *sems(3), to(far))]
            return [
                moved(g_ref.at[b, y_at, z, core], from_z.at[b, k], *sems(2), to(near))
                for k, z in enumerate((near, beyond(kind, near)))
            ]
        if kind == Y:
            return [
                moved(
                    g_ref.at[b, y_at, z_next(o), core], from_z.at[b, o - 1], *sems(2),
                    dp_device(y_at, z_next(o), core),
                )
                for o in (1, 2, 3)
            ]
        if phase == LAST[kind]:
            src = g_ref.at[b, 1 - y_at, z_at, core]
            return [moved(src, from_ys.at[b - 4], *sems(1), other_y)]
        if kind == Z:
            return [
                moved(
                    g_ref.at[b, :, z_next(o), core], from_zs.at[o - 1], *sems(2),
                    dp_device(y_at, z_next(o), core),
                )
                for o in (1, 2, 3)
            ]
        near, far = z_links(kind)
        if phase == 1:
            return [
                moved(g_ref.at[b, :, z, core], from_h.at[b - 5, k], *sems(2), to(near))
                for k, z in enumerate((near, beyond(kind, near)))
            ]
        return [moved(g_ref.at[b, :, far, core], from_h.at[b - 5, 2], *sems(3), to(far))]

    def dw_start(group, phase):
        for copy in dw_copies(group, phase):
            copy.start()

    def dw_finish(group, phase):
        index, kind, b = group
        together = None
        if kind == Y and phase == 2:
            together = from_z.at[b]
        elif kind == Z and phase == 1:
            together = from_zs
        elif kind in (EVEN, ODD) and phase == 1:
            together = from_h.at[b - 5, pl.ds(0, 2)]
        elif kind in (Y_EVEN, Y_ODD) and phase == 2:
            together = from_z.at[b, pl.ds(0, 2)]
        if together is None:
            dw_copies(group, phase)[0].wait()
        else:
            moved(together, together, dw_send.at[index], dw_recv.at[index, 2], other_core).wait()

        def add(place, *others):
            total = g_ref[place].astype(F32)
            for other in others:
                total = total + other.astype(F32)
            return total

        if phase == 0:

            def sum_y(y):
                place = (b, y, slice(None), core)
                g_ref[place] = add(place, from_core[b, y]).astype(BF)

            pl.loop(0, 2)(sum_y)
            return
        mine = (b, y_at, z_at, core)
        if phase == LAST[kind]:
            if kind == Y:
                others = [from_z[b, o] for o in range(3)]
            elif kind in Y_FIRST_KINDS:
                others = [from_z[b, 2]]
            else:
                others = [from_ys[b - 4]]
            dw_ref[b] = add(mine, *others)
            if b != 3:
                pltpu.make_async_copy(dw_ref.at[b], dw_out.at[b], out_sems.at[b]).start()
            return
        every = slice(None)
        if kind in Y_FIRST_KINDS and phase == 1:
            sums_of = [((b, y_at, every, core), [from_y[b]])]
        elif kind in (Y_EVEN, Y_ODD):
            sums_of = [((b, y_at, z, core), [from_z[b, k]]) for k, z in enumerate((z_at, z_links(kind)[1]))]
        elif kind == Z:
            sums_of = [((b, every, z_at, core), [from_zs[o] for o in range(3)])]
        elif phase == 1:
            places = (z_at, z_links(kind)[1])
            sums_of = [((b, every, z, core), [from_h[b - 5, k]]) for k, z in enumerate(places)]
        else:
            sums_of = [((b, every, z_at, core), [from_h[b - 5, 2]])]
        for place, others in sums_of:
            g_ref[place] = add(place, *others).astype(BF)

    def dw_turn(group, phase):
        dw_finish(group, phase)
        dw_start(group, phase + 1)

    OUT_W, OUT_R, IN_W, IN_R = (0, Y_EVEN, 1), (1, Y_ODD, 2), (2, EVEN, 5), (3, ODD, 6)
    ATTN_W, ATTN_R, CROSS = (4, Y, 0), (5, Z, 4), (6, Y, 3)

    def sm_copies(step, count):
        sems = (sm_send.at[0], sm_recv.at[step])
        if step == 0:
            return [moved(sums_t.at[me], sums_t.at[me], *sems, peer(o)) for o in range(1, TENSOR)]
        rows = pl.ds(0, count)
        src = sums.at[step - 1, rows]
        if step == 1:
            return [moved(src, sums_c.at[rows], *sems, other_core)]
        if step == 2:
            return [moved(src, sums_y.at[rows], *sems, other_y)]
        return [
            moved(src, sums_z.at[o - 1, rows], *sems, dp_device(y_at, z_next(o), core)) for o in (1, 2, 3)
        ]

    def sm_start(step, count=32):
        for copy in sm_copies(step, count):
            copy.start()

    def sm_wait(step, count=32):
        if step in (0, 3):
            place = sums_z.at[:, pl.ds(0, count)] if step == 3 else sums_t.at[pl.ds(0, TENSOR - 1)]
            moved(place, place, sm_send.at[0], sm_recv.at[step], other_core).wait()
        else:
            sm_copies(step, count)[0].wait()

    def small_norms():
        counts = jnp.logical_or(head, me < 2)
        for k in range(15):
            sums_t[me, k : k + 1, :] = jnp.where(counts, row_sums[k], 0.0)
        sums_t[me, 15:16, :] = jnp.zeros((1, D), F32)
        sm_start(0)

    def small_biases(count):
        sm_wait(0)
        total[...] = jnp.zeros((32, D), F32)
        norms = sums_t[0] + sums_t[1] + sums_t[2] + sums_t[3]
        total[0:12] = norms[:12]
        total[16:19] = norms[12:15]
        for mod in range(2):
            total[12 + mod : 13 + mod, :] = bsum[mod]
            total[14 + mod : 15 + mod, : 3 * HW] = bqsum[mod]
        total[19:20, : 3 * HW] = bqsum[2]
        sums[0] = total[...].astype(BF)
        sm_start(1, count)

    def small_y(count):
        sm_wait(1, count)
        total[:count] = total[:count] + sums_c[:count].astype(F32)
        sums[1] = total[...].astype(BF)
        sm_start(2, count)

    def small_z(count):
        sm_wait(2, count)
        total[:count] = total[:count] + sums_y[:count].astype(F32)
        sums[2] = total[...].astype(BF)
        sm_start(3, count)

    def small_last(count):
        sm_wait(3, count)
        for o in range(3):
            total[:count] = total[:count] + sums_z[o, :count].astype(F32)
        s_ref[...] = total[:24]

    def packet():
        return moved(pack.at[0], pack.at[1], pk_send, pk_recv, partner)

    def each(*steps, first=0, last=MB, after=()):
        def body(m):
            for step in steps:
                step(m)
            for k, extra in enumerate(after):
                if extra is not None:
                    pl.when(m == first + k)(extra)

        pl.loop(first, last)(body)

    def then(*steps):
        def run():
            for step in steps:
                step()

        return run

    def pair(step):
        pl.loop(0, 2)(step)

    @pl.when(head)
    def _():
        def to_partner(m):
            put_own_rows(midf, m, layer_d(m).astype(BF))
            mid_start(m)

        def from_partner(m):
            some_rows(midf, m, C, x_send.at[m], sec_recv.at[m]).wait_send()
            back_arrive(m)
            back_e(m, own_rows_of(back, m).astype(F32))

        def last(m):
            ag_start(ybuf, m, (res[m] + rs_finish(m)).astype(BF), x_send, y_recv)

        front, rear = dict(first=0, last=2), dict(first=2, last=4)
        wait_weights(0, 1)
        each(
            layer_a,
            after=(
                None, then(p(pl.semaphore_wait, barrier, 12), p(rs_start, 0), p(rs_start, 1)),
            ),
        )
        layer_b(0)
        rs_start(2)
        layer_b(1)
        rs_start(3)
        layer_b(2)
        wait_weights(2, 3)
        each(layer_c, **front)
        layer_b(3)
        layer_c(2)
        each(to_partner, **front)
        layer_c(3)
        each(to_partner, **rear)
        each(from_partner, last=3)
        each(back_f, after=(p(from_partner, 3), None, p(back_g, 0)))
        ffn_piece(2)
        dw_start(IN_R, 0)
        back_g(1)
        ffn_piece(3)
        dw_start(OUT_R, 0)
        back_g(2)
        dw_turn(IN_R, 0)
        ffn_piece(0)
        dw_start(IN_W, 0)
        dw_turn(OUT_R, 0)
        ffn_piece(1)
        dw_start(OUT_W, 0)
        back_g(3)
        each(
            back_h,
            after=(
                then(p(dw_turn, IN_W, 0), p(dw_turn, OUT_W, 0)), small_norms,
            ),
        )
        attn_piece(2)
        attn_piece(3)
        dw_start(ATTN_R, 0)
        dw_turn(OUT_R, 1)
        dw_turn(IN_R, 1)
        attn_piece(0)
        dw_turn(ATTN_R, 0)
        attn_piece(1)
        dw_start(ATTN_W, 0)
        dw_turn(IN_W, 1)
        small_biases(16)
        dw_turn(ATTN_W, 0)
        small_y(16)
        each(last)
        dw_turn(OUT_W, 1)
        dw_turn(OUT_R, 2)
        dw_turn(IN_R, 2)
        dw_turn(IN_W, 2)
        dw_turn(OUT_W, 2)
        small_z(16)
        dw_turn(ATTN_W, 1)
        dw_turn(ATTN_R, 1)

    @pl.when(cross)
    def _():
        for copy in bias_copies():
            copy.start()
        gather_start("x", W2)
        gather_wait("x", CWQKV, CWO)
        gather_start("z", CWQKV, CWO)
        gather_wait("x", WQKV, WO)
        gather_start("y", WQKV)
        gather_start("z", WO)
        gather_wait("x", W1)
        gather_start("y", W1)
        gather_wait("y", WQKV)
        gather_start("z", WQKV)
        gather_wait("z", CWQKV, CWO)
        gather_start("core", CWQKV, CWO)
        gather_wait("z", WO)
        gather_start("y", WO)
        gather_wait("y", W1)
        gather_start("z", W1)
        for copy in bias_copies():
            copy.wait()
        gather_wait("core", CWQKV, CWO)
        wait_weights(0, 1, 2, 3, 4, 5)
        pl.loop(0, 2)(mid_relay)
        gather_wait("x", W2)
        gather_start("y", W2)
        mid_relay(2)

        @pl.when(set_of == 1)
        def _():
            gather_wait("y", WO)
            gather_wait("z", WQKV)
            gather_start("core", WQKV, WO)
            mid_relay(3)

        cross_forward(0)

        @pl.when(set_of == 0)
        def _():
            gather_wait("y", WO)
            gather_wait("z", WQKV)
            gather_start("core", WQKV, WO)
            mid_relay(3)

        cross_forward(1)
        gather_wait("core", WQKV, WO)
        attn_forward(0)
        gather_wait("z", W1)
        gather_start("core", W1)
        gather_wait("y", W2)
        gather_start("core", W2)
        attn_forward(1)
        pair(ffn_forward)
        pair(ffn_turn)
        pair(attn_backward)
        pair(cross_backward)
        pair(to_section_0)
        mate_wait(CMIXED, XLOW, MIXED, ALOW, ACT, DYF, DUP)
        pass_start(DYF)
        mate_start_all(DYC, CDQKV)
        ffn_piece(2)
        dw_start(IN_R, 0)
        ffn_piece(0)
        dw_start(IN_W, 0)
        dw_turn(IN_R, 0)
        dw_turn(IN_W, 0)
        pass_wait(DYF)
        pass_start(XLOW)
        ffn_piece(3)
        dw_start(OUT_R, 0)
        ffn_piece(1)
        dw_start(OUT_W, 0)
        dw_turn(OUT_R, 0)
        small_norms()
        for mod, (lo, hi) in enumerate(SPANS):
            bsum[mod] = column_sums(dup, lo, hi)
        dw_turn(OUT_W, 0)
        mate_wait(DYC)
        pass_start(DYC)
        mate_start_all(DYA, DQKV)
        for k in range(2):
            mid_finish(2 * (1 - set_of) + k)
        dw_turn(IN_R, 1)
        dw_turn(IN_W, 1)
        mate_wait(CDQKV)
        dw_turn(OUT_R, 1)
        pass_wait(DYC)
        cross_outer()
        dw_start(CROSS, 0)
        bqsum[2] = column_sums(cdqkv, 0, R)
        dw_turn(CROSS, 0)
        mate_wait(DYA)
        pass_start(DYA)
        dw_turn(OUT_W, 1)
        dw_turn(IN_R, 2)
        dw_turn(IN_W, 2)
        dw_turn(OUT_R, 2)
        mate_wait(DQKV)
        mate_start_all(YBUF)
        pass_wait(XLOW)
        pass_wait(DYA)
        for mod, (lo, hi) in enumerate(SPANS):
            bqsum[mod] = column_sums(dqkv, lo, hi)
        small_biases(32)
        attn_piece(2)
        attn_piece(3)
        dw_start(ATTN_R, 0)
        small_y(32)
        attn_piece(0)
        attn_piece(1)
        dw_start(ATTN_W, 0)
        dw_turn(CROSS, 1)
        dw_turn(ATTN_R, 0)
        small_z(32)
        dw_turn(ATTN_W, 0)
        dw_turn(OUT_W, 2)
        mate_wait(YBUF)
        pass_start(YBUF)
        dw_finish(CROSS, 2)
        small_last(32)
        pack[0, :24] = dw_ref[3, :24]
        pack[0, 24:] = s_ref[...]
        packet().start()
        dc_ref[...] = dw_ref[3, 24:]
        sc_ref[...] = s_ref[...]
        dw_turn(ATTN_R, 1)
        dw_turn(ATTN_W, 1)
        pass_wait(YBUF)
        for j in range(2):
            rows = back.at[block_of(j), pl.ds(0, 2 * C)]
            moved(rows, rows, back_send.at[j], back_recv.at[0], partner).wait_send()

    def write(m):
        @pl.when(head)
        def _():
            ag_finish(ybuf, m, x_send, y_recv)

        pltpu.make_async_copy(ybuf.at[m], y_out.at[m], out_sems.at[7 + m]).start()

    each(write)
    dw_finish(OUT_R, 3)
    dw_finish(IN_R, 3)
    dw_finish(IN_W, 3)
    dw_finish(OUT_W, 3)
    pl.when(head)(p(small_last, 16))
    dw_finish(ATTN_W, 2)
    dw_finish(ATTN_R, 2)
    for b in (0, 1, 2, 4, 5, 6):
        pltpu.make_async_copy(dw_ref.at[b], dw_out.at[b], out_sems.at[b]).wait()
    for m in range(MB):
        pltpu.make_async_copy(ybuf.at[m], y_out.at[m], out_sems.at[7 + m]).wait()
    pl.when(cross)(lambda: packet().wait_send())

    @pl.when(head)
    def _():
        packet().wait_recv()
        dc_ref[...] = pack[1, :24]
        sc_ref[...] = pack[1, 24:]


def arrange(
    y_ref, dw_ref, s_ref, dc_ref, sc_ref,
    words, regions, qkv_g, qv_bias_g, out_g, in_g, b1_g, ffo_g, obias_g, gain_g, shift_g,
    cqkv_g, cqv_bias_g, cout_g, cobias_g, cgain_g, cshift_g,
):
    place = lax.axis_index("dp")
    both = lax.axis_index("section") * 16 + place

    def from_column(rows, column):
        return pltpu.roll(rows, lax.rem(D - column, D), 1)

    for ref, (lo, hi), length in zip((words, regions), SPANS, (WORDS, REGIONS)):
        padded = y_ref[:, lo:hi, :].reshape(MB * (hi - lo), D)
        rows = dot(spread(hi - lo, length, True), padded)
        ref[0] = rows.reshape(length, ITEMS_LOCAL, D)
    small = s_ref[...]
    for mod in range(2):
        attn = dw_ref[4 * mod]
        for j in range(3):
            qkv_g[0, mod, j] = attn[:, j * HW : (j + 1) * HW]
        out_g[0, mod] = attn[:, 3 * HW :]
        in_g[0, mod] = dw_ref[5 + mod]
        ffo_g[0, mod] = dw_ref[1 + mod]
    columns = from_column(small, 48 * place)[:, :48]
    for mod in range(2):
        for l in range(2):
            for k, ref in enumerate((gain_g, shift_g, obias_g)):
                at = 2 * (3 * l + k) + mod
                ref[0, mod, l : l + 1, :] = columns[at : at + 1]
    columns = from_column(small, 8 * place)
    for mod in range(2):
        for k in range(6):
            b1_g[0, k, mod : mod + 1, :] = columns[12 + mod : 13 + mod, 128 * k : 128 * k + 8]
    columns = from_column(small, 4 * place)
    for mod in range(2):
        for j in range(2):
            for h in range(LOCAL_HEADS):
                lo = 2 * j * HW + h * HEAD_DIM
                qv_bias_g[0, mod, h, j : j + 1, :] = columns[14 + mod : 15 + mod, lo : lo + 4]
    wide = dc_ref[...]
    for j in range(3):
        cqkv_g[j] = wide[:, j * HW : (j + 1) * HW]
    cout_g[...] = wide[:, 3 * HW :]
    small = sc_ref[...]
    columns = from_column(small, 24 * both)
    for k, ref in enumerate((cgain_g, cshift_g, cobias_g)):
        ref[...] = columns[16 + k, :24]
    columns = from_column(small, 2 * both)[19:20]
    for j in range(2):
        heads = []
        for h in range(LOCAL_HEADS):
            lo = 2 * j * HW + h * HEAD_DIM
            heads.append(columns[:, lo : lo + 2])
        cqv_bias_g[j] = jnp.concatenate(heads, axis=0).T


def local(
    words, regions, word_lengths, task_flags, attn_qkv, attn_qv_bias, attn_out, ffn_in, ffn_in_bias,
    ffn_out, out_bias, norm_gain, norm_bias, cross_qkv, cross_qv_bias, cross_out, cross_out_bias,
    cross_norm_gain, cross_norm_bias,
):
    inputs = (
        words.transpose(0, 2, 1, 3), regions.transpose(0, 2, 1, 3), word_lengths, task_flags,
        attn_qkv.transpose(0, 1, 3, 4, 2).reshape(2, 3 * HW, D), attn_qv_bias.transpose(0, 1, 3, 2, 4), attn_out[0],
        ffn_in[0], ffn_in_bias.transpose(0, 2, 1, 3), ffn_out[0], out_bias, norm_gain, norm_bias,
        cross_qkv.transpose(1, 2, 0).reshape(3 * HW, D), cross_qv_bias.transpose(1, 0, 2), cross_out,
        cross_out_bias, cross_norm_gain, cross_norm_bias,
    )

    vmem = pl.BlockSpec(memory_space=pltpu.VMEM)
    hbm = pl.BlockSpec(memory_space=pl.ANY)
    mb_rows = lambda width, dtype: pltpu.VMEM((MB, R, width), dtype)
    own_rows = lambda count: pltpu.VMEM((count, MB, C, D), F32)
    y, g, s, dc, sc = pl.pallas_call(
        kernel,
        out_shape=(
            jax.ShapeDtypeStruct((MB, R, D), BF),
            jax.ShapeDtypeStruct((7, 48, D), F32),
            jax.ShapeDtypeStruct((24, D), F32),
            jax.ShapeDtypeStruct((24, D), F32),
            jax.ShapeDtypeStruct((24, D), F32),
        ),
        in_specs=[hbm] * len(inputs),
        out_specs=[hbm] * 2 + [vmem] * 3,
        scratch_shapes=[
            *[
                (pltpu.SMEM if k in (2, 3) else pltpu.VMEM)(inputs[k].shape, inputs[k].dtype)
                for k in (0, 1, 2, 3, 5, 8, 10, 11, 12, 14, 16, 17, 18)
            ],
            pltpu.SemaphoreType.DMA((13,)),
            pltpu.VMEM((7, 48, D), F32),
            pltpu.SemaphoreType.DMA((7 + MB,)),
            mb_rows(D, BF),
            pltpu.VMEM((3, 1, 3 * HW), F32),
            pltpu.VMEM((2, 1, D), F32),
            pltpu.VMEM((3, D), F32),
            mb_rows(D, BF),
            pltpu.VMEM((MB, TENSOR - 1, C, D), BF),
            *[mb_rows(D, BF) for _ in range(8)],
            pltpu.VMEM((3, MB, R, HW), BF),
            mb_rows(HW, BF),
            mb_rows(3 * HW, BF),
            pltpu.VMEM((3, MB, R, HW), BF),
            mb_rows(HW, BF),
            mb_rows(3 * HW, BF),
            mb_rows(D, BF),
            mb_rows(D, BF),
            mb_rows(D, F32),
            pltpu.VMEM((MB, 3 * RW, RW), F32),
            pltpu.VMEM((MB, 3 * RR, RR), F32),
            pltpu.VMEM((MB, 3 * RW, RR), F32),
            pltpu.VMEM((MB, 3 * RR, RW), F32),
            pltpu.VMEM((MB, C, D), F32),
            pltpu.VMEM((MB, C, D), F32),
            pltpu.VMEM((2, MB, C, D), F32),
            pltpu.VMEM((2, MB, C, 128), F32),
            pltpu.VMEM((MB, 16, D), BF),
            pltpu.VMEM((MB, 16, D), BF),
            pltpu.VMEM((C, D), F32),
            pltpu.VMEM((C, D), BF),
            pltpu.VMEM((2, 1, D), F32),
            pltpu.VMEM((3, 1, 3 * HW), F32),
            pltpu.VMEM((2, 3 * HW, D), BF),
            pltpu.VMEM((2, HW, D), BF),
            pltpu.VMEM((2, D, D), BF),
            pltpu.VMEM((2, D, D), BF),
            pltpu.VMEM((3 * HW, D), BF),
            pltpu.VMEM((HW, D), BF),
            pltpu.VMEM((2, 3 * HW, D), BF),
            pltpu.VMEM((2, HW, D), BF),
            pltpu.VMEM((2, D, D), BF),
            pltpu.VMEM((2, D, D), BF),
            pltpu.VMEM((3 * HW, D), BF),
            pltpu.VMEM((HW, D), BF),
            pltpu.VMEM((3, 1, 3 * HW), F32),
            pltpu.VMEM((2, 1, D), F32),
            pltpu.VMEM((2, 2, R, D), BF),
            pltpu.VMEM((2, 2, 16, D // 2), BF),
            pltpu.VMEM((2, 2, 2, 16, D // 2), BF),
            *[pltpu.VMEM((2, R, w), BF) for w in (D, D, HW, 3 * HW, HW, 3 * HW)],
            pltpu.VMEM((2, R, D), F32),
            pltpu.VMEM((2, R, D), F32),
            pltpu.VMEM((2, 2, R, D), F32),
            pltpu.VMEM((2, 2, R, 128), F32),
            pltpu.VMEM((16, 1, D), F32),
            pltpu.VMEM((7, 2, 4, 2, 48, D), BF),
            pltpu.VMEM((7, 2, 4, 48, D), BF),
            pltpu.VMEM((4, 4, 48, D), BF),
            pltpu.VMEM((3, 2, 48, D), BF),
            pltpu.VMEM((2, 3, 2, 48, D), BF),
            pltpu.VMEM((4, 3, 48, D), BF),
            pltpu.VMEM((3, 48, D), BF),
            pltpu.VMEM((3, 32, D), BF),
            pltpu.VMEM((32, D), F32),
            pltpu.VMEM((TENSOR, 16, D), F32),
            pltpu.VMEM((32, D), BF),
            pltpu.VMEM((32, D), BF),
            pltpu.VMEM((3, 32, D), BF),
            pltpu.VMEM((2, 48, D), F32),
            *[pltpu.SemaphoreType.DMA((MB,)) for _ in range(5)],
            pltpu.SemaphoreType.DMA((7,)),
            pltpu.SemaphoreType.DMA((7, 4)),
            pltpu.SemaphoreType.DMA((1,)),
            pltpu.SemaphoreType.DMA((4,)),
            pltpu.SemaphoreType.DMA,
            pltpu.SemaphoreType.DMA,
            pltpu.SemaphoreType.DMA((2,)),
            pltpu.SemaphoreType.DMA((MB,)),
            pltpu.SemaphoreType.DMA((2, 4)),
            pltpu.SemaphoreType.DMA((2, 2, 4)),
            *[pltpu.SemaphoreType.DMA((12,)) for _ in range(2)],
            pltpu.SemaphoreType.DMA((8,)),
            pltpu.SemaphoreType.DMA((7, 4)),
            *[pltpu.SemaphoreType.DMA((6,)) for _ in range(2)],
            pltpu.SemaphoreType.DMA((6,)),
        ],
        compiler_params=pltpu.CompilerParams(
            collective_id=0, has_side_effects=True, vmem_limit_bytes=63 * 2**20
        ),
    )(*inputs)

    shapes = (
        (1, WORDS, ITEMS_LOCAL, D), (1, REGIONS, ITEMS_LOCAL, D), (1, 2, 3, 48, HW),
        (1, 2, LOCAL_HEADS, 2, 4), (1, 2, 48, HW), (1, 2, 48, D), (1, 6, 2, 8), (1, 2, 48, D),
        (1, 2, 2, 48), (1, 2, 2, 48), (1, 2, 2, 48), (3, 24, HW), (2, 2, LOCAL_HEADS), (24, HW),
        (24,), (24,), (24,),
    )
    orders = {
        0: (0, 2, 1, 3), 1: (0, 2, 1, 3), 2: (0, 1, 3, 2, 4), 3: (0, 1, 3, 2, 4), 4: (0, 1, 3, 2),
        6: (0, 2, 1, 3), 7: (0, 1, 3, 2), 11: (1, 0, 2), 12: (0, 2, 1), 13: (1, 0),
    }
    outs = pl.pallas_call(
        arrange,
        out_shape=tuple(jax.ShapeDtypeStruct(shape, F32) for shape in shapes),
        in_specs=[vmem] * 5,
        out_specs=[vmem] * len(shapes),
        compiler_params=pltpu.CompilerParams(vmem_limit_bytes=60 * 2**20),
    )(y, g, s, dc, sc)
    return tuple(out.transpose(orders[k]) if k in orders else out for k, out in enumerate(outs))


def solution(mesh):
    in_specs = (
        P("section", "dp", None, None),
        P("section", "dp", None, None),
        P("dp"),
        P("dp"),
        P("section", None, None, None, "tensor"),
        P("section", None, None, "tensor", None),
        P("section", None, "tensor", None),
        P("section", None, None, "tensor"),
        P("section", None, "tensor", None),
        P("section", None, "tensor", None),
        P("section", None, None, None),
        P("section", None, None, None),
        P("section", None, None, None),
        P(None, None, "tensor"),
        P(None, "tensor", None),
        P("tensor", None),
        P(),
        P(),
        P(),
    )
    out_specs = (
        P("section", "dp", None, None),
        P("section", "dp", None, None),
        P("section", None, "dp", None, "tensor"),
        P("section", None, None, "tensor", "dp"),
        P("section", None, "tensor", "dp"),
        P("section", None, "dp", "tensor"),
        P("section", None, "tensor", "dp"),
        P("section", None, "tensor", "dp"),
        P("section", None, None, "dp"),
        P("section", None, None, "dp"),
        P("section", None, None, "dp"),
        P(("section", "dp"), None, "tensor"),
        P(None, "tensor", ("section", "dp")),
        P("tensor", ("section", "dp")),
        P(("section", "dp")),
        P(("section", "dp")),
        P(("section", "dp")),
    )
    return jax.shard_map(local, mesh=mesh, in_specs=in_specs, out_specs=out_specs, check_vma=False)
```

```python
import functools

import jax
import jax.numpy as jnp
from jax import lax
from jax.experimental import pallas as pl
from jax.experimental.pallas import tpu as pltpu
from jax.sharding import PartitionSpec as P

MESH = pl.DeviceIdType.MESH
BF = jnp.bfloat16
F32 = jnp.float32
HEAD_DIM = 64
LOCAL_HEADS = 3
HW = HEAD_DIM * LOCAL_HEADS
WORDS = 20
REGIONS = 36
D = 768
ITEMS_LOCAL = 8
TENSOR = 4

ITEMS_MB = 2
MB = ITEMS_LOCAL // ITEMS_MB
RW = 48
RR = 80
R = RW + RR
C = R // TENSOR
SPANS = ((0, RW), (RW, R))

EPSILON = 1e-06
MASKED = -1000000000.0
SCALING = HEAD_DIM ** (-0.5)


def dot(a, b):
    return lax.dot_general(a, b, (((1,), (0,)), ((), ())), preferred_element_type=F32)


def dot_nt(a, b):
    return lax.dot_general(a, b, (((1,), (1,)), ((), ())), preferred_element_type=F32)


def dot_tn(a, b):
    return lax.dot_general(a, b, (((0,), (0,)), ((), ())), preferred_element_type=F32)


def head_masks():
    lane = lax.broadcasted_iota(jnp.int32, (1, HW), 1)
    return [
        ((lane >= h * HEAD_DIM) & (lane < (h + 1) * HEAD_DIM)).astype(F32) for h in range(LOCAL_HEADS)
    ]


def by_head(a):
    masks = [m.astype(BF) for m in head_masks()]
    return jnp.concatenate([a * m for m in masks], axis=0)


def join_heads(stacked):
    rows = stacked.shape[0] // LOCAL_HEADS
    masks = head_masks()
    total = stacked[:rows] * masks[0]
    for h in range(1, LOCAL_HEADS):
        total = total + stacked[h * rows : (h + 1) * rows] * masks[h]
    return total


def item_of(shape, axis, length):
    index = lax.broadcasted_iota(jnp.int32, shape, axis)
    item = jnp.zeros(shape, jnp.int32)
    for k in range(1, ITEMS_MB + 1):
        item = item + (index >= k * length).astype(jnp.int32)
    return item


def spread(rows, length, transposed=False):
    count = ITEMS_LOCAL * length
    shape = (count, MB * rows) if transposed else (MB * rows, count)
    at = lax.broadcasted_iota(jnp.int32, shape, 0 if transposed else 1)
    padded = lax.broadcasted_iota(jnp.int32, shape, 1 if transposed else 0)
    item, position = at & (ITEMS_LOCAL - 1), at >> 3
    block, within = item >> (ITEMS_MB.bit_length() - 1), item & (ITEMS_MB - 1)
    target = block * rows + within * length + position
    return (target == padded).astype(F32).astype(BF)


def key_mask(q_rows, q_len, k_rows, k_len, lengths=None):
    shape = (q_rows, k_rows)
    item = item_of(shape, 1, k_len)
    key = lax.broadcasted_iota(jnp.int32, shape, 1)
    mask = (item_of(shape, 0, q_len) == item) & (key < ITEMS_MB * k_len)
    if lengths is not None:
        for k, length in enumerate(lengths):
            mask = mask & ((item != k) | (key < k * k_len + length))
    return mask


def attend(cases):
    masks = [jnp.concatenate([mask] * LOCAL_HEADS, axis=0) for _, _, _, mask in cases]
    scores = [dot_nt(by_head(q), k) * SCALING for q, k, _, _ in cases]
    scores = [jnp.where(mask, score, MASKED) for mask, score in zip(masks, scores)]
    es = [jnp.exp(score - jnp.max(score, axis=-1, keepdims=True)) for score in scores]
    probs = [e / jnp.sum(e, axis=-1, keepdims=True) for e in es]
    mixed = [dot(p.astype(BF), v) for p, (_, _, v, _) in zip(probs, cases)]
    return [(p, join_heads(mix).astype(BF)) for p, mix in zip(probs, mixed)]


def attend_back(cases):
    d3s = [by_head(dmix) for dmix, _, _, _, _ in cases]
    dps = [dot_nt(d3, v) for d3, (_, _, _, _, v) in zip(d3s, cases)]
    dss = [
        (probs * (dp - jnp.sum(probs * dp, axis=-1, keepdims=True))).astype(BF)
        for dp, (_, probs, _, _, _) in zip(dps, cases)
    ]
    dqs = [dot(ds, k) for ds, (_, _, _, k, _) in zip(dss, cases)]
    dks = [dot_tn(ds, by_head(q)) for ds, (_, _, q, _, _) in zip(dss, cases)]
    dvs = [dot_tn(probs.astype(BF), d3) for d3, (_, probs, _, _, _) in zip(d3s, cases)]
    return [
        ((join_heads(dq) * SCALING).astype(BF), (dk * SCALING).astype(BF), dv.astype(BF))
        for dq, dk, dv in zip(dqs, dks, dvs)
    ]


def split_qkv(out):
    return out[:, :HW], out[:, HW : 2 * HW], out[:, 2 * HW :]


def gelu(up):
    cdf = 0.5 * (1.0 + lax.erf(up * (0.5**0.5)))
    return (up * cdf).astype(BF), cdf + up * jnp.exp(-0.5 * up * up) * 0.3989422804014327


def norm_forward(r, gain, shift):
    center = r - jnp.mean(r, axis=-1, keepdims=True)
    spread = jnp.mean(center * center, axis=-1, keepdims=True)
    rstd = lax.rsqrt(spread + EPSILON)
    n = center * rstd
    return n, rstd, n * gain + shift


def norm_back(dh, n, rstd, gain):
    dn = dh * gain
    return rstd * (
        dn - jnp.mean(dn, axis=-1, keepdims=True) - n * jnp.mean(dn * n, axis=-1, keepdims=True)
    )


def kernel(
    words_hbm, regions_hbm, lengths_hbm, flags_hbm, wqkv_in, qv_bias_hbm, wo_in, w1_in, b1_in_hbm,
    w2_in, out_bias_hbm, gain_hbm, shift_hbm, cwqkv_in, cqv_bias_hbm, cwo_in, cout_bias_hbm,
    cgain_hbm, cshift_hbm,
    y_out, dw_out, s_ref, dc_ref, sc_ref,
    words_ref, regions_ref, lengths_ref, flags_ref, qv_bias_ref, b1_in_ref, out_bias_ref, gain_ref, shift_ref, cqv_bias_ref, cout_bias_ref, cgain_ref, cshift_ref,
    small_loads, dw_ref, out_sems, x_ref, bqkv_ref, b1_ref, cvec_ref, send, recv, xlow, midf, alow, dyf, dya, dyc, ybuf, back,
    qkv, mixed, dqkv, cqkv, cmixed, cdqkv, act, dup, dgelu,
    p_w, p_r, cp_w, cp_r, cur, res, nrm, rstd, packed, gathered_end, total_ref, low_ref, bsum, bqsum,
    wqkv_ref, wo_ref, w1_ref, w2_ref, cwqkv_ref, cwo_ref, wqkv_m, wo_m, w1_m, w2_m, cwqkv_m, cwo_m, bqkv_m, b1_m,
    got, tails, got_tails, act_m, dup_m, mixed_m, dqkv_m, cmixed_m, cdqkv_m, cur_f, res_f, nrm_f, rstd_f, row_sums,
    g_ref, from_core, from_y, from_zs, from_h, from_z, from_ys, sums, total, sums_t, sums_c, sums_y, sums_z, pack,
    x_send, rs_recv, ag_recv, y_recv, sec_recv,
    dw_send, dw_recv, sm_send, sm_recv, pk_send, pk_recv,
    back_send, back_recv, ar_send, ar_recv, mt_send, mt_recv, ga_send, ga_recv, ps_send, ps_recv, loads,
):
    p = functools.partial
    sec = lax.axis_index("section")
    me = lax.axis_index("tensor")
    head = sec == 0
    cross = sec == 1

    def peer(o):
        return {"tensor": lax.rem(me + o, TENSOR)}

    partner = {"section": 1 - sec}
    place = lax.axis_index("dp")
    y_at, z_at, core = place // 8, lax.rem(place // 2, 4), lax.rem(place, 2)

    def dp_device(y, z, c):
        return {"dp": (y * 4 + z) * 2 + c}

    other_core = dp_device(y_at, z_at, 1 - core)
    other_y = dp_device(1 - y_at, z_at, core)

    def z_next(o):
        return lax.rem(z_at + o, 4)

    weights = tuple(
        pltpu.make_async_copy(src, dst, loads.at[k])
        for k, (src, dst) in enumerate((
            (wqkv_in, wqkv_ref), (wo_in, wo_ref), (w1_in, w1_ref), (w2_in, w2_ref),
            (cwqkv_in, cwqkv_ref), (cwo_in, cwo_ref),
        ))
    )

    def load_weights(*which):
        for k in which:
            weights[k].start()

    def wait_weights(*which):
        for k in which:
            weights[k].wait()

    barrier = pltpu.get_barrier_semaphore()
    for o in range(1, TENSOR):
        pl.semaphore_signal(barrier, inc=1, device_id=peer(o), device_id_type=MESH)
    mate, halver = {"tensor": me + 1 - 2 * lax.rem(me, 2)}, {"tensor": 3 - me}
    set_of = lax.rem((me + 1) // 2, 2)
    for t in range(TENSOR):
        pl.semaphore_signal(
            barrier, inc=1, device_id={"section": 1 - sec, "tensor": t}, device_id_type=MESH
        )
    for device in (other_core, other_y, *(dp_device(y_at, z_next(o), core) for o in (1, 2, 3))):
        pl.semaphore_signal(barrier, inc=1, device_id=device, device_id_type=MESH)

    small_inputs = tuple(
        pltpu.make_async_copy(src, dst, small_loads.at[k])
        for k, (src, dst) in enumerate((
            (words_hbm, words_ref), (regions_hbm, regions_ref), (lengths_hbm, lengths_ref), (flags_hbm, flags_ref), (qv_bias_hbm, qv_bias_ref), (b1_in_hbm, b1_in_ref), (out_bias_hbm, out_bias_ref), (gain_hbm, gain_ref), (shift_hbm, shift_ref), (cqv_bias_hbm, cqv_bias_ref), (cout_bias_hbm, cout_bias_ref), (cgain_hbm, cgain_ref), (cshift_hbm, cshift_ref),
        ))
    )
    for copy in small_inputs:
        copy.start()
    load_weights(0, 1)

    def moved(src, dst, send_sem, recv_sem, device):
        return pltpu.make_async_remote_copy(
            src_ref=src, dst_ref=dst, send_sem=send_sem, recv_sem=recv_sem, device_id=device,
            device_id_type=MESH,
        )

    both_mods = slice(0, 2)
    half_columns = pl.ds(pl.multiple_of(core * (D // 2), D // 2), D // 2)

    def z_rows(z, count):
        return pl.ds(pl.multiple_of(z * count, count), count)

    gathered = (
        (cwqkv_in, cwqkv_m, 3 * HW // 4, False), (cwo_in, cwo_m, HW // 4, False),
        (wqkv_in, wqkv_m, 3 * HW // 4, True), (wo_in, wo_m, HW // 4, True),
        (w1_in, w1_m, D // 4, True), (w2_in, w2_m, D // 4, True),
    )
    CWQKV, CWO, WQKV, WO, W1, W2 = range(6)
    Y_FIRST = (WQKV, W1)

    def gather_copies(k, step):
        src, dst, count, by_mod = gathered[k]
        sems = lambda i: (ga_send.at[k], ga_recv.at[k, i])
        at = lambda mods, rows: (mods, rows, half_columns) if by_mod else (rows, half_columns)
        mine = at(y_at, z_rows(z_at, count))
        column = at(y_at, slice(0, 4 * count)) if by_mod else None
        if step == "x":
            part = column if k == W2 else mine
            return [moved(src.at[part], dst.at[part], *sems(0), mate)]
        if step == "y":
            place = dst.at[mine] if k in Y_FIRST else dst.at[column]
            return [moved(place, place, *sems(1), other_y)]
        if step == "z":
            place = dst.at[at(both_mods if k in Y_FIRST else y_at, z_rows(z_at, count))]
            return [
                moved(place, place, *sems(2), dp_device(y_at, z_next(o), core)) for o in (1, 2, 3)
            ]
        place = dst.at[at(both_mods, slice(0, 4 * count))]
        return [moved(place, place, *sems(3), other_core)]

    def gather_start(step, *arrays):
        for k in arrays:
            for copy in gather_copies(k, step):
                copy.start()

    def gather_wait(step, *arrays):
        for k in arrays:
            if step != "z":
                gather_copies(k, step)[0].wait()
                continue
            _, dst, count, by_mod = gathered[k]
            rows = slice(0, 3 * count)
            mods = both_mods if k in Y_FIRST else y_at
            place = dst.at[(mods, rows, half_columns) if by_mod else (rows, half_columns)]
            moved(place, place, ga_send.at[k], ga_recv.at[k, 2], mate).wait()

    @pl.when(cross)
    def _():
        pl.semaphore_wait(barrier, 12)
        gather_start("x", CWQKV, CWO, WQKV, WO, W1)

    for copy in small_inputs:
        copy.wait()
    load_weights(2, 3)
    pl.when(cross)(lambda: load_weights(4, 5))
    def side_by_side(rows):
        return jnp.concatenate(rows, axis=1)

    for mod in range(2):
        b1_ref[mod] = side_by_side(
            [b1_in_ref[0, k, mod : mod + 1, :] for k in range(D // 128)]
        )
    for k, ref in enumerate((qv_bias_ref.at[0, 0], qv_bias_ref.at[0, 1], cqv_bias_ref)):
        heads = lambda j: [ref[h, j : j + 1, :] for h in range(LOCAL_HEADS)]
        bqkv_ref[k] = side_by_side([*heads(0), jnp.zeros((1, HW), F32), *heads(1)])
    for k, ref in enumerate((cout_bias_ref, cgain_ref, cshift_ref)):
        cvec_ref[k : k + 1, :] = ref[...].reshape(1, D)

    for ref, (lo, hi), length in zip((words_ref, regions_ref), SPANS, (WORDS, REGIONS)):
        given = ref[0].astype(F32).reshape(ITEMS_LOCAL * length, D).astype(BF)
        placed = dot(spread(hi - lo, length), given).astype(BF)
        x_ref[:, lo:hi, :] = placed.reshape(MB, hi - lo, D)
    bsum[...] = jnp.zeros_like(bsum)
    bqsum[...] = jnp.zeros_like(bqsum)
    row_sums[...] = jnp.zeros_like(row_sums)


    def place_of(t, m):
        return lax.rem(t + m, TENSOR)

    def rows_at(at):
        return pl.ds(pl.multiple_of(48 * at - 16 * (at // 2), 16), C)

    def by_place(at, heavy, light):
        pl.when(at != 3)(heavy)
        pl.when(at == 3)(light)

    WORD_END, REGION_END = pl.ds(32, 16), pl.ds(112, 16)
    no_rows = jnp.zeros((8, D), F32)

    def pack_rows(words_end, regions_end):
        return jnp.concatenate([words_end, regions_end], axis=0).astype(BF)

    def wait_rows(m, ss, rs, sent, received):
        out, come = send.at[m, pl.ds(0, sent)], send.at[m, pl.ds(0, received)]
        moved(out, out, ss.at[m], rs.at[m], peer(1)).wait_send()
        moved(come, come, ss.at[m], rs.at[m], peer(1)).wait_recv()

    def own_rows_of(ref, m):
        at = place_of(me, m)

        def heavy():
            low_ref[...] = ref[m, rows_at(at)]

        def light():
            low_ref[0:16] = ref[m, WORD_END]
            low_ref[16:32] = ref[m, REGION_END]

        by_place(at, heavy, light)
        return low_ref[...]

    def put_own_rows(ref, m, low):
        at = place_of(me, m)

        def heavy():
            ref[m, rows_at(at)] = low

        def light():
            ref[m, WORD_END] = low[:16]
            ref[m, REGION_END] = low[16:]

        by_place(at, heavy, light)

    def put_parts(m, parts):
        for (lo, hi), part in zip(SPANS, parts):
            send[m, lo:hi] = part.astype(BF)
        packed[m] = pack_rows(parts[0][32:40], parts[1][64:72])

    def rs_start(m):
        for o in range(1, TENSOR):
            at = place_of(me + o, m)

            def heavy(o=o, at=at):
                src, dst = send.at[m, rows_at(at)], recv.at[m, o - 1]
                moved(src, dst, x_send.at[m], rs_recv.at[m], peer(o)).start()

            def light(o=o):
                src, dst = packed.at[m], recv.at[m, o - 1, pl.ds(0, 16)]
                moved(src, dst, x_send.at[m], rs_recv.at[m], peer(o)).start()

            by_place(at, heavy, light)

    def rs_finish(m):
        at = place_of(me, m)

        def heavy():
            wait_rows(m, x_send, rs_recv, 80, 96)
            total = send[m, rows_at(at)].astype(F32)
            for o in range(TENSOR - 1):
                total = total + recv[m, o].astype(F32)
            total_ref[...] = total

        def light():
            wait_rows(m, x_send, rs_recv, 96, 48)
            total = packed[m].astype(F32)
            for o in range(TENSOR - 1):
                total = total + recv[m, o, 0:16].astype(F32)
            total_ref[...] = jnp.concatenate([total[:8], no_rows, total[8:], no_rows], axis=0)

        by_place(at, heavy, light)
        return total_ref[...]

    def ag_start(buf, m, low, ss=x_send, rs=ag_recv):
        put_own_rows(buf, m, low)
        at = place_of(me, m)

        def heavy():
            rows = buf.at[m, rows_at(at)]
            for o in range(1, TENSOR):
                moved(rows, rows, ss.at[m], rs.at[m], peer(o)).start()

        def light():
            wide = low.astype(F32)
            gathered_end[m] = pack_rows(wide[:8], wide[16:24])
            for o in range(1, TENSOR):
                end = gathered_end.at[m]
                moved(end, end, ss.at[m], rs.at[m], peer(o)).start()

        by_place(at, heavy, light)

    def ag_finish(buf, m, ss=x_send, rs=ag_recv):
        def heavy():
            wait_rows(m, ss, rs, 96, 80)
            end = gathered_end[m].astype(F32)
            buf[m, WORD_END] = pack_rows(end[:8], no_rows)
            buf[m, REGION_END] = pack_rows(end[8:], no_rows)

        def light():
            wait_rows(m, ss, rs, 48, 96)

        by_place(place_of(me, m), heavy, light)

    def start_rows(ref, m, at, ss, rs, *devices):
        def heavy():
            rows = ref.at[m, rows_at(at)]
            for device in devices:
                moved(rows, rows, ss, rs, device).start()

        def light():
            for end in (WORD_END, REGION_END):
                rows = ref.at[m, end]
                for device in devices:
                    moved(rows, rows, ss, rs, device).start()

        by_place(at, heavy, light)

    def some_rows(ref, m, count, ss, rs):
        rows = ref.at[m, pl.ds(0, count)]
        return moved(rows, rows, ss, rs, partner)

    def mid_start(m):
        start_rows(midf, m, place_of(me, m), x_send.at[m], sec_recv.at[m], partner)

    def mid_relay(m):
        some_rows(midf, m, C, x_send.at[m], sec_recv.at[m]).wait_recv()
        start_rows(midf, m, place_of(me, m), x_send.at[m], ag_recv.at[m], peer(1), peer(2), peer(3))

    def mid_finish(m):
        some_rows(midf, m, 3 * C, x_send.at[m], ag_recv.at[m]).wait()

    def back_start(j):
        m = 2 * set_of + j
        for k in range(2):
            t = 2 * (me // 2) + k
            device = {"section": 1 - sec, "tensor": t}
            start_rows(back, m, place_of(t, m), back_send.at[j], back_recv.at[m], device)

    def back_arrive(m):
        some_rows(back, m, C, back_send.at[0], back_recv.at[m]).wait_recv()

    def save_norm(l, m, n, r):
        nrm[l, m] = n
        rstd[l, m] = jnp.broadcast_to(r, (C, 128))

    def own_words(m):
        at = place_of(me, m)
        count = jnp.where(at == 0, C, jnp.where(at == 3, C // 2, 0))
        return lax.broadcasted_iota(jnp.int32, (C, 1), 0) < count

    def own_param(ref, l, m):
        return jnp.where(own_words(m), ref[0, 0, l : l + 1, :], ref[0, 1, l : l + 1, :])

    def norm_step_back(l, m, dh):
        n = nrm[l, m]
        dr = norm_back(dh, n, rstd[l, m][:, :1], own_param(gain_ref, l, m))
        low = dr.astype(BF)
        words_only = own_words(m)
        for k, value in enumerate((dh * n, dh, low.astype(F32))):
            part = jnp.where(words_only, value, 0.0)
            at = 2 * (3 * l + k)
            row_sums[at] += jnp.sum(part, axis=0, keepdims=True)
            row_sums[at + 1] += jnp.sum(value - part, axis=0, keepdims=True)
        res[m] = dr
        return low

    def word_keys(m, q_rows, q_len):
        return key_mask(
            q_rows, q_len, RW, WORDS, [lengths_ref[ITEMS_MB * m + k] for k in range(ITEMS_MB)]
        )

    def region_keys(q_rows, q_len):
        return key_mask(q_rows, q_len, RR, REGIONS)

    def layer_a(m):
        xlow[m] = x_ref[m]
        cur[m] = own_rows_of(x_ref, m).astype(F32)
        outs = [
            (dot_nt(xlow[m, lo:hi], wqkv_ref[mod]) + bqkv_ref[mod]).astype(BF)
            for mod, (lo, hi) in enumerate(SPANS)
        ]
        for (lo, hi), out in zip(SPANS, outs):
            for k, part in enumerate(split_qkv(out)):
                qkv[k, m, lo:hi] = part
        masks = (word_keys(m, RW, WORDS), region_keys(RR, REGIONS))
        done = attend([(*split_qkv(out), mask) for out, mask in zip(outs, masks)])
        for (lo, hi), keep, (probs, mix) in zip(SPANS, (p_w, p_r), done):
            keep[m] = probs
            mixed[m, lo:hi] = mix
        put_parts(m, [dot(mix, wo_ref[mod]) for mod, (_, mix) in enumerate(done)])

    def layer_b(m):
        r = cur[m] + rs_finish(m) + own_param(out_bias_ref, 0, m)
        n, rs, h = norm_forward(r, own_param(gain_ref, 0, m), own_param(shift_ref, 0, m))
        save_norm(0, m, n, rs)
        cur[m] = h
        ag_start(alow, m, h.astype(BF))

    def layer_c(m):
        ag_finish(alow, m)
        ups = [dot(alow[m, lo:hi], w1_ref[mod]) + b1_ref[mod] for mod, (lo, hi) in enumerate(SPANS)]
        pairs = [gelu(up) for up in ups]
        put_parts(m, [dot(active, w2_ref[mod]) for mod, (active, _) in enumerate(pairs)])
        rs_start(m)
        for (lo, hi), (active, slope) in zip(SPANS, pairs):
            act[m, lo:hi] = active
            dgelu[m, lo:hi] = slope

    def layer_d(m):
        r = cur[m] + rs_finish(m) + own_param(out_bias_ref, 1, m)
        n, rs, h = norm_forward(r, own_param(gain_ref, 1, m), own_param(shift_ref, 1, m))
        save_norm(1, m, n, rs)
        return h

    def back_e(m, dh):
        ag_start(dyf, m, norm_step_back(1, m, dh))

    def back_f(m):
        ag_finish(dyf, m)
        dacts = [dot_nt(dyf[m, lo:hi], w2_ref[mod]) for mod, (lo, hi) in enumerate(SPANS)]
        ds = [(dact * dgelu[m, lo:hi]).astype(BF) for dact, (lo, hi) in zip(dacts, SPANS)]
        put_parts(m, [dot_nt(d, w1_ref[mod]) for mod, d in enumerate(ds)])
        rs_start(m)
        for mod, (lo, hi) in enumerate(SPANS):
            dup[m, lo:hi] = ds[mod]
            bsum[mod] += jnp.sum(ds[mod].astype(F32), axis=0, keepdims=True)

    def back_g(m):
        dh = res[m] + rs_finish(m)
        ag_start(dya, m, norm_step_back(0, m, dh))

    def back_h(m):
        ag_finish(dya, m)
        dmixs = [
            dot_nt(dya[m, lo:hi], wo_ref[mod]).astype(BF) for mod, (lo, hi) in enumerate(SPANS)
        ]
        grads = attend_back([
            (dmix, keep[m], *(qkv[k, m, lo:hi] for k in range(3)))
            for dmix, keep, (lo, hi) in zip(dmixs, (p_w, p_r), SPANS)
        ])
        ds = [jnp.concatenate(grad, axis=1) for grad in grads]
        put_parts(m, [dot(d, wqkv_ref[mod]) for mod, d in enumerate(ds)])
        rs_start(m)
        for mod, (lo, hi) in enumerate(SPANS):
            dqkv[m, lo:hi] = ds[mod]
            bqsum[mod] += jnp.sum(ds[mod].astype(F32), axis=0, keepdims=True)

    def block_of(j):
        return 2 * set_of + j

    def ar_copies(j, mod, turn):
        lo, hi = SPANS[mod]
        rows = slice(lo, hi - 16)
        sems = lambda k: (ar_send.at[j, 2 * mod + k], ar_recv.at[turn, j, 2 * mod + k])
        return [
            moved(send.at[j, rows], got.at[turn, j, rows], *sems(0), halver),
            moved(tails.at[j, mod], got_tails.at[turn, j, mod], *sems(1), halver),
        ]

    def ar_start(j, mod, turn, part):
        lo, hi = SPANS[mod]
        full = hi - lo - 16
        send[j, lo : hi - 16] = part[:full].astype(BF)
        tail = part[full : full + 8]
        tails[j, mod] = jnp.concatenate([tail[:, : D // 2], tail[:, D // 2 :]], axis=0).astype(BF)
        for copy in ar_copies(j, mod, turn):
            copy.start()

    def ar_finish(j, mod, turn):
        lo, hi = SPANS[mod]
        for copy in ar_copies(j, mod, turn):
            copy.wait()
        rows = send[j, lo : hi - 16].astype(F32) + got[turn, j, lo : hi - 16].astype(F32)
        tail = tails[j, mod].astype(F32) + got_tails[turn, j, mod].astype(F32)
        return jnp.concatenate([rows, jnp.concatenate([tail[:8], tail[8:]], axis=1), no_rows], axis=0)

    shared = (xlow, alow, dyf, dya, dyc, ybuf)
    for_mate = ((act_m, act), (dup_m, dup), (mixed_m, mixed), (dqkv_m, dqkv), (cmixed_m, cmixed), (cdqkv_m, cdqkv))
    XLOW, ALOW, DYF, DYA, DYC, YBUF, ACT, DUP, MIXED, DQKV, CMIXED, CDQKV = range(12)

    halves = (XLOW, DYF, DYA, DYC, YBUF)

    def half_rows(which):
        return pl.ds(pl.multiple_of(which * (R // 2), R // 2), R // 2)

    def mate_copy(k, j):
        if k < 6:
            src = dst = shared[k]
            src = src.at[block_of(j)]
        else:
            src, dst = for_mate[k - 6]
            src = src.at[j]
        dst = dst.at[block_of(j)]
        if k in halves:
            src, dst = src.at[half_rows(me // 2)], dst.at[half_rows(me // 2)]
        return moved(src, dst, mt_send.at[k], mt_recv.at[k], mate)

    def mate_start(j, *kinds):
        for k in kinds:
            mate_copy(k, j).start()

    def mate_start_all(*kinds):
        for k in kinds:
            for j in range(2):
                mate_copy(k, j).start()

    def mate_wait(*kinds):
        for k in kinds:
            place = (shared[k] if k < 6 else for_mate[k - 6][1]).at[pl.ds(2 * (1 - set_of), 2)]
            if k in halves:
                place = place.at[:, half_rows(me // 2)]
            moved(place, place, mt_send.at[k], mt_recv.at[k], mate).wait()

    def pass_copy(k):
        place = shared[k].at[pl.ds(2 * (1 - set_of), 2), half_rows(me // 2)]
        return moved(place, place, ps_send.at[k], ps_recv.at[k], halver)

    def pass_start(k):
        pass_copy(k).start()

    def pass_wait(k):
        pass_copy(k).wait()

    def bias_copies():
        return [
            moved(bqkv_ref, bqkv_m, ga_send.at[6], ga_recv.at[6, 0], mate),
            moved(b1_ref, b1_m, ga_send.at[7], ga_recv.at[6, 1], mate),
        ]

    def save_norm_f(l, j, lo, hi, n, r):
        nrm_f[l, j, lo:hi] = n
        rstd_f[l, j, lo:hi] = jnp.broadcast_to(r, (hi - lo, 128))

    def count_rows(l, mod, dh, n, low):
        for k, value in enumerate((dh * n, dh, low.astype(F32))):
            at = 12 + k if l == 2 else 2 * (3 * l + k) + mod
            row_sums[at] += jnp.sum(value, axis=0, keepdims=True)

    def cross_forward(j):
        m = block_of(j)
        mid_finish(m)
        mid = midf[m]
        shards = ((cwqkv_ref, bqkv_ref, cwo_ref, cmixed, m), (cwqkv_m, bqkv_m, cwo_m, cmixed_m, j))
        qkvs = []
        for sh, (w, bias, w_out, keep, at) in enumerate(shards):
            out = (dot_nt(mid, w[...]) + bias[2]).astype(BF)
            q, k, v = split_qkv(out)
            cqkv[0, 2 * sh + j], cqkv[1, 2 * sh + j], cqkv[2, 2 * sh + j] = q, k, v
            qkvs.append((q, k, v))
        for mod, (lo, hi) in enumerate(SPANS):
            others = slice(*SPANS[1 - mod])
            mask = region_keys(RW, WORDS) if mod == 0 else word_keys(m, RR, REGIONS)
            done = attend([(q[lo:hi], k[others], v[others], mask) for q, k, v in qkvs])
            part = None
            for sh, (w, bias, w_out, keep, at) in enumerate(shards):
                probs, mix = done[sh]
                (cp_w, cp_r)[mod][2 * sh + j] = probs
                keep[at, lo:hi] = mix
                one = dot(mix, w_out[...])
                part = one if part is None else part + one
            ar_start(j, mod, 0, part)
        mate_start(j, CMIXED)

    def attn_forward(j):
        m = block_of(j)
        shards = (
            (wqkv_ref, bqkv_ref, wo_ref, mixed, m), (wqkv_m, bqkv_m, wo_m, mixed_m, j),
        )
        for mod, (lo, hi) in enumerate(SPANS):
            r = midf[m, lo:hi].astype(F32) + ar_finish(j, mod, 0) + cvec_ref[0:1, :]
            n, rs, h = norm_forward(r, cvec_ref[1:2, :], cvec_ref[2:3, :])
            save_norm_f(1, j, lo, hi, n, rs)
            cur_f[j, lo:hi] = h
            low = h.astype(BF)
            xlow[m, lo:hi] = low
            outs = [(dot_nt(low, w[mod]) + bias[mod]).astype(BF) for w, bias, _, _, _ in shards]
            for sh, out in enumerate(outs):
                for k, part in enumerate(split_qkv(out)):
                    qkv[k, 2 * sh + j, lo:hi] = part
            mask = word_keys(m, RW, WORDS) if mod == 0 else region_keys(RR, REGIONS)
            done = attend([(*split_qkv(out), mask) for out in outs])
            part = None
            for sh, (w, bias, w_out, keep, at) in enumerate(shards):
                probs, mix = done[sh]
                (p_w, p_r)[mod][2 * sh + j] = probs
                keep[at, lo:hi] = mix
                one = dot(mix, w_out[mod])
                part = one if part is None else part + one
            ar_start(j, mod, 1, part)
        mate_start(j, XLOW, MIXED)

    def ffn_forward(j):
        m = block_of(j)
        shards = ((w1_ref, b1_ref, w2_ref, act, m), (w1_m, b1_m, w2_m, act_m, j))
        for mod, (lo, hi) in enumerate(SPANS):
            r = cur_f[j, lo:hi] + ar_finish(j, mod, 1) + out_bias_ref[0, mod, 0:1, :]
            n, rs, h = norm_forward(r, gain_ref[0, mod, 0:1, :], shift_ref[0, mod, 0:1, :])
            save_norm_f(0, j, lo, hi, n, rs)
            cur_f[j, lo:hi] = h
            low = h.astype(BF)
            alow[m, lo:hi] = low
            if mod == 0:
                pl.when(j == 0)(lambda: gather_wait("core", W1))
            ups = [dot(low, w[mod]) + bias[mod] for w, bias, _, _, _ in shards]
            pairs = [gelu(up) for up in ups]
            if mod == 0:
                pl.when(j == 0)(lambda: gather_wait("core", W2))
            ones = [dot(active, w_out[mod]) for (active, _), (_, _, w_out, _, _) in zip(pairs, shards)]
            ar_start(j, mod, 0, ones[0] + ones[1])
            for sh, (_, _, _, keep, at) in enumerate(shards):
                keep[at, lo:hi], dgelu[2 * sh + j, lo:hi] = pairs[sh]
        mate_start(j, ALOW, ACT)

    def ffn_turn(j):
        m = block_of(j)
        shards = ((w1_ref, w2_ref, dup, m), (w1_m, w2_m, dup_m, j))
        for mod, (lo, hi) in enumerate(SPANS):
            r = cur_f[j, lo:hi] + ar_finish(j, mod, 0) + out_bias_ref[0, mod, 1:2, :]
            gain = gain_ref[0, mod, 1:2, :]
            n, rs, h = norm_forward(r, gain, shift_ref[0, mod, 1:2, :])
            ybuf[m, lo:hi] = h.astype(BF)
            scale = scales(m, 1 - mod, hi - lo, (WORDS, REGIONS)[mod])
            dh = x_ref[m, lo:hi].astype(F32) * scale
            dr = norm_back(dh, n, rs, gain)
            res_f[j, lo:hi] = dr
            low = dr.astype(BF)
            dyf[m, lo:hi] = low
            dacts = [dot_nt(low, w_out[mod]) for _, w_out, _, _ in shards]
            ds = [(dact * dgelu[2 * sh + j, lo:hi]).astype(BF) for sh, dact in enumerate(dacts)]
            ones = [dot_nt(d, w_in[mod]) for d, (w_in, _, _, _) in zip(ds, shards)]
            ar_start(j, mod, 1, ones[0] + ones[1])
            for d, (_, _, keep, at) in zip(ds, shards):
                keep[at, lo:hi] = d
            count_rows(1, mod, dh, n, low)
        mate_start(j, DYF, DUP)

    def attn_backward(j):
        m = block_of(j)
        shards = ((wqkv_ref, wo_ref, dqkv, m), (wqkv_m, wo_m, dqkv_m, j))
        for mod, (lo, hi) in enumerate(SPANS):
            dh = res_f[j, lo:hi] + ar_finish(j, mod, 1)
            n = nrm_f[0, j, lo:hi]
            dr = norm_back(dh, n, rstd_f[0, j, lo:hi][:, :1], gain_ref[0, mod, 0:1, :])
            res_f[j, lo:hi] = dr
            low = dr.astype(BF)
            dya[m, lo:hi] = low
            dmixs = [dot_nt(low, w_out[mod]).astype(BF) for _, w_out, _, _ in shards]
            grads = attend_back([
                (dmix, (p_w, p_r)[mod][2 * sh + j], *(qkv[k, 2 * sh + j, lo:hi] for k in range(3)))
                for sh, dmix in enumerate(dmixs)
            ])
            part = None
            for grad, (w, _, keep, at) in zip(grads, shards):
                d = jnp.concatenate(grad, axis=1)
                keep[at, lo:hi] = d
                one = dot(d, w[mod])
                part = one if part is None else part + one
            ar_start(j, mod, 0, part)
            count_rows(0, mod, dh, n, low)

    def cross_backward(j):
        m = block_of(j)
        for mod, (lo, hi) in enumerate(SPANS):
            dh = res_f[j, lo:hi] + ar_finish(j, mod, 0)
            n = nrm_f[1, j, lo:hi]
            dr = norm_back(dh, n, rstd_f[1, j, lo:hi][:, :1], cvec_ref[1:2, :])
            res_f[j, lo:hi] = dr
            low = dr.astype(BF)
            dyc[m, lo:hi] = low
            count_rows(2, mod, dh, n, low)
        shards = ((cwqkv_ref, cwo_ref, cdqkv, m), (cwqkv_m, cwo_m, cdqkv_m, j))
        dmixs = [dot_nt(dyc[m], w_out[...]).astype(BF) for _, w_out, _, _ in shards]
        cases = []
        for sh, dmix in enumerate(dmixs):
            slot = 2 * sh + j
            q, k, v = cqkv[0, slot], cqkv[1, slot], cqkv[2, slot]
            cases.append((dmix[:RW], cp_w[slot], q[:RW], k[RW:], v[RW:]))
            cases.append((dmix[RW:], cp_r[slot], q[RW:], k[:RW], v[:RW]))
        grads = attend_back(cases)
        part = None
        for sh, (w, _, keep, at) in enumerate(shards):
            (dq_w, dk_r, dv_r), (dq_r, dk_w, dv_w) = grads[2 * sh : 2 * sh + 2]
            keep[at, :RW] = jnp.concatenate([dq_w, dk_w, dv_w], axis=1)
            keep[at, RW:] = jnp.concatenate([dq_r, dk_r, dv_r], axis=1)
            one = dot(keep[at], w[...])
            part = one if part is None else part + one
        for mod, (lo, hi) in enumerate(SPANS):
            ar_start(j, mod, 1, part[lo:hi])

    def to_section_0(j):
        m = block_of(j)
        for mod, (lo, hi) in enumerate(SPANS):
            back[m, lo:hi] = (res_f[j, lo:hi] + ar_finish(j, mod, 1)).astype(BF)
        back_start(j)

    def column_sums(buf, lo, hi):
        rows = buf[:, lo:hi, :].astype(F32).reshape(MB * (hi - lo), buf.shape[-1])
        return jnp.sum(rows, axis=0, keepdims=True)

    def scales(m, flag, count, length):
        index = lax.broadcasted_iota(jnp.int32, (count, 1), 0)
        scale = jnp.ones((count, 1), F32)
        for k in range(ITEMS_MB):
            value = jnp.where(flags_ref[ITEMS_MB * m + k] == flag, 0.25, 1.0)
            scale = jnp.where(index >= k * length, value, scale)
        return scale

    def outer_tile(left, right, lo, hi, j, store):
        start = j * (D // 2)
        columns = pl.ds(start if isinstance(j, int) else pl.multiple_of(start, D // 2), D // 2)
        a = left[:, lo:hi, columns].reshape(MB * (hi - lo), D // 2)
        b = right[:, lo:hi, :].reshape(MB * (hi - lo), right.shape[-1])
        store(dot_tn(a, b))

    def outer(left, right, lo, hi, store):
        pl.loop(0, 2)(
            lambda j: outer_tile(left, right, lo, hi, j, p(store, j))
        )

    def store_at(block, lo, hi):
        def store(j, value):
            g_ref[block, j, :, :, :, lo:hi] = value.astype(BF).reshape(4, 2, 48, hi - lo)

        return store

    def ffn_piece(k):
        mod, second = k // 2, k % 2
        left, right = ((alow, dup), (dyf, act))[second]
        outer(left, right, *SPANS[mod], store_at((5, 1)[second] + mod, 0, D))

    def attn_piece(k):
        mod, second = k // 2, k % 2
        left, right = ((xlow, dqkv), (dya, mixed))[second]
        outer(left, right, *SPANS[mod], store_at(4 * mod, *((0, 3 * HW), (3 * HW, D))[second]))

    def cross_outer():
        def store(j, lo, hi):
            def put(value):
                value = value.astype(BF).reshape(2, 4, 2, 24, hi - lo)
                g_ref[3, :, :, :, 24 * j : 24 * j + 24, lo:hi] = value

            return put

        for j in range(2):
            outer_tile(midf, cdqkv, 0, R, j, store(j, 0, 3 * HW))
            outer_tile(dyc, cmixed, 0, R, j, store(j, 3 * HW, D))

    Y, Z, EVEN, ODD, Y_EVEN, Y_ODD = range(6)
    even_z, odd_z = z_at + 1 - 2 * lax.rem(z_at, 2), 3 - z_at
    LAST = {Y: 2, Z: 2, EVEN: 3, ODD: 3, Y_EVEN: 3, Y_ODD: 3}
    Y_FIRST_KINDS = (Y, Y_EVEN, Y_ODD)

    def z_links(kind):
        return (even_z, odd_z) if kind in (EVEN, Y_EVEN) else (odd_z, even_z)

    def beyond(kind, near):
        return 3 - near if kind in (EVEN, Y_EVEN) else near + 1 - 2 * lax.rem(near, 2)

    def dw_copies(group, phase):
        index, kind, b = group
        sems = lambda k: (dw_send.at[index], dw_recv.at[index, k])
        if phase == 0:
            return [moved(g_ref.at[b, :, :, 1 - core], from_core.at[b], *sems(0), other_core)]
        to = lambda z: dp_device(y_at, z, core)
        if kind in Y_FIRST_KINDS and phase == 1:
            return [moved(g_ref.at[b, 1 - y_at, :, core], from_y.at[b], *sems(1), other_y)]
        if kind in (Y_EVEN, Y_ODD):
            near, far = z_links(kind)
            if phase == 3:
                return [moved(g_ref.at[b, y_at, far, core], from_z.at[b, 2], *sems(3), to(far))]
            return [
                moved(g_ref.at[b, y_at, z, core], from_z.at[b, k], *sems(2), to(near))
                for k, z in enumerate((near, beyond(kind, near)))
            ]
        if kind == Y:
            return [
                moved(
                    g_ref.at[b, y_at, z_next(o), core], from_z.at[b, o - 1], *sems(2),
                    dp_device(y_at, z_next(o), core),
                )
                for o in (1, 2, 3)
            ]
        if phase == LAST[kind]:
            src = g_ref.at[b, 1 - y_at, z_at, core]
            return [moved(src, from_ys.at[b - 4], *sems(1), other_y)]
        if kind == Z:
            return [
                moved(
                    g_ref.at[b, :, z_next(o), core], from_zs.at[o - 1], *sems(2),
                    dp_device(y_at, z_next(o), core),
                )
                for o in (1, 2, 3)
            ]
        near, far = z_links(kind)
        if phase == 1:
            return [
                moved(g_ref.at[b, :, z, core], from_h.at[b - 5, k], *sems(2), to(near))
                for k, z in enumerate((near, beyond(kind, near)))
            ]
        return [moved(g_ref.at[b, :, far, core], from_h.at[b - 5, 2], *sems(3), to(far))]

    def dw_start(group, phase):
        for copy in dw_copies(group, phase):
            copy.start()

    def dw_finish(group, phase):
        index, kind, b = group
        together = None
        if kind == Y and phase == 2:
            together = from_z.at[b]
        elif kind == Z and phase == 1:
            together = from_zs
        elif kind in (EVEN, ODD) and phase == 1:
            together = from_h.at[b - 5, pl.ds(0, 2)]
        elif kind in (Y_EVEN, Y_ODD) and phase == 2:
            together = from_z.at[b, pl.ds(0, 2)]
        if together is None:
            dw_copies(group, phase)[0].wait()
        else:
            moved(together, together, dw_send.at[index], dw_recv.at[index, 2], other_core).wait()

        def add(place, *others):
            total = g_ref[place].astype(F32)
            for other in others:
                total = total + other.astype(F32)
            return total

        if phase == 0:

            def sum_y(y):
                place = (b, y, slice(None), core)
                g_ref[place] = add(place, from_core[b, y]).astype(BF)

            pl.loop(0, 2)(sum_y)
            return
        mine = (b, y_at, z_at, core)
        if phase == LAST[kind]:
            if kind == Y:
                others = [from_z[b, o] for o in range(3)]
            elif kind in Y_FIRST_KINDS:
                others = [from_z[b, 2]]
            else:
                others = [from_ys[b - 4]]
            dw_ref[b] = add(mine, *others)
            if b != 3:
                pltpu.make_async_copy(dw_ref.at[b], dw_out.at[b], out_sems.at[b]).start()
            return
        every = slice(None)
        if kind in Y_FIRST_KINDS and phase == 1:
            sums_of = [((b, y_at, every, core), [from_y[b]])]
        elif kind in (Y_EVEN, Y_ODD):
            sums_of = [((b, y_at, z, core), [from_z[b, k]]) for k, z in enumerate((z_at, z_links(kind)[1]))]
        elif kind == Z:
            sums_of = [((b, every, z_at, core), [from_zs[o] for o in range(3)])]
        elif phase == 1:
            places = (z_at, z_links(kind)[1])
            sums_of = [((b, every, z, core), [from_h[b - 5, k]]) for k, z in enumerate(places)]
        else:
            sums_of = [((b, every, z_at, core), [from_h[b - 5, 2]])]
        for place, others in sums_of:
            g_ref[place] = add(place, *others).astype(BF)

    def dw_turn(group, phase):
        dw_finish(group, phase)
        dw_start(group, phase + 1)

    OUT_W, OUT_R, IN_W, IN_R = (0, Y_EVEN, 1), (1, Y_ODD, 2), (2, EVEN, 5), (3, ODD, 6)
    ATTN_W, ATTN_R, CROSS = (4, Y, 0), (5, Z, 4), (6, Y, 3)

    def sm_copies(step, count):
        sems = (sm_send.at[0], sm_recv.at[step])
        if step == 0:
            return [moved(sums_t.at[me], sums_t.at[me], *sems, peer(o)) for o in range(1, TENSOR)]
        rows = pl.ds(0, count)
        src = sums.at[step - 1, rows]
        if step == 1:
            return [moved(src, sums_c.at[rows], *sems, other_core)]
        if step == 2:
            return [moved(src, sums_y.at[rows], *sems, other_y)]
        return [
            moved(src, sums_z.at[o - 1, rows], *sems, dp_device(y_at, z_next(o), core)) for o in (1, 2, 3)
        ]

    def sm_start(step, count=32):
        for copy in sm_copies(step, count):
            copy.start()

    def sm_wait(step, count=32):
        if step in (0, 3):
            place = sums_z.at[:, pl.ds(0, count)] if step == 3 else sums_t.at[pl.ds(0, TENSOR - 1)]
            moved(place, place, sm_send.at[0], sm_recv.at[step], other_core).wait()
        else:
            sm_copies(step, count)[0].wait()

    def small_norms():
        counts = jnp.logical_or(head, me < 2)
        for k in range(15):
            sums_t[me, k : k + 1, :] = jnp.where(counts, row_sums[k], 0.0)
        sums_t[me, 15:16, :] = jnp.zeros((1, D), F32)
        sm_start(0)

    def small_biases(count):
        sm_wait(0)
        total[...] = jnp.zeros((32, D), F32)
        norms = sums_t[0] + sums_t[1] + sums_t[2] + sums_t[3]
        total[0:12] = norms[:12]
        total[16:19] = norms[12:15]
        for mod in range(2):
            total[12 + mod : 13 + mod, :] = bsum[mod]
            total[14 + mod : 15 + mod, : 3 * HW] = bqsum[mod]
        total[19:20, : 3 * HW] = bqsum[2]
        sums[0] = total[...].astype(BF)
        sm_start(1, count)

    def small_y(count):
        sm_wait(1, count)
        total[:count] = total[:count] + sums_c[:count].astype(F32)
        sums[1] = total[...].astype(BF)
        sm_start(2, count)

    def small_z(count):
        sm_wait(2, count)
        total[:count] = total[:count] + sums_y[:count].astype(F32)
        sums[2] = total[...].astype(BF)
        sm_start(3, count)

    def small_last(count):
        sm_wait(3, count)
        for o in range(3):
            total[:count] = total[:count] + sums_z[o, :count].astype(F32)
        s_ref[...] = total[:24]

    def packet():
        return moved(pack.at[0], pack.at[1], pk_send, pk_recv, partner)

    def each(*steps, first=0, last=MB, after=()):
        def body(m):
            for step in steps:
                step(m)
            for k, extra in enumerate(after):
                if extra is not None:
                    pl.when(m == first + k)(extra)

        pl.loop(first, last)(body)

    def then(*steps):
        def run():
            for step in steps:
                step()

        return run

    def pair(step):
        pl.loop(0, 2)(step)

    @pl.when(head)
    def _():
        def to_partner(m):
            put_own_rows(midf, m, layer_d(m).astype(BF))
            mid_start(m)

        def from_partner(m):
            some_rows(midf, m, C, x_send.at[m], sec_recv.at[m]).wait_send()
            back_arrive(m)
            back_e(m, own_rows_of(back, m).astype(F32))

        def last(m):
            ag_start(ybuf, m, (res[m] + rs_finish(m)).astype(BF), x_send, y_recv)

        front, rear = dict(first=0, last=2), dict(first=2, last=4)
        wait_weights(0, 1)
        each(
            layer_a,
            after=(
                None, then(p(pl.semaphore_wait, barrier, 12), p(rs_start, 0), p(rs_start, 1)),
            ),
        )
        layer_b(0)
        rs_start(2)
        layer_b(1)
        rs_start(3)
        layer_b(2)
        wait_weights(2, 3)
        each(layer_c, **front)
        layer_b(3)
        layer_c(2)
        each(to_partner, **front)
        layer_c(3)
        each(to_partner, **rear)
        each(from_partner, last=3)
        each(back_f, after=(p(from_partner, 3), None, p(back_g, 0)))
        ffn_piece(2)
        dw_start(IN_R, 0)
        back_g(1)
        ffn_piece(3)
        dw_start(OUT_R, 0)
        back_g(2)
        dw_turn(IN_R, 0)
        ffn_piece(0)
        dw_start(IN_W, 0)
        dw_turn(OUT_R, 0)
        ffn_piece(1)
        dw_start(OUT_W, 0)
        back_g(3)
        each(
            back_h,
            after=(
                then(p(dw_turn, IN_W, 0), p(dw_turn, OUT_W, 0)), small_norms,
            ),
        )
        attn_piece(2)
        attn_piece(3)
        dw_start(ATTN_R, 0)
        dw_turn(OUT_R, 1)
        dw_turn(IN_R, 1)
        attn_piece(0)
        dw_turn(ATTN_R, 0)
        attn_piece(1)
        dw_start(ATTN_W, 0)
        dw_turn(IN_W, 1)
        small_biases(16)
        dw_turn(ATTN_W, 0)
        small_y(16)
        each(last)
        dw_turn(OUT_W, 1)
        dw_turn(OUT_R, 2)
        dw_turn(IN_R, 2)
        dw_turn(IN_W, 2)
        dw_turn(OUT_W, 2)
        small_z(16)
        dw_turn(ATTN_W, 1)
        dw_turn(ATTN_R, 1)

    @pl.when(cross)
    def _():
        for copy in bias_copies():
            copy.start()
        gather_start("x", W2)
        gather_wait("x", CWQKV, CWO)
        gather_start("z", CWQKV, CWO)
        gather_wait("x", WQKV, WO)
        gather_start("y", WQKV)
        gather_start("z", WO)
        gather_wait("x", W1)
        gather_start("y", W1)
        gather_wait("y", WQKV)
        gather_start("z", WQKV)
        gather_wait("z", CWQKV, CWO)
        gather_start("core", CWQKV, CWO)
        gather_wait("z", WO)
        gather_start("y", WO)
        gather_wait("y", W1)
        gather_start("z", W1)
        for copy in bias_copies():
            copy.wait()
        gather_wait("core", CWQKV, CWO)
        wait_weights(0, 1, 2, 3, 4, 5)
        pl.loop(0, 2)(mid_relay)
        gather_wait("x", W2)
        gather_start("y", W2)
        mid_relay(2)

        @pl.when(set_of == 1)
        def _():
            gather_wait("y", WO)
            gather_wait("z", WQKV)
            gather_start("core", WQKV, WO)
            mid_relay(3)

        cross_forward(0)

        @pl.when(set_of == 0)
        def _():
            gather_wait("y", WO)
            gather_wait("z", WQKV)
            gather_start("core", WQKV, WO)
            mid_relay(3)

        cross_forward(1)
        gather_wait("core", WQKV, WO)
        attn_forward(0)
        gather_wait("z", W1)
        gather_start("core", W1)
        gather_wait("y", W2)
        gather_start("core", W2)
        attn_forward(1)
        pair(ffn_forward)
        pair(ffn_turn)
        pair(attn_backward)
        pair(cross_backward)
        pair(to_section_0)
        mate_wait(CMIXED, XLOW, MIXED, ALOW, ACT, DYF, DUP)
        pass_start(DYF)
        mate_start_all(DYC, CDQKV)
        ffn_piece(2)
        dw_start(IN_R, 0)
        ffn_piece(0)
        dw_start(IN_W, 0)
        dw_turn(IN_R, 0)
        dw_turn(IN_W, 0)
        pass_wait(DYF)
        pass_start(XLOW)
        ffn_piece(3)
        dw_start(OUT_R, 0)
        ffn_piece(1)
        dw_start(OUT_W, 0)
        dw_turn(OUT_R, 0)
        small_norms()
        for mod, (lo, hi) in enumerate(SPANS):
            bsum[mod] = column_sums(dup, lo, hi)
        dw_turn(OUT_W, 0)
        mate_wait(DYC)
        pass_start(DYC)
        mate_start_all(DYA, DQKV)
        for k in range(2):
            mid_finish(2 * (1 - set_of) + k)
        dw_turn(IN_R, 1)
        dw_turn(IN_W, 1)
        mate_wait(CDQKV)
        dw_turn(OUT_R, 1)
        pass_wait(DYC)
        cross_outer()
        dw_start(CROSS, 0)
        bqsum[2] = column_sums(cdqkv, 0, R)
        dw_turn(CROSS, 0)
        mate_wait(DYA)
        pass_start(DYA)
        dw_turn(OUT_W, 1)
        dw_turn(IN_R, 2)
        dw_turn(IN_W, 2)
        dw_turn(OUT_R, 2)
        mate_wait(DQKV)
        mate_start_all(YBUF)
        pass_wait(XLOW)
        pass_wait(DYA)
        for mod, (lo, hi) in enumerate(SPANS):
            bqsum[mod] = column_sums(dqkv, lo, hi)
        small_biases(32)
        attn_piece(2)
        attn_piece(3)
        dw_start(ATTN_R, 0)
        small_y(32)
        attn_piece(0)
        attn_piece(1)
        dw_start(ATTN_W, 0)
        dw_turn(CROSS, 1)
        dw_turn(ATTN_R, 0)
        small_z(32)
        dw_turn(ATTN_W, 0)
        dw_turn(OUT_W, 2)
        mate_wait(YBUF)
        pass_start(YBUF)
        dw_finish(CROSS, 2)
        small_last(32)
        pack[0, :24] = dw_ref[3, :24]
        pack[0, 24:] = s_ref[...]
        packet().start()
        dc_ref[...] = dw_ref[3, 24:]
        sc_ref[...] = s_ref[...]
        dw_turn(ATTN_R, 1)
        dw_turn(ATTN_W, 1)
        pass_wait(YBUF)
        for j in range(2):
            rows = back.at[block_of(j), pl.ds(0, 2 * C)]
            moved(rows, rows, back_send.at[j], back_recv.at[0], partner).wait_send()

    def write(m):
        @pl.when(head)
        def _():
            ag_finish(ybuf, m, x_send, y_recv)

        pltpu.make_async_copy(ybuf.at[m], y_out.at[m], out_sems.at[7 + m]).start()

    each(write)
    dw_finish(OUT_R, 3)
    dw_finish(IN_R, 3)
    dw_finish(IN_W, 3)
    dw_finish(OUT_W, 3)
    pl.when(head)(p(small_last, 16))
    dw_finish(ATTN_W, 2)
    dw_finish(ATTN_R, 2)
    for b in (0, 1, 2, 4, 5, 6):
        pltpu.make_async_copy(dw_ref.at[b], dw_out.at[b], out_sems.at[b]).wait()
    for m in range(MB):
        pltpu.make_async_copy(ybuf.at[m], y_out.at[m], out_sems.at[7 + m]).wait()
    pl.when(cross)(lambda: packet().wait_send())

    @pl.when(head)
    def _():
        packet().wait_recv()
        dc_ref[...] = pack[1, :24]
        sc_ref[...] = pack[1, 24:]


def arrange(
    y_ref, dw_ref, s_ref, dc_ref, sc_ref,
    words, regions, qkv_g, qv_bias_g, out_g, in_g, b1_g, ffo_g, obias_g, gain_g, shift_g,
    cqkv_g, cqv_bias_g, cout_g, cobias_g, cgain_g, cshift_g,
):
    place = lax.axis_index("dp")
    both = lax.axis_index("section") * 16 + place

    def from_column(rows, column):
        return pltpu.roll(rows, lax.rem(D - column, D), 1)

    for ref, (lo, hi), length in zip((words, regions), SPANS, (WORDS, REGIONS)):
        padded = y_ref[:, lo:hi, :].reshape(MB * (hi - lo), D)
        rows = dot(spread(hi - lo, length, True), padded)
        ref[0] = rows.reshape(length, ITEMS_LOCAL, D)
    small = s_ref[...]
    for mod in range(2):
        attn = dw_ref[4 * mod]
        for j in range(3):
            qkv_g[0, mod, j] = attn[:, j * HW : (j + 1) * HW]
        out_g[0, mod] = attn[:, 3 * HW :]
        in_g[0, mod] = dw_ref[5 + mod]
        ffo_g[0, mod] = dw_ref[1 + mod]
    columns = from_column(small, 48 * place)[:, :48]
    for mod in range(2):
        for l in range(2):
            for k, ref in enumerate((gain_g, shift_g, obias_g)):
                at = 2 * (3 * l + k) + mod
                ref[0, mod, l : l + 1, :] = columns[at : at + 1]
    columns = from_column(small, 8 * place)
    for mod in range(2):
        for k in range(6):
            b1_g[0, k, mod : mod + 1, :] = columns[12 + mod : 13 + mod, 128 * k : 128 * k + 8]
    columns = from_column(small, 4 * place)
    for mod in range(2):
        for j in range(2):
            for h in range(LOCAL_HEADS):
                lo = 2 * j * HW + h * HEAD_DIM
                qv_bias_g[0, mod, h, j : j + 1, :] = columns[14 + mod : 15 + mod, lo : lo + 4]
    wide = dc_ref[...]
    for j in range(3):
        cqkv_g[j] = wide[:, j * HW : (j + 1) * HW]
    cout_g[...] = wide[:, 3 * HW :]
    small = sc_ref[...]
    columns = from_column(small, 24 * both)
    for k, ref in enumerate((cgain_g, cshift_g, cobias_g)):
        ref[...] = columns[16 + k, :24]
    columns = from_column(small, 2 * both)[19:20]
    for j in range(2):
        heads = []
        for h in range(LOCAL_HEADS):
            lo = 2 * j * HW + h * HEAD_DIM
            heads.append(columns[:, lo : lo + 2])
        cqv_bias_g[j] = jnp.concatenate(heads, axis=0).T


def local(
    words, regions, word_lengths, task_flags, attn_qkv, attn_qv_bias, attn_out, ffn_in, ffn_in_bias,
    ffn_out, out_bias, norm_gain, norm_bias, cross_qkv, cross_qv_bias, cross_out, cross_out_bias,
    cross_norm_gain, cross_norm_bias,
):
    inputs = (
        words.transpose(0, 2, 1, 3), regions.transpose(0, 2, 1, 3), word_lengths, task_flags,
        attn_qkv.transpose(0, 1, 3, 4, 2).reshape(2, 3 * HW, D), attn_qv_bias.transpose(0, 1, 3, 2, 4), attn_out[0],
        ffn_in[0], ffn_in_bias.transpose(0, 2, 1, 3), ffn_out[0], out_bias, norm_gain, norm_bias,
        cross_qkv.transpose(1, 2, 0).reshape(3 * HW, D), cross_qv_bias.transpose(1, 0, 2), cross_out,
        cross_out_bias, cross_norm_gain, cross_norm_bias,
    )

    vmem = pl.BlockSpec(memory_space=pltpu.VMEM)
    hbm = pl.BlockSpec(memory_space=pl.ANY)
    mb_rows = lambda width, dtype: pltpu.VMEM((MB, R, width), dtype)
    own_rows = lambda count: pltpu.VMEM((count, MB, C, D), F32)
    y, g, s, dc, sc = pl.pallas_call(
        kernel,
        out_shape=(
            jax.ShapeDtypeStruct((MB, R, D), BF),
            jax.ShapeDtypeStruct((7, 48, D), F32),
            jax.ShapeDtypeStruct((24, D), F32),
            jax.ShapeDtypeStruct((24, D), F32),
            jax.ShapeDtypeStruct((24, D), F32),
        ),
        in_specs=[hbm] * len(inputs),
        out_specs=[hbm] * 2 + [vmem] * 3,
        scratch_shapes=[
            *[
                (pltpu.SMEM if k in (2, 3) else pltpu.VMEM)(inputs[k].shape, inputs[k].dtype)
                for k in (0, 1, 2, 3, 5, 8, 10, 11, 12, 14, 16, 17, 18)
            ],
            pltpu.SemaphoreType.DMA((13,)),
            pltpu.VMEM((7, 48, D), F32),
            pltpu.SemaphoreType.DMA((7 + MB,)),
            mb_rows(D, BF),
            pltpu.VMEM((3, 1, 3 * HW), F32),
            pltpu.VMEM((2, 1, D), F32),
            pltpu.VMEM((3, D), F32),
            mb_rows(D, BF),
            pltpu.VMEM((MB, TENSOR - 1, C, D), BF),
            *[mb_rows(D, BF) for _ in range(8)],
            pltpu.VMEM((3, MB, R, HW), BF),
            mb_rows(HW, BF),
            mb_rows(3 * HW, BF),
            pltpu.VMEM((3, MB, R, HW), BF),
            mb_rows(HW, BF),
            mb_rows(3 * HW, BF),
            mb_rows(D, BF),
            mb_rows(D, BF),
            mb_rows(D, F32),
            pltpu.VMEM((MB, 3 * RW, RW), F32),
            pltpu.VMEM((MB, 3 * RR, RR), F32),
            pltpu.VMEM((MB, 3 * RW, RR), F32),
            pltpu.VMEM((MB, 3 * RR, RW), F32),
            pltpu.VMEM((MB, C, D), F32),
            pltpu.VMEM((MB, C, D), F32),
            pltpu.VMEM((2, MB, C, D), F32),
            pltpu.VMEM((2, MB, C, 128), F32),
            pltpu.VMEM((MB, 16, D), BF),
            pltpu.VMEM((MB, 16, D), BF),
            pltpu.VMEM((C, D), F32),
            pltpu.VMEM((C, D), BF),
            pltpu.VMEM((2, 1, D), F32),
            pltpu.VMEM((3, 1, 3 * HW), F32),
            pltpu.VMEM((2, 3 * HW, D), BF),
            pltpu.VMEM((2, HW, D), BF),
            pltpu.VMEM((2, D, D), BF),
            pltpu.VMEM((2, D, D), BF),
            pltpu.VMEM((3 * HW, D), BF),
            pltpu.VMEM((HW, D), BF),
            pltpu.VMEM((2, 3 * HW, D), BF),
            pltpu.VMEM((2, HW, D), BF),
            pltpu.VMEM((2, D, D), BF),
            pltpu.VMEM((2, D, D), BF),
            pltpu.VMEM((3 * HW, D), BF),
            pltpu.VMEM((HW, D), BF),
            pltpu.VMEM((3, 1, 3 * HW), F32),
            pltpu.VMEM((2, 1, D), F32),
            pltpu.VMEM((2, 2, R, D), BF),
            pltpu.VMEM((2, 2, 16, D // 2), BF),
            pltpu.VMEM((2, 2, 2, 16, D // 2), BF),
            *[pltpu.VMEM((2, R, w), BF) for w in (D, D, HW, 3 * HW, HW, 3 * HW)],
            pltpu.VMEM((2, R, D), F32),
            pltpu.VMEM((2, R, D), F32),
            pltpu.VMEM((2, 2, R, D), F32),
            pltpu.VMEM((2, 2, R, 128), F32),
            pltpu.VMEM((16, 1, D), F32),
            pltpu.VMEM((7, 2, 4, 2, 48, D), BF),
            pltpu.VMEM((7, 2, 4, 48, D), BF),
            pltpu.VMEM((4, 4, 48, D), BF),
            pltpu.VMEM((3, 2, 48, D), BF),
            pltpu.VMEM((2, 3, 2, 48, D), BF),
            pltpu.VMEM((4, 3, 48, D), BF),
            pltpu.VMEM((3, 48, D), BF),
            pltpu.VMEM((3, 32, D), BF),
            pltpu.VMEM((32, D), F32),
            pltpu.VMEM((TENSOR, 16, D), F32),
            pltpu.VMEM((32, D), BF),
            pltpu.VMEM((32, D), BF),
            pltpu.VMEM((3, 32, D), BF),
            pltpu.VMEM((2, 48, D), F32),
            *[pltpu.SemaphoreType.DMA((MB,)) for _ in range(5)],
            pltpu.SemaphoreType.DMA((7,)),
            pltpu.SemaphoreType.DMA((7, 4)),
            pltpu.SemaphoreType.DMA((1,)),
            pltpu.SemaphoreType.DMA((4,)),
            pltpu.SemaphoreType.DMA,
            pltpu.SemaphoreType.DMA,
            pltpu.SemaphoreType.DMA((2,)),
            pltpu.SemaphoreType.DMA((MB,)),
            pltpu.SemaphoreType.DMA((2, 4)),
            pltpu.SemaphoreType.DMA((2, 2, 4)),
            *[pltpu.SemaphoreType.DMA((12,)) for _ in range(2)],
            pltpu.SemaphoreType.DMA((8,)),
            pltpu.SemaphoreType.DMA((7, 4)),
            *[pltpu.SemaphoreType.DMA((6,)) for _ in range(2)],
            pltpu.SemaphoreType.DMA((6,)),
        ],
        compiler_params=pltpu.CompilerParams(
            collective_id=0, has_side_effects=True, vmem_limit_bytes=63 * 2**20
        ),
    )(*inputs)

    shapes = (
        (1, WORDS, ITEMS_LOCAL, D), (1, REGIONS, ITEMS_LOCAL, D), (1, 2, 3, 48, HW),
        (1, 2, LOCAL_HEADS, 2, 4), (1, 2, 48, HW), (1, 2, 48, D), (1, 6, 2, 8), (1, 2, 48, D),
        (1, 2, 2, 48), (1, 2, 2, 48), (1, 2, 2, 48), (3, 24, HW), (2, 2, LOCAL_HEADS), (24, HW),
        (24,), (24,), (24,),
    )
    orders = {
        0: (0, 2, 1, 3), 1: (0, 2, 1, 3), 2: (0, 1, 3, 2, 4), 3: (0, 1, 3, 2, 4), 4: (0, 1, 3, 2),
        6: (0, 2, 1, 3), 7: (0, 1, 3, 2), 11: (1, 0, 2), 12: (0, 2, 1), 13: (1, 0),
    }
    outs = pl.pallas_call(
        arrange,
        out_shape=tuple(jax.ShapeDtypeStruct(shape, F32) for shape in shapes),
        in_specs=[vmem] * 5,
        out_specs=[vmem] * len(shapes),
        compiler_params=pltpu.CompilerParams(vmem_limit_bytes=60 * 2**20),
    )(y, g, s, dc, sc)
    return tuple(out.transpose(orders[k]) if k in orders else out for k, out in enumerate(outs))


def solution(mesh):
    in_specs = (
        P("section", "dp", None, None),
        P("section", "dp", None, None),
        P("dp"),
        P("dp"),
        P("section", None, None, None, "tensor"),
        P("section", None, None, "tensor", None),
        P("section", None, "tensor", None),
        P("section", None, None, "tensor"),
        P("section", None, "tensor", None),
        P("section", None, "tensor", None),
        P("section", None, None, None),
        P("section", None, None, None),
        P("section", None, None, None),
        P(None, None, "tensor"),
        P(None, "tensor", None),
        P("tensor", None),
        P(),
        P(),
        P(),
    )
    out_specs = (
        P("section", "dp", None, None),
        P("section", "dp", None, None),
        P("section", None, "dp", None, "tensor"),
        P("section", None, None, "tensor", "dp"),
        P("section", None, "tensor", "dp"),
        P("section", None, "dp", "tensor"),
        P("section", None, "tensor", "dp"),
        P("section", None, "tensor", "dp"),
        P("section", None, None, "dp"),
        P("section", None, None, "dp"),
        P("section", None, None, "dp"),
        P(("section", "dp"), None, "tensor"),
        P(None, "tensor", ("section", "dp")),
        P("tensor", ("section", "dp")),
        P(("section", "dp")),
        P(("section", "dp")),
        P(("section", "dp")),
    )
    return jax.shard_map(local, mesh=mesh, in_specs=in_specs, out_specs=out_specs, check_vma=False)
```
